32 devices in a mesh: gx: 8 (over y, x, core), gy: 4 (over z).
Axes of the slice: x: 2, y: 2, z: 4, core: 2. Of those that a mesh axis runs over, the one named last changes fastest.
Arguments:
- fields: float32 [3, 16, 256, 512], P(None, None, 'gx', 'gy'), may hold values from -5 to 5
- levels: int32 [8], replicated, may hold values from 0 to 15, as said below
- cuts: int32 [3, 8], replicated, may hold values from 8 to 32
- parent_modes: float32 [32, 2, 24, 4096], P(('gx', 'gy')), may hold values from -24 to 24
- owners: int32 [2], replicated, may hold values from 0 to 31
- plume: float32 [16, 256, 512], P(None, 'gx', 'gy'), may hold values from 0 to 2
- source: float32 [16, 256, 512], P(None, 'gx', 'gy'), may hold values from 0 to 1
Outputs:
- fields_out: float32 [3, 16, 256, 512], P(None, None, 'gx', 'gy')
- plume_out: float32 [16, 256, 512], P(None, 'gx', 'gy')
The draws below stay inside these ranges and needn't reach their ends.
Inputs may be any that keep to these rules, and one draw needn't show every extreme that they name: 8 distinct level indices; the first and last model levels are always among them.
All inputs are finite; a program needn't handle non-finite values.
Results may differ from the reference program's by a relative error of at most 0.0001.
Values sent between devices are 32-bit elements; how exact they have to be, the bound alone decides.
No kernel may reach another device: no remote copies, remote signals or barrier semaphores. Data moves between devices by JAX's collectives and lax.ppermute only.
A program may use at most 64 MiB of HBM per device.

```python
import math
import jax
import jax.numpy as jnp
from jax import lax

KX = 32
LEV = 8
LEVALL = 16
STEPS = 2
NX = 256
NY = 512
N_GX = 8
N_GY = 4


def draw_levels(key, part):
    key = jax.random.fold_in(key, 11)
    first_key, second_key = jax.random.split(key)
    middle = 1 + jax.random.permutation(first_key, LEVALL - 2)[:LEV - 2]
    chosen = jnp.concatenate([jnp.array([LEVALL - 1, 0], dtype=jnp.int32), middle.astype(jnp.int32)])
    order = jax.random.permutation(second_key, LEV)
    return chosen[order].astype(jnp.int32)


def place_ends(result, key, least, top_value):
    spot = [jax.random.randint(jax.random.fold_in(key, axis), (), 0, length) for axis, length in enumerate(result.shape)]
    widest = result.shape.index(max(result.shape))
    neighbour = spot[:widest] + [(spot[widest] + 1) % result.shape[widest]] + spot[widest + 1:]
    return result.at[tuple(spot)].set(least).at[tuple(neighbour)].set(top_value)


def level_of(stream_key, extent, cuts, low, top_value):
    level, own = 1.0, jax.random.fold_in(stream_key, 6)
    for dim, parts in cuts:
        heights = jnp.exp(jax.random.uniform(jax.random.fold_in(own, dim), (parts,), jnp.float32, low / len(cuts), top_value / len(cuts)))
        level = level * jnp.repeat(heights, extent[dim] // parts).reshape([-1 if axis == dim else 1 for axis in range(len(extent))])
    return level


def centred(key, dims, spread, bound, cuts=(), held_as=jnp.bfloat16):
    drawn = jax.random.normal(key, dims, jnp.float32) * spread
    if len(cuts) > 0:
        drawn = level_of(key, dims, cuts, -0.22, 0.18) * drawn
    return jnp.clip(drawn, min=-bound, max=bound).astype(held_as)


def setup_inputs(seed: int = 0) -> dict:
    splits = jax.random.split(jax.random.key(seed), 8)
    fields = centred(splits[0], (3, LEVALL, NX, NY), 1.0, 5.0, ((2, 8), (3, 4)), jnp.float32)
    levels = draw_levels(jax.random.fold_in(splits[7], 71), 0)
    cuts = place_ends(jax.random.randint(splits[2], (3, LEV), KX // 4, KX + 1), jax.random.fold_in(splits[2], 1), KX // 4, KX).astype(jnp.int32)
    parent_modes = centred(splits[3], (N_GX * N_GY, STEPS, 3 * LEV, 4 * KX * KX), 4.0, 24.0, ((0, 32),), jnp.float32)
    owners = jax.random.randint(splits[4], (STEPS,), 0, N_GX * N_GY).astype(jnp.int32)
    plume = jnp.clip(2.0 * jax.random.uniform(splits[5], (LEVALL, NX, NY), jnp.float32) ** level_of(splits[5], (LEVALL, NX, NY), ((1, 8), (2, 4)), -0.2, 0.2), 0.0, 2.0)
    source = jnp.clip(1.0 * jax.random.uniform(splits[6], (LEVALL, NX, NY), jnp.float32) ** level_of(splits[6], (LEVALL, NX, NY), ((1, 8), (2, 4)), -0.2, 0.2), 0.0, 1.0)
    return dict(fields=fields, levels=levels, cuts=cuts, parent_modes=parent_modes, owners=owners, plume=plume, source=source)


def tables(length_cells, first_cell, period):
    wavenum = jnp.arange(KX, dtype=jnp.int32)[:, None]
    position = first_cell + jnp.arange(length_cells, dtype=jnp.int32)[None, :]
    phase = (wavenum * position % period).astype(jnp.float32) * (2.0 * math.pi / period)
    return jnp.concatenate([jnp.cos(phase), jnp.sin(phase)], axis=0)

def spectral_weights(cuts, period_x, period_y):
    rows = jnp.arange(2 * KX, dtype=jnp.int32)
    wavenum = rows % KX
    factor = jnp.where(rows == 0, 1.0, 2.0).astype(jnp.float32)
    weighting = factor[:, None] * factor[None, :] / math.sqrt(period_x * period_y)
    limit = cuts.reshape(-1)[:, None, None]
    keep_mask = ((wavenum[None, :, None] < limit) & (wavenum[None, None, :] < limit)).astype(jnp.float32)
    return keep_mask * weighting[None]

def transport(values, padded, east_wind, north_wind):
    per_group = east_wind.shape[0]
    groups = values.shape[0] // per_group

    def split(array):
        return array.reshape((groups, per_group) + array.shape[1:])
    centre = split(values)
    west_side = split(padded[:, :-2, 1:-1])
    east_side = split(padded[:, 2:, 1:-1])
    south_side = split(padded[:, 1:-1, :-2])
    north_side = split(padded[:, 1:-1, 2:])
    upwind = jnp.maximum(east_wind, 0.0) * (centre - west_side) + jnp.minimum(east_wind, 0.0) * (east_side - centre) + jnp.maximum(north_wind, 0.0) * (centre - south_side) + jnp.minimum(north_wind, 0.0) * (north_side - centre)
    laplace = east_side + west_side + north_side + south_side - 4.0 * centre
    return (0.1 * laplace - 0.1 * upwind).reshape(values.shape)

def settle(concentration, moved, source):
    above = jnp.concatenate([concentration[1:], jnp.zeros_like(concentration[:1])], axis=0)
    return concentration + moved - 0.3 * concentration + 0.3 * above + source

def reference(fields, levels, cuts, parent_modes, owners, plume, source):
    hi = lax.Precision.HIGHEST
    x_table = tables(NX, 0, NX)
    y_table = tables(NY, 0, NY)
    scaling = 1.0 / math.sqrt(NX * NY)
    weighted = spectral_weights(cuts, NX, NY)
    nudged = 3 * LEV
    for step_index in range(STEPS):
        chosen = fields[:, levels].reshape(nudged, NX, NY)
        halfway = jnp.einsum('kx,cxy->cky', x_table, chosen, precision=hi)
        modes = jnp.einsum('cky,jy->ckj', halfway, y_table, precision=hi) * scaling
        parent = parent_modes[owners[step_index], step_index].reshape(nudged, 2 * KX, 2 * KX)
        mismatch = (parent - modes) * weighted
        back = jnp.einsum('ckj,jy->cky', mismatch, y_table, precision=hi)
        update = jnp.einsum('kx,cky->cxy', x_table, back, precision=hi)
        fields = fields.at[:, levels].add(update.reshape(3, LEV, NX, NY))
        east_wind = fields[0]
        north_wind = fields[1]
        plume_pad = jnp.pad(plume, ((0, 0), (1, 1), (1, 1)))
        plume = settle(plume, transport(plume, plume_pad, east_wind, north_wind), source)
        flat = fields.reshape(3 * LEVALL, NX, NY)
        flat_pad = jnp.pad(flat, ((0, 0), (1, 1), (1, 1)))
        flat = flat + transport(flat, flat_pad, east_wind, north_wind)
        fields = flat.reshape(3, LEVALL, NX, NY)
    return (fields, plume)
```

```python
import functools
import math

import jax
import jax.numpy as jnp
import numpy as np
from jax import lax
from jax.experimental import pallas as pl
from jax.experimental.pallas import tpu as pltpu
from jax.sharding import PartitionSpec as P

KX = 32
STEPS = 2
HI = lax.Precision.HIGHEST
VMEM = pl.BlockSpec(memory_space=pltpu.VMEM)
SMEM = pl.BlockSpec(memory_space=pltpu.SMEM)
AXES = ("gx", "gy")


def wave_table(positions, period):
    wavenum = np.arange(KX)[:, None]
    phase = (wavenum * positions[None, :] % period) * (2.0 * math.pi / period)
    inside = (positions >= 0) & (positions < period)
    return np.concatenate([np.cos(phase), np.sin(phase)], axis=0) * inside[None, :]


def build_tables(n_gx, n_gy, cells_x, cells_y):
    period_x, period_y = n_gx * cells_x, n_gy * cells_y
    order = np.concatenate([np.arange(0, 2 * KX, 2), np.arange(1, 2 * KX, 2)])
    scaling = 1.0 / math.sqrt(period_x * period_y)
    x_fwd, x_back, y_fwd, y_back = [], [], [], []
    for g in range(n_gx):
        first = g * cells_x
        x_fwd.append(wave_table(first + np.arange(cells_x), period_x)[order])
        rows = np.concatenate([first + np.arange(cells_x), [first - 1, first + cells_x]])
        back = np.zeros((cells_x + 8, 2 * KX))
        back[: cells_x + 2] = wave_table(rows, period_x)[order].T
        x_back.append(back)
    for g in range(n_gy):
        first = g * cells_y
        table = wave_table(first + np.arange(cells_y), period_y)
        edge = np.zeros((2 * KX, cells_y))
        edge[:, [0, -1]] = wave_table(np.array([first - 1, first + cells_y]), period_y)
        y_fwd.append(np.concatenate([table.T, table.T], axis=1) * scaling)
        none = np.zeros_like(table)
        y_back.append(
            np.concatenate(
                [
                    np.concatenate([table, edge, none, none], axis=1),
                    np.concatenate([none, none, table, edge], axis=1),
                ],
                axis=0,
            )
        )
    return [np.stack(t).astype(np.float32) for t in (x_fwd, x_back, y_fwd, y_back)]


def dot(a, b):
    return jnp.dot(a, b, precision=HI, preferred_element_type=jnp.float32)


def emit_modes(read, parent_ref, x_fwd, y_fwd, is_owner, sel_ref, half_ref, modes_ref, nudged):
    cells_x = x_fwd.shape[1]
    for c in range(nudged):
        sel_ref[c] = read(c)
    flat = sel_ref[...].reshape(nudged * cells_x, -1)
    half_ref[...] = dot(flat, y_fwd).reshape(half_ref.shape)
    lane = lax.broadcasted_iota(jnp.int32, (KX, 4 * KX), 1)

    def body(c, carry):
        both = dot(x_fwd, half_ref[c])
        modes_ref[c] = -jnp.where(lane < 2 * KX, both[:KX], both[KX:])
        return carry

    lax.fori_loop(0, nudged, body, 0, unroll=4)

    @pl.when(is_owner)
    def _():
        for i in range(KX):
            tile = parent_ref[:, i * 4 * KX : (i + 1) * 4 * KX]
            modes_ref[:, i, :] = modes_ref[:, i, :] + tile


def emit_edges(read, total, west_ref, east_ref, cols_ref):
    cells_x = cols_ref.shape[0]
    lane = lax.broadcasted_iota(jnp.int32, cols_ref.shape, 1)
    acc = jnp.zeros(cols_ref.shape, jnp.float32)
    for c in range(total):
        a = read(c)
        west_ref[c : c + 1, :] = a[:1]
        east_ref[c : c + 1, :] = a[cells_x - 1 :]
        acc = jnp.where(lane == c, a[:, :1], acc)
        acc = jnp.where(lane == total + c, a[:, a.shape[1] - 1 :], acc)
    cols_ref[...] = acc


def first_kernel(n_gy, levels, owners, fields, plume, parent, x_fwd, y_fwd,
                 modes, west, east, cols, sel, half, parent_here, parent_sem):
    fetch = pltpu.make_async_copy(parent.at[0, 0], parent_here, parent_sem)
    fetch.start()
    level_total = plume.shape[0]
    nudged = sel.shape[0]
    level_count = nudged // 3
    me = lax.axis_index("gx") * n_gy + lax.axis_index("gy")
    fetch.wait()
    emit_modes(
        lambda c: fields[(c // level_count) * level_total + levels[c % level_count]],
        parent_here, x_fwd[0], y_fwd[0], owners[0] == me, sel, half, modes, nudged,
    )
    field_rows = fields.shape[0]
    emit_edges(
        lambda c: fields[c] if c < field_rows else plume[c - field_rows],
        field_rows + level_total, west, east, cols,
    )


def share_kernel(n_gy, period, copies, cuts, parts, out):
    count, rows, lanes = parts.shape
    me = lax.axis_index("gx") * n_gy + lax.axis_index("gy")
    total = parts[0]
    for p in range(1, count):
        total = total + parts[p]
    row = me * rows + lax.broadcasted_iota(jnp.int32, (rows, lanes), 0)
    lane = lax.broadcasted_iota(jnp.int32, (rows, lanes), 1)
    slab, pair = row // KX, row % KX
    r = 2 * pair + lane // (2 * KX)
    s = lane % (2 * KX)
    limit = jnp.zeros((rows, lanes), jnp.int32)
    for c in range(cuts.shape[0]):
        limit = jnp.where(slab == c, cuts[c], limit)
    keep = ((r % KX) < limit) & ((s % KX) < limit)
    factor = jnp.where(r == 0, 1.0, 2.0) * jnp.where(s == 0, 1.0, 2.0) * (1.0 / math.sqrt(period))
    result = jnp.where(keep, total * factor, 0.0)
    if copies:
        for p in range(count):
            out[p] = result
    else:
        out[...] = result


def step_kernel(n_gy, step, last, levels, owners, mismatch, fields, plume, source, west, east,
                south, north, parent, x_fwd, y_fwd, x_back, y_back, *rest):
    if last:
        fields_out, plume_out, back, nudged_ref, rows_ref, cols_ref = rest
    else:
        (fields_out, plume_out, modes, west_out, east_out, cols_out,
         back, nudged_ref, rows_ref, cols_ref, sel, half, parent_here, parent_sem) = rest
        fetch = pltpu.make_async_copy(parent.at[0, step + 1], parent_here, parent_sem)
        fetch.start()
    level_total, cells_x, cells_y = plume.shape
    field_rows = fields.shape[0]
    total = field_rows + level_total
    nudged = mismatch.shape[0] // KX
    level_count = nudged // 3
    back[...] = dot(mismatch[...], y_back[0])
    for c in range(field_rows):
        nudged_ref[c] = fields[c]
    rows_ref[...] = jnp.zeros_like(rows_ref)
    cols_ref[...] = jnp.zeros_like(cols_ref)
    x_table = x_back[0]
    for c in range(nudged):
        pair = back[c * KX : (c + 1) * KX]
        stacked = jnp.concatenate([pair[:, : 2 * cells_y], pair[:, 2 * cells_y :]], axis=0)
        update = dot(x_table, stacked)
        spot = (c // level_count) * level_total + levels[c % level_count]
        nudged_ref[spot] = nudged_ref[spot] + update[:cells_x, :cells_y]
        rows_ref[spot] = update[cells_x:, :cells_y]
        cols_ref[spot] = update[:cells_x, cells_y:]

    row = lax.broadcasted_iota(jnp.int32, (cells_x, cells_y), 0)
    lane = lax.broadcasted_iota(jnp.int32, (cells_x, cells_y), 1)

    def move(a, c, spot, up, um, vp, vm):
        west_row, east_row = west[c : c + 1, :], east[c : c + 1, :]
        south_col, north_col = south[:, total + c : total + c + 1], north[:, c : c + 1]
        if spot is not None:
            west_row = west_row + rows_ref[spot, 0:1]
            east_row = east_row + rows_ref[spot, 1:2]
            south_col = south_col + cols_ref[spot]
            north_col = north_col + cols_ref[spot]
        a_west = jnp.where(row == 0, west_row, pltpu.roll(a, 1, 0))
        a_east = jnp.where(row == cells_x - 1, east_row, pltpu.roll(a, cells_x - 1, 0))
        a_south = jnp.where(lane == 0, south_col, pltpu.roll(a, 1, 1))
        a_north = jnp.where(lane == cells_y - 1, north_col, pltpu.roll(a, cells_y - 1, 1))
        upwind = up * (a - a_west) + um * (a_east - a) + vp * (a - a_south) + vm * (a_north - a)
        laplace = a_east + a_west + a_north + a_south - 4.0 * a
        return 0.1 * laplace - 0.1 * upwind

    for l in range(level_total):
        u, v = nudged_ref[l], nudged_ref[level_total + l]
        up, um = jnp.maximum(u, 0.0), jnp.minimum(u, 0.0)
        vp, vm = jnp.maximum(v, 0.0), jnp.minimum(v, 0.0)
        for f in range(3):
            c = f * level_total + l
            a = nudged_ref[c]
            fields_out[c] = a + move(a, c, c, up, um, vp, vm)
        q = plume[l]
        above = plume[l + 1] if l + 1 < level_total else jnp.zeros_like(q)
        moved = move(q, field_rows + l, None, up, um, vp, vm)
        plume_out[l] = q + moved - 0.3 * q + 0.3 * above + source[l]

    if last:
        return
    fetch.wait()
    me = lax.axis_index("gx") * n_gy + lax.axis_index("gy")
    emit_modes(
        lambda c: fields_out[(c // level_count) * level_total + levels[c % level_count]],
        parent_here, x_fwd[0], y_fwd[0], owners[step + 1] == me, sel, half, modes, nudged,
    )
    emit_edges(
        lambda c: fields_out[c] if c < field_rows else plume_out[c - field_rows],
        total, west_out, east_out, cols_out,
    )


def swap_edges(west, east, cols):
    n_gx, n_gy = lax.axis_size("gx"), lax.axis_size("gy")
    up_x = [(i, i + 1) for i in range(n_gx - 1)]
    up_y = [(i, i + 1) for i in range(n_gy - 1)]
    down_x = [(b, a) for a, b in up_x]
    down_y = [(b, a) for a, b in up_y]
    return (
        lax.ppermute(east, "gx", up_x),
        lax.ppermute(west, "gx", down_x),
        lax.ppermute(cols, "gy", up_y),
        lax.ppermute(cols, "gy", down_y),
    )


def local(tables, fields, levels, cuts, parent_modes, owners, plume, source):
    n_gx, n_gy = lax.axis_size("gx"), lax.axis_size("gy")
    devices = n_gx * n_gy
    level_total, cells_x, cells_y = plume.shape
    period = n_gx * cells_x * n_gy * cells_y
    level_count = levels.shape[0]
    nudged = 3 * level_count
    field_rows = 3 * level_total
    total = field_rows + level_total
    lanes = 4 * KX
    flat = fields.reshape(field_rows, cells_x, cells_y)
    cuts = cuts.reshape(-1)
    gx, gy = lax.axis_index("gx"), lax.axis_index("gy")
    f32 = functools.partial(jax.ShapeDtypeStruct, dtype=jnp.float32)
    params = pltpu.CompilerParams(vmem_limit_bytes=40 * 1024 * 1024)
    x_fwd, x_back, y_fwd, y_back = (
        lax.dynamic_slice_in_dim(jnp.asarray(t), g, 1) for t, g in zip(tables, (gx, gx, gy, gy))
    )
    edge_shapes = [f32((total, cells_y)), f32((total, cells_y)), f32((cells_x, 2 * total))]
    mode_shape = f32((nudged, KX, lanes))
    mode_scratch = [pltpu.VMEM((nudged, cells_x, cells_y), jnp.float32),
                    pltpu.VMEM((nudged, cells_x, lanes), jnp.float32),
                    pltpu.VMEM((nudged, 4 * KX * KX), jnp.float32),
                    pltpu.SemaphoreType.DMA]
    step_scratch = [pltpu.VMEM((nudged * KX, 4 * cells_y), jnp.float32),
                    pltpu.VMEM((field_rows, cells_x, cells_y), jnp.float32),
                    pltpu.VMEM((field_rows, 8, cells_y), jnp.float32),
                    pltpu.VMEM((field_rows, cells_x, cells_y), jnp.float32)]
    parent_spec = pl.BlockSpec(memory_space=pl.ANY)

    modes, west, east, cols = pl.pallas_call(
        functools.partial(first_kernel, n_gy),
        out_shape=[mode_shape] + edge_shapes,
        in_specs=[SMEM, SMEM, VMEM, VMEM, parent_spec, VMEM, VMEM],
        out_specs=[VMEM] * 4,
        scratch_shapes=mode_scratch,
        compiler_params=params,
        name="first_modes",
    )(levels, owners, flat, plume, parent_modes, x_fwd, y_fwd)
    for step in range(STEPS):
        last = step == STEPS - 1
        halo = swap_edges(west, east, cols)
        rows = nudged * KX // devices
        parts = lax.all_to_all(modes.reshape(devices, rows, lanes), AXES, 0, 0, tiled=True)
        direct = step == 0
        share = pl.pallas_call(
            functools.partial(share_kernel, n_gy, period, direct),
            out_shape=f32((devices, rows, lanes) if direct else (rows, lanes)),
            in_specs=[SMEM, VMEM],
            out_specs=VMEM,
            compiler_params=params,
            name="share_sum",
        )(cuts, parts)
        if direct:
            mismatch = lax.all_to_all(share, AXES, 0, 0, tiled=True)
        else:
            mismatch = lax.all_gather(share, AXES, axis=0, tiled=True)
        out_shape = [f32(flat.shape), f32(plume.shape)]
        if not last:
            out_shape += [mode_shape] + edge_shapes
        results = pl.pallas_call(
            functools.partial(step_kernel, n_gy, step, last),
            out_shape=out_shape,
            in_specs=[SMEM, SMEM] + [VMEM] * 8 + [parent_spec] + [VMEM] * 4,
            out_specs=[VMEM] * len(out_shape),
            scratch_shapes=step_scratch + ([] if last else mode_scratch),
            compiler_params=params,
            name="final_step" if last else "inner_step",
        )(levels, owners, mismatch.reshape(nudged * KX, lanes), flat, plume, source, *halo,
          parent_modes, x_fwd, y_fwd, x_back, y_back)
        if last:
            flat, plume = results
        else:
            flat, plume, modes, west, east, cols = results
    return flat.reshape(fields.shape), plume


def solution(mesh):
    in_specs = (
        P(None, None, "gx", "gy"),
        P(),
        P(),
        P(("gx", "gy"), None, None, None),
        P(),
        P(None, "gx", "gy"),
        P(None, "gx", "gy"),
    )
    out_specs = (P(None, None, "gx", "gy"), P(None, "gx", "gy"))
    n_gx, n_gy = mesh.shape["gx"], mesh.shape["gy"]

    def whole(fields, levels, cuts, parent_modes, owners, plume, source):
        tables = build_tables(n_gx, n_gy, plume.shape[1] // n_gx, plume.shape[2] // n_gy)
        return jax.shard_map(
            functools.partial(local, tables), mesh=mesh, in_specs=in_specs, out_specs=out_specs,
            check_vma=False,
        )(fields, levels, cuts, parent_modes, owners, plume, source)

    return whole
```

```python
import functools
import math

import jax
import jax.numpy as jnp
import numpy as np
from jax import lax
from jax.experimental import pallas as pl
from jax.experimental.pallas import tpu as pltpu
from jax.sharding import PartitionSpec as P

KX = 32
STEPS = 2
FIRST_VMEM = 60 * 1024 * 1024
HI = lax.Precision.HIGHEST
VMEM = pl.BlockSpec(memory_space=pltpu.VMEM)
SMEM = pl.BlockSpec(memory_space=pltpu.SMEM)
HBM = pl.BlockSpec(memory_space=pltpu.HBM)
AXES = ("gx", "gy")


def wave_table(positions, period):
    wavenum = np.arange(KX)[:, None]
    phase = (wavenum * positions[None, :] % period) * (2.0 * math.pi / period)
    inside = (positions >= 0) & (positions < period)
    return np.concatenate([np.cos(phase), np.sin(phase)], axis=0) * inside[None, :]


def build_tables(n_gx, n_gy, cells_x, cells_y):
    period_x, period_y = n_gx * cells_x, n_gy * cells_y
    order = np.concatenate([np.arange(0, 2 * KX, 2), np.arange(1, 2 * KX, 2)])
    scaling = 1.0 / math.sqrt(period_x * period_y)
    x_fwd, x_back, y_fwd, y_back = [], [], [], []
    for g in range(n_gx):
        first = g * cells_x
        x_fwd.append(wave_table(first + np.arange(cells_x), period_x)[order])
        rows = np.concatenate([first + np.arange(cells_x), [first - 1, first + cells_x]])
        back = np.zeros((cells_x + 8, 2 * KX))
        back[: cells_x + 2] = wave_table(rows, period_x)[order].T
        x_back.append(back)
    for g in range(n_gy):
        first = g * cells_y
        table = wave_table(first + np.arange(cells_y), period_y)
        edge = np.zeros((2 * KX, cells_y))
        edge[:, [0, -1]] = wave_table(np.array([first - 1, first + cells_y]), period_y)
        y_fwd.append(np.concatenate([table.T, table.T], axis=1) * scaling)
        none = np.zeros_like(table)
        y_back.append(
            np.concatenate(
                [
                    np.concatenate([table, edge, none, none], axis=1),
                    np.concatenate([none, none, table, edge], axis=1),
                ],
                axis=0,
            )
        )
    return [np.stack(t).astype(np.float32) for t in (x_fwd, x_back, y_fwd, y_back)]


def dot(a, b):
    return jnp.dot(a, b, precision=HI, preferred_element_type=jnp.float32)


def emit_modes(read, parent_ref, x_fwd, y_fwd, is_owner, sel_ref, half_ref, modes_ref, nudged):
    cells_x = x_fwd.shape[1]
    for c in range(nudged):
        sel_ref[c] = read(c)
    flat = sel_ref[...].reshape(nudged * cells_x, -1)
    half_ref[...] = dot(flat, y_fwd).reshape(half_ref.shape)
    lane = lax.broadcasted_iota(jnp.int32, (KX, 4 * KX), 1)

    def body(c, carry):
        both = dot(x_fwd, half_ref[c])
        modes_ref[c] = -jnp.where(lane < 2 * KX, both[:KX], both[KX:])
        return carry

    lax.fori_loop(0, nudged, body, 0, unroll=4)

    @pl.when(is_owner)
    def _():
        for i in range(KX):
            tile = parent_ref[:, i * 4 * KX : (i + 1) * 4 * KX]
            modes_ref[:, i, :] = modes_ref[:, i, :] + tile


def emit_edges(read, total, west_ref, east_ref, cols_ref):
    cells_x = cols_ref.shape[0]
    lane = lax.broadcasted_iota(jnp.int32, cols_ref.shape, 1)
    acc = jnp.zeros(cols_ref.shape, jnp.float32)
    for c in range(total):
        a = read(c)
        west_ref[c : c + 1, :] = a[:1]
        east_ref[c : c + 1, :] = a[cells_x - 1 :]
        acc = jnp.where(lane == c, a[:, :1], acc)
        acc = jnp.where(lane == total + c, a[:, a.shape[1] - 1 :], acc)
    cols_ref[...] = acc


def fetch_all(sems, pairs):
    copies = [pltpu.make_async_copy(a, b, sems.at[i]) for i, (a, b) in enumerate(pairs)]
    for copy in copies:
        copy.start()
    return copies


def first_kernel(n_gy, levels, owners, fields_all, plume_all, parent, x_fwd_all, y_fwd_all,
                 modes, west, east, cols, sel, half, parent_here, x_fwd, y_fwd, fields, plume,
                 sems):
    gx, gy = lax.axis_index("gx"), lax.axis_index("gy")
    copies = fetch_all(sems, [
        (x_fwd_all.at[gx], x_fwd.at[0]), (y_fwd_all.at[gy], y_fwd.at[0]), (fields_all, fields),
        (parent.at[0, 0], parent_here), (plume_all, plume)])
    level_total = plume.shape[0]
    nudged = sel.shape[0]
    level_count = nudged // 3
    me = lax.axis_index("gx") * n_gy + lax.axis_index("gy")
    for copy in copies:
        copy.wait()
    emit_modes(
        lambda c: fields[(c // level_count) * level_total + levels[c % level_count]],
        parent_here, x_fwd[0], y_fwd[0], owners[0] == me, sel, half, modes, nudged,
    )
    field_rows = fields.shape[0]
    emit_edges(
        lambda c: fields[c] if c < field_rows else plume[c - field_rows],
        field_rows + level_total, west, east, cols,
    )


def share_kernel(n_gy, period, copies, cuts, parts, out):
    count, rows, lanes = parts.shape
    me = lax.axis_index("gx") * n_gy + lax.axis_index("gy")
    total = parts[0]
    for p in range(1, count):
        total = total + parts[p]
    row = me * rows + lax.broadcasted_iota(jnp.int32, (rows, lanes), 0)
    lane = lax.broadcasted_iota(jnp.int32, (rows, lanes), 1)
    slab, pair = row // KX, row % KX
    r = 2 * pair + lane // (2 * KX)
    s = lane % (2 * KX)
    limit = jnp.zeros((rows, lanes), jnp.int32)
    for c in range(cuts.shape[0]):
        limit = jnp.where(slab == c, cuts[c], limit)
    keep = ((r % KX) < limit) & ((s % KX) < limit)
    factor = jnp.where(r == 0, 1.0, 2.0) * jnp.where(s == 0, 1.0, 2.0) * (1.0 / math.sqrt(period))
    result = jnp.where(keep, total * factor, 0.0)
    if copies:
        for p in range(count):
            out[p] = result
    else:
        out[...] = result


def step_kernel(n_gy, step, last, levels, owners, mismatch, fields_all, plume_all, source_all,
                west, east, south, north, parent, x_fwd_all, y_fwd_all, x_back_all, y_back_all,
                *rest):
    gx, gy = lax.axis_index("gx"), lax.axis_index("gy")
    if last:
        (fields_out, plume_out, x_back, y_back, back, nudged_ref, rows_ref, cols_ref, source,
         sems) = rest
        fields, plume = fields_all, plume_all
        extra = []
    else:
        (fields_out, plume_out, modes, west_out, east_out, cols_out,
         x_back, y_back, back, nudged_ref, rows_ref, cols_ref, source, sems,
         sel, half, parent_here, x_fwd, y_fwd, fields, plume) = rest
        extra = [(fields_all, fields), (plume_all, plume), (x_fwd_all.at[gx], x_fwd.at[0]),
                 (y_fwd_all.at[gy], y_fwd.at[0]), (parent.at[0, step + 1], parent_here)]
    copies = fetch_all(sems, [
        (y_back_all.at[gy], y_back.at[0]), (x_back_all.at[gx], x_back.at[0]),
        (source_all, source)] + extra)
    for copy in copies:
        copy.wait()
    level_total, cells_x, cells_y = plume.shape
    field_rows = fields.shape[0]
    total = field_rows + level_total
    nudged = mismatch.shape[0] // KX
    level_count = nudged // 3
    back[...] = dot(mismatch[...], y_back[0])
    for c in range(field_rows):
        nudged_ref[c] = fields[c]
    rows_ref[...] = jnp.zeros_like(rows_ref)
    cols_ref[...] = jnp.zeros_like(cols_ref)
    x_table = x_back[0]
    for c in range(nudged):
        pair = back[c * KX : (c + 1) * KX]
        stacked = jnp.concatenate([pair[:, : 2 * cells_y], pair[:, 2 * cells_y :]], axis=0)
        update = dot(x_table, stacked)
        spot = (c // level_count) * level_total + levels[c % level_count]
        nudged_ref[spot] = nudged_ref[spot] + update[:cells_x, :cells_y]
        rows_ref[spot] = update[cells_x:, :cells_y]
        cols_ref[spot] = update[:cells_x, cells_y:]

    row = lax.broadcasted_iota(jnp.int32, (cells_x, cells_y), 0)
    lane = lax.broadcasted_iota(jnp.int32, (cells_x, cells_y), 1)

    def move(a, c, spot, up, um, vp, vm):
        west_row, east_row = west[c : c + 1, :], east[c : c + 1, :]
        south_col, north_col = south[:, total + c : total + c + 1], north[:, c : c + 1]
        if spot is not None:
            west_row = west_row + rows_ref[spot, 0:1]
            east_row = east_row + rows_ref[spot, 1:2]
            south_col = south_col + cols_ref[spot]
            north_col = north_col + cols_ref[spot]
        a_west = jnp.where(row == 0, west_row, pltpu.roll(a, 1, 0))
        a_east = jnp.where(row == cells_x - 1, east_row, pltpu.roll(a, cells_x - 1, 0))
        a_south = jnp.where(lane == 0, south_col, pltpu.roll(a, 1, 1))
        a_north = jnp.where(lane == cells_y - 1, north_col, pltpu.roll(a, cells_y - 1, 1))
        upwind = up * (a - a_west) + um * (a_east - a) + vp * (a - a_south) + vm * (a_north - a)
        laplace = a_east + a_west + a_north + a_south - 4.0 * a
        return 0.1 * laplace - 0.1 * upwind

    for l in range(level_total):
        u, v = nudged_ref[l], nudged_ref[level_total + l]
        up, um = jnp.maximum(u, 0.0), jnp.minimum(u, 0.0)
        vp, vm = jnp.maximum(v, 0.0), jnp.minimum(v, 0.0)
        for f in range(3):
            c = f * level_total + l
            a = nudged_ref[c]
            fields_out[c] = a + move(a, c, c, up, um, vp, vm)
        q = plume[l]
        above = plume[l + 1] if l + 1 < level_total else jnp.zeros_like(q)
        moved = move(q, field_rows + l, None, up, um, vp, vm)
        plume_out[l] = q + moved - 0.3 * q + 0.3 * above + source[l]

    if last:
        return
    me = lax.axis_index("gx") * n_gy + lax.axis_index("gy")
    emit_modes(
        lambda c: fields_out[(c // level_count) * level_total + levels[c % level_count]],
        parent_here, x_fwd[0], y_fwd[0], owners[step + 1] == me, sel, half, modes, nudged,
    )
    emit_edges(
        lambda c: fields_out[c] if c < field_rows else plume_out[c - field_rows],
        total, west_out, east_out, cols_out,
    )


def swap_edges(west, east, cols):
    n_gx, n_gy = lax.axis_size("gx"), lax.axis_size("gy")
    up_x = [(i, i + 1) for i in range(n_gx - 1)]
    up_y = [(i, i + 1) for i in range(n_gy - 1)]
    down_x = [(b, a) for a, b in up_x]
    down_y = [(b, a) for a, b in up_y]
    return (
        lax.ppermute(east, "gx", up_x),
        lax.ppermute(west, "gx", down_x),
        lax.ppermute(cols, "gy", up_y),
        lax.ppermute(cols, "gy", down_y),
    )


def local(tables, fields, levels, cuts, parent_modes, owners, plume, source):
    n_gx, n_gy = lax.axis_size("gx"), lax.axis_size("gy")
    devices = n_gx * n_gy
    level_total, cells_x, cells_y = plume.shape
    period = n_gx * cells_x * n_gy * cells_y
    level_count = levels.shape[0]
    nudged = 3 * level_count
    field_rows = 3 * level_total
    total = field_rows + level_total
    lanes = 4 * KX
    flat = fields.reshape(field_rows, cells_x, cells_y)
    cuts = cuts.reshape(-1)
    f32 = functools.partial(jax.ShapeDtypeStruct, dtype=jnp.float32)
    params = pltpu.CompilerParams(vmem_limit_bytes=40 * 1024 * 1024)
    x_fwd, x_back, y_fwd, y_back = (jnp.asarray(t) for t in tables)
    edge_shapes = [f32((total, cells_y)), f32((total, cells_y)), f32((cells_x, 2 * total))]
    mode_shape = f32((nudged, KX, lanes))
    vmem = lambda *shape: pltpu.VMEM(shape, jnp.float32)
    slabs, ash = vmem(field_rows, cells_x, cells_y), vmem(level_total, cells_x, cells_y)
    mode_scratch = [vmem(nudged, cells_x, cells_y), vmem(nudged, cells_x, lanes),
                    vmem(nudged, 4 * KX * KX), vmem(1, *x_fwd.shape[1:]), vmem(1, *y_fwd.shape[1:]),
                    slabs, ash]
    step_scratch = [vmem(1, *x_back.shape[1:]), vmem(1, *y_back.shape[1:]),
                    vmem(nudged * KX, 4 * cells_y), slabs, vmem(field_rows, 8, cells_y), slabs,
                    ash, pltpu.SemaphoreType.DMA((8,))]

    modes, west, east, cols = pl.pallas_call(
        functools.partial(first_kernel, n_gy),
        out_shape=[mode_shape] + edge_shapes,
        in_specs=[SMEM, SMEM] + [HBM] * 5,
        out_specs=[VMEM] * 4,
        scratch_shapes=mode_scratch + [pltpu.SemaphoreType.DMA((5,))],
        compiler_params=pltpu.CompilerParams(vmem_limit_bytes=FIRST_VMEM),
        name="first_modes",
    )(levels, owners, flat, plume, parent_modes, x_fwd, y_fwd)
    for step in range(STEPS):
        last = step == STEPS - 1
        halo = swap_edges(west, east, cols)
        rows = nudged * KX // devices
        parts = lax.all_to_all(modes.reshape(devices, rows, lanes), AXES, 0, 0, tiled=True)
        direct = step == 0
        share = pl.pallas_call(
            functools.partial(share_kernel, n_gy, period, direct),
            out_shape=f32((devices, rows, lanes) if direct else (rows, lanes)),
            in_specs=[SMEM, VMEM],
            out_specs=VMEM,
            compiler_params=params,
            name="share_sum",
        )(cuts, parts)
        if direct:
            mismatch = lax.all_to_all(share, AXES, 0, 0, tiled=True)
        else:
            line = lax.all_to_all(
                jnp.broadcast_to(share[None], (n_gy, rows, lanes)), "gy", 0, 0, tiled=True
            ).reshape(n_gy * rows, lanes)
            mismatch = lax.all_to_all(
                jnp.broadcast_to(line[None], (n_gx, n_gy * rows, lanes)), "gx", 0, 0, tiled=True
            )
        out_shape = [f32(flat.shape), f32(plume.shape)]
        if not last:
            out_shape += [mode_shape] + edge_shapes
        results = pl.pallas_call(
            functools.partial(step_kernel, n_gy, step, last),
            out_shape=out_shape,
            in_specs=[SMEM, SMEM, VMEM] + [VMEM if last else HBM] * 2 + [HBM] + [VMEM] * 4 + [HBM] * 5,
            out_specs=[VMEM] * len(out_shape),
            scratch_shapes=step_scratch + ([] if last else mode_scratch),
            compiler_params=params,
            name="final_step" if last else "inner_step",
        )(levels, owners, mismatch.reshape(nudged * KX, lanes), flat, plume, source, *halo,
          parent_modes, x_fwd, y_fwd, x_back, y_back)
        if last:
            flat, plume = results
        else:
            flat, plume, modes, west, east, cols = results
    return flat.reshape(fields.shape), plume


def solution(mesh):
    in_specs = (
        P(None, None, "gx", "gy"),
        P(),
        P(),
        P(("gx", "gy"), None, None, None),
        P(),
        P(None, "gx", "gy"),
        P(None, "gx", "gy"),
    )
    out_specs = (P(None, None, "gx", "gy"), P(None, "gx", "gy"))
    n_gx, n_gy = mesh.shape["gx"], mesh.shape["gy"]

    def whole(fields, levels, cuts, parent_modes, owners, plume, source):
        tables = build_tables(n_gx, n_gy, plume.shape[1] // n_gx, plume.shape[2] // n_gy)
        return jax.shard_map(
            functools.partial(local, tables), mesh=mesh, in_specs=in_specs, out_specs=out_specs,
            check_vma=False,
        )(fields, levels, cuts, parent_modes, owners, plume, source)

    return whole
```

```python
import functools
import math

import jax
import jax.numpy as jnp
import ml_dtypes
import numpy as np
from jax import lax
from jax.experimental import pallas as pl
from jax.experimental.pallas import tpu as pltpu
from jax.sharding import PartitionSpec as P

KX = 32
STEPS = 2
FIRST_MIB = 60
PAD = 8
VMEM = pl.BlockSpec(memory_space=pltpu.VMEM)
SMEM = pl.BlockSpec(memory_space=pltpu.SMEM)
HBM = pl.BlockSpec(memory_space=pltpu.HBM)
AXES = ("gx", "gy")


def wave_table(positions, period):
    wavenum = np.arange(KX)[:, None]
    phase = (wavenum * positions[None, :] % period) * (2.0 * math.pi / period)
    inside = (positions >= 0) & (positions < period)
    return np.concatenate([np.cos(phase), np.sin(phase)], axis=0) * inside[None, :]


def split(a):
    head = a.astype(jnp.bfloat16)
    return head, (a - head.astype(jnp.float32)).astype(jnp.bfloat16)


def split_table(table, axis, order):
    head = table.astype(ml_dtypes.bfloat16)
    rest = (table - head.astype(np.float64)).astype(ml_dtypes.bfloat16)
    return np.concatenate([head if part == "h" else rest for part in order], axis=axis)


def build_tables(n_gx, n_gy, cells_x, cells_y):
    period_x, period_y = n_gx * cells_x, n_gy * cells_y
    order = np.concatenate([np.arange(0, 2 * KX, 2), np.arange(1, 2 * KX, 2)])
    scaling = 1.0 / math.sqrt(period_x * period_y)
    x_fwd, x_back, y_fwd, y_back = [], [], [], []
    for g in range(n_gx):
        first = g * cells_x
        forward = wave_table(first + np.arange(cells_x), period_x)[order]
        x_fwd.append(split_table(forward, 1, "hlh"))
        rows = np.concatenate([first + np.arange(cells_x), [first - 1, first + cells_x]])
        back = np.zeros((cells_x + 16, 2 * KX))
        back[: cells_x + 2] = wave_table(rows, period_x)[order].T
        x_back.append(split_table(back, 1, "hlh"))
    for g in range(n_gy):
        first = g * cells_y
        table = wave_table(first + np.arange(cells_y), period_y)
        edge = np.zeros((2 * KX, cells_y))
        edge[:, [0, -1]] = wave_table(np.array([first - 1, first + cells_y]), period_y)
        forward = np.concatenate([table.T, table.T], axis=1) * scaling
        y_fwd.append(split_table(forward, 0, "hhl"))
        none = np.zeros_like(table)
        back = np.concatenate(
            [
                np.concatenate([table, edge, none, none], axis=1),
                np.concatenate([none, none, table, edge], axis=1),
            ],
            axis=0,
        )
        y_back.append(split_table(back, 0, "hhl"))
    return [np.stack(t) for t in (x_fwd, x_back, y_fwd, y_back)]


def data_dot(a, table):
    head, rest = split(a)
    return jnp.dot(
        jnp.concatenate([head, rest, head], axis=1), table, preferred_element_type=jnp.float32
    )


def table_dot(table, a):
    head, rest = split(a)
    return jnp.dot(
        table, jnp.concatenate([head, head, rest], axis=0), preferred_element_type=jnp.float32
    )


def emit_modes(read, x_fwd, y_fwd, modes_ref):
    nudged = modes_ref.shape[0]
    slabs = [read(c) for c in range(nudged)]
    cells_x = slabs[0].shape[0]
    half = data_dot(jnp.concatenate(slabs, axis=0), y_fwd)
    lane = lax.broadcasted_iota(jnp.int32, (KX, 4 * KX), 1)
    for c in range(nudged):
        both = table_dot(x_fwd, half[c * cells_x : (c + 1) * cells_x])
        modes_ref[c] = -jnp.where(lane < 2 * KX, both[:KX], both[KX:])


def add_parent(parent, is_owner, modes_ref):
    @pl.when(is_owner)
    def _():
        for i in range(KX):
            tile = parent[:, i * 4 * KX : (i + 1) * 4 * KX]
            modes_ref[:, i, :] = modes_ref[:, i, :] + tile


def fetch_all(sems, pairs):
    copies = [pltpu.make_async_copy(a, b, sems.at[i]) for i, (a, b) in enumerate(pairs)]
    for copy in copies:
        copy.start()
    return copies


def slab_of(levels, c, level_count, level_total):
    return (c // level_count) * level_total + levels[c % level_count]


def first_kernel(n_gy, level_total, levels, owners, fields_all, parent_all, x_fwd_all, y_fwd_all,
                 modes, x_fwd, y_fwd, fields, parent, sems):
    gx, gy = lax.axis_index("gx"), lax.axis_index("gy")
    copies = fetch_all(sems, [
        (fields_all, fields), (x_fwd_all.at[gx], x_fwd), (y_fwd_all.at[gy], y_fwd),
        (parent_all.at[0, 0], parent)])
    for copy in copies[:3]:
        copy.wait()
    level_count = modes.shape[0] // 3
    emit_modes(
        lambda c: fields[slab_of(levels, c, level_count, level_total)], x_fwd[...], y_fwd[...],
        modes,
    )
    copies[3].wait()
    add_parent(parent, owners[0] == gx * n_gy + gy, modes)


def edge_kernel(fields, plume, west, east, cols):
    cells_x, cells_y = plume.shape[1:]
    field_rows = fields.shape[0]
    lane = lax.broadcasted_iota(jnp.int32, cols.shape, 1)
    acc = jnp.zeros(cols.shape, jnp.float32)
    for c in range(field_rows + plume.shape[0]):
        a = fields[c] if c < field_rows else plume[c - field_rows]
        west[c : c + 1, :] = a[:1]
        east[c : c + 1, :] = a[cells_x - 1 :]
        acc = jnp.where(lane // 2 == c, pltpu.roll(a, 2 * c + 1, 1), acc)
    cols[...] = acc


def share_kernel(n_gy, period, cuts, parts, out):
    count, rows, lanes = parts.shape
    me = lax.axis_index("gx") * n_gy + lax.axis_index("gy")
    total = parts[0]
    for p in range(1, count):
        total = total + parts[p]
    row = me * rows + lax.broadcasted_iota(jnp.int32, (rows, lanes), 0)
    lane = lax.broadcasted_iota(jnp.int32, (rows, lanes), 1)
    slab, pair = row // KX, row % KX
    r = 2 * pair + lane // (2 * KX)
    s = lane % (2 * KX)
    limit = jnp.zeros((rows, lanes), jnp.int32)
    for c in range(cuts.shape[0]):
        limit = jnp.where(slab == c, cuts[c], limit)
    keep = ((r % KX) < limit) & ((s % KX) < limit)
    factor = jnp.where(r == 0, 1.0, 2.0) * jnp.where(s == 0, 1.0, 2.0) * (1.0 / math.sqrt(period))
    result = jnp.where(keep, total * factor, 0.0)
    for p in range(count):
        out[p] = result


def step_kernel(n_gy, step, last, levels, owners, mismatch, fields, plume, source,
                west, east, south, north, x_back_all, y_back_all, *rest):
    gx, gy = lax.axis_index("gx"), lax.axis_index("gy")
    extra = []
    if last:
        fields_out, plume_out, x_back, y_back, slabs, beside, sems = rest
    else:
        (parent_all, x_fwd_all, y_fwd_all, fields_out, plume_out, modes,
         x_back, y_back, slabs, beside, sems, parent, x_fwd, y_fwd) = rest
        extra = [(x_fwd_all.at[gx], x_fwd), (y_fwd_all.at[gy], y_fwd),
                 (parent_all.at[0, step + 1], parent)]
    copies = fetch_all(
        sems, [(y_back_all.at[gy], y_back), (x_back_all.at[gx], x_back)] + extra)
    level_total, cells_x, cells_y = plume.shape
    field_rows = fields.shape[0]
    total = field_rows + level_total
    nudged = mismatch.shape[0] // KX
    level_count = nudged // 3
    inner = slice(PAD, PAD + cells_x)
    for c in range(total):
        slabs[c, inner] = fields[c] if c < field_rows else plume[c - field_rows]
        slabs[c, PAD - 1 : PAD] = west[c : c + 1, :]
        slabs[c, PAD + cells_x : PAD + cells_x + 1] = east[c : c + 1, :]
    beside[...] = jnp.zeros_like(beside)
    for copy in copies:
        copy.wait()
    back = data_dot(mismatch[...], y_back[...])
    x_table = x_back[...]
    for c in range(nudged):
        pair = back[c * KX : (c + 1) * KX]
        update = table_dot(
            x_table, jnp.concatenate([pair[:, : 2 * cells_y], pair[:, 2 * cells_y :]], axis=0))
        spot = slab_of(levels, c, level_count, level_total)
        slabs[spot, inner] += update[:cells_x, :cells_y]
        slabs[spot, PAD - 1 : PAD] += update[cells_x : cells_x + 1, :cells_y]
        slabs[spot, PAD + cells_x : PAD + cells_x + 1] += update[cells_x + 1 : cells_x + 2, :cells_y]
        beside[spot] = update[:cells_x, cells_y:]

    lane = lax.broadcasted_iota(jnp.int32, (cells_x, cells_y), 1)
    first, final = lane == 0, lane == cells_y - 1
    columns = jnp.where(
        lane % 2 == 0, pltpu.roll(north[...], cells_y - 1, 1), pltpu.roll(south[...], 1, 1))

    def advance(c, parts):
        centre, to_west, to_east, to_south, to_north = parts
        a = slabs[c, inner]
        column = pltpu.roll(columns, cells_y - 1 - 2 * c, 1)
        if c < field_rows:
            column = column + beside[c]
        return (
            centre * a
            + to_west * slabs[c, PAD - 1 : PAD - 1 + cells_x]
            + to_east * slabs[c, PAD + 1 : PAD + 1 + cells_x]
            + to_south * jnp.where(first, column, pltpu.roll(a, 1, 1))
            + to_north * jnp.where(final, column, pltpu.roll(a, cells_y - 1, 1))
        )

    for l in range(level_total):
        u, v = slabs[l, inner], slabs[level_total + l, inner]
        beside_parts = (
            0.1 + 0.1 * jnp.maximum(u, 0.0), 0.1 - 0.1 * jnp.minimum(u, 0.0),
            0.1 + 0.1 * jnp.maximum(v, 0.0), 0.1 - 0.1 * jnp.minimum(v, 0.0),
        )
        centre = 1.0 - (beside_parts[0] + beside_parts[1] + beside_parts[2] + beside_parts[3])
        for f in range(3):
            fields_out[f * level_total + l] = advance(
                f * level_total + l, (centre,) + beside_parts)
        settled = advance(field_rows + l, (centre - 0.3,) + beside_parts) + source[l]
        if l + 1 < level_total:
            settled = settled + 0.3 * plume[l + 1]
        plume_out[l] = settled

    if last:
        return
    emit_modes(
        lambda c: fields_out[slab_of(levels, c, level_count, level_total)], x_fwd[...], y_fwd[...],
        modes,
    )
    add_parent(parent, owners[step + 1] == gx * n_gy + gy, modes)


def swap_edges(west, east, cols):
    n_gx, n_gy = lax.axis_size("gx"), lax.axis_size("gy")
    up_x = [(i, i + 1) for i in range(n_gx - 1)]
    up_y = [(i, i + 1) for i in range(n_gy - 1)]
    down_x = [(b, a) for a, b in up_x]
    down_y = [(b, a) for a, b in up_y]
    return (
        lax.ppermute(east, "gx", up_x),
        lax.ppermute(west, "gx", down_x),
        lax.ppermute(cols, "gy", up_y),
        lax.ppermute(cols, "gy", down_y),
    )


def local(tables, fields, levels, cuts, parent_modes, owners, plume, source):
    n_gx, n_gy = lax.axis_size("gx"), lax.axis_size("gy")
    devices = n_gx * n_gy
    level_total, cells_x, cells_y = plume.shape
    period = n_gx * cells_x * n_gy * cells_y
    nudged = 3 * levels.shape[0]
    field_rows = 3 * level_total
    total = field_rows + level_total
    lanes = 4 * KX
    rows = nudged * KX // devices
    flat = fields.reshape(field_rows, cells_x, cells_y)
    cuts = cuts.reshape(-1)
    f32 = functools.partial(jax.ShapeDtypeStruct, dtype=jnp.float32)
    x_fwd, x_back, y_fwd, y_back = (jnp.asarray(t) for t in tables)

    def vmem(*shape):
        return pltpu.VMEM(shape, jnp.float32)

    def table_space(table):
        return pltpu.VMEM(table.shape[1:], table.dtype)

    def limit(mib):
        return pltpu.CompilerParams(vmem_limit_bytes=mib * 1024 * 1024)

    mode_shape = f32((nudged, KX, lanes))
    parent_space = vmem(nudged, 4 * KX * KX)
    step_scratch = [table_space(x_back), table_space(y_back),
                    vmem(total, cells_x + 2 * PAD, cells_y), vmem(field_rows, cells_x, cells_y),
                    pltpu.SemaphoreType.DMA((5,))]
    mode_scratch = [parent_space, table_space(x_fwd), table_space(y_fwd)]

    modes = pl.pallas_call(
        functools.partial(first_kernel, n_gy, level_total),
        out_shape=mode_shape,
        in_specs=[SMEM, SMEM] + [HBM] * 4,
        out_specs=VMEM,
        scratch_shapes=[table_space(x_fwd), table_space(y_fwd),
                        vmem(field_rows, cells_x, cells_y), parent_space,
                        pltpu.SemaphoreType.DMA((4,))],
        compiler_params=limit(FIRST_MIB),
        name="first_modes",
    )(levels, owners, flat, parent_modes, x_fwd, y_fwd)
    for step in range(STEPS):
        last = step == STEPS - 1
        edges = pl.pallas_call(
            edge_kernel,
            out_shape=[f32((total, cells_y)), f32((total, cells_y)), f32((cells_x, 2 * total))],
            in_specs=[VMEM, VMEM],
            out_specs=[VMEM] * 3,
            compiler_params=limit(8),
            name="edges",
        )(flat, plume)
        halo = swap_edges(*edges)
        parts = lax.all_to_all(modes.reshape(devices, rows, lanes), AXES, 0, 0, tiled=True)
        share = pl.pallas_call(
            functools.partial(share_kernel, n_gy, period),
            out_shape=f32((devices, rows, lanes)),
            in_specs=[SMEM, VMEM],
            out_specs=VMEM,
            compiler_params=limit(4),
            name="share_sum",
        )(cuts, parts)
        mismatch = lax.all_to_all(share, AXES, 0, 0, tiled=True)
        out_shape = [f32(flat.shape), f32(plume.shape)]
        operands = [levels, owners, mismatch.reshape(nudged * KX, lanes), flat, plume, source,
                    *halo, x_back, y_back]
        if not last:
            out_shape.append(mode_shape)
            operands += [parent_modes, x_fwd, y_fwd]
        results = pl.pallas_call(
            functools.partial(step_kernel, n_gy, step, last),
            out_shape=out_shape,
            in_specs=[SMEM, SMEM] + [VMEM] * 8 + [HBM] * (len(operands) - 10),
            out_specs=[VMEM] * len(out_shape),
            scratch_shapes=step_scratch + ([] if last else mode_scratch),
            compiler_params=limit(20),
            name="final_step" if last else "inner_step",
        )(*operands)
        if last:
            flat, plume = results
        else:
            flat, plume, modes = results
    return flat.reshape(fields.shape), plume


def solution(mesh):
    in_specs = (
        P(None, None, "gx", "gy"),
        P(),
        P(),
        P(("gx", "gy"), None, None, None),
        P(),
        P(None, "gx", "gy"),
        P(None, "gx", "gy"),
    )
    out_specs = (P(None, None, "gx", "gy"), P(None, "gx", "gy"))
    n_gx, n_gy = mesh.shape["gx"], mesh.shape["gy"]

    def whole(fields, levels, cuts, parent_modes, owners, plume, source):
        tables = build_tables(n_gx, n_gy, plume.shape[1] // n_gx, plume.shape[2] // n_gy)
        return jax.shard_map(
            functools.partial(local, tables), mesh=mesh, in_specs=in_specs, out_specs=out_specs,
            check_vma=False,
        )(fields, levels, cuts, parent_modes, owners, plume, source)

    return whole
```

```python
import functools
import math

import jax
import jax.numpy as jnp
import ml_dtypes
import numpy as np
from jax import lax
from jax.experimental import pallas as pl
from jax.experimental.pallas import tpu as pltpu
from jax.sharding import PartitionSpec as P

KX = 32
STEPS = 2
PAD = 8
VMEM = pl.BlockSpec(memory_space=pltpu.VMEM)
SMEM = pl.BlockSpec(memory_space=pltpu.SMEM)
HBM = pl.BlockSpec(memory_space=pltpu.HBM)
AXES = ("gx", "gy")


def in_hbm(array):
    return pltpu.with_memory_space_constraint(array, pltpu.HBM)


def wave_table(positions, period):
    wavenum = np.arange(KX)[:, None]
    phase = (wavenum * positions[None, :] % period) * (2.0 * math.pi / period)
    inside = (positions >= 0) & (positions < period)
    return np.concatenate([np.cos(phase), np.sin(phase)], axis=0) * inside[None, :]


def split(a):
    head = a.astype(jnp.bfloat16)
    return head, (a - head.astype(jnp.float32)).astype(jnp.bfloat16)


def split_table(table, axis, order):
    head = table.astype(ml_dtypes.bfloat16)
    rest = (table - head.astype(np.float64)).astype(ml_dtypes.bfloat16)
    return np.concatenate([head if part == "h" else rest for part in order], axis=axis)


def build_tables(n_gx, n_gy, cells_x, cells_y):
    period_x, period_y = n_gx * cells_x, n_gy * cells_y
    order = np.concatenate([np.arange(0, 2 * KX, 2), np.arange(1, 2 * KX, 2)])
    scaling = 1.0 / math.sqrt(period_x * period_y)
    x_fwd, x_back, y_fwd, y_back = [], [], [], []
    for g in range(n_gx):
        first = g * cells_x
        forward = wave_table(first + np.arange(cells_x), period_x)[order]
        x_fwd.append(split_table(forward, 1, "hlh"))
        rows = np.concatenate([first + np.arange(cells_x), [first - 1, first + cells_x]])
        back = np.zeros((cells_x + 16, 2 * KX))
        back[: cells_x + 2] = wave_table(rows, period_x)[order].T
        x_back.append(split_table(back, 1, "hlh"))
    for g in range(n_gy):
        first = g * cells_y
        table = wave_table(first + np.arange(cells_y), period_y)
        edge = np.zeros((2 * KX, cells_y))
        edge[:, [0, -1]] = wave_table(np.array([first - 1, first + cells_y]), period_y)
        forward = np.concatenate([table.T, table.T], axis=1) * scaling
        y_fwd.append(split_table(forward, 0, "hhl"))
        none = np.zeros_like(table)
        back = np.concatenate(
            [
                np.concatenate([table, edge, none, none], axis=1),
                np.concatenate([none, none, table, edge], axis=1),
            ],
            axis=0,
        )
        y_back.append(split_table(back, 0, "hhl"))
    return [np.stack(t) for t in (x_fwd, x_back, y_fwd, y_back)]


def data_dot(a, table):
    head, rest = split(a)
    return jnp.dot(
        jnp.concatenate([head, rest, head], axis=1), table, preferred_element_type=jnp.float32
    )


def table_dot(table, a):
    head, rest = split(a)
    return jnp.dot(
        table, jnp.concatenate([head, head, rest], axis=0), preferred_element_type=jnp.float32
    )


def emit_modes(read, x_fwd, y_fwd, modes_ref):
    nudged = modes_ref.shape[0]
    slabs = [read(c) for c in range(nudged)]
    cells_x = slabs[0].shape[0]
    half = data_dot(jnp.concatenate(slabs, axis=0), y_fwd)
    lane = lax.broadcasted_iota(jnp.int32, (KX, 4 * KX), 1)
    for c in range(nudged):
        both = table_dot(x_fwd, half[c * cells_x : (c + 1) * cells_x])
        modes_ref[c] = -jnp.where(lane < 2 * KX, both[:KX], both[KX:])


def add_parent(parent, is_owner, modes_ref):
    @pl.when(is_owner)
    def _():
        for i in range(KX):
            tile = parent[:, i * 4 * KX : (i + 1) * 4 * KX]
            modes_ref[:, i, :] = modes_ref[:, i, :] + tile


def fetch_all(sems, pairs):
    copies = [pltpu.make_async_copy(a, b, sems.at[i]) for i, (a, b) in enumerate(pairs)]
    for copy in copies:
        copy.start()
    return copies


def slab_of(levels, c, level_count, level_total):
    return (c // level_count) * level_total + levels[c % level_count]


def first_kernel(n_gy, level_total, levels, owners, fields_all, parent_all, x_fwd_all, y_fwd_all,
                 modes, x_fwd, y_fwd, fields, parent, sems):
    gx, gy = lax.axis_index("gx"), lax.axis_index("gy")
    copies = fetch_all(sems, [
        (fields_all, fields), (x_fwd_all.at[gx], x_fwd), (y_fwd_all.at[gy], y_fwd),
        (parent_all.at[0, 0], parent)])
    for copy in copies[:3]:
        copy.wait()
    level_count = modes.shape[0] // 3
    emit_modes(
        lambda c: fields[slab_of(levels, c, level_count, level_total)], x_fwd[...], y_fwd[...],
        modes,
    )
    copies[3].wait()
    add_parent(parent, owners[0] == gx * n_gy + gy, modes)


def edge_kernel(fields, plume, west, east, cols):
    cells_x, cells_y = plume.shape[1:]
    field_rows = fields.shape[0]
    lane = lax.broadcasted_iota(jnp.int32, cols.shape, 1)
    acc = jnp.zeros(cols.shape, jnp.float32)
    for c in range(field_rows + plume.shape[0]):
        a = fields[c] if c < field_rows else plume[c - field_rows]
        west[c : c + 1, :] = a[:1]
        east[c : c + 1, :] = a[cells_x - 1 :]
        acc = jnp.where(lane // 2 == c, pltpu.roll(a, 2 * c + 1, 1), acc)
    cols[...] = acc


def share_kernel(n_gy, period, cuts, parts, out):
    count, rows, lanes = parts.shape
    me = lax.axis_index("gx") * n_gy + lax.axis_index("gy")
    total = parts[0]
    for p in range(1, count):
        total = total + parts[p]
    row = me * rows + lax.broadcasted_iota(jnp.int32, (rows, lanes), 0)
    lane = lax.broadcasted_iota(jnp.int32, (rows, lanes), 1)
    slab, pair = row // KX, row % KX
    r = 2 * pair + lane // (2 * KX)
    s = lane % (2 * KX)
    limit = jnp.zeros((rows, lanes), jnp.int32)
    for c in range(cuts.shape[0]):
        limit = jnp.where(slab == c, cuts[c], limit)
    keep = ((r % KX) < limit) & ((s % KX) < limit)
    factor = jnp.where(r == 0, 1.0, 2.0) * jnp.where(s == 0, 1.0, 2.0) * (1.0 / math.sqrt(period))
    result = jnp.where(keep, total * factor, 0.0)
    for p in range(count):
        out[p] = result


def step_kernel(n_gy, step, last, levels, owners, mismatch, fields, plume, source,
                west, east, south, north, x_back_all, y_back_all, *rest):
    gx, gy = lax.axis_index("gx"), lax.axis_index("gy")
    extra = []
    if last:
        fields_out, plume_out, x_back, y_back, slabs, beside, sems = rest
    else:
        (parent_all, x_fwd_all, y_fwd_all, fields_out, plume_out, modes,
         x_back, y_back, slabs, beside, sems, parent, x_fwd, y_fwd) = rest
        extra = [(x_fwd_all.at[gx], x_fwd), (y_fwd_all.at[gy], y_fwd),
                 (parent_all.at[0, step + 1], parent)]
    copies = fetch_all(
        sems, [(y_back_all.at[gy], y_back), (x_back_all.at[gx], x_back)] + extra)
    level_total, cells_x, cells_y = plume.shape
    field_rows = fields.shape[0]
    total = field_rows + level_total
    nudged = mismatch.shape[0] // KX
    level_count = nudged // 3
    inner = slice(PAD, PAD + cells_x)
    for c in range(total):
        slabs[c, inner] = fields[c] if c < field_rows else plume[c - field_rows]
        slabs[c, PAD - 1 : PAD] = west[c : c + 1, :]
        slabs[c, PAD + cells_x : PAD + cells_x + 1] = east[c : c + 1, :]
    beside[...] = jnp.zeros_like(beside)
    for copy in copies:
        copy.wait()
    back = data_dot(mismatch[...], y_back[...])
    x_table = x_back[...]
    for c in range(nudged):
        pair = back[c * KX : (c + 1) * KX]
        update = table_dot(
            x_table, jnp.concatenate([pair[:, : 2 * cells_y], pair[:, 2 * cells_y :]], axis=0))
        spot = slab_of(levels, c, level_count, level_total)
        slabs[spot, inner] += update[:cells_x, :cells_y]
        slabs[spot, PAD - 1 : PAD] += update[cells_x : cells_x + 1, :cells_y]
        slabs[spot, PAD + cells_x : PAD + cells_x + 1] += update[cells_x + 1 : cells_x + 2, :cells_y]
        beside[spot] = update[:cells_x, cells_y:]

    lane = lax.broadcasted_iota(jnp.int32, (cells_x, cells_y), 1)
    first, final = lane == 0, lane == cells_y - 1
    columns = jnp.where(
        lane % 2 == 0, pltpu.roll(north[...], cells_y - 1, 1), pltpu.roll(south[...], 1, 1))

    def advance(c, parts):
        centre, to_west, to_east, to_south, to_north = parts
        a = slabs[c, inner]
        column = pltpu.roll(columns, cells_y - 1 - 2 * c, 1)
        if c < field_rows:
            column = column + beside[c]
        return (
            centre * a
            + to_west * slabs[c, PAD - 1 : PAD - 1 + cells_x]
            + to_east * slabs[c, PAD + 1 : PAD + 1 + cells_x]
            + to_south * jnp.where(first, column, pltpu.roll(a, 1, 1))
            + to_north * jnp.where(final, column, pltpu.roll(a, cells_y - 1, 1))
        )

    for l in range(level_total):
        u, v = slabs[l, inner], slabs[level_total + l, inner]
        beside_parts = (
            0.1 + 0.1 * jnp.maximum(u, 0.0), 0.1 - 0.1 * jnp.minimum(u, 0.0),
            0.1 + 0.1 * jnp.maximum(v, 0.0), 0.1 - 0.1 * jnp.minimum(v, 0.0),
        )
        centre = 1.0 - (beside_parts[0] + beside_parts[1] + beside_parts[2] + beside_parts[3])
        for f in range(3):
            fields_out[f * level_total + l] = advance(
                f * level_total + l, (centre,) + beside_parts)
        settled = advance(field_rows + l, (centre - 0.3,) + beside_parts) + source[l]
        if l + 1 < level_total:
            settled = settled + 0.3 * plume[l + 1]
        plume_out[l] = settled

    if last:
        return
    emit_modes(
        lambda c: fields_out[slab_of(levels, c, level_count, level_total)], x_fwd[...], y_fwd[...],
        modes,
    )
    add_parent(parent, owners[step + 1] == gx * n_gy + gy, modes)


def swap_edges(west, east, cols):
    n_gx, n_gy = lax.axis_size("gx"), lax.axis_size("gy")
    up_x = [(i, i + 1) for i in range(n_gx - 1)]
    up_y = [(i, i + 1) for i in range(n_gy - 1)]
    down_x = [(b, a) for a, b in up_x]
    down_y = [(b, a) for a, b in up_y]
    return (
        lax.ppermute(east, "gx", up_x),
        lax.ppermute(west, "gx", down_x),
        lax.ppermute(cols, "gy", up_y),
        lax.ppermute(cols, "gy", down_y),
    )


def local(tables, fields, levels, cuts, parent_modes, owners, plume, source):
    n_gx, n_gy = lax.axis_size("gx"), lax.axis_size("gy")
    devices = n_gx * n_gy
    level_total, cells_x, cells_y = plume.shape
    period = n_gx * cells_x * n_gy * cells_y
    nudged = 3 * levels.shape[0]
    field_rows = 3 * level_total
    total = field_rows + level_total
    lanes = 4 * KX
    rows = nudged * KX // devices
    flat = fields.reshape(field_rows, cells_x, cells_y)
    cuts = cuts.reshape(-1)
    f32 = functools.partial(jax.ShapeDtypeStruct, dtype=jnp.float32)
    x_fwd, x_back, y_fwd, y_back = (jnp.asarray(t) for t in tables)

    def vmem(*shape):
        return pltpu.VMEM(shape, jnp.float32)

    def table_space(table):
        return pltpu.VMEM(table.shape[1:], table.dtype)

    def limit(mib):
        return pltpu.CompilerParams(vmem_limit_bytes=mib * 1024 * 1024)

    mode_shape = f32((nudged, KX, lanes))
    parent_space = vmem(nudged, 4 * KX * KX)
    step_scratch = [table_space(x_back), table_space(y_back),
                    vmem(total, cells_x + 2 * PAD, cells_y), vmem(field_rows, cells_x, cells_y),
                    pltpu.SemaphoreType.DMA((5,))]
    mode_scratch = [parent_space, table_space(x_fwd), table_space(y_fwd)]

    modes = pl.pallas_call(
        functools.partial(first_kernel, n_gy, level_total),
        out_shape=mode_shape,
        in_specs=[SMEM, SMEM] + [HBM] * 4,
        out_specs=VMEM,
        scratch_shapes=[table_space(x_fwd), table_space(y_fwd),
                        vmem(field_rows, cells_x, cells_y), parent_space,
                        pltpu.SemaphoreType.DMA((4,))],
        compiler_params=limit(8),
        name="first_modes",
    )(levels, owners, in_hbm(flat), in_hbm(parent_modes), in_hbm(x_fwd), in_hbm(y_fwd))
    for step in range(STEPS):
        last = step == STEPS - 1
        edges = pl.pallas_call(
            edge_kernel,
            out_shape=[f32((total, cells_y)), f32((total, cells_y)), f32((cells_x, 2 * total))],
            in_specs=[VMEM, VMEM],
            out_specs=[VMEM] * 3,
            compiler_params=limit(8),
            name="edges",
        )(flat, plume)
        halo = swap_edges(*edges)
        parts = lax.all_to_all(modes.reshape(devices, rows, lanes), AXES, 0, 0, tiled=True)
        parts, *halo = lax.optimization_barrier((parts, *halo))
        share = pl.pallas_call(
            functools.partial(share_kernel, n_gy, period),
            out_shape=f32((devices, rows, lanes)),
            in_specs=[SMEM, VMEM],
            out_specs=VMEM,
            compiler_params=limit(4),
            name="share_sum",
        )(cuts, parts)
        mismatch = lax.all_to_all(share, AXES, 0, 0, tiled=True)
        out_shape = [f32(flat.shape), f32(plume.shape)]
        operands = [levels, owners, mismatch.reshape(nudged * KX, lanes), flat, plume, source,
                    *halo, in_hbm(x_back), in_hbm(y_back)]
        if not last:
            out_shape.append(mode_shape)
            operands += [in_hbm(parent_modes), in_hbm(x_fwd), in_hbm(y_fwd)]
        results = pl.pallas_call(
            functools.partial(step_kernel, n_gy, step, last),
            out_shape=out_shape,
            in_specs=[SMEM, SMEM] + [VMEM] * 8 + [HBM] * (len(operands) - 10),
            out_specs=[VMEM] * len(out_shape),
            scratch_shapes=step_scratch + ([] if last else mode_scratch),
            compiler_params=limit(20),
            name="final_step" if last else "inner_step",
        )(*operands)
        if last:
            flat, plume = results
        else:
            flat, plume, modes = results
    return flat.reshape(fields.shape), plume


def solution(mesh):
    in_specs = (
        P(None, None, "gx", "gy"),
        P(),
        P(),
        P(("gx", "gy"), None, None, None),
        P(),
        P(None, "gx", "gy"),
        P(None, "gx", "gy"),
    )
    out_specs = (P(None, None, "gx", "gy"), P(None, "gx", "gy"))
    n_gx, n_gy = mesh.shape["gx"], mesh.shape["gy"]

    def whole(fields, levels, cuts, parent_modes, owners, plume, source):
        tables = build_tables(n_gx, n_gy, plume.shape[1] // n_gx, plume.shape[2] // n_gy)
        return jax.shard_map(
            functools.partial(local, tables), mesh=mesh, in_specs=in_specs, out_specs=out_specs,
            check_vma=False,
        )(fields, levels, cuts, parent_modes, owners, plume, source)

    return whole
```

```python
import functools
import math

import jax
import jax.numpy as jnp
import ml_dtypes
import numpy as np
from jax import lax
from jax.experimental import pallas as pl
from jax.experimental.pallas import tpu as pltpu
from jax.sharding import PartitionSpec as P

KX = 32
STEPS = 2
PAD = 8
VMEM = pl.BlockSpec(memory_space=pltpu.VMEM)
SMEM = pl.BlockSpec(memory_space=pltpu.SMEM)
HBM = pl.BlockSpec(memory_space=pltpu.HBM)
AXES = ("gx", "gy")


def in_hbm(array):
    return pltpu.with_memory_space_constraint(array, pltpu.HBM)


def wave_table(positions, period):
    wavenum = np.arange(KX)[:, None]
    phase = (wavenum * positions[None, :] % period) * (2.0 * math.pi / period)
    inside = (positions >= 0) & (positions < period)
    return np.concatenate([np.cos(phase), np.sin(phase)], axis=0) * inside[None, :]


def split(a):
    head = a.astype(jnp.bfloat16)
    return head, (a - head.astype(jnp.float32)).astype(jnp.bfloat16)


def split_table(table, axis, order):
    head = table.astype(ml_dtypes.bfloat16)
    rest = (table - head.astype(np.float64)).astype(ml_dtypes.bfloat16)
    return np.concatenate([head if part == "h" else rest for part in order], axis=axis)


def build_tables(n_gx, n_gy, cells_x, cells_y):
    period_x, period_y = n_gx * cells_x, n_gy * cells_y
    order = np.concatenate([np.arange(0, 2 * KX, 2), np.arange(1, 2 * KX, 2)])
    scaling = 1.0 / math.sqrt(period_x * period_y)
    x_fwd, x_back, y_fwd, y_back = [], [], [], []
    for g in range(n_gx):
        first = g * cells_x
        forward = wave_table(first + np.arange(cells_x), period_x)[order]
        x_fwd.append(split_table(forward, 1, "hlh"))
        rows = np.concatenate([first + np.arange(cells_x), [first - 1, first + cells_x]])
        back = np.zeros((cells_x + 16, 2 * KX))
        back[: cells_x + 2] = wave_table(rows, period_x)[order].T
        x_back.append(split_table(back, 1, "hlh"))
    for g in range(n_gy):
        first = g * cells_y
        table = wave_table(first + np.arange(cells_y), period_y)
        edge = np.zeros((2 * KX, cells_y))
        edge[:, [0, -1]] = wave_table(np.array([first - 1, first + cells_y]), period_y)
        forward = np.concatenate([table.T, table.T], axis=1) * scaling
        y_fwd.append(split_table(forward, 0, "hhl"))
        none = np.zeros_like(table)
        back = np.concatenate(
            [
                np.concatenate([table, edge, none, none], axis=1),
                np.concatenate([none, none, table, edge], axis=1),
            ],
            axis=0,
        )
        y_back.append(split_table(back, 0, "hhl"))
    return [np.stack(t) for t in (x_fwd, x_back, y_fwd, y_back)]


def data_dot(a, table):
    head, rest = split(a)
    return jnp.dot(
        jnp.concatenate([head, rest, head], axis=1), table, preferred_element_type=jnp.float32
    )


def table_dot(table, a):
    head, rest = split(a)
    return jnp.dot(
        table, jnp.concatenate([head, head, rest], axis=0), preferred_element_type=jnp.float32
    )


def emit_modes(read, x_fwd, y_fwd, winds, heat):
    wind_slabs = winds.shape[0]
    nudged = wind_slabs + heat.shape[0]
    slabs = [read(c) for c in range(nudged)]
    cells_x = slabs[0].shape[0]
    half = data_dot(jnp.concatenate(slabs, axis=0), y_fwd)
    lane = lax.broadcasted_iota(jnp.int32, (KX, 4 * KX), 1)
    for c in range(nudged):
        both = table_dot(x_fwd, half[c * cells_x : (c + 1) * cells_x])
        modes = -jnp.where(lane < 2 * KX, both[:KX], both[KX:])
        if c < wind_slabs:
            winds[c] = modes
        else:
            heat[c - wind_slabs] = modes


def add_parent(parent, is_owner, winds, heat):
    @pl.when(is_owner)
    def _():
        for i in range(KX):
            tile = parent[:, i * 4 * KX : (i + 1) * 4 * KX]
            winds[:, i, :] = winds[:, i, :] + tile[: winds.shape[0]]
            heat[:, i, :] = heat[:, i, :] + tile[winds.shape[0] :]


def fetch_all(sems, pairs):
    copies = [pltpu.make_async_copy(a, b, sems.at[i]) for i, (a, b) in enumerate(pairs)]
    for copy in copies:
        copy.start()
    return copies


def slab_of(levels, c, level_count, level_total):
    return (c // level_count) * level_total + levels[c % level_count]


def first_kernel(n_gy, level_total, levels, owners, fields_all, parent_all, x_fwd_all, y_fwd_all,
                 winds, heat, x_fwd, y_fwd, fields, parent, sems):
    gx, gy = lax.axis_index("gx"), lax.axis_index("gy")
    copies = fetch_all(sems, [
        (fields_all, fields), (x_fwd_all.at[gx], x_fwd), (y_fwd_all.at[gy], y_fwd),
        (parent_all.at[0, 0], parent)])
    for copy in copies[:3]:
        copy.wait()
    level_count = heat.shape[0]
    emit_modes(
        lambda c: fields[slab_of(levels, c, level_count, level_total)], x_fwd[...], y_fwd[...],
        winds, heat,
    )
    copies[3].wait()
    add_parent(parent, owners[0] == gx * n_gy + gy, winds, heat)


def edge_kernel(fields, plume, west, east, cols):
    cells_x, cells_y = plume.shape[1:]
    field_rows = fields.shape[0]
    lane = lax.broadcasted_iota(jnp.int32, cols.shape, 1)
    acc = jnp.zeros(cols.shape, jnp.float32)
    for c in range(field_rows + plume.shape[0]):
        a = fields[c] if c < field_rows else plume[c - field_rows]
        west[c : c + 1, :] = a[:1]
        east[c : c + 1, :] = a[cells_x - 1 :]
        acc = jnp.where(lane // 2 == c, pltpu.roll(a, 2 * c + 1, 1), acc)
    cols[...] = acc


def share_kernel(n_gy, period, first_slab, cuts, parts, out):
    count, rows, lanes = parts.shape
    me = lax.axis_index("gx") * n_gy + lax.axis_index("gy")
    total = parts[0]
    for p in range(1, count):
        total = total + parts[p]
    row = me * rows + lax.broadcasted_iota(jnp.int32, (rows, lanes), 0)
    lane = lax.broadcasted_iota(jnp.int32, (rows, lanes), 1)
    slab, pair = row // KX, row % KX
    r = 2 * pair + lane // (2 * KX)
    s = lane % (2 * KX)
    limit = jnp.zeros((rows, lanes), jnp.int32)
    for c in range(first_slab, cuts.shape[0]):
        limit = jnp.where(slab == c - first_slab, cuts[c], limit)
    keep = ((r % KX) < limit) & ((s % KX) < limit)
    factor = jnp.where(r == 0, 1.0, 2.0) * jnp.where(s == 0, 1.0, 2.0) * (1.0 / math.sqrt(period))
    result = jnp.where(keep, total * factor, 0.0)
    for p in range(count):
        out[p] = result


def step_kernel(n_gy, step, last, levels, owners, winds_in, heat_in, fields, plume, source,
                west, east, south, north, x_back_all, y_back_all, *rest):
    gx, gy = lax.axis_index("gx"), lax.axis_index("gy")
    extra = []
    if last:
        fields_out, plume_out, x_back, y_back, slabs, beside, sems = rest
    else:
        (parent_all, x_fwd_all, y_fwd_all, fields_out, plume_out, winds, heat,
         x_back, y_back, slabs, beside, sems, parent, x_fwd, y_fwd) = rest
        extra = [(x_fwd_all.at[gx], x_fwd), (y_fwd_all.at[gy], y_fwd),
                 (parent_all.at[0, step + 1], parent)]
    copies = fetch_all(
        sems, [(y_back_all.at[gy], y_back), (x_back_all.at[gx], x_back)] + extra)
    level_total, cells_x, cells_y = plume.shape
    field_rows = fields.shape[0]
    total = field_rows + level_total
    level_count = heat_in.shape[0] // KX
    nudged = 3 * level_count
    inner = slice(PAD, PAD + cells_x)
    for c in range(total):
        slabs[c, inner] = fields[c] if c < field_rows else plume[c - field_rows]
        slabs[c, PAD - 1 : PAD] = west[c : c + 1, :]
        slabs[c, PAD + cells_x : PAD + cells_x + 1] = east[c : c + 1, :]
    beside[...] = jnp.zeros_like(beside)
    for copy in copies:
        copy.wait()
    back = data_dot(jnp.concatenate([winds_in[...], heat_in[...]], axis=0), y_back[...])
    x_table = x_back[...]
    for c in range(nudged):
        pair = back[c * KX : (c + 1) * KX]
        update = table_dot(
            x_table, jnp.concatenate([pair[:, : 2 * cells_y], pair[:, 2 * cells_y :]], axis=0))
        spot = slab_of(levels, c, level_count, level_total)
        slabs[spot, inner] += update[:cells_x, :cells_y]
        slabs[spot, PAD - 1 : PAD] += update[cells_x : cells_x + 1, :cells_y]
        slabs[spot, PAD + cells_x : PAD + cells_x + 1] += update[cells_x + 1 : cells_x + 2, :cells_y]
        beside[spot] = update[:cells_x, cells_y:]

    lane = lax.broadcasted_iota(jnp.int32, (cells_x, cells_y), 1)
    first, final = lane == 0, lane == cells_y - 1
    columns = jnp.where(
        lane % 2 == 0, pltpu.roll(north[...], cells_y - 1, 1), pltpu.roll(south[...], 1, 1))

    def advance(c, parts):
        centre, to_west, to_east, to_south, to_north = parts
        a = slabs[c, inner]
        column = pltpu.roll(columns, cells_y - 1 - 2 * c, 1)
        if c < field_rows:
            column = column + beside[c]
        return (
            centre * a
            + to_west * slabs[c, PAD - 1 : PAD - 1 + cells_x]
            + to_east * slabs[c, PAD + 1 : PAD + 1 + cells_x]
            + to_south * jnp.where(first, column, pltpu.roll(a, 1, 1))
            + to_north * jnp.where(final, column, pltpu.roll(a, cells_y - 1, 1))
        )

    for l in range(level_total):
        u, v = slabs[l, inner], slabs[level_total + l, inner]
        beside_parts = (
            0.1 + 0.1 * jnp.maximum(u, 0.0), 0.1 - 0.1 * jnp.minimum(u, 0.0),
            0.1 + 0.1 * jnp.maximum(v, 0.0), 0.1 - 0.1 * jnp.minimum(v, 0.0),
        )
        centre = 1.0 - (beside_parts[0] + beside_parts[1] + beside_parts[2] + beside_parts[3])
        for f in range(3):
            fields_out[f * level_total + l] = advance(
                f * level_total + l, (centre,) + beside_parts)
        settled = advance(field_rows + l, (centre - 0.3,) + beside_parts) + source[l]
        if l + 1 < level_total:
            settled = settled + 0.3 * plume[l + 1]
        plume_out[l] = settled

    if last:
        return
    emit_modes(
        lambda c: fields_out[slab_of(levels, c, level_count, level_total)], x_fwd[...], y_fwd[...],
        winds, heat,
    )
    add_parent(parent, owners[step + 1] == gx * n_gy + gy, winds, heat)


def swap_edges(west, east, cols):
    n_gx, n_gy = lax.axis_size("gx"), lax.axis_size("gy")
    up_x = [(i, i + 1) for i in range(n_gx - 1)]
    up_y = [(i, i + 1) for i in range(n_gy - 1)]
    down_x = [(b, a) for a, b in up_x]
    down_y = [(b, a) for a, b in up_y]
    return (
        lax.ppermute(east, "gx", up_x),
        lax.ppermute(west, "gx", down_x),
        lax.ppermute(cols, "gy", up_y),
        lax.ppermute(cols, "gy", down_y),
    )


def local(tables, fields, levels, cuts, parent_modes, owners, plume, source):
    n_gx, n_gy = lax.axis_size("gx"), lax.axis_size("gy")
    devices = n_gx * n_gy
    level_total, cells_x, cells_y = plume.shape
    period = n_gx * cells_x * n_gy * cells_y
    nudged = 3 * levels.shape[0]
    field_rows = 3 * level_total
    total = field_rows + level_total
    lanes = 4 * KX
    flat = fields.reshape(field_rows, cells_x, cells_y)
    cuts = cuts.reshape(-1)
    f32 = functools.partial(jax.ShapeDtypeStruct, dtype=jnp.float32)
    x_fwd, x_back, y_fwd, y_back = (jnp.asarray(t) for t in tables)

    def vmem(*shape):
        return pltpu.VMEM(shape, jnp.float32)

    def table_space(table):
        return pltpu.VMEM(table.shape[1:], table.dtype)

    def limit(mib):
        return pltpu.CompilerParams(vmem_limit_bytes=mib * 1024 * 1024)

    level_count = levels.shape[0]
    mode_shapes = [f32((2 * level_count, KX, lanes)), f32((level_count, KX, lanes))]
    parent_space = vmem(nudged, 4 * KX * KX)
    step_scratch = [table_space(x_back), table_space(y_back),
                    vmem(total, cells_x + 2 * PAD, cells_y), vmem(field_rows, cells_x, cells_y),
                    pltpu.SemaphoreType.DMA((5,))]
    mode_scratch = [parent_space, table_space(x_fwd), table_space(y_fwd)]

    modes = pl.pallas_call(
        functools.partial(first_kernel, n_gy, level_total),
        out_shape=mode_shapes,
        in_specs=[SMEM, SMEM] + [HBM] * 4,
        out_specs=[VMEM] * 2,
        scratch_shapes=[table_space(x_fwd), table_space(y_fwd),
                        vmem(field_rows, cells_x, cells_y), parent_space,
                        pltpu.SemaphoreType.DMA((4,))],
        compiler_params=limit(8),
        name="first_modes",
    )(levels, owners, in_hbm(flat), in_hbm(parent_modes), in_hbm(x_fwd), in_hbm(y_fwd))
    for step in range(STEPS):
        last = step == STEPS - 1
        edges = pl.pallas_call(
            edge_kernel,
            out_shape=[f32((total, cells_y)), f32((total, cells_y)), f32((cells_x, 2 * total))],
            in_specs=[VMEM, VMEM],
            out_specs=[VMEM] * 3,
            compiler_params=limit(8),
            name="edges",
        )(flat, plume)
        west, east, south, north = swap_edges(*edges)
        parts = [
            lax.all_to_all(m.reshape(devices, -1, lanes), AXES, 0, 0, tiled=True) for m in modes
        ]
        parts[1], west, east = lax.optimization_barrier((parts[1], west, east))
        halo = west, east, south, north
        mismatch = []
        for part, first_slab in zip(parts, (0, 2 * level_count)):
            share = pl.pallas_call(
                functools.partial(share_kernel, n_gy, period, first_slab),
                out_shape=f32(part.shape),
                in_specs=[SMEM, VMEM],
                out_specs=VMEM,
                compiler_params=limit(4),
                name="share_heat" if first_slab else "share_winds",
            )(cuts, part)
            mismatch.append(lax.all_to_all(share, AXES, 0, 0, tiled=True).reshape(-1, lanes))
        out_shape = [f32(flat.shape), f32(plume.shape)]
        operands = [levels, owners, *mismatch, flat, plume, source,
                    *halo, in_hbm(x_back), in_hbm(y_back)]
        if not last:
            out_shape += mode_shapes
            operands += [in_hbm(parent_modes), in_hbm(x_fwd), in_hbm(y_fwd)]
        results = pl.pallas_call(
            functools.partial(step_kernel, n_gy, step, last),
            out_shape=out_shape,
            in_specs=[SMEM, SMEM] + [VMEM] * 9 + [HBM] * (len(operands) - 11),
            out_specs=[VMEM] * len(out_shape),
            scratch_shapes=step_scratch + ([] if last else mode_scratch),
            compiler_params=limit(20),
            name="final_step" if last else "inner_step",
        )(*operands)
        if last:
            flat, plume = results
        else:
            flat, plume, *modes = results
    return flat.reshape(fields.shape), plume


def solution(mesh):
    in_specs = (
        P(None, None, "gx", "gy"),
        P(),
        P(),
        P(("gx", "gy"), None, None, None),
        P(),
        P(None, "gx", "gy"),
        P(None, "gx", "gy"),
    )
    out_specs = (P(None, None, "gx", "gy"), P(None, "gx", "gy"))
    n_gx, n_gy = mesh.shape["gx"], mesh.shape["gy"]

    def whole(fields, levels, cuts, parent_modes, owners, plume, source):
        tables = build_tables(n_gx, n_gy, plume.shape[1] // n_gx, plume.shape[2] // n_gy)
        return jax.shard_map(
            functools.partial(local, tables), mesh=mesh, in_specs=in_specs, out_specs=out_specs,
            check_vma=False,
        )(fields, levels, cuts, parent_modes, owners, plume, source)

    return whole
```

```python
import functools
import math

import jax
import jax.numpy as jnp
import ml_dtypes
import numpy as np
from jax import lax
from jax.experimental import pallas as pl
from jax.experimental.pallas import tpu as pltpu
from jax.sharding import PartitionSpec as P

KX = 32
STEPS = 2
PAD = 8
VMEM = pl.BlockSpec(memory_space=pltpu.VMEM)
SMEM = pl.BlockSpec(memory_space=pltpu.SMEM)
HBM = pl.BlockSpec(memory_space=pltpu.HBM)
AXES = ("gx", "gy")


def in_hbm(array):
    return pltpu.with_memory_space_constraint(array, pltpu.HBM)


def wave_table(positions, period):
    wavenum = np.arange(KX)[:, None]
    phase = (wavenum * positions[None, :] % period) * (2.0 * math.pi / period)
    inside = (positions >= 0) & (positions < period)
    return np.concatenate([np.cos(phase), np.sin(phase)], axis=0) * inside[None, :]


def split(a):
    head = a.astype(jnp.bfloat16)
    return head, (a - head.astype(jnp.float32)).astype(jnp.bfloat16)


def split_table(table, axis, order):
    head = table.astype(ml_dtypes.bfloat16)
    rest = (table - head.astype(np.float64)).astype(ml_dtypes.bfloat16)
    return np.concatenate([head if part == "h" else rest for part in order], axis=axis)


def build_tables(n_gx, n_gy, cells_x, cells_y):
    period_x, period_y = n_gx * cells_x, n_gy * cells_y
    order = np.concatenate([np.arange(0, 2 * KX, 2), np.arange(1, 2 * KX, 2)])
    scaling = 1.0 / math.sqrt(period_x * period_y)
    x_fwd, x_back, y_fwd, y_back = [], [], [], []
    for g in range(n_gx):
        first = g * cells_x
        forward = wave_table(first + np.arange(cells_x), period_x)[order]
        x_fwd.append(split_table(forward, 1, "hlh"))
        rows = np.concatenate([first + np.arange(cells_x), [first - 1, first + cells_x]])
        back = np.zeros((cells_x + 16, 2 * KX))
        back[: cells_x + 2] = wave_table(rows, period_x)[order].T
        x_back.append(split_table(back, 1, "hlh"))
    for g in range(n_gy):
        first = g * cells_y
        table = wave_table(first + np.arange(cells_y), period_y)
        edge = np.zeros((2 * KX, cells_y))
        edge[:, [0, -1]] = wave_table(np.array([first - 1, first + cells_y]), period_y)
        forward = np.concatenate([table.T, table.T], axis=1) * scaling
        y_fwd.append(split_table(forward, 0, "hhl"))
        none = np.zeros_like(table)
        back = np.concatenate(
            [
                np.concatenate([table, edge, none, none], axis=1),
                np.concatenate([none, none, table, edge], axis=1),
            ],
            axis=0,
        )
        y_back.append(split_table(back, 0, "hhl"))
    return [np.stack(t) for t in (x_fwd, x_back, y_fwd, y_back)]


def data_dot(a, table):
    head, rest = split(a)
    return jnp.dot(
        jnp.concatenate([head, rest, head], axis=1), table, preferred_element_type=jnp.float32
    )


def table_dot(table, a):
    head, rest = split(a)
    return jnp.dot(
        table, jnp.concatenate([head, head, rest], axis=0), preferred_element_type=jnp.float32
    )


def emit_modes(read, x_fwd, y_fwd, modes_ref):
    nudged = modes_ref.shape[0]
    slabs = [read(c) for c in range(nudged)]
    cells_x = slabs[0].shape[0]
    half = data_dot(jnp.concatenate(slabs, axis=0), y_fwd)
    lane = lax.broadcasted_iota(jnp.int32, (KX, 4 * KX), 1)
    for c in range(nudged):
        both = table_dot(x_fwd, half[c * cells_x : (c + 1) * cells_x])
        modes_ref[c] = -jnp.where(lane < 2 * KX, both[:KX], both[KX:])


def add_parent(parent, is_owner, modes_ref):
    @pl.when(is_owner)
    def _():
        for i in range(KX):
            tile = parent[:, i * 4 * KX : (i + 1) * 4 * KX]
            modes_ref[:, i, :] = modes_ref[:, i, :] + tile


def fetch_all(sems, pairs):
    copies = [pltpu.make_async_copy(a, b, sems.at[i]) for i, (a, b) in enumerate(pairs)]
    for copy in copies:
        copy.start()
    return copies


def slab_of(levels, c, level_count, level_total):
    return (c // level_count) * level_total + levels[c % level_count]


def first_kernel(n_gy, level_total, levels, owners, fields_all, parent_all, x_fwd_all, y_fwd_all,
                 modes, x_fwd, y_fwd, fields, parent, sems):
    gx, gy = lax.axis_index("gx"), lax.axis_index("gy")
    copies = fetch_all(sems, [
        (fields_all, fields), (x_fwd_all.at[gx], x_fwd), (y_fwd_all.at[gy], y_fwd),
        (parent_all.at[0, 0], parent)])
    for copy in copies[:3]:
        copy.wait()
    level_count = modes.shape[0] // 3
    emit_modes(
        lambda c: fields[slab_of(levels, c, level_count, level_total)], x_fwd[...], y_fwd[...],
        modes,
    )
    copies[3].wait()
    add_parent(parent, owners[0] == gx * n_gy + gy, modes)


def edge_kernel(fields, plume, *rest):
    copies = []
    if len(rest) > 3:
        x_back_all, y_back_all, west, east, cols, x_back, y_back, sems = rest
        copies = fetch_all(sems, [(x_back_all.at[lax.axis_index("gx")], x_back),
                                  (y_back_all.at[lax.axis_index("gy")], y_back)])
    else:
        west, east, cols = rest
    cells_x, cells_y = plume.shape[1:]
    field_rows = fields.shape[0]
    lane = lax.broadcasted_iota(jnp.int32, cols.shape, 1)
    acc = jnp.zeros(cols.shape, jnp.float32)
    for c in range(field_rows + plume.shape[0]):
        a = fields[c] if c < field_rows else plume[c - field_rows]
        west[c : c + 1, :] = a[:1]
        east[c : c + 1, :] = a[cells_x - 1 :]
        acc = jnp.where(lane // 2 == c, pltpu.roll(a, 2 * c + 1, 1), acc)
    cols[...] = acc
    for copy in copies:
        copy.wait()


def share_kernel(n_gy, period, cuts, parts, out):
    count, rows, lanes = parts.shape
    me = lax.axis_index("gx") * n_gy + lax.axis_index("gy")
    total = parts[0]
    for p in range(1, count):
        total = total + parts[p]
    row = me * rows + lax.broadcasted_iota(jnp.int32, (rows, lanes), 0)
    lane = lax.broadcasted_iota(jnp.int32, (rows, lanes), 1)
    slab, pair = row // KX, row % KX
    r = 2 * pair + lane // (2 * KX)
    s = lane % (2 * KX)
    limit = jnp.zeros((rows, lanes), jnp.int32)
    for c in range(cuts.shape[0]):
        limit = jnp.where(slab == c, cuts[c], limit)
    keep = ((r % KX) < limit) & ((s % KX) < limit)
    factor = jnp.where(r == 0, 1.0, 2.0) * jnp.where(s == 0, 1.0, 2.0) * (1.0 / math.sqrt(period))
    result = jnp.where(keep, total * factor, 0.0)
    for p in range(count):
        out[p] = result


def step_kernel(n_gy, step, last, levels, owners, mismatch, fields, plume, source,
                west, east, south, north, x_back, y_back, *rest):
    gx, gy = lax.axis_index("gx"), lax.axis_index("gy")
    copies = []
    if last:
        fields_out, plume_out, slabs, beside = rest
    else:
        (parent_all, x_fwd_all, y_fwd_all, fields_out, plume_out, modes,
         slabs, beside, sems, parent, x_fwd, y_fwd) = rest
        copies = fetch_all(sems, [(x_fwd_all.at[gx], x_fwd), (y_fwd_all.at[gy], y_fwd),
                                  (parent_all.at[0, step + 1], parent)])
    level_total, cells_x, cells_y = plume.shape
    field_rows = fields.shape[0]
    total = field_rows + level_total
    nudged = mismatch.shape[0] // KX
    level_count = nudged // 3
    inner = slice(PAD, PAD + cells_x)
    for c in range(total):
        slabs[c, inner] = fields[c] if c < field_rows else plume[c - field_rows]
        slabs[c, PAD - 1 : PAD] = west[c : c + 1, :]
        slabs[c, PAD + cells_x : PAD + cells_x + 1] = east[c : c + 1, :]
    beside[...] = jnp.zeros_like(beside)
    back = data_dot(mismatch[...], y_back[...])
    x_table = x_back[...]
    for c in range(nudged):
        pair = back[c * KX : (c + 1) * KX]
        update = table_dot(
            x_table, jnp.concatenate([pair[:, : 2 * cells_y], pair[:, 2 * cells_y :]], axis=0))
        spot = slab_of(levels, c, level_count, level_total)
        slabs[spot, inner] += update[:cells_x, :cells_y]
        slabs[spot, PAD - 1 : PAD] += update[cells_x : cells_x + 1, :cells_y]
        slabs[spot, PAD + cells_x : PAD + cells_x + 1] += update[cells_x + 1 : cells_x + 2, :cells_y]
        beside[spot] = update[:cells_x, cells_y:]

    lane = lax.broadcasted_iota(jnp.int32, (cells_x, cells_y), 1)
    first, final = lane == 0, lane == cells_y - 1
    columns = jnp.where(
        lane % 2 == 0, pltpu.roll(north[...], cells_y - 1, 1), pltpu.roll(south[...], 1, 1))

    def advance(c, parts):
        centre, to_west, to_east, to_south, to_north = parts
        a = slabs[c, inner]
        column = pltpu.roll(columns, cells_y - 1 - 2 * c, 1)
        if c < field_rows:
            column = column + beside[c]
        return (
            centre * a
            + to_west * slabs[c, PAD - 1 : PAD - 1 + cells_x]
            + to_east * slabs[c, PAD + 1 : PAD + 1 + cells_x]
            + to_south * jnp.where(first, column, pltpu.roll(a, 1, 1))
            + to_north * jnp.where(final, column, pltpu.roll(a, cells_y - 1, 1))
        )

    for l in range(level_total):
        u, v = slabs[l, inner], slabs[level_total + l, inner]
        beside_parts = (
            0.1 + 0.1 * jnp.maximum(u, 0.0), 0.1 - 0.1 * jnp.minimum(u, 0.0),
            0.1 + 0.1 * jnp.maximum(v, 0.0), 0.1 - 0.1 * jnp.minimum(v, 0.0),
        )
        centre = 1.0 - (beside_parts[0] + beside_parts[1] + beside_parts[2] + beside_parts[3])
        for f in range(3):
            fields_out[f * level_total + l] = advance(
                f * level_total + l, (centre,) + beside_parts)
        settled = advance(field_rows + l, (centre - 0.3,) + beside_parts) + source[l]
        if l + 1 < level_total:
            settled = settled + 0.3 * plume[l + 1]
        plume_out[l] = settled

    if last:
        return
    for copy in copies:
        copy.wait()
    emit_modes(
        lambda c: fields_out[slab_of(levels, c, level_count, level_total)], x_fwd[...], y_fwd[...],
        modes,
    )
    add_parent(parent, owners[step + 1] == gx * n_gy + gy, modes)


def swap(axis, to_next, to_previous):
    count = lax.axis_size(axis)
    up = [(i, i + 1) for i in range(count - 1)]
    down = [(b, a) for a, b in up]
    return lax.ppermute(to_next, axis, up), lax.ppermute(to_previous, axis, down)


def local(tables, fields, levels, cuts, parent_modes, owners, plume, source):
    n_gx, n_gy = lax.axis_size("gx"), lax.axis_size("gy")
    devices = n_gx * n_gy
    level_total, cells_x, cells_y = plume.shape
    period = n_gx * cells_x * n_gy * cells_y
    nudged = 3 * levels.shape[0]
    field_rows = 3 * level_total
    total = field_rows + level_total
    lanes = 4 * KX
    rows = nudged * KX // devices
    flat = fields.reshape(field_rows, cells_x, cells_y)
    cuts = cuts.reshape(-1)
    f32 = functools.partial(jax.ShapeDtypeStruct, dtype=jnp.float32)
    x_fwd, x_back, y_fwd, y_back = (jnp.asarray(t) for t in tables)

    def vmem(*shape):
        return pltpu.VMEM(shape, jnp.float32)

    def table_space(table):
        return pltpu.VMEM(table.shape[1:], table.dtype)

    def limit(mib):
        return pltpu.CompilerParams(vmem_limit_bytes=mib * 1024 * 1024)

    mode_shape = f32((nudged, KX, lanes))
    parent_space = vmem(nudged, 4 * KX * KX)
    step_scratch = [vmem(total, cells_x + 2 * PAD, cells_y), vmem(field_rows, cells_x, cells_y)]
    mode_scratch = [pltpu.SemaphoreType.DMA((3,)), parent_space, table_space(x_fwd),
                    table_space(y_fwd)]
    levels, owners = in_hbm(levels), in_hbm(owners)

    modes = pl.pallas_call(
        functools.partial(first_kernel, n_gy, level_total),
        out_shape=mode_shape,
        in_specs=[SMEM, SMEM] + [HBM] * 4,
        out_specs=VMEM,
        scratch_shapes=[table_space(x_fwd), table_space(y_fwd),
                        vmem(field_rows, cells_x, cells_y), parent_space,
                        pltpu.SemaphoreType.DMA((4,))],
        compiler_params=limit(8),
        name="first_modes",
    )(levels, owners, in_hbm(flat), in_hbm(parent_modes), in_hbm(x_fwd), in_hbm(y_fwd))
    for step in range(STEPS):
        last = step == STEPS - 1
        edge_shapes = [f32((total, cells_y)), f32((total, cells_y)), f32((cells_x, 2 * total))]
        edge_operands = [flat, plume]
        if step == 0:
            edge_shapes += [jax.ShapeDtypeStruct(t.shape[1:], t.dtype) for t in (x_back, y_back)]
            edge_operands += [in_hbm(x_back), in_hbm(y_back)]
        edges = pl.pallas_call(
            edge_kernel,
            out_shape=edge_shapes,
            in_specs=[VMEM, VMEM] + [HBM] * (len(edge_operands) - 2),
            out_specs=[VMEM] * len(edge_shapes),
            scratch_shapes=[pltpu.SemaphoreType.DMA((2,))] if step == 0 else [],
            compiler_params=limit(8),
            name="edges",
        )(*edge_operands)
        if step == 0:
            back_tables = edges[3:]
        to_west, to_east, cols = edges[:3]
        west, east = swap("gx", to_east, to_west)
        parts = lax.all_to_all(modes.reshape(devices, rows, lanes), AXES, 0, 0, tiled=True)
        parts, west, east = lax.optimization_barrier((parts, west, east))
        share = pl.pallas_call(
            functools.partial(share_kernel, n_gy, period),
            out_shape=f32((devices, rows, lanes)),
            in_specs=[SMEM, VMEM],
            out_specs=VMEM,
            compiler_params=limit(4),
            name="share_sum",
        )(cuts, parts)
        share, cols = lax.optimization_barrier((share, cols))
        south, north = swap("gy", cols, cols)
        mismatch = lax.all_to_all(share, AXES, 0, 0, tiled=True)
        out_shape = [f32(flat.shape), f32(plume.shape)]
        operands = [levels, owners, mismatch.reshape(nudged * KX, lanes), flat, plume, source,
                    west, east, south, north, *back_tables]
        if not last:
            out_shape.append(mode_shape)
            operands += [in_hbm(parent_modes), in_hbm(x_fwd), in_hbm(y_fwd)]
        results = pl.pallas_call(
            functools.partial(step_kernel, n_gy, step, last),
            out_shape=out_shape,
            in_specs=[SMEM, SMEM] + [VMEM] * 10 + [HBM] * (len(operands) - 12),
            out_specs=[VMEM] * len(out_shape),
            scratch_shapes=step_scratch + ([] if last else mode_scratch),
            compiler_params=limit(20),
            name="final_step" if last else "inner_step",
        )(*operands)
        if last:
            flat, plume = results
        else:
            flat, plume, modes = results
    return flat.reshape(fields.shape), plume


def solution(mesh):
    in_specs = (
        P(None, None, "gx", "gy"),
        P(),
        P(),
        P(("gx", "gy"), None, None, None),
        P(),
        P(None, "gx", "gy"),
        P(None, "gx", "gy"),
    )
    out_specs = (P(None, None, "gx", "gy"), P(None, "gx", "gy"))
    n_gx, n_gy = mesh.shape["gx"], mesh.shape["gy"]

    def whole(fields, levels, cuts, parent_modes, owners, plume, source):
        tables = build_tables(n_gx, n_gy, plume.shape[1] // n_gx, plume.shape[2] // n_gy)
        return jax.shard_map(
            functools.partial(local, tables), mesh=mesh, in_specs=in_specs, out_specs=out_specs,
            check_vma=False,
        )(fields, levels, cuts, parent_modes, owners, plume, source)

    return whole
```

```python
import functools
import math

import jax
import jax.numpy as jnp
import ml_dtypes
import numpy as np
from jax import lax
from jax.experimental import pallas as pl
from jax.experimental.pallas import tpu as pltpu
from jax.sharding import PartitionSpec as P

KX = 32
STEPS = 2
PAD = 8
VMEM = pl.BlockSpec(memory_space=pltpu.VMEM)
SMEM = pl.BlockSpec(memory_space=pltpu.SMEM)
HBM = pl.BlockSpec(memory_space=pltpu.HBM)
AXES = ("gx", "gy")


def in_hbm(array):
    return pltpu.with_memory_space_constraint(array, pltpu.HBM)


def wave_table(positions, period):
    wavenum = np.arange(KX)[:, None]
    phase = (wavenum * positions[None, :] % period) * (2.0 * math.pi / period)
    inside = (positions >= 0) & (positions < period)
    return np.concatenate([np.cos(phase), np.sin(phase)], axis=0) * inside[None, :]


def split(a):
    head = a.astype(jnp.bfloat16)
    return head, (a - head.astype(jnp.float32)).astype(jnp.bfloat16)


def split_table(table, axis, order):
    head = table.astype(ml_dtypes.bfloat16)
    rest = (table - head.astype(np.float64)).astype(ml_dtypes.bfloat16)
    return np.concatenate([head if part == "h" else rest for part in order], axis=axis)


def build_tables(n_gx, n_gy, cells_x, cells_y):
    period_x, period_y = n_gx * cells_x, n_gy * cells_y
    order = np.concatenate([np.arange(0, 2 * KX, 2), np.arange(1, 2 * KX, 2)])
    scaling = 1.0 / math.sqrt(period_x * period_y)
    x_fwd, x_back, y_fwd, y_back = [], [], [], []
    for g in range(n_gx):
        first = g * cells_x
        forward = wave_table(first + np.arange(cells_x), period_x)[order]
        x_fwd.append(split_table(forward, 1, "hlh"))
        rows = np.concatenate([first + np.arange(cells_x), [first - 1, first + cells_x]])
        back = np.zeros((cells_x + 16, 2 * KX))
        back[: cells_x + 2] = wave_table(rows, period_x)[order].T
        x_back.append(split_table(back, 1, "hlh"))
    for g in range(n_gy):
        first = g * cells_y
        table = wave_table(first + np.arange(cells_y), period_y)
        edge = np.zeros((2 * KX, cells_y))
        edge[:, [0, -1]] = wave_table(np.array([first - 1, first + cells_y]), period_y)
        forward = np.concatenate([table.T, table.T], axis=1) * scaling
        y_fwd.append(split_table(forward, 0, "hhl"))
        none = np.zeros_like(table)
        back = np.concatenate(
            [
                np.concatenate([table, edge, none, none], axis=1),
                np.concatenate([none, none, table, edge], axis=1),
            ],
            axis=0,
        )
        y_back.append(split_table(back, 0, "hhl"))
    return [np.stack(t) for t in (x_fwd, x_back, y_fwd, y_back)]


def data_dot(a, table):
    head, rest = split(a)
    return jnp.dot(
        jnp.concatenate([head, rest, head], axis=1), table, preferred_element_type=jnp.float32
    )


def table_dot(table, a):
    head, rest = split(a)
    return jnp.dot(
        table, jnp.concatenate([head, head, rest], axis=0), preferred_element_type=jnp.float32
    )


def emit_modes(read, x_fwd, y_fwd, modes_ref):
    nudged = modes_ref.shape[0]
    slabs = [read(c) for c in range(nudged)]
    cells_x = slabs[0].shape[0]
    half = data_dot(jnp.concatenate(slabs, axis=0), y_fwd)
    lane = lax.broadcasted_iota(jnp.int32, (KX, 4 * KX), 1)
    for c in range(nudged):
        both = table_dot(x_fwd, half[c * cells_x : (c + 1) * cells_x])
        modes_ref[c] = -jnp.where(lane < 2 * KX, both[:KX], both[KX:])


def add_parent(parent, is_owner, modes_ref):
    @pl.when(is_owner)
    def _():
        for i in range(KX):
            tile = parent[:, i * 4 * KX : (i + 1) * 4 * KX]
            modes_ref[:, i, :] = modes_ref[:, i, :] + tile


def fetch_all(sems, pairs):
    copies = [pltpu.make_async_copy(a, b, sems.at[i]) for i, (a, b) in enumerate(pairs)]
    for copy in copies:
        copy.start()
    return copies


def slab_of(levels, c, level_count, level_total):
    return (c // level_count) * level_total + levels[c % level_count]


def first_kernel(n_gy, level_total, levels, owners, fields_all, parent_all, x_fwd_all, y_fwd_all,
                 modes, x_fwd, y_fwd, fields, parent, sems):
    gx, gy = lax.axis_index("gx"), lax.axis_index("gy")
    copies = fetch_all(sems, [
        (fields_all, fields), (x_fwd_all.at[gx], x_fwd), (y_fwd_all.at[gy], y_fwd),
        (parent_all.at[0, 0], parent)])
    for copy in copies[:3]:
        copy.wait()
    level_count = modes.shape[0] // 3
    emit_modes(
        lambda c: fields[slab_of(levels, c, level_count, level_total)], x_fwd[...], y_fwd[...],
        modes,
    )
    copies[3].wait()
    add_parent(parent, owners[0] == gx * n_gy + gy, modes)


def edge_kernel(fields, plume, *rest):
    copies = []
    if len(rest) > 3:
        x_back_all, y_back_all, west, east, cols, x_back, y_back, sems = rest
        copies = fetch_all(sems, [(x_back_all.at[lax.axis_index("gx")], x_back),
                                  (y_back_all.at[lax.axis_index("gy")], y_back)])
    else:
        west, east, cols = rest
    cells_x, cells_y = plume.shape[1:]
    field_rows = fields.shape[0]
    lane = lax.broadcasted_iota(jnp.int32, cols.shape, 1)
    acc = jnp.zeros(cols.shape, jnp.float32)
    for c in range(field_rows + plume.shape[0]):
        a = fields[c] if c < field_rows else plume[c - field_rows]
        west[c : c + 1, :] = a[:1]
        east[c : c + 1, :] = a[cells_x - 1 :]
        acc = jnp.where(lane // 2 == c, pltpu.roll(a, 2 * c + 1, 1), acc)
    cols[...] = acc
    for copy in copies:
        copy.wait()


def share_kernel(n_gy, period, cuts, parts, out):
    count, rows, lanes = parts.shape
    me = lax.axis_index("gx") * n_gy + lax.axis_index("gy")
    total = parts[0]
    for p in range(1, count):
        total = total + parts[p]
    row = me * rows + lax.broadcasted_iota(jnp.int32, (rows, lanes), 0)
    lane = lax.broadcasted_iota(jnp.int32, (rows, lanes), 1)
    slab, pair = row // KX, row % KX
    r = 2 * pair + lane // (2 * KX)
    s = lane % (2 * KX)
    limit = jnp.zeros((rows, lanes), jnp.int32)
    for c in range(cuts.shape[0]):
        limit = jnp.where(slab == c, cuts[c], limit)
    keep = ((r % KX) < limit) & ((s % KX) < limit)
    factor = jnp.where(r == 0, 1.0, 2.0) * jnp.where(s == 0, 1.0, 2.0) * (1.0 / math.sqrt(period))
    result = jnp.where(keep, total * factor, 0.0)
    for p in range(count):
        out[p] = result


def step_kernel(n_gy, step, last, levels, owners, mismatch, fields, plume, source,
                west, east, south, north, x_back, y_back, *rest):
    gx, gy = lax.axis_index("gx"), lax.axis_index("gy")
    copies = []
    if last:
        fields_out, plume_out, slabs, beside = rest
    else:
        (parent_all, x_fwd_all, y_fwd_all, fields_out, plume_out, modes,
         slabs, beside, sems, parent, x_fwd, y_fwd) = rest
        copies = fetch_all(sems, [(x_fwd_all.at[gx], x_fwd), (y_fwd_all.at[gy], y_fwd),
                                  (parent_all.at[0, step + 1], parent)])
    level_total, cells_x, cells_y = plume.shape
    field_rows = fields.shape[0]
    total = field_rows + level_total
    nudged = mismatch.shape[0] // KX
    level_count = nudged // 3
    inner = slice(PAD, PAD + cells_x)
    for c in range(total):
        slabs[c, inner] = fields[c] if c < field_rows else plume[c - field_rows]
        slabs[c, PAD - 1 : PAD] = west[c : c + 1, :]
        slabs[c, PAD + cells_x : PAD + cells_x + 1] = east[c : c + 1, :]
    beside[...] = jnp.zeros_like(beside)
    back = data_dot(mismatch[...], y_back[...])
    x_table = x_back[...]
    for c in range(nudged):
        pair = back[c * KX : (c + 1) * KX]
        update = table_dot(
            x_table, jnp.concatenate([pair[:, : 2 * cells_y], pair[:, 2 * cells_y :]], axis=0))
        spot = slab_of(levels, c, level_count, level_total)
        slabs[spot, inner] += update[:cells_x, :cells_y]
        slabs[spot, PAD - 1 : PAD] += update[cells_x : cells_x + 1, :cells_y]
        slabs[spot, PAD + cells_x : PAD + cells_x + 1] += update[cells_x + 1 : cells_x + 2, :cells_y]
        beside[spot] = update[:cells_x, cells_y:]

    lane = lax.broadcasted_iota(jnp.int32, (cells_x, cells_y), 1)
    first, final = lane == 0, lane == cells_y - 1
    columns = jnp.where(
        lane % 2 == 0, pltpu.roll(north[...], cells_y - 1, 1), pltpu.roll(south[...], 1, 1))

    def advance(c, parts):
        centre, to_west, to_east, to_south, to_north = parts
        a = slabs[c, inner]
        column = pltpu.roll(columns, cells_y - 1 - 2 * c, 1)
        if c < field_rows:
            column = column + beside[c]
        return (
            centre * a
            + to_west * slabs[c, PAD - 1 : PAD - 1 + cells_x]
            + to_east * slabs[c, PAD + 1 : PAD + 1 + cells_x]
            + to_south * jnp.where(first, column, pltpu.roll(a, 1, 1))
            + to_north * jnp.where(final, column, pltpu.roll(a, cells_y - 1, 1))
        )

    for l in range(level_total):
        u, v = slabs[l, inner], slabs[level_total + l, inner]
        beside_parts = (
            0.1 + 0.1 * jnp.maximum(u, 0.0), 0.1 - 0.1 * jnp.minimum(u, 0.0),
            0.1 + 0.1 * jnp.maximum(v, 0.0), 0.1 - 0.1 * jnp.minimum(v, 0.0),
        )
        centre = 1.0 - (beside_parts[0] + beside_parts[1] + beside_parts[2] + beside_parts[3])
        for f in range(3):
            fields_out[f * level_total + l] = advance(
                f * level_total + l, (centre,) + beside_parts)
        settled = advance(field_rows + l, (centre - 0.3,) + beside_parts) + source[l]
        if l + 1 < level_total:
            settled = settled + 0.3 * plume[l + 1]
        plume_out[l] = settled

    if last:
        return
    for copy in copies:
        copy.wait()
    emit_modes(
        lambda c: fields_out[slab_of(levels, c, level_count, level_total)], x_fwd[...], y_fwd[...],
        modes,
    )
    add_parent(parent, owners[step + 1] == gx * n_gy + gy, modes)


def swap(axis, to_next, to_previous):
    count = lax.axis_size(axis)
    up = [(i, i + 1) for i in range(count - 1)]
    down = [(b, a) for a, b in up]
    return lax.ppermute(to_next, axis, up), lax.ppermute(to_previous, axis, down)


def local(tables, fields, levels, cuts, parent_modes, owners, plume, source):
    n_gx, n_gy = lax.axis_size("gx"), lax.axis_size("gy")
    devices = n_gx * n_gy
    level_total, cells_x, cells_y = plume.shape
    period = n_gx * cells_x * n_gy * cells_y
    nudged = 3 * levels.shape[0]
    field_rows = 3 * level_total
    total = field_rows + level_total
    lanes = 4 * KX
    rows = nudged * KX // devices
    flat = fields.reshape(field_rows, cells_x, cells_y)
    cuts = cuts.reshape(-1)
    f32 = functools.partial(jax.ShapeDtypeStruct, dtype=jnp.float32)
    x_fwd, x_back, y_fwd, y_back = (jnp.asarray(t) for t in tables)

    def vmem(*shape):
        return pltpu.VMEM(shape, jnp.float32)

    def table_space(table):
        return pltpu.VMEM(table.shape[1:], table.dtype)

    def limit(mib):
        return pltpu.CompilerParams(vmem_limit_bytes=mib * 1024 * 1024)

    mode_shape = vmem(nudged, KX, lanes)
    parent_space = vmem(nudged, 4 * KX * KX)
    step_scratch = [vmem(total, cells_x + 2 * PAD, cells_y), vmem(field_rows, cells_x, cells_y)]
    mode_scratch = [pltpu.SemaphoreType.DMA((3,)), parent_space, table_space(x_fwd),
                    table_space(y_fwd)]
    levels, owners = in_hbm(levels), in_hbm(owners)

    modes = pl.pallas_call(
        functools.partial(first_kernel, n_gy, level_total),
        out_shape=mode_shape,
        in_specs=[SMEM, SMEM] + [HBM] * 4,
        out_specs=VMEM,
        scratch_shapes=[table_space(x_fwd), table_space(y_fwd),
                        vmem(field_rows, cells_x, cells_y), parent_space,
                        pltpu.SemaphoreType.DMA((4,))],
        compiler_params=limit(8),
        name="first_modes",
    )(levels, owners, in_hbm(flat), in_hbm(parent_modes), in_hbm(x_fwd), in_hbm(y_fwd))
    for step in range(STEPS):
        last = step == STEPS - 1
        edge_shapes = [f32((total, cells_y)), f32((total, cells_y)), f32((cells_x, 2 * total))]
        edge_operands = [flat, plume]
        if step == 0:
            edge_shapes += [jax.ShapeDtypeStruct(t.shape[1:], t.dtype) for t in (x_back, y_back)]
            edge_operands += [in_hbm(x_back), in_hbm(y_back)]
        edges = pl.pallas_call(
            edge_kernel,
            out_shape=edge_shapes,
            in_specs=[VMEM, VMEM] + [HBM] * (len(edge_operands) - 2),
            out_specs=[VMEM] * len(edge_shapes),
            scratch_shapes=[pltpu.SemaphoreType.DMA((2,))] if step == 0 else [],
            compiler_params=limit(8),
            name="edges",
        )(*edge_operands)
        if step == 0:
            back_tables = edges[3:]
        to_west, to_east, cols = edges[:3]
        west, east = swap("gx", to_east, to_west)
        parts = lax.all_to_all(modes.reshape(devices, rows, lanes), AXES, 0, 0, tiled=True)
        parts, west, east = lax.optimization_barrier((parts, west, east))
        share = pl.pallas_call(
            functools.partial(share_kernel, n_gy, period),
            out_shape=vmem(devices, rows, lanes),
            in_specs=[SMEM, VMEM],
            out_specs=VMEM,
            compiler_params=limit(4),
            name="share_sum",
        )(cuts, parts)
        share, cols = lax.optimization_barrier((share, cols))
        south, north = swap("gy", cols, cols)
        mismatch = lax.all_to_all(share, AXES, 0, 0, tiled=True)
        out_shape = [f32(flat.shape), f32(plume.shape)]
        operands = [levels, owners, mismatch.reshape(nudged * KX, lanes), flat, plume, source,
                    west, east, south, north, *back_tables]
        if not last:
            out_shape.append(mode_shape)
            operands += [in_hbm(parent_modes), in_hbm(x_fwd), in_hbm(y_fwd)]
        results = pl.pallas_call(
            functools.partial(step_kernel, n_gy, step, last),
            out_shape=out_shape,
            in_specs=[SMEM, SMEM] + [VMEM] * 10 + [HBM] * (len(operands) - 12),
            out_specs=[VMEM] * len(out_shape),
            scratch_shapes=step_scratch + ([] if last else mode_scratch),
            compiler_params=limit(20),
            name="final_step" if last else "inner_step",
        )(*operands)
        if last:
            flat, plume = results
        else:
            flat, plume, modes = results
    return flat.reshape(fields.shape), plume


def solution(mesh):
    in_specs = (
        P(None, None, "gx", "gy"),
        P(),
        P(),
        P(("gx", "gy"), None, None, None),
        P(),
        P(None, "gx", "gy"),
        P(None, "gx", "gy"),
    )
    out_specs = (P(None, None, "gx", "gy"), P(None, "gx", "gy"))
    n_gx, n_gy = mesh.shape["gx"], mesh.shape["gy"]

    def whole(fields, levels, cuts, parent_modes, owners, plume, source):
        tables = build_tables(n_gx, n_gy, plume.shape[1] // n_gx, plume.shape[2] // n_gy)
        return jax.shard_map(
            functools.partial(local, tables), mesh=mesh, in_specs=in_specs, out_specs=out_specs,
            check_vma=False,
        )(fields, levels, cuts, parent_modes, owners, plume, source)

    return whole
```

```python
import functools
import math

import jax
import jax.numpy as jnp
import ml_dtypes
import numpy as np
from jax import lax
from jax.experimental import pallas as pl
from jax.experimental.pallas import tpu as pltpu
from jax.sharding import PartitionSpec as P

KX = 32
STEPS = 2
GROUP = 4
LANES = GROUP * KX
PAD = 8
VMEM = pl.BlockSpec(memory_space=pltpu.VMEM)
SMEM = pl.BlockSpec(memory_space=pltpu.SMEM)
HBM = pl.BlockSpec(memory_space=pltpu.HBM)
AXES = ("gx", "gy")


def in_hbm(array):
    return pltpu.with_memory_space_constraint(array, pltpu.HBM)


def wave_table(positions, period):
    wavenum = np.arange(KX)[:, None]
    phase = (wavenum * positions[None, :] % period) * (2.0 * math.pi / period)
    inside = (positions >= 0) & (positions < period)
    return np.concatenate([np.cos(phase), np.sin(phase)], axis=0) * inside[None, :]


def split(a):
    head = a.astype(jnp.bfloat16)
    return head, (a - head.astype(jnp.float32)).astype(jnp.bfloat16)


def split_table(table, axis, order):
    head = table.astype(ml_dtypes.bfloat16)
    rest = (table - head.astype(np.float64)).astype(ml_dtypes.bfloat16)
    return np.concatenate([head if part == "h" else rest for part in order], axis=axis)


def per_slab(table):
    return np.kron(np.eye(GROUP), table)


def build_tables(n_gx, n_gy, cells_x, cells_y):
    period_x, period_y = n_gx * cells_x, n_gy * cells_y
    scaling = 1.0 / math.sqrt(period_x * period_y)
    parity = [np.arange(p, 2 * KX, 2) for p in range(2)]
    x_fwd, y_fwd, y_back, inner, outer = [], [], [], [], []
    for g in range(n_gx):
        first = g * cells_x
        table = wave_table(first + np.arange(cells_x), period_x)
        x_fwd.append(split_table(
            np.concatenate([per_slab(table[rows].T) for rows in parity], axis=1), 0, "hhl"))
        beside = wave_table(np.array([first - 1, first + cells_x]), period_x)
        inner.append(np.concatenate([per_slab(table[rows]) for rows in parity], axis=0))
        outer.append(np.concatenate([per_slab(beside[rows]) for rows in parity], axis=0))
    spare = -(2 * GROUP * n_gx) % LANES
    x_back = np.concatenate(inner + outer + [np.zeros((2 * LANES, spare))], axis=1)
    for g in range(n_gy):
        first = g * cells_y
        table = wave_table(first + np.arange(cells_y), period_y)
        edge = np.zeros((2 * KX, cells_y))
        edge[:, [0, -1]] = wave_table(np.array([first - 1, first + cells_y]), period_y)
        y_fwd.append(split_table(table * scaling, 1, "hlh"))
        y_back.append(split_table(np.concatenate([table, edge], axis=1), 0, "hhl"))
    return [np.stack(x_fwd), np.stack(y_fwd), np.stack(y_back), split_table(x_back, 0, "hhl")]


def data_dot(a, table):
    head, rest = split(a)
    return jnp.dot(
        jnp.concatenate([head, rest, head], axis=1), table, preferred_element_type=jnp.float32
    )


def columns_dot(a, table):
    head, rest = split(a)
    stacked = jnp.concatenate([head, rest, head], axis=0)
    return lax.dot_general(
        stacked, table, (((0,), (0,)), ((), ())), preferred_element_type=jnp.float32)


def emit_modes(read, parent, is_owner, x_fwd, y_fwd, modes, turned, work):
    devices, rows = modes.shape[0], modes.shape[1] // 2
    slabs = parent.shape[0]
    groups = slabs // GROUP
    head, rest = split(jnp.concatenate([read(c) for c in range(slabs)], axis=0))
    half = lax.dot_general(
        y_fwd, jnp.concatenate([head, head, rest], axis=1), (((1,), (1,)), ((), ())),
        preferred_element_type=jnp.float32)
    half = jnp.concatenate([half[:, t * LANES : (t + 1) * LANES] for t in range(groups)], axis=0)
    count = groups * 2 * KX
    work[0:count] = -data_dot(half, x_fwd)
    if count < devices * rows:
        work[count:] = jnp.zeros((devices * rows - count, 2 * LANES), jnp.float32)

    @pl.when(is_owner)
    def _():
        for i in range(KX):
            turned[:, i, :] = parent[:, i * LANES : (i + 1) * LANES]
        for t in range(groups):
            block = turned[t * GROUP : (t + 1) * GROUP].reshape(LANES, LANES).T
            span = slice(t * 2 * KX, (t + 1) * 2 * KX)
            for p in range(2):
                work[span, p * LANES : (p + 1) * LANES] += block[p * 2 * KX : (p + 1) * 2 * KX]

    for d in range(devices):
        for p in range(2):
            modes[d, p * rows : (p + 1) * rows, :] = work[
                d * rows : (d + 1) * rows, p * LANES : (p + 1) * LANES]


def fetch_all(sems, pairs):
    copies = [pltpu.make_async_copy(a, b, sems.at[i]) for i, (a, b) in enumerate(pairs)]
    for copy in copies:
        copy.start()
    return copies


def slab_of(levels, c, level_count, level_total):
    return (c // level_count) * level_total + levels[c % level_count]


def first_kernel(n_gy, level_total, levels, owners, fields_all, parent_all, x_fwd_all, y_fwd_all,
                 modes, fields, sems, parent, x_fwd, y_fwd, turned, work):
    gx, gy = lax.axis_index("gx"), lax.axis_index("gy")
    copies = fetch_all(sems, [
        (fields_all, fields), (x_fwd_all.at[gx], x_fwd), (y_fwd_all.at[gy], y_fwd),
        (parent_all.at[0, 0], parent)])
    for copy in copies:
        copy.wait()
    level_count = parent.shape[0] // 3
    emit_modes(
        lambda c: fields[slab_of(levels, c, level_count, level_total)],
        parent, owners[0] == gx * n_gy + gy, x_fwd[...], y_fwd[...], modes, turned, work,
    )


def edge_kernel(fields, plume, *rest):
    copies = []
    if len(rest) > 3:
        y_back_all, west, east, cols, y_back, sems = rest
        copies = fetch_all(sems, [(y_back_all.at[lax.axis_index("gy")], y_back)])
    else:
        west, east, cols = rest
    cells_x, cells_y = plume.shape[1:]
    field_rows = fields.shape[0]
    lane = lax.broadcasted_iota(jnp.int32, cols.shape, 1)
    acc = jnp.zeros(cols.shape, jnp.float32)
    for c in range(field_rows + plume.shape[0]):
        a = fields[c] if c < field_rows else plume[c - field_rows]
        west[c : c + 1, :] = a[:1]
        east[c : c + 1, :] = a[cells_x - 1 :]
        acc = jnp.where(lane // 2 == c, pltpu.roll(a, 2 * c + 1, 1), acc)
    cols[...] = acc
    for copy in copies:
        copy.wait()


def beside_rows(rows):
    return -(-rows // 3)


def share_kernel(n_gx, n_gy, period, cuts, parts, x_back, out):
    devices = parts.shape[0]
    rows = parts.shape[1] // 2
    me = lax.axis_index("gx") * n_gy + lax.axis_index("gy")
    total = parts[0]
    for d in range(1, devices):
        total = total + parts[d]
    shape = total.shape
    place = lax.broadcasted_iota(jnp.int32, shape, 0)
    lane = lax.broadcasted_iota(jnp.int32, shape, 1)
    p = (place >= rows).astype(jnp.int32)
    row = me * rows + place - p * rows
    k = 2 * (lane % KX) + p
    j = row % (2 * KX)
    slab = GROUP * (row // (2 * KX)) + lane // KX
    limit = jnp.zeros(shape, jnp.int32)
    for c in range(cuts.shape[0]):
        limit = jnp.where(slab == c, cuts[c], limit)
    keep = ((k % KX) < limit) & ((j % KX) < limit)
    factor = jnp.where(k == 0, 1.0, 2.0) * jnp.where(j == 0, 1.0, 2.0) * (1.0 / math.sqrt(period))
    mismatch = jnp.where(keep, total * factor, 0.0)
    both = jnp.concatenate([mismatch[:rows], mismatch[rows:]], axis=1)
    spare = -rows % 16
    if spare:
        both = jnp.concatenate([both, jnp.zeros((spare, 2 * LANES), jnp.float32)], axis=0)
    half = data_dot(both, x_back[...])
    packed = beside_rows(rows)
    width = 2 * GROUP
    spot = lax.broadcasted_iota(jnp.int32, (packed, LANES), 1) // width
    for g in range(n_gx):
        first = (n_gx + g * width // LANES) * LANES
        edge = half[:, first : first + LANES]
        beside = jnp.zeros((packed, LANES), jnp.float32)
        for m in range(3):
            piece = edge[m * packed : (m + 1) * packed]
            beside = jnp.where(
                spot == m, pltpu.roll(piece, (m - g) * width % LANES, 1), beside)
        for h in range(n_gy):
            out[g * n_gy + h, :rows, :] = half[:rows, g * LANES : (g + 1) * LANES]
            out[g * n_gy + h, rows:, :] = beside


def step_kernel(n_gy, step, last, levels, owners, shares, fields, plume, source,
                west, east, south, north, y_back, *rest):
    gx, gy = lax.axis_index("gx"), lax.axis_index("gy")
    copies = []
    if last:
        fields_out, plume_out, slabs, beside, spread, spread_edges = rest
    else:
        (parent_all, x_fwd_all, y_fwd_all, fields_out, plume_out, modes,
         slabs, beside, spread, spread_edges, sems, parent, x_fwd, y_fwd, turned, work) = rest
        copies = fetch_all(sems, [(x_fwd_all.at[gx], x_fwd), (y_fwd_all.at[gy], y_fwd),
                                  (parent_all.at[0, step + 1], parent)])
    level_total, cells_x, cells_y = plume.shape
    field_rows = fields.shape[0]
    total = field_rows + level_total
    level_count = levels.shape[0]
    nudged = 3 * level_count
    inner = slice(PAD, PAD + cells_x)
    for c in range(total):
        slabs[c, inner] = fields[c] if c < field_rows else plume[c - field_rows]
        slabs[c, PAD - 1 : PAD] = west[c : c + 1, :]
        slabs[c, PAD + cells_x : PAD + cells_x + 1] = east[c : c + 1, :]
    beside[...] = jnp.zeros_like(beside)
    devices = shares.shape[0]
    rows = spread.shape[0] // devices
    packed = beside_rows(rows)
    width = 2 * GROUP
    for d in range(devices):
        spread[d * rows : (d + 1) * rows] = shares[d, :rows, :]
        edge = shares[d, rows:, :]
        for m in range(3):
            count = min(packed, rows - m * packed)
            if count > 0:
                moved = pltpu.roll(edge, -m * width % LANES, 1) if m else edge
                start = d * rows + m * packed
                spread_edges[start : start + count] = moved[:count]
    y_table = y_back[...]
    groups = nudged // GROUP
    spot_of = lax.broadcasted_iota(jnp.int32, (2 * KX, LANES), 1) // width
    edges = jnp.zeros((2 * KX, LANES), jnp.float32)
    for t in range(groups):
        piece = spread_edges[t * 2 * KX : (t + 1) * 2 * KX]
        edges = jnp.where(spot_of == t, pltpu.roll(piece, t * width, 1) if t else piece, edges)
    update_rows = columns_dot(edges, y_table)
    for t in range(groups):
        update = columns_dot(spread[t * 2 * KX : (t + 1) * 2 * KX], y_table)
        for n in range(GROUP):
            c = t * GROUP + n
            part = update[n * cells_x : (n + 1) * cells_x]
            spot = slab_of(levels, c, level_count, level_total)
            slabs[spot, inner] += part[:, :cells_y]
            slabs[spot, PAD - 1 : PAD] += update_rows[2 * c : 2 * c + 1, :cells_y]
            slabs[spot, PAD + cells_x : PAD + cells_x + 1] += update_rows[
                2 * c + 1 : 2 * c + 2, :cells_y]
            beside[spot] = part[:, cells_y:]

    lane = lax.broadcasted_iota(jnp.int32, (cells_x, cells_y), 1)
    first, final = lane == 0, lane == cells_y - 1
    columns = jnp.where(
        lane % 2 == 0, pltpu.roll(north[...], cells_y - 1, 1), pltpu.roll(south[...], 1, 1))

    def advance(c, parts):
        centre, to_west, to_east, to_south, to_north = parts
        a = slabs[c, inner]
        column = pltpu.roll(columns, cells_y - 1 - 2 * c, 1)
        if c < field_rows:
            column = column + beside[c]
        return (
            centre * a
            + to_west * slabs[c, PAD - 1 : PAD - 1 + cells_x]
            + to_east * slabs[c, PAD + 1 : PAD + 1 + cells_x]
            + to_south * jnp.where(first, column, pltpu.roll(a, 1, 1))
            + to_north * jnp.where(final, column, pltpu.roll(a, cells_y - 1, 1))
        )

    for l in range(level_total):
        u, v = slabs[l, inner], slabs[level_total + l, inner]
        beside_parts = (
            0.1 + 0.1 * jnp.maximum(u, 0.0), 0.1 - 0.1 * jnp.minimum(u, 0.0),
            0.1 + 0.1 * jnp.maximum(v, 0.0), 0.1 - 0.1 * jnp.minimum(v, 0.0),
        )
        centre = 1.0 - (beside_parts[0] + beside_parts[1] + beside_parts[2] + beside_parts[3])
        for f in range(3):
            fields_out[f * level_total + l] = advance(
                f * level_total + l, (centre,) + beside_parts)
        settled = advance(field_rows + l, (centre - 0.3,) + beside_parts) + source[l]
        if l + 1 < level_total:
            settled = settled + 0.3 * plume[l + 1]
        plume_out[l] = settled

    if last:
        return
    for copy in copies:
        copy.wait()
    emit_modes(
        lambda c: fields_out[slab_of(levels, c, level_count, level_total)],
        parent, owners[step + 1] == gx * n_gy + gy, x_fwd[...], y_fwd[...], modes, turned, work,
    )


def swap(axis, to_next, to_previous):
    count = lax.axis_size(axis)
    up = [(i, i + 1) for i in range(count - 1)]
    down = [(b, a) for a, b in up]
    return lax.ppermute(to_next, axis, up), lax.ppermute(to_previous, axis, down)


def local(tables, fields, levels, cuts, parent_modes, owners, plume, source):
    n_gx, n_gy = lax.axis_size("gx"), lax.axis_size("gy")
    devices = n_gx * n_gy
    level_total, cells_x, cells_y = plume.shape
    period = n_gx * cells_x * n_gy * cells_y
    nudged = 3 * levels.shape[0]
    field_rows = 3 * level_total
    total = field_rows + level_total
    rows = -(-(nudged // GROUP * 2 * KX) // devices)
    flat = fields.reshape(field_rows, cells_x, cells_y)
    cuts = cuts.reshape(-1)
    f32 = functools.partial(jax.ShapeDtypeStruct, dtype=jnp.float32)
    x_fwd, y_fwd, y_back, x_back = (jnp.asarray(t) for t in tables)

    def vmem(*shape):
        return pltpu.VMEM(shape, jnp.float32)

    def table_space(table):
        return pltpu.VMEM(table.shape[1:], table.dtype)

    def limit(mib):
        return pltpu.CompilerParams(vmem_limit_bytes=mib * 1024 * 1024)

    mode_shape = f32((devices, 2 * rows, LANES))
    step_scratch = [vmem(total, cells_x + 2 * PAD, cells_y), vmem(field_rows, cells_x, cells_y),
                    vmem(devices * rows, LANES), vmem(devices * rows, LANES)]
    mode_scratch = [pltpu.SemaphoreType.DMA((4,)), vmem(nudged, 4 * KX * KX), table_space(x_fwd),
                    table_space(y_fwd), vmem(nudged, KX, LANES),
                    vmem(devices * rows, 2 * LANES)]
    levels, owners = in_hbm(levels), in_hbm(owners)

    modes = pl.pallas_call(
        functools.partial(first_kernel, n_gy, level_total),
        out_shape=mode_shape,
        in_specs=[SMEM, SMEM] + [HBM] * 4,
        out_specs=VMEM,
        scratch_shapes=[vmem(field_rows, cells_x, cells_y)] + mode_scratch,
        compiler_params=limit(8),
        name="first_modes",
    )(levels, owners, in_hbm(flat), in_hbm(parent_modes), in_hbm(x_fwd), in_hbm(y_fwd))
    for step in range(STEPS):
        last = step == STEPS - 1
        edge_shapes = [f32((total, cells_y)), f32((total, cells_y)), f32((cells_x, 2 * total))]
        edge_operands = [flat, plume]
        if step == 0:
            edge_shapes.append(jax.ShapeDtypeStruct(y_back.shape[1:], y_back.dtype))
            edge_operands.append(in_hbm(y_back))
        edges = pl.pallas_call(
            edge_kernel,
            out_shape=edge_shapes,
            in_specs=[VMEM, VMEM] + [HBM] * (len(edge_operands) - 2),
            out_specs=[VMEM] * len(edge_shapes),
            scratch_shapes=[pltpu.SemaphoreType.DMA((1,))] if step == 0 else [],
            compiler_params=limit(8),
            name="edges",
        )(*edge_operands)
        if step == 0:
            back_table = edges[3]
        to_west, to_east, cols = edges[:3]
        west, east = swap("gx", to_east, to_west)
        parts = lax.all_to_all(modes, AXES, 0, 0, tiled=True)
        parts, west, east = lax.optimization_barrier((parts, west, east))
        share = pl.pallas_call(
            functools.partial(share_kernel, n_gx, n_gy, period),
            out_shape=f32((devices, rows + beside_rows(rows), LANES)),
            in_specs=[SMEM, VMEM, VMEM],
            out_specs=VMEM,
            compiler_params=limit(12),
            name="share_sum",
        )(cuts, parts, x_back)
        share, cols = lax.optimization_barrier((share, cols))
        south, north = swap("gy", cols, cols)
        shares = lax.all_to_all(share, AXES, 0, 0, tiled=True)
        out_shape = [f32(flat.shape), f32(plume.shape)]
        operands = [levels, owners, shares, flat, plume, source, west, east, south, north,
                    back_table]
        if not last:
            out_shape.append(mode_shape)
            operands += [in_hbm(parent_modes), in_hbm(x_fwd), in_hbm(y_fwd)]
        results = pl.pallas_call(
            functools.partial(step_kernel, n_gy, step, last),
            out_shape=out_shape,
            in_specs=[SMEM, SMEM] + [VMEM] * 9 + [HBM] * (len(operands) - 11),
            out_specs=[VMEM] * len(out_shape),
            scratch_shapes=step_scratch + ([] if last else mode_scratch),
            compiler_params=limit(20),
            name="final_step" if last else "inner_step",
        )(*operands)
        if last:
            flat, plume = results
        else:
            flat, plume, modes = results
    return flat.reshape(fields.shape), plume


def solution(mesh):
    in_specs = (
        P(None, None, "gx", "gy"),
        P(),
        P(),
        P(("gx", "gy"), None, None, None),
        P(),
        P(None, "gx", "gy"),
        P(None, "gx", "gy"),
    )
    out_specs = (P(None, None, "gx", "gy"), P(None, "gx", "gy"))
    n_gx, n_gy = mesh.shape["gx"], mesh.shape["gy"]

    def whole(fields, levels, cuts, parent_modes, owners, plume, source):
        tables = build_tables(n_gx, n_gy, plume.shape[1] // n_gx, plume.shape[2] // n_gy)
        return jax.shard_map(
            functools.partial(local, tables), mesh=mesh, in_specs=in_specs, out_specs=out_specs,
            check_vma=False,
        )(fields, levels, cuts, parent_modes, owners, plume, source)

    return whole
```

```python
import functools
import math

import jax
import jax.numpy as jnp
import ml_dtypes
import numpy as np
from jax import lax
from jax.experimental import pallas as pl
from jax.experimental.pallas import tpu as pltpu
from jax.sharding import PartitionSpec as P

KX = 32
STEPS = 2
GROUP = 4
LANES = GROUP * KX
PAD = 8
VMEM = pl.BlockSpec(memory_space=pltpu.VMEM)
SMEM = pl.BlockSpec(memory_space=pltpu.SMEM)
HBM = pl.BlockSpec(memory_space=pltpu.HBM)
AXES = ("gx", "gy")


def in_hbm(array):
    return pltpu.with_memory_space_constraint(array, pltpu.HBM)


def wave_table(positions, period):
    wavenum = np.arange(KX)[:, None]
    phase = (wavenum * positions[None, :] % period) * (2.0 * math.pi / period)
    inside = (positions >= 0) & (positions < period)
    return np.concatenate([np.cos(phase), np.sin(phase)], axis=0) * inside[None, :]


def split(a):
    head = a.astype(jnp.bfloat16)
    return head, (a - head.astype(jnp.float32)).astype(jnp.bfloat16)


def split_table(table, axis, order):
    head = table.astype(ml_dtypes.bfloat16)
    rest = (table - head.astype(np.float64)).astype(ml_dtypes.bfloat16)
    return np.concatenate([head if part == "h" else rest for part in order], axis=axis)


def per_slab(table):
    return np.kron(np.eye(GROUP), table)


def build_tables(n_gx, n_gy, cells_x, cells_y):
    period_x, period_y = n_gx * cells_x, n_gy * cells_y
    scaling = 1.0 / math.sqrt(period_x * period_y)
    parity = [np.arange(p, 2 * KX, 2) for p in range(2)]
    x_fwd, y_fwd, y_back, inner, outer = [], [], [], [], []
    for g in range(n_gx):
        first = g * cells_x
        table = wave_table(first + np.arange(cells_x), period_x)
        x_fwd.append(split_table(
            np.concatenate([per_slab(table[rows].T) for rows in parity], axis=1), 0, "hhl"))
        beside = wave_table(np.array([first - 1, first + cells_x]), period_x)
        inner.append(np.concatenate([per_slab(table[rows]) for rows in parity], axis=0))
        outer.append(np.concatenate([per_slab(beside[rows]) for rows in parity], axis=0))
    spare = -(2 * GROUP * n_gx) % LANES
    x_back = np.concatenate(inner + outer + [np.zeros((2 * LANES, spare))], axis=1)
    for g in range(n_gy):
        first = g * cells_y
        table = wave_table(first + np.arange(cells_y), period_y)
        edge = np.zeros((2 * KX, cells_y))
        edge[:, [0, -1]] = wave_table(np.array([first - 1, first + cells_y]), period_y)
        y_fwd.append(split_table(table * scaling, 1, "hlh"))
        y_back.append(split_table(np.concatenate([table, edge], axis=1), 0, "hhl"))
    return [np.stack(x_fwd), np.stack(y_fwd), np.stack(y_back), split_table(x_back, 0, "hl")]


def data_dot(a, table):
    head, rest = split(a)
    return jnp.dot(
        jnp.concatenate([head, rest, head], axis=1), table, preferred_element_type=jnp.float32
    )


def columns_dot(a, table):
    head, rest = split(a)
    stacked = jnp.concatenate([head, rest, head], axis=0)
    return lax.dot_general(
        stacked, table, (((0,), (0,)), ((), ())), preferred_element_type=jnp.float32)


def emit_modes(read, parent, is_owner, x_fwd, y_fwd, modes, turned, work):
    devices, rows = modes.shape[0], modes.shape[1] // 2
    slabs = parent.shape[0]
    groups = slabs // GROUP
    head, rest = split(jnp.concatenate([read(c) for c in range(slabs)], axis=0))
    half = lax.dot_general(
        y_fwd, jnp.concatenate([head, head, rest], axis=1), (((1,), (1,)), ((), ())),
        preferred_element_type=jnp.float32)
    half = jnp.concatenate([half[:, t * LANES : (t + 1) * LANES] for t in range(groups)], axis=0)
    count = groups * 2 * KX
    work[0:count] = -data_dot(half, x_fwd)
    if count < devices * rows:
        work[count:] = jnp.zeros((devices * rows - count, 2 * LANES), jnp.float32)

    @pl.when(is_owner)
    def _():
        for i in range(KX):
            turned[:, i, :] = parent[:, i * LANES : (i + 1) * LANES]
        for t in range(groups):
            block = turned[t * GROUP : (t + 1) * GROUP].reshape(LANES, LANES).T
            span = slice(t * 2 * KX, (t + 1) * 2 * KX)
            for p in range(2):
                work[span, p * LANES : (p + 1) * LANES] += block[p * 2 * KX : (p + 1) * 2 * KX]

    for d in range(devices):
        for p in range(2):
            modes[d, p * rows : (p + 1) * rows, :] = work[
                d * rows : (d + 1) * rows, p * LANES : (p + 1) * LANES]


def fetch_all(sems, pairs):
    copies = [pltpu.make_async_copy(a, b, sems.at[i]) for i, (a, b) in enumerate(pairs)]
    for copy in copies:
        copy.start()
    return copies


def slab_of(levels, c, level_count, level_total):
    return (c // level_count) * level_total + levels[c % level_count]


def first_kernel(n_gy, level_total, levels, owners, fields_all, parent_all, x_fwd_all, y_fwd_all,
                 modes, fields, sems, parent, x_fwd, y_fwd, turned, work):
    gx, gy = lax.axis_index("gx"), lax.axis_index("gy")
    copies = fetch_all(sems, [
        (fields_all, fields), (x_fwd_all.at[gx], x_fwd), (y_fwd_all.at[gy], y_fwd),
        (parent_all.at[0, 0], parent)])
    for copy in copies:
        copy.wait()
    level_count = parent.shape[0] // 3
    emit_modes(
        lambda c: fields[slab_of(levels, c, level_count, level_total)],
        parent, owners[0] == gx * n_gy + gy, x_fwd[...], y_fwd[...], modes, turned, work,
    )


def edge_kernel(fields, plume, *rest):
    copies = []
    if len(rest) > 3:
        y_back_all, west, east, cols, y_back, sems = rest
        copies = fetch_all(sems, [(y_back_all.at[lax.axis_index("gy")], y_back)])
    else:
        west, east, cols = rest
    cells_x, cells_y = plume.shape[1:]
    field_rows = fields.shape[0]
    lane = lax.broadcasted_iota(jnp.int32, cols.shape, 1)
    acc = jnp.zeros(cols.shape, jnp.float32)
    for c in range(field_rows + plume.shape[0]):
        a = fields[c] if c < field_rows else plume[c - field_rows]
        west[c : c + 1, :] = a[:1]
        east[c : c + 1, :] = a[cells_x - 1 :]
        acc = jnp.where(lane // 2 == c, pltpu.roll(a, 2 * c + 1, 1), acc)
    cols[...] = acc
    for copy in copies:
        copy.wait()


def beside_rows(rows):
    return -(-rows // 3)


def share_kernel(n_gx, n_gy, period, cuts, parts, x_back, out):
    devices = parts.shape[0]
    rows = parts.shape[1] // 2
    me = lax.axis_index("gx") * n_gy + lax.axis_index("gy")
    total = parts[0]
    for d in range(1, devices):
        total = total + parts[d]
    shape = total.shape
    place = lax.broadcasted_iota(jnp.int32, shape, 0)
    lane = lax.broadcasted_iota(jnp.int32, shape, 1)
    p = (place >= rows).astype(jnp.int32)
    row = me * rows + place - p * rows
    k = 2 * (lane % KX) + p
    j = row % (2 * KX)
    slab = GROUP * (row // (2 * KX)) + lane // KX
    limit = jnp.zeros(shape, jnp.int32)
    for c in range(cuts.shape[0]):
        limit = jnp.where(slab == c, cuts[c], limit)
    keep = ((k % KX) < limit) & ((j % KX) < limit)
    factor = jnp.where(k == 0, 1.0, 2.0) * jnp.where(j == 0, 1.0, 2.0) * (1.0 / math.sqrt(period))
    mismatch = jnp.where(keep, total * factor, 0.0)
    both = jnp.concatenate([mismatch[:rows], mismatch[rows:]], axis=1)
    spare = -rows % 16
    if spare:
        both = jnp.concatenate([both, jnp.zeros((spare, 2 * LANES), jnp.float32)], axis=0)
    head, rest = split(both)
    depth = 2 * LANES
    heads = jnp.dot(
        jnp.concatenate([head, rest], axis=0), x_back[:depth], preferred_element_type=jnp.float32)
    half = heads[: rows + spare] + heads[rows + spare :] + jnp.dot(
        head, x_back[depth:], preferred_element_type=jnp.float32)
    packed = beside_rows(rows)
    width = 2 * GROUP
    spot = lax.broadcasted_iota(jnp.int32, (packed, LANES), 1) // width
    for g in range(n_gx):
        first = (n_gx + g * width // LANES) * LANES
        edge = half[:, first : first + LANES]
        beside = jnp.zeros((packed, LANES), jnp.float32)
        for m in range(3):
            piece = edge[m * packed : (m + 1) * packed]
            beside = jnp.where(
                spot == m, pltpu.roll(piece, (m - g) * width % LANES, 1), beside)
        for h in range(n_gy):
            out[g * n_gy + h, :rows, :] = half[:rows, g * LANES : (g + 1) * LANES]
            out[g * n_gy + h, rows:, :] = beside


def step_kernel(n_gy, step, last, levels, owners, shares, fields, plume,
                west, east, south, north, y_back, source_all, *rest):
    gx, gy = lax.axis_index("gx"), lax.axis_index("gy")
    extra = []
    if last:
        fields_out, plume_out, slabs, beside, spread, spread_edges, source, sems = rest
    else:
        (parent_all, x_fwd_all, y_fwd_all, fields_out, plume_out, modes,
         slabs, beside, spread, spread_edges, source, sems, parent, x_fwd, y_fwd, turned,
         work) = rest
        extra = [(x_fwd_all.at[gx], x_fwd), (y_fwd_all.at[gy], y_fwd),
                 (parent_all.at[0, step + 1], parent)]
    copies = fetch_all(sems, [(source_all, source)] + extra)
    level_total, cells_x, cells_y = plume.shape
    field_rows = fields.shape[0]
    total = field_rows + level_total
    level_count = levels.shape[0]
    nudged = 3 * level_count
    inner = slice(PAD, PAD + cells_x)
    for c in range(total):
        slabs[c, inner] = fields[c] if c < field_rows else plume[c - field_rows]
        slabs[c, PAD - 1 : PAD] = west[c : c + 1, :]
        slabs[c, PAD + cells_x : PAD + cells_x + 1] = east[c : c + 1, :]
    beside[...] = jnp.zeros_like(beside)
    devices = shares.shape[0]
    rows = spread.shape[0] // devices
    packed = beside_rows(rows)
    width = 2 * GROUP
    for d in range(devices):
        spread[d * rows : (d + 1) * rows] = shares[d, :rows, :]
        edge = shares[d, rows:, :]
        for m in range(3):
            count = min(packed, rows - m * packed)
            if count > 0:
                moved = pltpu.roll(edge, -m * width % LANES, 1) if m else edge
                start = d * rows + m * packed
                spread_edges[start : start + count] = moved[:count]
    y_table = y_back[...]
    groups = nudged // GROUP
    spot_of = lax.broadcasted_iota(jnp.int32, (2 * KX, LANES), 1) // width
    edges = jnp.zeros((2 * KX, LANES), jnp.float32)
    for t in range(groups):
        piece = spread_edges[t * 2 * KX : (t + 1) * 2 * KX]
        edges = jnp.where(spot_of == t, pltpu.roll(piece, t * width, 1) if t else piece, edges)
    update_rows = columns_dot(edges, y_table)
    for t in range(groups):
        update = columns_dot(spread[t * 2 * KX : (t + 1) * 2 * KX], y_table)
        for n in range(GROUP):
            c = t * GROUP + n
            part = update[n * cells_x : (n + 1) * cells_x]
            spot = slab_of(levels, c, level_count, level_total)
            slabs[spot, inner] += part[:, :cells_y]
            slabs[spot, PAD - 1 : PAD] += update_rows[2 * c : 2 * c + 1, :cells_y]
            slabs[spot, PAD + cells_x : PAD + cells_x + 1] += update_rows[
                2 * c + 1 : 2 * c + 2, :cells_y]
            beside[spot] = part[:, cells_y:]

    lane = lax.broadcasted_iota(jnp.int32, (cells_x, cells_y), 1)
    first, final = lane == 0, lane == cells_y - 1
    columns = jnp.where(
        lane % 2 == 0, pltpu.roll(north[...], cells_y - 1, 1), pltpu.roll(south[...], 1, 1))

    copies[0].wait()

    def advance(c, parts):
        centre, to_west, to_east, to_south, to_north = parts
        a = slabs[c, inner]
        column = pltpu.roll(columns, cells_y - 1 - 2 * c, 1)
        if c < field_rows:
            column = column + beside[c]
        return (
            centre * a
            + to_west * slabs[c, PAD - 1 : PAD - 1 + cells_x]
            + to_east * slabs[c, PAD + 1 : PAD + 1 + cells_x]
            + to_south * jnp.where(first, column, pltpu.roll(a, 1, 1))
            + to_north * jnp.where(final, column, pltpu.roll(a, cells_y - 1, 1))
        )

    for l in range(level_total):
        u, v = slabs[l, inner], slabs[level_total + l, inner]
        beside_parts = (
            0.1 + 0.1 * jnp.maximum(u, 0.0), 0.1 - 0.1 * jnp.minimum(u, 0.0),
            0.1 + 0.1 * jnp.maximum(v, 0.0), 0.1 - 0.1 * jnp.minimum(v, 0.0),
        )
        centre = 1.0 - (beside_parts[0] + beside_parts[1] + beside_parts[2] + beside_parts[3])
        for f in range(3):
            fields_out[f * level_total + l] = advance(
                f * level_total + l, (centre,) + beside_parts)
        settled = advance(field_rows + l, (centre - 0.3,) + beside_parts) + source[l]
        if l + 1 < level_total:
            settled = settled + 0.3 * plume[l + 1]
        plume_out[l] = settled

    if last:
        return
    for copy in copies[1:]:
        copy.wait()
    emit_modes(
        lambda c: fields_out[slab_of(levels, c, level_count, level_total)],
        parent, owners[step + 1] == gx * n_gy + gy, x_fwd[...], y_fwd[...], modes, turned, work,
    )


def swap(axis, to_next, to_previous):
    count = lax.axis_size(axis)
    up = [(i, i + 1) for i in range(count - 1)]
    down = [(b, a) for a, b in up]
    return lax.ppermute(to_next, axis, up), lax.ppermute(to_previous, axis, down)


def local(tables, fields, levels, cuts, parent_modes, owners, plume, source):
    n_gx, n_gy = lax.axis_size("gx"), lax.axis_size("gy")
    devices = n_gx * n_gy
    level_total, cells_x, cells_y = plume.shape
    period = n_gx * cells_x * n_gy * cells_y
    nudged = 3 * levels.shape[0]
    field_rows = 3 * level_total
    total = field_rows + level_total
    rows = -(-(nudged // GROUP * 2 * KX) // devices)
    flat = fields.reshape(field_rows, cells_x, cells_y)
    cuts = cuts.reshape(-1)
    f32 = functools.partial(jax.ShapeDtypeStruct, dtype=jnp.float32)
    x_fwd, y_fwd, y_back, x_back = (jnp.asarray(t) for t in tables)

    def vmem(*shape):
        return pltpu.VMEM(shape, jnp.float32)

    def table_space(table):
        return pltpu.VMEM(table.shape[1:], table.dtype)

    def limit(mib):
        return pltpu.CompilerParams(vmem_limit_bytes=mib * 1024 * 1024)

    mode_shape = f32((devices, 2 * rows, LANES))
    step_scratch = [vmem(total, cells_x + 2 * PAD, cells_y), vmem(field_rows, cells_x, cells_y),
                    vmem(devices * rows, LANES), vmem(devices * rows, LANES),
                    vmem(level_total, cells_x, cells_y), pltpu.SemaphoreType.DMA((4,))]
    mode_scratch = [vmem(nudged, 4 * KX * KX), table_space(x_fwd),
                    table_space(y_fwd), vmem(nudged, KX, LANES),
                    vmem(devices * rows, 2 * LANES)]
    levels, owners = in_hbm(levels), in_hbm(owners)

    modes = pl.pallas_call(
        functools.partial(first_kernel, n_gy, level_total),
        out_shape=mode_shape,
        in_specs=[SMEM, SMEM] + [HBM] * 4,
        out_specs=VMEM,
        scratch_shapes=[vmem(field_rows, cells_x, cells_y), pltpu.SemaphoreType.DMA((4,))]
        + mode_scratch,
        compiler_params=limit(8),
        name="first_modes",
    )(levels, owners, in_hbm(flat), in_hbm(parent_modes), in_hbm(x_fwd), in_hbm(y_fwd))
    for step in range(STEPS):
        last = step == STEPS - 1
        edge_shapes = [f32((total, cells_y)), f32((total, cells_y)), f32((cells_x, 2 * total))]
        edge_operands = [flat, plume]
        if step == 0:
            edge_shapes.append(jax.ShapeDtypeStruct(y_back.shape[1:], y_back.dtype))
            edge_operands.append(in_hbm(y_back))
        edges = pl.pallas_call(
            edge_kernel,
            out_shape=edge_shapes,
            in_specs=[VMEM, VMEM] + [HBM] * (len(edge_operands) - 2),
            out_specs=[VMEM] * len(edge_shapes),
            scratch_shapes=[pltpu.SemaphoreType.DMA((1,))] if step == 0 else [],
            compiler_params=limit(8),
            name="edges",
        )(*edge_operands)
        if step == 0:
            back_table = edges[3]
        to_west, to_east, cols = edges[:3]
        west, east = swap("gx", to_east, to_west)
        parts = lax.all_to_all(modes, AXES, 0, 0, tiled=True)
        parts, west, east = lax.optimization_barrier((parts, west, east))
        share = pl.pallas_call(
            functools.partial(share_kernel, n_gx, n_gy, period),
            out_shape=f32((devices, rows + beside_rows(rows), LANES)),
            in_specs=[SMEM, VMEM, VMEM],
            out_specs=VMEM,
            compiler_params=limit(8),
            name="share_sum",
        )(cuts, parts, x_back)
        share, cols = lax.optimization_barrier((share, cols))
        south, north = swap("gy", cols, cols)
        shares = lax.all_to_all(share, AXES, 0, 0, tiled=True)
        out_shape = [f32(flat.shape), f32(plume.shape)]
        operands = [levels, owners, shares, flat, plume, west, east, south, north, back_table,
                    in_hbm(source)]
        if not last:
            out_shape.append(mode_shape)
            operands += [in_hbm(parent_modes), in_hbm(x_fwd), in_hbm(y_fwd)]
        results = pl.pallas_call(
            functools.partial(step_kernel, n_gy, step, last),
            out_shape=out_shape,
            in_specs=[SMEM, SMEM] + [VMEM] * 8 + [HBM] * (len(operands) - 10),
            out_specs=[VMEM] * len(out_shape),
            scratch_shapes=step_scratch + ([] if last else mode_scratch),
            compiler_params=limit(20),
            name="final_step" if last else "inner_step",
        )(*operands)
        if last:
            flat, plume = results
        else:
            flat, plume, modes = results
    return flat.reshape(fields.shape), plume


def solution(mesh):
    in_specs = (
        P(None, None, "gx", "gy"),
        P(),
        P(),
        P(("gx", "gy"), None, None, None),
        P(),
        P(None, "gx", "gy"),
        P(None, "gx", "gy"),
    )
    out_specs = (P(None, None, "gx", "gy"), P(None, "gx", "gy"))
    n_gx, n_gy = mesh.shape["gx"], mesh.shape["gy"]

    def whole(fields, levels, cuts, parent_modes, owners, plume, source):
        tables = build_tables(n_gx, n_gy, plume.shape[1] // n_gx, plume.shape[2] // n_gy)
        return jax.shard_map(
            functools.partial(local, tables), mesh=mesh, in_specs=in_specs, out_specs=out_specs,
            check_vma=False,
        )(fields, levels, cuts, parent_modes, owners, plume, source)

    return whole
```

```python
import functools
import math

import jax
import jax.numpy as jnp
import ml_dtypes
import numpy as np
from jax import lax
from jax.experimental import pallas as pl
from jax.experimental.pallas import tpu as pltpu
from jax.sharding import PartitionSpec as P

KX = 32
STEPS = 2
GROUP = 4
LANES = GROUP * KX
PAD = 8
VMEM = pl.BlockSpec(memory_space=pltpu.VMEM)
SMEM = pl.BlockSpec(memory_space=pltpu.SMEM)
HBM = pl.BlockSpec(memory_space=pltpu.HBM)
AXES = ("gx", "gy")


def in_hbm(array):
    return pltpu.with_memory_space_constraint(array, pltpu.HBM)


def wave_table(positions, period):
    wavenum = np.arange(KX)[:, None]
    phase = (wavenum * positions[None, :] % period) * (2.0 * math.pi / period)
    inside = (positions >= 0) & (positions < period)
    return np.concatenate([np.cos(phase), np.sin(phase)], axis=0) * inside[None, :]


def split(a):
    head = a.astype(jnp.bfloat16)
    return head, (a - head.astype(jnp.float32)).astype(jnp.bfloat16)


def split_table(table, axis, order):
    head = table.astype(ml_dtypes.bfloat16)
    rest = (table - head.astype(np.float64)).astype(ml_dtypes.bfloat16)
    return np.concatenate([head if part == "h" else rest for part in order], axis=axis)


def per_slab(table):
    return np.kron(np.eye(GROUP), table)


def build_tables(n_gx, n_gy, cells_x, cells_y):
    period_x, period_y = n_gx * cells_x, n_gy * cells_y
    scaling = 1.0 / math.sqrt(period_x * period_y)
    parity = [np.arange(p, 2 * KX, 2) for p in range(2)]
    x_fwd, y_fwd, y_back, inner, outer = [], [], [], [], []
    for g in range(n_gx):
        first = g * cells_x
        table = wave_table(first + np.arange(cells_x), period_x)
        x_fwd.append(split_table(
            np.concatenate([per_slab(table[rows].T) for rows in parity], axis=1), 0, "hhl"))
        beside = wave_table(np.array([first - 1, first + cells_x]), period_x)
        inner.append(np.concatenate([np.tile(table[rows], (GROUP, 1)) for rows in parity], axis=0))
        outer.append(np.concatenate([per_slab(beside[rows]) for rows in parity], axis=0))
    spare = -(2 * GROUP * n_gx) % LANES
    x_back = np.concatenate(inner, axis=1)
    x_beside = np.concatenate(outer + [np.zeros((2 * LANES, spare))], axis=1)
    for g in range(n_gy):
        first = g * cells_y
        table = wave_table(first + np.arange(cells_y), period_y)
        edge = np.zeros((2 * KX, cells_y))
        edge[:, [0, -1]] = wave_table(np.array([first - 1, first + cells_y]), period_y)
        y_fwd.append(split_table(table * scaling, 1, "hlh"))
        y_back.append(split_table(np.concatenate([table, edge], axis=1), 0, "hhl"))
    return [np.stack(x_fwd), np.stack(y_fwd), np.stack(y_back),
            split_table(x_back, 0, "hl"), split_table(x_beside, 0, "hl")]


def data_dot(a, table):
    head, rest = split(a)
    return jnp.dot(
        jnp.concatenate([head, rest, head], axis=1), table, preferred_element_type=jnp.float32
    )


def two_part_dot(a, table):
    head, rest = split(a)
    depth = a.shape[1]
    heads = jnp.dot(
        jnp.concatenate([head, rest], axis=0), table[:depth], preferred_element_type=jnp.float32)
    rests = jnp.dot(head, table[depth:], preferred_element_type=jnp.float32)
    return heads[: a.shape[0]] + heads[a.shape[0] :] + rests


def columns_dot(a, table):
    head, rest = split(a)
    stacked = jnp.concatenate([head, rest, head], axis=0)
    return lax.dot_general(
        stacked, table, (((0,), (0,)), ((), ())), preferred_element_type=jnp.float32)


def emit_modes(read, parent, is_owner, x_fwd, y_fwd, modes, turned, work):
    devices, rows = modes.shape[0], modes.shape[1] // 2
    slabs = parent.shape[0]
    groups = slabs // GROUP
    head, rest = split(jnp.concatenate([read(c) for c in range(slabs)], axis=0))
    half = lax.dot_general(
        y_fwd, jnp.concatenate([head, head, rest], axis=1), (((1,), (1,)), ((), ())),
        preferred_element_type=jnp.float32)
    half = jnp.concatenate([half[:, t * LANES : (t + 1) * LANES] for t in range(groups)], axis=0)
    count = groups * 2 * KX
    work[0:count] = -data_dot(half, x_fwd)
    if count < devices * rows:
        work[count:] = jnp.zeros((devices * rows - count, 2 * LANES), jnp.float32)

    @pl.when(is_owner)
    def _():
        for i in range(KX):
            turned[:, i, :] = parent[:, i * LANES : (i + 1) * LANES]
        for t in range(groups):
            block = turned[t * GROUP : (t + 1) * GROUP].reshape(LANES, LANES).T
            span = slice(t * 2 * KX, (t + 1) * 2 * KX)
            for p in range(2):
                work[span, p * LANES : (p + 1) * LANES] += block[p * 2 * KX : (p + 1) * 2 * KX]

    for d in range(devices):
        for p in range(2):
            modes[d, p * rows : (p + 1) * rows, :] = work[
                d * rows : (d + 1) * rows, p * LANES : (p + 1) * LANES]


def fetch_all(sems, pairs):
    copies = [pltpu.make_async_copy(a, b, sems.at[i]) for i, (a, b) in enumerate(pairs)]
    for copy in copies:
        copy.start()
    return copies


def slab_of(levels, c, level_count, level_total):
    return (c // level_count) * level_total + levels[c % level_count]


def first_kernel(n_gy, level_total, levels, owners, fields_all, parent_all, x_fwd_all, y_fwd_all,
                 modes, fields, sems, parent, x_fwd, y_fwd, turned, work):
    gx, gy = lax.axis_index("gx"), lax.axis_index("gy")
    copies = fetch_all(sems, [
        (fields_all, fields), (x_fwd_all.at[gx], x_fwd), (y_fwd_all.at[gy], y_fwd),
        (parent_all.at[0, 0], parent)])
    for copy in copies:
        copy.wait()
    level_count = parent.shape[0] // 3
    emit_modes(
        lambda c: fields[slab_of(levels, c, level_count, level_total)],
        parent, owners[0] == gx * n_gy + gy, x_fwd[...], y_fwd[...], modes, turned, work,
    )


def edge_kernel(fields, plume, *rest):
    copies = []
    if len(rest) > 3:
        y_back_all, west, east, cols, y_back, sems = rest
        copies = fetch_all(sems, [(y_back_all.at[lax.axis_index("gy")], y_back)])
    else:
        west, east, cols = rest
    cells_x, cells_y = plume.shape[1:]
    field_rows = fields.shape[0]
    lane = lax.broadcasted_iota(jnp.int32, cols.shape, 1)
    acc = jnp.zeros(cols.shape, jnp.float32)
    for c in range(field_rows + plume.shape[0]):
        a = fields[c] if c < field_rows else plume[c - field_rows]
        west[c : c + 1, :] = a[:1]
        east[c : c + 1, :] = a[cells_x - 1 :]
        acc = jnp.where(lane // 2 == c, pltpu.roll(a, 2 * c + 1, 1), acc)
    cols[...] = acc
    for copy in copies:
        copy.wait()


def beside_rows(rows):
    return -(-rows // 3)


def share_kernel(n_gx, n_gy, period, cuts, parts, x_back, x_beside, out):
    devices = parts.shape[0]
    rows = parts.shape[1] // 2
    me = lax.axis_index("gx") * n_gy + lax.axis_index("gy")
    total = parts[0]
    for d in range(1, devices):
        total = total + parts[d]
    shape = total.shape
    place = lax.broadcasted_iota(jnp.int32, shape, 0)
    lane = lax.broadcasted_iota(jnp.int32, shape, 1)
    p = (place >= rows).astype(jnp.int32)
    row = me * rows + place - p * rows
    k = 2 * (lane % KX) + p
    j = row % (2 * KX)
    slab = GROUP * (row // (2 * KX)) + lane // KX
    limit = jnp.zeros(shape, jnp.int32)
    for c in range(cuts.shape[0]):
        limit = jnp.where(slab == c, cuts[c], limit)
    keep = ((k % KX) < limit) & ((j % KX) < limit)
    factor = jnp.where(k == 0, 1.0, 2.0) * jnp.where(j == 0, 1.0, 2.0) * (1.0 / math.sqrt(period))
    mismatch = jnp.where(keep, total * factor, 0.0)
    both = jnp.concatenate([mismatch[:rows], mismatch[rows:]], axis=1)
    spare = -rows % 16
    if spare:
        both = jnp.concatenate([both, jnp.zeros((spare, 2 * LANES), jnp.float32)], axis=0)
    slab_lane = lax.broadcasted_iota(jnp.int32, both.shape, 1) % LANES // KX
    chosen = [jnp.where(slab_lane == n, both, 0.0) for n in range(GROUP)]
    inner = two_part_dot(jnp.concatenate(chosen, axis=0), x_back)
    edge_all = two_part_dot(both, x_beside)
    height = rows + spare
    packed = beside_rows(rows)
    width = 2 * GROUP
    cells_x = LANES // GROUP
    slot = lax.broadcasted_iota(jnp.int32, (height, LANES), 1) // cells_x
    spot = lax.broadcasted_iota(jnp.int32, (packed, LANES), 1) // width
    for g in range(n_gx):
        first = g * cells_x // LANES * LANES
        tile = jnp.zeros((height, LANES), jnp.float32)
        for n in range(GROUP):
            piece = inner[n * height : (n + 1) * height, first : first + LANES]
            tile = jnp.where(slot == n, pltpu.roll(piece, (n - g) * cells_x % LANES, 1), tile)
        first = g * width // LANES * LANES
        beside = jnp.zeros((packed, LANES), jnp.float32)
        for m in range(3):
            piece = edge_all[m * packed : (m + 1) * packed, first : first + LANES]
            beside = jnp.where(
                spot == m, pltpu.roll(piece, (m - g) * width % LANES, 1), beside)
        for h in range(n_gy):
            out[g * n_gy + h, :rows, :] = tile[:rows]
            out[g * n_gy + h, rows:, :] = beside


def step_kernel(n_gy, step, last, levels, owners, shares, fields, plume,
                west, east, south, north, y_back, source_all, *rest):
    gx, gy = lax.axis_index("gx"), lax.axis_index("gy")
    extra = []
    if last:
        fields_out, plume_out, slabs, beside, spread, spread_edges, source, sems = rest
    else:
        (parent_all, x_fwd_all, y_fwd_all, fields_out, plume_out, modes,
         slabs, beside, spread, spread_edges, source, sems, parent, x_fwd, y_fwd, turned,
         work) = rest
        extra = [(x_fwd_all.at[gx], x_fwd), (y_fwd_all.at[gy], y_fwd),
                 (parent_all.at[0, step + 1], parent)]
    copies = fetch_all(sems, [(source_all, source)] + extra)
    level_total, cells_x, cells_y = plume.shape
    field_rows = fields.shape[0]
    total = field_rows + level_total
    level_count = levels.shape[0]
    nudged = 3 * level_count
    inner = slice(PAD, PAD + cells_x)
    for c in range(total):
        slabs[c, inner] = fields[c] if c < field_rows else plume[c - field_rows]
        slabs[c, PAD - 1 : PAD] = west[c : c + 1, :]
        slabs[c, PAD + cells_x : PAD + cells_x + 1] = east[c : c + 1, :]
    beside[...] = jnp.zeros_like(beside)
    devices = shares.shape[0]
    rows = spread.shape[0] // devices
    packed = beside_rows(rows)
    width = 2 * GROUP
    for d in range(devices):
        spread[d * rows : (d + 1) * rows] = shares[d, :rows, :]
        edge = shares[d, rows:, :]
        for m in range(3):
            count = min(packed, rows - m * packed)
            if count > 0:
                moved = pltpu.roll(edge, -m * width % LANES, 1) if m else edge
                start = d * rows + m * packed
                spread_edges[start : start + count] = moved[:count]
    y_table = y_back[...]
    groups = nudged // GROUP
    spot_of = lax.broadcasted_iota(jnp.int32, (2 * KX, LANES), 1) // width
    edges = jnp.zeros((2 * KX, LANES), jnp.float32)
    for t in range(groups):
        piece = spread_edges[t * 2 * KX : (t + 1) * 2 * KX]
        edges = jnp.where(spot_of == t, pltpu.roll(piece, t * width, 1) if t else piece, edges)
    update_rows = columns_dot(edges, y_table)
    for t in range(groups):
        update = columns_dot(spread[t * 2 * KX : (t + 1) * 2 * KX], y_table)
        for n in range(GROUP):
            c = t * GROUP + n
            part = update[n * cells_x : (n + 1) * cells_x]
            spot = slab_of(levels, c, level_count, level_total)
            slabs[spot, inner] += part[:, :cells_y]
            slabs[spot, PAD - 1 : PAD] += update_rows[2 * c : 2 * c + 1, :cells_y]
            slabs[spot, PAD + cells_x : PAD + cells_x + 1] += update_rows[
                2 * c + 1 : 2 * c + 2, :cells_y]
            beside[spot] = part[:, cells_y:]

    lane = lax.broadcasted_iota(jnp.int32, (cells_x, cells_y), 1)
    first, final = lane == 0, lane == cells_y - 1
    columns = jnp.where(
        lane % 2 == 0, pltpu.roll(north[...], cells_y - 1, 1), pltpu.roll(south[...], 1, 1))

    copies[0].wait()

    def advance(c, parts):
        centre, to_west, to_east, to_south, to_north = parts
        a = slabs[c, inner]
        column = pltpu.roll(columns, cells_y - 1 - 2 * c, 1)
        if c < field_rows:
            column = column + beside[c]
        return (
            centre * a
            + to_west * slabs[c, PAD - 1 : PAD - 1 + cells_x]
            + to_east * slabs[c, PAD + 1 : PAD + 1 + cells_x]
            + to_south * jnp.where(first, column, pltpu.roll(a, 1, 1))
            + to_north * jnp.where(final, column, pltpu.roll(a, cells_y - 1, 1))
        )

    for l in range(level_total):
        u, v = slabs[l, inner], slabs[level_total + l, inner]
        beside_parts = (
            0.1 + 0.1 * jnp.maximum(u, 0.0), 0.1 - 0.1 * jnp.minimum(u, 0.0),
            0.1 + 0.1 * jnp.maximum(v, 0.0), 0.1 - 0.1 * jnp.minimum(v, 0.0),
        )
        centre = 1.0 - (beside_parts[0] + beside_parts[1] + beside_parts[2] + beside_parts[3])
        for f in range(3):
            fields_out[f * level_total + l] = advance(
                f * level_total + l, (centre,) + beside_parts)
        settled = advance(field_rows + l, (centre - 0.3,) + beside_parts) + source[l]
        if l + 1 < level_total:
            settled = settled + 0.3 * plume[l + 1]
        plume_out[l] = settled

    if last:
        return
    for copy in copies[1:]:
        copy.wait()
    emit_modes(
        lambda c: fields_out[slab_of(levels, c, level_count, level_total)],
        parent, owners[step + 1] == gx * n_gy + gy, x_fwd[...], y_fwd[...], modes, turned, work,
    )


def swap(axis, to_next, to_previous):
    count = lax.axis_size(axis)
    up = [(i, i + 1) for i in range(count - 1)]
    down = [(b, a) for a, b in up]
    return lax.ppermute(to_next, axis, up), lax.ppermute(to_previous, axis, down)


def local(tables, fields, levels, cuts, parent_modes, owners, plume, source):
    n_gx, n_gy = lax.axis_size("gx"), lax.axis_size("gy")
    devices = n_gx * n_gy
    level_total, cells_x, cells_y = plume.shape
    period = n_gx * cells_x * n_gy * cells_y
    nudged = 3 * levels.shape[0]
    field_rows = 3 * level_total
    total = field_rows + level_total
    rows = -(-(nudged // GROUP * 2 * KX) // devices)
    flat = fields.reshape(field_rows, cells_x, cells_y)
    cuts = cuts.reshape(-1)
    f32 = functools.partial(jax.ShapeDtypeStruct, dtype=jnp.float32)
    x_fwd, y_fwd, y_back, x_back, x_beside = (jnp.asarray(t) for t in tables)

    def vmem(*shape):
        return pltpu.VMEM(shape, jnp.float32)

    def table_space(table):
        return pltpu.VMEM(table.shape[1:], table.dtype)

    def limit(mib):
        return pltpu.CompilerParams(vmem_limit_bytes=mib * 1024 * 1024)

    mode_shape = f32((devices, 2 * rows, LANES))
    step_scratch = [vmem(total, cells_x + 2 * PAD, cells_y), vmem(field_rows, cells_x, cells_y),
                    vmem(devices * rows, LANES), vmem(devices * rows, LANES),
                    vmem(level_total, cells_x, cells_y), pltpu.SemaphoreType.DMA((4,))]
    mode_scratch = [vmem(nudged, 4 * KX * KX), table_space(x_fwd),
                    table_space(y_fwd), vmem(nudged, KX, LANES),
                    vmem(devices * rows, 2 * LANES)]
    levels, owners = in_hbm(levels), in_hbm(owners)

    modes = pl.pallas_call(
        functools.partial(first_kernel, n_gy, level_total),
        out_shape=mode_shape,
        in_specs=[SMEM, SMEM] + [HBM] * 4,
        out_specs=VMEM,
        scratch_shapes=[vmem(field_rows, cells_x, cells_y), pltpu.SemaphoreType.DMA((4,))]
        + mode_scratch,
        compiler_params=limit(8),
        name="first_modes",
    )(levels, owners, in_hbm(flat), in_hbm(parent_modes), in_hbm(x_fwd), in_hbm(y_fwd))
    for step in range(STEPS):
        last = step == STEPS - 1
        edge_shapes = [f32((total, cells_y)), f32((total, cells_y)), f32((cells_x, 2 * total))]
        edge_operands = [flat, plume]
        if step == 0:
            edge_shapes.append(jax.ShapeDtypeStruct(y_back.shape[1:], y_back.dtype))
            edge_operands.append(in_hbm(y_back))
        edges = pl.pallas_call(
            edge_kernel,
            out_shape=edge_shapes,
            in_specs=[VMEM, VMEM] + [HBM] * (len(edge_operands) - 2),
            out_specs=[VMEM] * len(edge_shapes),
            scratch_shapes=[pltpu.SemaphoreType.DMA((1,))] if step == 0 else [],
            compiler_params=limit(8),
            name="edges",
        )(*edge_operands)
        if step == 0:
            back_table = edges[3]
        to_west, to_east, cols = edges[:3]
        west, east = swap("gx", to_east, to_west)
        parts = lax.all_to_all(modes, AXES, 0, 0, tiled=True)
        parts, west, east = lax.optimization_barrier((parts, west, east))
        share = pl.pallas_call(
            functools.partial(share_kernel, n_gx, n_gy, period),
            out_shape=f32((devices, rows + beside_rows(rows), LANES)),
            in_specs=[SMEM, VMEM, VMEM, VMEM],
            out_specs=VMEM,
            compiler_params=limit(8),
            name="share_sum",
        )(cuts, parts, x_back, x_beside)
        share, cols = lax.optimization_barrier((share, cols))
        south, north = swap("gy", cols, cols)
        shares = lax.all_to_all(share, AXES, 0, 0, tiled=True)
        out_shape = [f32(flat.shape), f32(plume.shape)]
        operands = [levels, owners, shares, flat, plume, west, east, south, north, back_table,
                    in_hbm(source)]
        if not last:
            out_shape.append(mode_shape)
            operands += [in_hbm(parent_modes), in_hbm(x_fwd), in_hbm(y_fwd)]
        results = pl.pallas_call(
            functools.partial(step_kernel, n_gy, step, last),
            out_shape=out_shape,
            in_specs=[SMEM, SMEM] + [VMEM] * 8 + [HBM] * (len(operands) - 10),
            out_specs=[VMEM] * len(out_shape),
            scratch_shapes=step_scratch + ([] if last else mode_scratch),
            compiler_params=limit(20),
            name="final_step" if last else "inner_step",
        )(*operands)
        if last:
            flat, plume = results
        else:
            flat, plume, modes = results
    return flat.reshape(fields.shape), plume


def solution(mesh):
    in_specs = (
        P(None, None, "gx", "gy"),
        P(),
        P(),
        P(("gx", "gy"), None, None, None),
        P(),
        P(None, "gx", "gy"),
        P(None, "gx", "gy"),
    )
    out_specs = (P(None, None, "gx", "gy"), P(None, "gx", "gy"))
    n_gx, n_gy = mesh.shape["gx"], mesh.shape["gy"]

    def whole(fields, levels, cuts, parent_modes, owners, plume, source):
        tables = build_tables(n_gx, n_gy, plume.shape[1] // n_gx, plume.shape[2] // n_gy)
        return jax.shard_map(
            functools.partial(local, tables), mesh=mesh, in_specs=in_specs, out_specs=out_specs,
            check_vma=False,
        )(fields, levels, cuts, parent_modes, owners, plume, source)

    return whole
```

```python
import functools
import math

import jax
import jax.numpy as jnp
import ml_dtypes
import numpy as np
from jax import lax
from jax.experimental import pallas as pl
from jax.experimental.pallas import tpu as pltpu
from jax.sharding import PartitionSpec as P

KX = 32
STEPS = 2
GROUP = 4
LANES = GROUP * KX
PAD = 8
VMEM = pl.BlockSpec(memory_space=pltpu.VMEM)
SMEM = pl.BlockSpec(memory_space=pltpu.SMEM)
HBM = pl.BlockSpec(memory_space=pltpu.HBM)
AXES = ("gx", "gy")


def in_hbm(array):
    return pltpu.with_memory_space_constraint(array, pltpu.HBM)


def wave_table(positions, period):
    wavenum = np.arange(KX)[:, None]
    phase = (wavenum * positions[None, :] % period) * (2.0 * math.pi / period)
    inside = (positions >= 0) & (positions < period)
    return np.concatenate([np.cos(phase), np.sin(phase)], axis=0) * inside[None, :]


def split(a):
    head = a.astype(jnp.bfloat16)
    return head, (a - head.astype(jnp.float32)).astype(jnp.bfloat16)


def split_table(table, axis, order):
    head = table.astype(ml_dtypes.bfloat16)
    rest = (table - head.astype(np.float64)).astype(ml_dtypes.bfloat16)
    return np.concatenate([head if part == "h" else rest for part in order], axis=axis)


def per_slab(table):
    return np.kron(np.eye(GROUP), table)


def build_tables(n_gx, n_gy, cells_x, cells_y):
    period_x, period_y = n_gx * cells_x, n_gy * cells_y
    scaling = 1.0 / math.sqrt(period_x * period_y)
    parity = [np.arange(p, 2 * KX, 2) for p in range(2)]
    x_fwd, y_fwd, y_back, inner, outer = [], [], [], [], []
    for g in range(n_gx):
        first = g * cells_x
        table = wave_table(first + np.arange(cells_x), period_x)
        x_fwd.append(split_table(
            np.concatenate([per_slab(table[rows].T) for rows in parity], axis=1), 0, "hhl"))
        beside = wave_table(np.array([first - 1, first + cells_x]), period_x)
        inner.append(np.concatenate([np.tile(table[rows], (GROUP, 1)) for rows in parity], axis=0))
        outer.append(np.concatenate([per_slab(beside[rows]) for rows in parity], axis=0))
    spare = -(2 * GROUP * n_gx) % LANES
    x_back = np.concatenate(inner, axis=1)
    x_beside = np.concatenate(outer + [np.zeros((2 * LANES, spare))], axis=1)
    for g in range(n_gy):
        first = g * cells_y
        table = wave_table(first + np.arange(cells_y), period_y)
        edge = np.zeros((2 * KX, cells_y))
        edge[:, [0, -1]] = wave_table(np.array([first - 1, first + cells_y]), period_y)
        y_fwd.append(split_table(table * scaling, 1, "hlh"))
        y_back.append(split_table(np.concatenate([table, edge], axis=1), 0, "hhl"))
    return [np.stack(x_fwd), np.stack(y_fwd), np.stack(y_back),
            split_table(x_back, 0, "hl"), split_table(x_beside, 0, "hl")]


def data_dot(a, table):
    head, rest = split(a)
    return jnp.dot(
        jnp.concatenate([head, rest, head], axis=1), table, preferred_element_type=jnp.float32
    )


def two_part_dot(a, table):
    head, rest = split(a)
    depth = a.shape[1]
    heads = jnp.dot(
        jnp.concatenate([head, rest], axis=0), table[:depth], preferred_element_type=jnp.float32)
    rests = jnp.dot(head, table[depth:], preferred_element_type=jnp.float32)
    return heads[: a.shape[0]] + heads[a.shape[0] :] + rests


def columns_dot(a, table):
    head, rest = split(a)
    stacked = jnp.concatenate([head, rest, head], axis=0)
    return lax.dot_general(
        stacked, table, (((0,), (0,)), ((), ())), preferred_element_type=jnp.float32)


def emit_modes(read, parent, is_owner, x_fwd, y_fwd, modes, turned, work):
    devices, rows = modes.shape[0], modes.shape[1] // 2
    slabs = parent.shape[0]
    groups = slabs // GROUP
    head, rest = split(jnp.concatenate([read(c) for c in range(slabs)], axis=0))
    half = lax.dot_general(
        y_fwd, jnp.concatenate([head, head, rest], axis=1), (((1,), (1,)), ((), ())),
        preferred_element_type=jnp.float32)
    half = jnp.concatenate([half[:, t * LANES : (t + 1) * LANES] for t in range(groups)], axis=0)
    count = groups * 2 * KX
    work[0:count] = -data_dot(half, x_fwd)
    if count < devices * rows:
        work[count:] = jnp.zeros((devices * rows - count, 2 * LANES), jnp.float32)

    @pl.when(is_owner)
    def _():
        for i in range(KX):
            turned[:, i, :] = parent[:, i * LANES : (i + 1) * LANES]
        for t in range(groups):
            block = turned[t * GROUP : (t + 1) * GROUP].reshape(LANES, LANES).T
            span = slice(t * 2 * KX, (t + 1) * 2 * KX)
            for p in range(2):
                work[span, p * LANES : (p + 1) * LANES] += block[p * 2 * KX : (p + 1) * 2 * KX]

    for d in range(devices):
        for p in range(2):
            modes[d, p * rows : (p + 1) * rows, :] = work[
                d * rows : (d + 1) * rows, p * LANES : (p + 1) * LANES]


def fetch_all(sems, pairs):
    copies = [pltpu.make_async_copy(a, b, sems.at[i]) for i, (a, b) in enumerate(pairs)]
    for copy in copies:
        copy.start()
    return copies


def slab_of(levels, c, level_count, level_total):
    return (c // level_count) * level_total + levels[c % level_count]


def first_kernel(n_gy, level_total, levels_all, owners_all, fields_all, parent_all, x_fwd_all,
                 y_fwd_all, modes, levels, owners, fields, sems, parent, x_fwd, y_fwd, turned,
                 work):
    gx, gy = lax.axis_index("gx"), lax.axis_index("gy")
    copies = fetch_all(sems, [
        (levels_all, levels), (owners_all, owners), (fields_all, fields),
        (x_fwd_all.at[gx], x_fwd), (y_fwd_all.at[gy], y_fwd), (parent_all.at[0, 0], parent)])
    for copy in copies:
        copy.wait()
    level_count = parent.shape[0] // 3
    emit_modes(
        lambda c: fields[slab_of(levels, c, level_count, level_total)],
        parent, owners[0] == gx * n_gy + gy, x_fwd[...], y_fwd[...], modes, turned, work,
    )


def edge_kernel(fields, plume, *rest):
    copies = []
    if len(rest) > 3:
        y_back_all, west, east, cols, y_back, sems = rest
        copies = fetch_all(sems, [(y_back_all.at[lax.axis_index("gy")], y_back)])
    else:
        west, east, cols = rest
    cells_x, cells_y = plume.shape[1:]
    field_rows = fields.shape[0]
    lane = lax.broadcasted_iota(jnp.int32, cols.shape, 1)
    acc = jnp.zeros(cols.shape, jnp.float32)
    for c in range(field_rows + plume.shape[0]):
        a = fields[c] if c < field_rows else plume[c - field_rows]
        west[c : c + 1, :] = a[:1]
        east[c : c + 1, :] = a[cells_x - 1 :]
        acc = jnp.where(lane // 2 == c, pltpu.roll(a, 2 * c + 1, 1), acc)
    cols[...] = acc
    for copy in copies:
        copy.wait()


def beside_rows(rows):
    return -(-rows // 3)


def share_kernel(n_gx, n_gy, period, cuts, parts, x_back, x_beside, out):
    devices = parts.shape[0]
    rows = parts.shape[1] // 2
    me = lax.axis_index("gx") * n_gy + lax.axis_index("gy")
    total = parts[0]
    for d in range(1, devices):
        total = total + parts[d]
    shape = total.shape
    place = lax.broadcasted_iota(jnp.int32, shape, 0)
    lane = lax.broadcasted_iota(jnp.int32, shape, 1)
    p = (place >= rows).astype(jnp.int32)
    row = me * rows + place - p * rows
    k = 2 * (lane % KX) + p
    j = row % (2 * KX)
    slab = GROUP * (row // (2 * KX)) + lane // KX
    limit = jnp.zeros(shape, jnp.int32)
    for c in range(cuts.shape[0]):
        limit = jnp.where(slab == c, cuts[c], limit)
    keep = ((k % KX) < limit) & ((j % KX) < limit)
    factor = jnp.where(k == 0, 1.0, 2.0) * jnp.where(j == 0, 1.0, 2.0) * (1.0 / math.sqrt(period))
    mismatch = jnp.where(keep, total * factor, 0.0)
    both = jnp.concatenate([mismatch[:rows], mismatch[rows:]], axis=1)
    spare = -rows % 16
    if spare:
        both = jnp.concatenate([both, jnp.zeros((spare, 2 * LANES), jnp.float32)], axis=0)
    slab_lane = lax.broadcasted_iota(jnp.int32, both.shape, 1) % LANES // KX
    chosen = [jnp.where(slab_lane == n, both, 0.0) for n in range(GROUP)]
    inner = two_part_dot(jnp.concatenate(chosen, axis=0), x_back)
    edge_all = two_part_dot(both, x_beside)
    height = rows + spare
    packed = beside_rows(rows)
    width = 2 * GROUP
    cells_x = LANES // GROUP
    slot = lax.broadcasted_iota(jnp.int32, (height, LANES), 1) // cells_x
    spot = lax.broadcasted_iota(jnp.int32, (packed, LANES), 1) // width
    for g in range(n_gx):
        first = g * cells_x // LANES * LANES
        tile = jnp.zeros((height, LANES), jnp.float32)
        for n in range(GROUP):
            piece = inner[n * height : (n + 1) * height, first : first + LANES]
            tile = jnp.where(slot == n, pltpu.roll(piece, (n - g) * cells_x % LANES, 1), tile)
        first = g * width // LANES * LANES
        beside = jnp.zeros((packed, LANES), jnp.float32)
        for m in range(3):
            piece = edge_all[m * packed : (m + 1) * packed, first : first + LANES]
            beside = jnp.where(
                spot == m, pltpu.roll(piece, (m - g) * width % LANES, 1), beside)
        for h in range(n_gy):
            out[g * n_gy + h, :rows, :] = tile[:rows]
            out[g * n_gy + h, rows:, :] = beside


def step_kernel(n_gy, step, last, levels, owners, shares, fields, plume, source,
                west, east, south, north, y_back, *rest):
    gx, gy = lax.axis_index("gx"), lax.axis_index("gy")
    copies = []
    if last:
        fields_out, plume_out, slabs, beside, spread, spread_edges = rest
    else:
        (parent_all, x_fwd_all, y_fwd_all, fields_out, plume_out, modes,
         slabs, beside, spread, spread_edges, sems, parent, x_fwd, y_fwd, turned, work) = rest
        copies = fetch_all(sems, [(x_fwd_all.at[gx], x_fwd), (y_fwd_all.at[gy], y_fwd),
                                  (parent_all.at[0, step + 1], parent)])
    level_total, cells_x, cells_y = plume.shape
    field_rows = fields.shape[0]
    total = field_rows + level_total
    level_count = levels.shape[0]
    nudged = 3 * level_count
    inner = slice(PAD, PAD + cells_x)
    for c in range(total):
        slabs[c, inner] = fields[c] if c < field_rows else plume[c - field_rows]
        slabs[c, PAD - 1 : PAD] = west[c : c + 1, :]
        slabs[c, PAD + cells_x : PAD + cells_x + 1] = east[c : c + 1, :]
    beside[...] = jnp.zeros_like(beside)
    devices = shares.shape[0]
    rows = spread.shape[0] // devices
    packed = beside_rows(rows)
    width = 2 * GROUP
    for d in range(devices):
        spread[d * rows : (d + 1) * rows] = shares[d, :rows, :]
        edge = shares[d, rows:, :]
        for m in range(3):
            count = min(packed, rows - m * packed)
            if count > 0:
                moved = pltpu.roll(edge, -m * width % LANES, 1) if m else edge
                start = d * rows + m * packed
                spread_edges[start : start + count] = moved[:count]
    y_table = y_back[...]
    groups = nudged // GROUP
    spot_of = lax.broadcasted_iota(jnp.int32, (2 * KX, LANES), 1) // width
    edges = jnp.zeros((2 * KX, LANES), jnp.float32)
    for t in range(groups):
        piece = spread_edges[t * 2 * KX : (t + 1) * 2 * KX]
        edges = jnp.where(spot_of == t, pltpu.roll(piece, t * width, 1) if t else piece, edges)
    update_rows = columns_dot(edges, y_table)
    for t in range(groups):
        update = columns_dot(spread[t * 2 * KX : (t + 1) * 2 * KX], y_table)
        for n in range(GROUP):
            c = t * GROUP + n
            part = update[n * cells_x : (n + 1) * cells_x]
            spot = slab_of(levels, c, level_count, level_total)
            slabs[spot, inner] += part[:, :cells_y]
            slabs[spot, PAD - 1 : PAD] += update_rows[2 * c : 2 * c + 1, :cells_y]
            slabs[spot, PAD + cells_x : PAD + cells_x + 1] += update_rows[
                2 * c + 1 : 2 * c + 2, :cells_y]
            beside[spot] = part[:, cells_y:]

    lane = lax.broadcasted_iota(jnp.int32, (cells_x, cells_y), 1)
    first, final = lane == 0, lane == cells_y - 1
    columns = jnp.where(
        lane % 2 == 0, pltpu.roll(north[...], cells_y - 1, 1), pltpu.roll(south[...], 1, 1))

    def advance(c, parts):
        centre, to_west, to_east, to_south, to_north = parts
        a = slabs[c, inner]
        column = pltpu.roll(columns, cells_y - 1 - 2 * c, 1)
        if c < field_rows:
            column = column + beside[c]
        return (
            centre * a
            + to_west * slabs[c, PAD - 1 : PAD - 1 + cells_x]
            + to_east * slabs[c, PAD + 1 : PAD + 1 + cells_x]
            + to_south * jnp.where(first, column, pltpu.roll(a, 1, 1))
            + to_north * jnp.where(final, column, pltpu.roll(a, cells_y - 1, 1))
        )

    for l in range(level_total):
        u, v = slabs[l, inner], slabs[level_total + l, inner]
        beside_parts = (
            0.1 + 0.1 * jnp.maximum(u, 0.0), 0.1 - 0.1 * jnp.minimum(u, 0.0),
            0.1 + 0.1 * jnp.maximum(v, 0.0), 0.1 - 0.1 * jnp.minimum(v, 0.0),
        )
        centre = 1.0 - (beside_parts[0] + beside_parts[1] + beside_parts[2] + beside_parts[3])
        for f in range(3):
            fields_out[f * level_total + l] = advance(
                f * level_total + l, (centre,) + beside_parts)
        settled = advance(field_rows + l, (centre - 0.3,) + beside_parts) + source[l]
        if l + 1 < level_total:
            settled = settled + 0.3 * plume[l + 1]
        plume_out[l] = settled

    if last:
        return
    for copy in copies:
        copy.wait()
    emit_modes(
        lambda c: fields_out[slab_of(levels, c, level_count, level_total)],
        parent, owners[step + 1] == gx * n_gy + gy, x_fwd[...], y_fwd[...], modes, turned, work,
    )


def swap(axis, to_next, to_previous):
    count = lax.axis_size(axis)
    up = [(i, i + 1) for i in range(count - 1)]
    down = [(b, a) for a, b in up]
    return lax.ppermute(to_next, axis, up), lax.ppermute(to_previous, axis, down)


def local(tables, fields, levels, cuts, parent_modes, owners, plume, source):
    n_gx, n_gy = lax.axis_size("gx"), lax.axis_size("gy")
    devices = n_gx * n_gy
    level_total, cells_x, cells_y = plume.shape
    period = n_gx * cells_x * n_gy * cells_y
    nudged = 3 * levels.shape[0]
    field_rows = 3 * level_total
    total = field_rows + level_total
    rows = -(-(nudged // GROUP * 2 * KX) // devices)
    flat = fields.reshape(field_rows, cells_x, cells_y)
    cuts = cuts.reshape(-1)
    f32 = functools.partial(jax.ShapeDtypeStruct, dtype=jnp.float32)
    x_fwd, y_fwd, y_back, x_back, x_beside = (jnp.asarray(t) for t in tables)

    def vmem(*shape):
        return pltpu.VMEM(shape, jnp.float32)

    def table_space(table):
        return pltpu.VMEM(table.shape[1:], table.dtype)

    def limit(mib):
        return pltpu.CompilerParams(vmem_limit_bytes=mib * 1024 * 1024)

    mode_shape = f32((devices, 2 * rows, LANES))
    step_scratch = [vmem(total, cells_x + 2 * PAD, cells_y), vmem(field_rows, cells_x, cells_y),
                    vmem(devices * rows, LANES), vmem(devices * rows, LANES)]
    mode_scratch = [vmem(nudged, 4 * KX * KX), table_space(x_fwd),
                    table_space(y_fwd), vmem(nudged, KX, LANES),
                    vmem(devices * rows, 2 * LANES)]

    modes = pl.pallas_call(
        functools.partial(first_kernel, n_gy, level_total),
        out_shape=mode_shape,
        in_specs=[HBM] * 6,
        out_specs=VMEM,
        scratch_shapes=[pltpu.SMEM(levels.shape, jnp.int32), pltpu.SMEM(owners.shape, jnp.int32),
                        vmem(field_rows, cells_x, cells_y), pltpu.SemaphoreType.DMA((6,))]
        + mode_scratch,
        compiler_params=limit(8),
        name="first_modes",
    )(*map(in_hbm, (levels, owners, flat, parent_modes, x_fwd, y_fwd)))
    for step in range(STEPS):
        last = step == STEPS - 1
        edge_shapes = [f32((total, cells_y)), f32((total, cells_y)), f32((cells_x, 2 * total))]
        edge_operands = [flat, plume]
        if step == 0:
            edge_shapes.append(jax.ShapeDtypeStruct(y_back.shape[1:], y_back.dtype))
            edge_operands.append(in_hbm(y_back))
        edges = pl.pallas_call(
            edge_kernel,
            out_shape=edge_shapes,
            in_specs=[VMEM, VMEM] + [HBM] * (len(edge_operands) - 2),
            out_specs=[VMEM] * len(edge_shapes),
            scratch_shapes=[pltpu.SemaphoreType.DMA((1,))] if step == 0 else [],
            compiler_params=limit(8),
            name="edges",
        )(*edge_operands)
        if step == 0:
            back_table = edges[3]
        to_west, to_east, cols = edges[:3]
        west, east = swap("gx", to_east, to_west)
        parts = lax.all_to_all(modes, AXES, 0, 0, tiled=True)
        parts, west, east = lax.optimization_barrier((parts, west, east))
        share = pl.pallas_call(
            functools.partial(share_kernel, n_gx, n_gy, period),
            out_shape=f32((devices, rows + beside_rows(rows), LANES)),
            in_specs=[SMEM, VMEM, VMEM, VMEM],
            out_specs=VMEM,
            compiler_params=limit(8),
            name="share_sum",
        )(cuts, parts, x_back, x_beside)
        share, cols = lax.optimization_barrier((share, cols))
        south, north = swap("gy", cols, cols)
        shares = lax.all_to_all(share, AXES, 0, 0, tiled=True)
        out_shape = [f32(flat.shape), f32(plume.shape)]
        operands = [levels, owners, shares, flat, plume, source, west, east, south, north,
                    back_table]
        if not last:
            out_shape.append(mode_shape)
            operands += [in_hbm(parent_modes), in_hbm(x_fwd), in_hbm(y_fwd)]
        results = pl.pallas_call(
            functools.partial(step_kernel, n_gy, step, last),
            out_shape=out_shape,
            in_specs=[SMEM, SMEM] + [VMEM] * 9 + [HBM] * (len(operands) - 11),
            out_specs=[VMEM] * len(out_shape),
            scratch_shapes=step_scratch
            + ([] if last else [pltpu.SemaphoreType.DMA((3,))] + mode_scratch),
            compiler_params=limit(20),
            name="final_step" if last else "inner_step",
        )(*operands)
        if last:
            flat, plume = results
        else:
            flat, plume, modes = results
    return flat.reshape(fields.shape), plume


def solution(mesh):
    in_specs = (
        P(None, None, "gx", "gy"),
        P(),
        P(),
        P(("gx", "gy"), None, None, None),
        P(),
        P(None, "gx", "gy"),
        P(None, "gx", "gy"),
    )
    out_specs = (P(None, None, "gx", "gy"), P(None, "gx", "gy"))
    n_gx, n_gy = mesh.shape["gx"], mesh.shape["gy"]

    def whole(fields, levels, cuts, parent_modes, owners, plume, source):
        tables = build_tables(n_gx, n_gy, plume.shape[1] // n_gx, plume.shape[2] // n_gy)
        return jax.shard_map(
            functools.partial(local, tables), mesh=mesh, in_specs=in_specs, out_specs=out_specs,
            check_vma=False,
        )(fields, levels, cuts, parent_modes, owners, plume, source)

    return whole
```

```python
import functools
import math

import jax
import jax.numpy as jnp
import ml_dtypes
import numpy as np
from jax import lax
from jax.experimental import pallas as pl
from jax.experimental.pallas import tpu as pltpu
from jax.sharding import PartitionSpec as P

KX = 32
STEPS = 2
GROUP = 4
LANES = GROUP * KX
PAD = 8
VMEM = pl.BlockSpec(memory_space=pltpu.VMEM)
SMEM = pl.BlockSpec(memory_space=pltpu.SMEM)
HBM = pl.BlockSpec(memory_space=pltpu.HBM)
AXES = ("gx", "gy")


def in_hbm(array):
    return pltpu.with_memory_space_constraint(array, pltpu.HBM)


def wave_table(positions, period):
    wavenum = np.arange(KX)[:, None]
    phase = (wavenum * positions[None, :] % period) * (2.0 * math.pi / period)
    inside = (positions >= 0) & (positions < period)
    return np.concatenate([np.cos(phase), np.sin(phase)], axis=0) * inside[None, :]


def split(a):
    head = a.astype(jnp.bfloat16)
    return head, (a - head.astype(jnp.float32)).astype(jnp.bfloat16)


def split_table(table, axis, order):
    head = table.astype(ml_dtypes.bfloat16)
    rest = (table - head.astype(np.float64)).astype(ml_dtypes.bfloat16)
    return np.concatenate([head if part == "h" else rest for part in order], axis=axis)


def per_slab(table):
    return np.kron(np.eye(GROUP), table)


def build_tables(n_gx, n_gy, cells_x, cells_y):
    period_x, period_y = n_gx * cells_x, n_gy * cells_y
    scaling = 1.0 / math.sqrt(period_x * period_y)
    parity = [np.arange(p, 2 * KX, 2) for p in range(2)]
    x_fwd, y_fwd, y_back, inner, outer = [], [], [], [], []
    for g in range(n_gx):
        first = g * cells_x
        table = wave_table(first + np.arange(cells_x), period_x)
        x_fwd.append(split_table(
            np.concatenate([per_slab(table[rows].T) for rows in parity], axis=1), 0, "hhl"))
        beside = wave_table(np.array([first - 1, first + cells_x]), period_x)
        inner.append(np.concatenate([np.tile(table[rows], (GROUP, 1)) for rows in parity], axis=0))
        outer.append(np.concatenate([per_slab(beside[rows]) for rows in parity], axis=0))
    spare = -(2 * GROUP * n_gx) % LANES
    x_back = np.concatenate(inner, axis=1)
    x_beside = np.concatenate(outer + [np.zeros((2 * LANES, spare))], axis=1)
    for g in range(n_gy):
        first = g * cells_y
        table = wave_table(first + np.arange(cells_y), period_y)
        edge = np.zeros((2 * KX, cells_y))
        edge[:, [0, -1]] = wave_table(np.array([first - 1, first + cells_y]), period_y)
        y_fwd.append(split_table(table * scaling, 1, "hlh"))
        y_back.append(split_table(np.concatenate([table, edge], axis=1), 0, "hhl"))
    return [np.stack(x_fwd), np.stack(y_fwd), np.stack(y_back),
            split_table(x_back, 0, "hl"), split_table(x_beside, 0, "hl")]


def data_dot(a, table):
    head, rest = split(a)
    return jnp.dot(
        jnp.concatenate([head, rest, head], axis=1), table, preferred_element_type=jnp.float32
    )


def two_part_dot(a, table):
    head, rest = split(a)
    depth = a.shape[1]
    heads = jnp.dot(
        jnp.concatenate([head, rest], axis=0), table[:depth], preferred_element_type=jnp.float32)
    rests = jnp.dot(head, table[depth:], preferred_element_type=jnp.float32)
    return heads[: a.shape[0]] + heads[a.shape[0] :] + rests


def columns_dot(a, table):
    head, rest = split(a)
    stacked = jnp.concatenate([head, rest, head], axis=0)
    return lax.dot_general(
        stacked, table, (((0,), (0,)), ((), ())), preferred_element_type=jnp.float32)


def emit_modes(read, parent, is_owner, x_fwd, y_fwd, modes, turned, work):
    devices, rows = modes.shape[0], modes.shape[1] // 2
    slabs = parent.shape[0]
    groups = slabs // GROUP
    head, rest = split(jnp.concatenate([read(c) for c in range(slabs)], axis=0))
    half = lax.dot_general(
        y_fwd, jnp.concatenate([head, head, rest], axis=1), (((1,), (1,)), ((), ())),
        preferred_element_type=jnp.float32)
    half = jnp.concatenate([half[:, t * LANES : (t + 1) * LANES] for t in range(groups)], axis=0)
    count = groups * 2 * KX
    work[0:count] = -data_dot(half, x_fwd)
    if count < devices * rows:
        work[count:] = jnp.zeros((devices * rows - count, 2 * LANES), jnp.float32)

    @pl.when(is_owner)
    def _():
        for i in range(KX):
            turned[:, i, :] = parent[:, i * LANES : (i + 1) * LANES]
        for t in range(groups):
            block = turned[t * GROUP : (t + 1) * GROUP].reshape(LANES, LANES).T
            span = slice(t * 2 * KX, (t + 1) * 2 * KX)
            for p in range(2):
                work[span, p * LANES : (p + 1) * LANES] += block[p * 2 * KX : (p + 1) * 2 * KX]

    for d in range(devices):
        for p in range(2):
            modes[d, p * rows : (p + 1) * rows, :] = work[
                d * rows : (d + 1) * rows, p * LANES : (p + 1) * LANES]


def fetch_all(sems, pairs):
    copies = [pltpu.make_async_copy(a, b, sems.at[i]) for i, (a, b) in enumerate(pairs)]
    for copy in copies:
        copy.start()
    return copies


def slab_of(levels, c, level_count, level_total):
    return (c // level_count) * level_total + levels[c % level_count]


def first_kernel(n_gy, level_total, levels_all, owners_all, fields_all, parent_all, x_fwd_all,
                 y_fwd_all, modes, levels, owners, fields, sems, parent, x_fwd, y_fwd, turned,
                 work):
    gx, gy = lax.axis_index("gx"), lax.axis_index("gy")
    copies = fetch_all(sems, [
        (levels_all, levels), (owners_all, owners), (fields_all, fields),
        (x_fwd_all.at[gx], x_fwd), (y_fwd_all.at[gy], y_fwd), (parent_all.at[0, 0], parent)])
    for copy in copies:
        copy.wait()
    level_count = parent.shape[0] // 3
    emit_modes(
        lambda c: fields[slab_of(levels, c, level_count, level_total)],
        parent, owners[0] == gx * n_gy + gy, x_fwd[...], y_fwd[...], modes, turned, work,
    )


def is_even(axis):
    return lax.rem(lax.axis_index(axis), 2) == 0


def edge_kernel(n_gy, period, fields, plume, *rest):
    if len(rest) > 3:
        cuts, first, second, cols, weights = rest
        weights[...] = share_weights(n_gy, period, cuts, weights.shape)
    else:
        first, second, cols = rest
    even = is_even("gx")
    cells_x, cells_y = plume.shape[1:]
    field_rows = fields.shape[0]
    lane = lax.broadcasted_iota(jnp.int32, cols.shape, 1)
    acc = jnp.zeros(cols.shape, jnp.float32)
    for c in range(field_rows + plume.shape[0]):
        a = fields[c] if c < field_rows else plume[c - field_rows]
        west, east = a[:1], a[cells_x - 1 :]
        first[c : c + 1, :] = jnp.where(even, east, west)
        second[c : c + 1, :] = jnp.where(even, west, east)
        acc = jnp.where(lane // 2 == c, pltpu.roll(a, 2 * c + 1, 1), acc)
    cols[...] = acc


def share_weights(n_gy, period, cuts, shape):
    rows = shape[0] // 2
    me = lax.axis_index("gx") * n_gy + lax.axis_index("gy")
    place = lax.broadcasted_iota(jnp.int32, shape, 0)
    lane = lax.broadcasted_iota(jnp.int32, shape, 1)
    p = (place >= rows).astype(jnp.int32)
    row = me * rows + place - p * rows
    k = 2 * (lane % KX) + p
    j = row % (2 * KX)
    slab = GROUP * (row // (2 * KX)) + lane // KX
    limit = jnp.zeros(shape, jnp.int32)
    for c in range(cuts.shape[0]):
        limit = jnp.where(slab == c, cuts[c], limit)
    keep = ((k % KX) < limit) & ((j % KX) < limit)
    factor = jnp.where(k == 0, 1.0, 2.0) * jnp.where(j == 0, 1.0, 2.0) * (1.0 / math.sqrt(period))
    return jnp.where(keep, factor, 0.0)


def beside_rows(rows):
    return -(-rows // 3)


def share_kernel(n_gx, n_gy, weights, parts, x_back, x_beside, out):
    devices = parts.shape[0]
    rows = parts.shape[1] // 2
    total = parts[0]
    for d in range(1, devices):
        total = total + parts[d]
    mismatch = total * weights[...]
    both = jnp.concatenate([mismatch[:rows], mismatch[rows:]], axis=1)
    spare = -rows % 16
    if spare:
        both = jnp.concatenate([both, jnp.zeros((spare, 2 * LANES), jnp.float32)], axis=0)
    slab_lane = lax.broadcasted_iota(jnp.int32, both.shape, 1) % LANES // KX
    chosen = [jnp.where(slab_lane == n, both, 0.0) for n in range(GROUP)]
    inner = two_part_dot(jnp.concatenate(chosen, axis=0), x_back)
    edge_all = two_part_dot(both, x_beside)
    height = rows + spare
    packed = beside_rows(rows)
    width = 2 * GROUP
    cells_x = LANES // GROUP
    slot = lax.broadcasted_iota(jnp.int32, (height, LANES), 1) // cells_x
    spot = lax.broadcasted_iota(jnp.int32, (packed, LANES), 1) // width
    for g in range(n_gx):
        first = g * cells_x // LANES * LANES
        tile = jnp.zeros((height, LANES), jnp.float32)
        for n in range(GROUP):
            piece = inner[n * height : (n + 1) * height, first : first + LANES]
            tile = jnp.where(slot == n, pltpu.roll(piece, (n - g) * cells_x % LANES, 1), tile)
        first = g * width // LANES * LANES
        beside = jnp.zeros((packed, LANES), jnp.float32)
        for m in range(3):
            piece = edge_all[m * packed : (m + 1) * packed, first : first + LANES]
            beside = jnp.where(
                spot == m, pltpu.roll(piece, (m - g) * width % LANES, 1), beside)
        for h in range(n_gy):
            out[g * n_gy + h, :rows, :] = tile[:rows]
            out[g * n_gy + h, rows:, :] = beside


def step_kernel(n_gy, step, last, shares, fields, plume, source, row_first, row_second,
                col_first, col_second, y_back, levels_all, *rest):
    gx, gy = lax.axis_index("gx"), lax.axis_index("gy")
    extra = []
    if last:
        (fields_out, plume_out, levels, slabs, beside, spread, spread_edges, west, east,
         sems) = rest
    else:
        (owners_all, parent_all, x_fwd_all, y_fwd_all, fields_out, plume_out, modes,
         levels, slabs, beside, spread, spread_edges, west, east, sems,
         owners, parent, x_fwd, y_fwd, turned, work) = rest
        extra = [(owners_all, owners), (x_fwd_all.at[gx], x_fwd), (y_fwd_all.at[gy], y_fwd),
                 (parent_all.at[0, step + 1], parent)]
    copies = fetch_all(sems, [(levels_all, levels)] + extra)
    even = is_even("gx")
    west[...] = jnp.where(even, row_second[...], row_first[...])
    east[...] = jnp.where(even, row_first[...], row_second[...])
    level_total, cells_x, cells_y = plume.shape
    field_rows = fields.shape[0]
    total = field_rows + level_total
    level_count = levels.shape[0]
    nudged = 3 * level_count
    inner = slice(PAD, PAD + cells_x)
    for c in range(total):
        slabs[c, inner] = fields[c] if c < field_rows else plume[c - field_rows]
        slabs[c, PAD - 1 : PAD] = west[c : c + 1, :]
        slabs[c, PAD + cells_x : PAD + cells_x + 1] = east[c : c + 1, :]
    beside[...] = jnp.zeros_like(beside)
    devices = shares.shape[0]
    rows = spread.shape[0] // devices
    packed = beside_rows(rows)
    width = 2 * GROUP
    for d in range(devices):
        spread[d * rows : (d + 1) * rows] = shares[d, :rows, :]
        edge = shares[d, rows:, :]
        for m in range(3):
            count = min(packed, rows - m * packed)
            if count > 0:
                moved = pltpu.roll(edge, -m * width % LANES, 1) if m else edge
                start = d * rows + m * packed
                spread_edges[start : start + count] = moved[:count]
    y_table = y_back[gy]
    groups = nudged // GROUP
    spot_of = lax.broadcasted_iota(jnp.int32, (2 * KX, LANES), 1) // width
    edges = jnp.zeros((2 * KX, LANES), jnp.float32)
    for t in range(groups):
        piece = spread_edges[t * 2 * KX : (t + 1) * 2 * KX]
        edges = jnp.where(spot_of == t, pltpu.roll(piece, t * width, 1) if t else piece, edges)
    update_rows = columns_dot(edges, y_table)
    copies[0].wait()
    for t in range(groups):
        update = columns_dot(spread[t * 2 * KX : (t + 1) * 2 * KX], y_table)
        for n in range(GROUP):
            c = t * GROUP + n
            part = update[n * cells_x : (n + 1) * cells_x]
            spot = slab_of(levels, c, level_count, level_total)
            slabs[spot, inner] += part[:, :cells_y]
            slabs[spot, PAD - 1 : PAD] += update_rows[2 * c : 2 * c + 1, :cells_y]
            slabs[spot, PAD + cells_x : PAD + cells_x + 1] += update_rows[
                2 * c + 1 : 2 * c + 2, :cells_y]
            beside[spot] = part[:, cells_y:]

    lane = lax.broadcasted_iota(jnp.int32, (cells_x, cells_y), 1)
    first, final = lane == 0, lane == cells_y - 1
    even = is_even("gy")
    north = jnp.where(even, col_first[...], col_second[...])
    south = jnp.where(even, col_second[...], col_first[...])
    columns = jnp.where(
        lane % 2 == 0, pltpu.roll(north, cells_y - 1, 1), pltpu.roll(south, 1, 1))

    def advance(c, parts):
        centre, to_west, to_east, to_south, to_north = parts
        a = slabs[c, inner]
        column = pltpu.roll(columns, cells_y - 1 - 2 * c, 1)
        if c < field_rows:
            column = column + beside[c]
        return (
            centre * a
            + to_west * slabs[c, PAD - 1 : PAD - 1 + cells_x]
            + to_east * slabs[c, PAD + 1 : PAD + 1 + cells_x]
            + to_south * jnp.where(first, column, pltpu.roll(a, 1, 1))
            + to_north * jnp.where(final, column, pltpu.roll(a, cells_y - 1, 1))
        )

    for l in range(level_total):
        u, v = slabs[l, inner], slabs[level_total + l, inner]
        beside_parts = (
            0.1 + 0.1 * jnp.maximum(u, 0.0), 0.1 - 0.1 * jnp.minimum(u, 0.0),
            0.1 + 0.1 * jnp.maximum(v, 0.0), 0.1 - 0.1 * jnp.minimum(v, 0.0),
        )
        centre = 1.0 - (beside_parts[0] + beside_parts[1] + beside_parts[2] + beside_parts[3])
        for f in range(3):
            fields_out[f * level_total + l] = advance(
                f * level_total + l, (centre,) + beside_parts)
        settled = advance(field_rows + l, (centre - 0.3,) + beside_parts) + source[l]
        if l + 1 < level_total:
            settled = settled + 0.3 * plume[l + 1]
        plume_out[l] = settled

    if last:
        return
    for copy in copies[1:]:
        copy.wait()
    emit_modes(
        lambda c: fields_out[slab_of(levels, c, level_count, level_total)],
        parent, owners[step + 1] == gx * n_gy + gy, x_fwd[...], y_fwd[...], modes, turned, work,
    )


def exchange(axis, first, second):
    count = lax.axis_size(axis)
    received = []
    for start, data in ((0, first), (1, second)):
        pairs = [(i, i + 1) for i in range(start, count - 1, 2)]
        received.append(lax.ppermute(data, axis, pairs + [(b, a) for a, b in pairs]))
    return received


def local(tables, fields, levels, cuts, parent_modes, owners, plume, source):
    n_gx, n_gy = lax.axis_size("gx"), lax.axis_size("gy")
    devices = n_gx * n_gy
    level_total, cells_x, cells_y = plume.shape
    period = n_gx * cells_x * n_gy * cells_y
    nudged = 3 * levels.shape[0]
    field_rows = 3 * level_total
    total = field_rows + level_total
    rows = -(-(nudged // GROUP * 2 * KX) // devices)
    flat = fields.reshape(field_rows, cells_x, cells_y)
    cuts = cuts.reshape(-1)
    f32 = functools.partial(jax.ShapeDtypeStruct, dtype=jnp.float32)
    x_fwd, y_fwd, y_back, x_back, x_beside = (jnp.asarray(t) for t in tables)

    def vmem(*shape):
        return pltpu.VMEM(shape, jnp.float32)

    def table_space(table):
        return pltpu.VMEM(table.shape[1:], table.dtype)

    def limit(mib):
        return pltpu.CompilerParams(vmem_limit_bytes=mib * 1024 * 1024)

    mode_shape = f32((devices, 2 * rows, LANES))
    step_scratch = [vmem(total, cells_x + 2 * PAD, cells_y), vmem(field_rows, cells_x, cells_y),
                    vmem(devices * rows, LANES), vmem(devices * rows, LANES),
                    vmem(total, cells_y), vmem(total, cells_y), pltpu.SemaphoreType.DMA((5,))]
    levels_space = pltpu.SMEM(levels.shape, jnp.int32)
    owners_space = pltpu.SMEM(owners.shape, jnp.int32)
    levels, owners = in_hbm(levels), in_hbm(owners)
    mode_scratch = [vmem(nudged, 4 * KX * KX), table_space(x_fwd),
                    table_space(y_fwd), vmem(nudged, KX, LANES),
                    vmem(devices * rows, 2 * LANES)]

    modes = pl.pallas_call(
        functools.partial(first_kernel, n_gy, level_total),
        out_shape=mode_shape,
        in_specs=[HBM] * 6,
        out_specs=VMEM,
        scratch_shapes=[levels_space, owners_space, vmem(field_rows, cells_x, cells_y), pltpu.SemaphoreType.DMA((6,))]
        + mode_scratch,
        compiler_params=limit(8),
        name="first_modes",
    )(levels, owners, *map(in_hbm, (flat, parent_modes, x_fwd, y_fwd)))
    for step in range(STEPS):
        last = step == STEPS - 1
        edge_shapes = [f32((total, cells_y)), f32((total, cells_y)), f32((cells_x, 2 * total))]
        edge_operands = [flat, plume]
        if step == 0:
            edge_shapes.append(f32((2 * rows, LANES)))
            edge_operands.append(cuts)
        edges = pl.pallas_call(
            functools.partial(edge_kernel, n_gy, period),
            out_shape=edge_shapes,
            in_specs=[VMEM, VMEM, SMEM][: len(edge_operands)],
            out_specs=[VMEM] * len(edge_shapes),
            compiler_params=limit(8),
            name="edges",
        )(*edge_operands)
        if step == 0:
            weights = edges[3]
        cols = edges[2]
        row_first, row_second = exchange("gx", *edges[:2])
        parts = lax.all_to_all(modes, AXES, 0, 0, tiled=True)
        parts, row_first, row_second = lax.optimization_barrier((parts, row_first, row_second))
        share = pl.pallas_call(
            functools.partial(share_kernel, n_gx, n_gy),
            out_shape=f32((devices, rows + beside_rows(rows), LANES)),
            in_specs=[VMEM] * 4,
            out_specs=VMEM,
            compiler_params=limit(8),
            name="share_sum",
        )(weights, parts, x_back, x_beside)
        share, cols = lax.optimization_barrier((share, cols))
        col_first, col_second = exchange("gy", cols, cols)
        shares = lax.all_to_all(share, AXES, 0, 0, tiled=True)
        out_shape = [f32(flat.shape), f32(plume.shape)]
        operands = [shares, flat, plume, source, row_first, row_second, col_first, col_second,
                    y_back, levels]
        if not last:
            out_shape.append(mode_shape)
            operands += [owners, in_hbm(parent_modes), in_hbm(x_fwd), in_hbm(y_fwd)]
        results = pl.pallas_call(
            functools.partial(step_kernel, n_gy, step, last),
            out_shape=out_shape,
            in_specs=[VMEM] * 9 + [HBM] * (len(operands) - 9),
            out_specs=[VMEM] * len(out_shape),
            scratch_shapes=[levels_space] + step_scratch
            + ([] if last else [owners_space] + mode_scratch),
            compiler_params=limit(20),
            name="final_step" if last else "inner_step",
        )(*operands)
        if last:
            flat, plume = results
        else:
            flat, plume, modes = results
    return flat.reshape(fields.shape), plume


def solution(mesh):
    in_specs = (
        P(None, None, "gx", "gy"),
        P(),
        P(),
        P(("gx", "gy"), None, None, None),
        P(),
        P(None, "gx", "gy"),
        P(None, "gx", "gy"),
    )
    out_specs = (P(None, None, "gx", "gy"), P(None, "gx", "gy"))
    n_gx, n_gy = mesh.shape["gx"], mesh.shape["gy"]

    def whole(fields, levels, cuts, parent_modes, owners, plume, source):
        tables = build_tables(n_gx, n_gy, plume.shape[1] // n_gx, plume.shape[2] // n_gy)
        return jax.shard_map(
            functools.partial(local, tables), mesh=mesh, in_specs=in_specs, out_specs=out_specs,
            check_vma=False,
        )(fields, levels, cuts, parent_modes, owners, plume, source)

    return whole
```

```python
import functools
import math

import jax
import jax.numpy as jnp
import ml_dtypes
import numpy as np
from jax import lax
from jax.experimental import pallas as pl
from jax.experimental.pallas import tpu as pltpu
from jax.sharding import PartitionSpec as P

KX = 32
STEPS = 2
GROUP = 4
PIECES = 4
LANES = GROUP * KX
PAD = 8
VMEM = pl.BlockSpec(memory_space=pltpu.VMEM)
SMEM = pl.BlockSpec(memory_space=pltpu.SMEM)
HBM = pl.BlockSpec(memory_space=pltpu.HBM)
AXES = ("gx", "gy")


def in_hbm(array):
    return pltpu.with_memory_space_constraint(array, pltpu.HBM)


def wave_table(positions, period):
    wavenum = np.arange(KX)[:, None]
    phase = (wavenum * positions[None, :] % period) * (2.0 * math.pi / period)
    inside = (positions >= 0) & (positions < period)
    return np.concatenate([np.cos(phase), np.sin(phase)], axis=0) * inside[None, :]


def split(a):
    head = a.astype(jnp.bfloat16)
    return head, (a - head.astype(jnp.float32)).astype(jnp.bfloat16)


def split_table(table, axis, order):
    head = table.astype(ml_dtypes.bfloat16)
    rest = (table - head.astype(np.float64)).astype(ml_dtypes.bfloat16)
    return np.concatenate([head if part == "h" else rest for part in order], axis=axis)


def per_slab(table):
    return np.kron(np.eye(GROUP), table)


def build_tables(n_gx, n_gy, cells_x, cells_y):
    period_x, period_y = n_gx * cells_x, n_gy * cells_y
    scaling = 1.0 / math.sqrt(period_x * period_y)
    parity = [np.arange(p, 2 * KX, 2) for p in range(2)]
    x_fwd, y_fwd, y_back, inner, outer = [], [], [], [], []
    for g in range(n_gx):
        first = g * cells_x
        table = wave_table(first + np.arange(cells_x), period_x)
        x_fwd.append(split_table(
            np.concatenate([per_slab(table[rows].T) for rows in parity], axis=1), 0, "hhl"))
        beside = wave_table(np.array([first - 1, first + cells_x]), period_x)
        inner.append(np.concatenate([np.tile(table[rows], (GROUP, 1)) for rows in parity], axis=0))
        outer.append(np.concatenate([per_slab(beside[rows]) for rows in parity], axis=0))
    spare = -(2 * GROUP * n_gx) % LANES
    x_back = np.concatenate(inner, axis=1)
    x_beside = np.concatenate(outer + [np.zeros((2 * LANES, spare))], axis=1)
    for g in range(n_gy):
        first = g * cells_y
        table = wave_table(first + np.arange(cells_y), period_y)
        edge = np.zeros((2 * KX, cells_y))
        edge[:, [0, -1]] = wave_table(np.array([first - 1, first + cells_y]), period_y)
        y_fwd.append(split_table(table * scaling, 1, "hlh"))
        y_back.append(split_table(np.concatenate([table, edge], axis=1), 0, "hhl"))
    return [np.stack(x_fwd), np.stack(y_fwd), np.stack(y_back),
            split_table(x_back, 0, "hl"), split_table(x_beside, 0, "hl")]


def data_dot(a, table):
    head, rest = split(a)
    return jnp.dot(
        jnp.concatenate([head, rest, head], axis=1), table, preferred_element_type=jnp.float32
    )


def two_part_dot(a, table):
    head, rest = split(a)
    depth = a.shape[1]
    heads = jnp.dot(
        jnp.concatenate([head, rest], axis=0), table[:depth], preferred_element_type=jnp.float32)
    rests = jnp.dot(head, table[depth:], preferred_element_type=jnp.float32)
    return heads[: a.shape[0]] + heads[a.shape[0] :] + rests


def columns_dot(a, table):
    head, rest = split(a)
    stacked = jnp.concatenate([head, rest, head], axis=0)
    return lax.dot_general(
        stacked, table, (((0,), (0,)), ((), ())), preferred_element_type=jnp.float32)


def emit_modes(chosen, parent, is_owner, x_fwd, y_fwd, modes, turned, work):
    devices, rows = modes.shape[0], modes.shape[1] // 2
    slabs = parent.shape[0]
    groups = slabs // GROUP
    head, rest = split(jnp.concatenate(chosen, axis=0))
    half = lax.dot_general(
        y_fwd, jnp.concatenate([head, head, rest], axis=1), (((1,), (1,)), ((), ())),
        preferred_element_type=jnp.float32)
    half = jnp.concatenate([half[:, t * LANES : (t + 1) * LANES] for t in range(groups)], axis=0)
    count = groups * 2 * KX
    work[0:count] = -data_dot(half, x_fwd)
    if count < devices * rows:
        work[count:] = jnp.zeros((devices * rows - count, 2 * LANES), jnp.float32)

    @pl.when(is_owner)
    def _():
        for i in range(KX):
            turned[:, i, :] = parent[:, i * LANES : (i + 1) * LANES]
        for t in range(groups):
            block = turned[t * GROUP : (t + 1) * GROUP].reshape(LANES, LANES).T
            span = slice(t * 2 * KX, (t + 1) * 2 * KX)
            for p in range(2):
                work[span, p * LANES : (p + 1) * LANES] += block[p * 2 * KX : (p + 1) * 2 * KX]

    for d in range(devices):
        for p in range(2):
            modes[d, p * rows : (p + 1) * rows, :] = work[
                d * rows : (d + 1) * rows, p * LANES : (p + 1) * LANES]


def fetch_all(sems, pairs):
    copies = [pltpu.make_async_copy(a, b, sems.at[i]) for i, (a, b) in enumerate(pairs)]
    for copy in copies:
        copy.start()
    return copies


def slab_of(levels, c, level_count, level_total):
    return (c // level_count) * level_total + levels[c % level_count]


def first_kernel(n_gy, level_total, levels_all, owners_all, fields_all, parent_all, x_fwd_all,
                 y_fwd_all, modes, levels, owners, fields, sems, parent, x_fwd, y_fwd, turned,
                 work):
    gx, gy = lax.axis_index("gx"), lax.axis_index("gy")
    copies = fetch_all(sems, [
        (levels_all, levels), (owners_all, owners), (fields_all, fields),
        (x_fwd_all.at[gx], x_fwd), (y_fwd_all.at[gy], y_fwd), (parent_all.at[0, 0], parent)])
    for copy in copies:
        copy.wait()
    level_count = parent.shape[0] // 3
    emit_modes(
        [fields[slab_of(levels, c, level_count, level_total)] for c in range(parent.shape[0])],
        parent, owners[0] == gx * n_gy + gy, x_fwd[...], y_fwd[...], modes, turned, work,
    )


def is_even(axis):
    return lax.rem(lax.axis_index(axis), 2) == 0


def edge_kernel(n_gy, period, fields, plume, *rest):
    if len(rest) > 3:
        cuts, levels, first, second, cols, weights, order = rest
        weights[...] = share_weights(n_gy, period, cuts, weights.shape)
        count = levels.shape[0]
        for n in range(count):
            order[n] = levels[n]
        spot = jnp.int32(count)
        for l in range(plume.shape[0]):
            found = levels[0] == l
            for n in range(1, count):
                found = found | (levels[n] == l)
            order[spot] = jnp.int32(l)
            spot = spot + jnp.where(found, 0, 1)
        for n in range(order.shape[0] - 1, plume.shape[0] - 1, -1):
            order[n] = jnp.int32(0)
    else:
        first, second, cols = rest
    even = is_even("gx")
    cells_x, cells_y = plume.shape[1:]
    field_rows = fields.shape[0]
    lane = lax.broadcasted_iota(jnp.int32, cols.shape, 1)
    acc = jnp.zeros(cols.shape, jnp.float32)
    for c in range(field_rows + plume.shape[0]):
        a = fields[c] if c < field_rows else plume[c - field_rows]
        west, east = a[:1], a[cells_x - 1 :]
        first[c : c + 1, :] = jnp.where(even, east, west)
        second[c : c + 1, :] = jnp.where(even, west, east)
        acc = jnp.where(lane // 2 == c, pltpu.roll(a, 2 * c + 1, 1), acc)
    cols[...] = acc


def share_weights(n_gy, period, cuts, shape):
    rows = shape[0] // 2
    me = lax.axis_index("gx") * n_gy + lax.axis_index("gy")
    place = lax.broadcasted_iota(jnp.int32, shape, 0)
    lane = lax.broadcasted_iota(jnp.int32, shape, 1)
    p = (place >= rows).astype(jnp.int32)
    row = me * rows + place - p * rows
    k = 2 * (lane % KX) + p
    j = row % (2 * KX)
    slab = GROUP * (row // (2 * KX)) + lane // KX
    limit = jnp.zeros(shape, jnp.int32)
    for c in range(cuts.shape[0]):
        limit = jnp.where(slab == c, cuts[c], limit)
    keep = ((k % KX) < limit) & ((j % KX) < limit)
    factor = jnp.where(k == 0, 1.0, 2.0) * jnp.where(j == 0, 1.0, 2.0) * (1.0 / math.sqrt(period))
    return jnp.where(keep, factor, 0.0)


def beside_rows(rows):
    return -(-rows // 3)


def share_kernel(n_gx, n_gy, weights, parts, x_back, x_beside, out):
    devices = parts.shape[0]
    rows = parts.shape[1] // 2
    total = parts[0]
    for d in range(1, devices):
        total = total + parts[d]
    mismatch = total * weights[...]
    both = jnp.concatenate([mismatch[:rows], mismatch[rows:]], axis=1)
    spare = -rows % 16
    if spare:
        both = jnp.concatenate([both, jnp.zeros((spare, 2 * LANES), jnp.float32)], axis=0)
    slab_lane = lax.broadcasted_iota(jnp.int32, both.shape, 1) % LANES // KX
    chosen = [jnp.where(slab_lane == n, both, 0.0) for n in range(GROUP)]
    inner = two_part_dot(jnp.concatenate(chosen, axis=0), x_back)
    edge_all = two_part_dot(both, x_beside)
    height = rows + spare
    packed = beside_rows(rows)
    width = 2 * GROUP
    cells_x = LANES // GROUP
    slot = lax.broadcasted_iota(jnp.int32, (height, LANES), 1) // cells_x
    spot = lax.broadcasted_iota(jnp.int32, (packed, LANES), 1) // width
    for g in range(n_gx):
        first = g * cells_x // LANES * LANES
        tile = jnp.zeros((height, LANES), jnp.float32)
        for n in range(GROUP):
            piece = inner[n * height : (n + 1) * height, first : first + LANES]
            tile = jnp.where(slot == n, pltpu.roll(piece, (n - g) * cells_x % LANES, 1), tile)
        first = g * width // LANES * LANES
        beside = jnp.zeros((packed, LANES), jnp.float32)
        for m in range(3):
            piece = edge_all[m * packed : (m + 1) * packed, first : first + LANES]
            beside = jnp.where(
                spot == m, pltpu.roll(piece, (m - g) * width % LANES, 1), beside)
        for h in range(n_gy):
            out[g * n_gy + h, :rows, :] = tile[:rows]
            out[g * n_gy + h, rows:, :] = beside


def step_kernel(n_gy, step, last, level_count, shares, fields, plume, source, row_first, row_second,
                col_first, col_second, y_back, order_all, *rest):
    gx, gy = lax.axis_index("gx"), lax.axis_index("gy")
    extra = []
    if last:
        (fields_all, plume_all, order, slabs, beside, spread, spread_edges, west, east, sems,
         fields_out, plume_out, out_sems) = rest
    else:
        (owners_all, parent_all, x_fwd_all, y_fwd_all, fields_out, plume_out, modes_all,
         order, slabs, beside, spread, spread_edges, west, east, sems,
         owners, modes, out_sems, parent, x_fwd, y_fwd, turned, work) = rest
        extra = [(owners_all, owners), (x_fwd_all.at[gx], x_fwd), (y_fwd_all.at[gy], y_fwd),
                 (parent_all.at[0, step + 1], parent)]
    copies = fetch_all(sems, [(order_all, order)] + extra)
    even = is_even("gx")
    west[...] = jnp.where(even, row_second[...], row_first[...])
    east[...] = jnp.where(even, row_first[...], row_second[...])
    level_total, cells_x, cells_y = plume.shape
    field_rows = fields.shape[0]
    total = field_rows + level_total
    nudged = 3 * level_count
    inner = slice(PAD, PAD + cells_x)
    for c in range(total):
        slabs[c, inner] = fields[c] if c < field_rows else plume[c - field_rows]
        slabs[c, PAD - 1 : PAD] = west[c : c + 1, :]
        slabs[c, PAD + cells_x : PAD + cells_x + 1] = east[c : c + 1, :]
    beside[...] = jnp.zeros_like(beside)
    devices = shares.shape[0]
    rows = spread.shape[0] // devices
    packed = beside_rows(rows)
    width = 2 * GROUP
    for d in range(devices):
        spread[d * rows : (d + 1) * rows] = shares[d, :rows, :]
        edge = shares[d, rows:, :]
        for m in range(3):
            count = min(packed, rows - m * packed)
            if count > 0:
                moved = pltpu.roll(edge, -m * width % LANES, 1) if m else edge
                start = d * rows + m * packed
                spread_edges[start : start + count] = moved[:count]
    y_table = y_back[gy]
    groups = nudged // GROUP
    spot_of = lax.broadcasted_iota(jnp.int32, (2 * KX, LANES), 1) // width
    edges = jnp.zeros((2 * KX, LANES), jnp.float32)
    for t in range(groups):
        piece = spread_edges[t * 2 * KX : (t + 1) * 2 * KX]
        edges = jnp.where(spot_of == t, pltpu.roll(piece, t * width, 1) if t else piece, edges)
    update_rows = columns_dot(edges, y_table)
    copies[0].wait()
    for t in range(groups):
        update = columns_dot(spread[t * 2 * KX : (t + 1) * 2 * KX], y_table)
        for n in range(GROUP):
            c = t * GROUP + n
            part = update[n * cells_x : (n + 1) * cells_x]
            spot = slab_of(order, c, level_count, level_total)
            slabs[spot, inner] += part[:, :cells_y]
            slabs[spot, PAD - 1 : PAD] += update_rows[2 * c : 2 * c + 1, :cells_y]
            slabs[spot, PAD + cells_x : PAD + cells_x + 1] += update_rows[
                2 * c + 1 : 2 * c + 2, :cells_y]
            beside[spot] = part[:, cells_y:]

    lane = lax.broadcasted_iota(jnp.int32, (cells_x, cells_y), 1)
    first, final = lane == 0, lane == cells_y - 1
    even = is_even("gy")
    north = jnp.where(even, col_first[...], col_second[...])
    south = jnp.where(even, col_second[...], col_first[...])
    columns = jnp.where(
        lane % 2 == 0, pltpu.roll(north, cells_y - 1, 1), pltpu.roll(south, 1, 1))

    def advance(c, parts, is_field=True):
        centre, to_west, to_east, to_south, to_north = parts
        a = slabs[c, inner]
        column = pltpu.roll(columns, cells_y - 1 - 2 * c, 1)
        if is_field:
            column = column + beside[c]
        return (
            centre * a
            + to_west * slabs[c, PAD - 1 : PAD - 1 + cells_x]
            + to_east * slabs[c, PAD + 1 : PAD + 1 + cells_x]
            + to_south * jnp.where(first, column, pltpu.roll(a, 1, 1))
            + to_north * jnp.where(final, column, pltpu.roll(a, cells_y - 1, 1))
        )

    def weights_at(l):
        u, v = slabs[l, inner], slabs[level_total + l, inner]
        neighbours = (
            0.1 + 0.1 * jnp.maximum(u, 0.0), 0.1 - 0.1 * jnp.minimum(u, 0.0),
            0.1 + 0.1 * jnp.maximum(v, 0.0), 0.1 - 0.1 * jnp.minimum(v, 0.0),
        )
        centre = 1.0 - (neighbours[0] + neighbours[1] + neighbours[2] + neighbours[3])
        return centre, neighbours

    def advance_fields(l, parts):
        results = []
        for f in range(3):
            c = f * level_total + l
            results.append(advance(c, (parts[0],) + parts[1]))
            fields_out[c] = results[f]
        return results

    def advance_ash(l, parts):
        settled = advance(field_rows + l, (parts[0] - 0.3,) + parts[1], False) + source[l]
        if l + 1 < level_total:
            settled = settled + 0.3 * plume[l + 1]
        plume_out[l] = settled

    if last:
        pieces = out_sems.shape[0] // 4
        per_piece = level_total // pieces
        for l in range(level_total):
            parts = weights_at(l)
            advance_fields(l, parts)
            advance_ash(l, parts)
            if (l + 1) % per_piece == 0:
                start = l + 1 - per_piece
                pairs = []
                for f in range(3):
                    span = pl.ds(f * level_total + start, per_piece)
                    pairs.append((fields_out.at[span], fields_all.at[span]))
                span = pl.ds(start, per_piece)
                pairs.append((plume_out.at[span], plume_all.at[span]))
                copies += fetch_all(out_sems.at[pl.ds(start // per_piece * 4, 4)], pairs)
        for copy in copies[1:]:
            copy.wait()
        return
    results = [advance_fields(l, weights_at(l)) for l in (order[n] for n in range(level_count))]
    for copy in copies[1:]:
        copy.wait()
    emit_modes(
        [results[n][f] for f in range(3) for n in range(level_count)],
        parent, owners[step + 1] == gx * n_gy + gy, x_fwd[...], y_fwd[...], modes, turned, work,
    )
    sent = fetch_all(out_sems, [(modes, modes_all)])
    for n in range(level_count, level_total):
        l = order[n]
        advance_fields(l, weights_at(l))
    for l in range(level_total):
        advance_ash(l, weights_at(l))
    sent[0].wait()


def exchange(axis, first, second):
    count = lax.axis_size(axis)
    received = []
    for start, data in ((0, first), (1, second)):
        pairs = [(i, i + 1) for i in range(start, count - 1, 2)]
        received.append(lax.ppermute(data, axis, pairs + [(b, a) for a, b in pairs]))
    return received


def local(tables, fields, levels, cuts, parent_modes, owners, plume, source):
    n_gx, n_gy = lax.axis_size("gx"), lax.axis_size("gy")
    devices = n_gx * n_gy
    level_total, cells_x, cells_y = plume.shape
    period = n_gx * cells_x * n_gy * cells_y
    nudged = 3 * levels.shape[0]
    field_rows = 3 * level_total
    total = field_rows + level_total
    rows = -(-(nudged // GROUP * 2 * KX) // devices)
    flat = fields.reshape(field_rows, cells_x, cells_y)
    cuts = cuts.reshape(-1)
    f32 = functools.partial(jax.ShapeDtypeStruct, dtype=jnp.float32)
    x_fwd, y_fwd, y_back, x_back, x_beside = (jnp.asarray(t) for t in tables)

    def vmem(*shape):
        return pltpu.VMEM(shape, jnp.float32)

    def table_space(table):
        return pltpu.VMEM(table.shape[1:], table.dtype)

    def limit(mib):
        return pltpu.CompilerParams(vmem_limit_bytes=mib * 1024 * 1024)

    mode_shape = f32((devices, 2 * rows, LANES))
    step_scratch = [vmem(total, cells_x + 2 * PAD, cells_y), vmem(field_rows, cells_x, cells_y),
                    vmem(devices * rows, LANES), vmem(devices * rows, LANES),
                    vmem(total, cells_y), vmem(total, cells_y), pltpu.SemaphoreType.DMA((5,))]
    levels_space = pltpu.SMEM(levels.shape, jnp.int32)
    owners_space = pltpu.SMEM(owners.shape, jnp.int32)
    order_space = pltpu.SMEM((2 * level_total,), jnp.int32)
    raw_levels = levels
    levels, owners = in_hbm(levels), in_hbm(owners)
    mode_scratch = [vmem(nudged, 4 * KX * KX), table_space(x_fwd),
                    table_space(y_fwd), vmem(nudged, KX, LANES),
                    vmem(devices * rows, 2 * LANES)]
    inner_scratch = [owners_space, vmem(*mode_shape.shape), pltpu.SemaphoreType.DMA((1,))]
    inner_scratch += mode_scratch
    last_scratch = [vmem(field_rows, cells_x, cells_y), vmem(level_total, cells_x, cells_y),
                    pltpu.SemaphoreType.DMA((4 * PIECES,))]

    modes = pl.pallas_call(
        functools.partial(first_kernel, n_gy, level_total),
        out_shape=mode_shape,
        in_specs=[HBM] * 6,
        out_specs=VMEM,
        scratch_shapes=[levels_space, owners_space, vmem(field_rows, cells_x, cells_y),
                        pltpu.SemaphoreType.DMA((6,))] + mode_scratch,
        compiler_params=limit(8),
        name="first_modes",
    )(levels, owners, *map(in_hbm, (flat, parent_modes, x_fwd, y_fwd)))
    for step in range(STEPS):
        last = step == STEPS - 1
        edge_shapes = [f32((total, cells_y)), f32((total, cells_y)), f32((cells_x, 2 * total))]
        edge_operands = [flat, plume]
        if step == 0:
            edge_shapes += [f32((2 * rows, LANES)),
                            jax.ShapeDtypeStruct((2 * level_total,), jnp.int32)]
            edge_operands += [cuts, raw_levels]
        edges = pl.pallas_call(
            functools.partial(edge_kernel, n_gy, period),
            out_shape=edge_shapes,
            in_specs=[VMEM, VMEM, SMEM, SMEM][: len(edge_operands)],
            out_specs=[VMEM, VMEM, VMEM, VMEM, SMEM][: len(edge_shapes)],
            compiler_params=limit(8),
            name="edges",
        )(*edge_operands)
        if step == 0:
            weights, order = edges[3], in_hbm(edges[4])
        to_first, to_second, cols = edges[:3]
        col_first, col_second = exchange("gy", cols, cols)
        parts = lax.all_to_all(modes, AXES, 0, 0, tiled=True)
        parts, col_first, col_second = lax.optimization_barrier((parts, col_first, col_second))
        share = pl.pallas_call(
            functools.partial(share_kernel, n_gx, n_gy),
            out_shape=f32((devices, rows + beside_rows(rows), LANES)),
            in_specs=[VMEM] * 4,
            out_specs=VMEM,
            compiler_params=limit(8),
            name="share_sum",
        )(weights, parts, x_back, x_beside)
        share, to_first, to_second = lax.optimization_barrier((share, to_first, to_second))
        row_first, row_second = exchange("gx", to_first, to_second)
        shares = lax.all_to_all(share, AXES, 0, 0, tiled=True)
        out_shape = [f32(flat.shape), f32(plume.shape)]
        out_specs = [HBM if last else VMEM] * 2
        operands = [shares, flat, plume, source, row_first, row_second, col_first, col_second,
                    y_back, order]
        if not last:
            out_shape.append(pltpu.HBM(mode_shape.shape, jnp.float32))
            out_specs.append(HBM)
            operands += [owners, in_hbm(parent_modes), in_hbm(x_fwd), in_hbm(y_fwd)]
        results = pl.pallas_call(
            functools.partial(step_kernel, n_gy, step, last, levels.shape[0]),
            out_shape=out_shape,
            in_specs=[VMEM] * 9 + [HBM] * (len(operands) - 9),
            out_specs=out_specs,
            scratch_shapes=[order_space] + step_scratch + (last_scratch if last else inner_scratch),
            compiler_params=limit(20),
            name="final_step" if last else "inner_step",
        )(*operands)
        if last:
            flat, plume = results
        else:
            flat, plume, modes = results
    return flat.reshape(fields.shape), plume


def solution(mesh):
    in_specs = (
        P(None, None, "gx", "gy"),
        P(),
        P(),
        P(("gx", "gy"), None, None, None),
        P(),
        P(None, "gx", "gy"),
        P(None, "gx", "gy"),
    )
    out_specs = (P(None, None, "gx", "gy"), P(None, "gx", "gy"))
    n_gx, n_gy = mesh.shape["gx"], mesh.shape["gy"]

    def whole(fields, levels, cuts, parent_modes, owners, plume, source):
        tables = build_tables(n_gx, n_gy, plume.shape[1] // n_gx, plume.shape[2] // n_gy)
        return jax.shard_map(
            functools.partial(local, tables), mesh=mesh, in_specs=in_specs, out_specs=out_specs,
            check_vma=False,
        )(fields, levels, cuts, parent_modes, owners, plume, source)

    return whole
```

```python
import functools
import math

import jax
import jax.numpy as jnp
import ml_dtypes
import numpy as np
from jax import lax
from jax.experimental import pallas as pl
from jax.experimental.pallas import tpu as pltpu
from jax.sharding import PartitionSpec as P

KX = 32
STEPS = 2
GROUP = 4
LANES = GROUP * KX
PAD = 8
VMEM = pl.BlockSpec(memory_space=pltpu.VMEM)
SMEM = pl.BlockSpec(memory_space=pltpu.SMEM)
HBM = pl.BlockSpec(memory_space=pltpu.HBM)
AXES = ("gx", "gy")


def in_hbm(array):
    return pltpu.with_memory_space_constraint(array, pltpu.HBM)


def wave_table(positions, period):
    wavenum = np.arange(KX)[:, None]
    phase = (wavenum * positions[None, :] % period) * (2.0 * math.pi / period)
    inside = (positions >= 0) & (positions < period)
    return np.concatenate([np.cos(phase), np.sin(phase)], axis=0) * inside[None, :]


def split(a):
    head = a.astype(jnp.bfloat16)
    return head, (a - head.astype(jnp.float32)).astype(jnp.bfloat16)


def split_table(table, axis, order):
    head = table.astype(ml_dtypes.bfloat16)
    rest = (table - head.astype(np.float64)).astype(ml_dtypes.bfloat16)
    return np.concatenate([head if part == "h" else rest for part in order], axis=axis)


def per_slab(table):
    return np.kron(np.eye(GROUP), table)


def build_tables(n_gx, n_gy, cells_x, cells_y):
    period_x, period_y = n_gx * cells_x, n_gy * cells_y
    scaling = 1.0 / math.sqrt(period_x * period_y)
    parity = [np.arange(p, 2 * KX, 2) for p in range(2)]
    x_fwd, y_fwd, y_back, inner, outer = [], [], [], [], []
    for g in range(n_gx):
        first = g * cells_x
        table = wave_table(first + np.arange(cells_x), period_x)
        x_fwd.append(split_table(
            np.concatenate([per_slab(table[rows].T) for rows in parity], axis=1), 0, "hhl"))
        beside = wave_table(np.array([first - 1, first + cells_x]), period_x)
        inner.append(np.concatenate([np.tile(table[rows], (GROUP, 1)) for rows in parity], axis=0))
        outer.append(np.concatenate([per_slab(beside[rows]) for rows in parity], axis=0))
    spare = -(2 * GROUP * n_gx) % LANES
    x_back = np.concatenate(inner, axis=1)
    x_beside = np.concatenate(outer + [np.zeros((2 * LANES, spare))], axis=1)
    for g in range(n_gy):
        first = g * cells_y
        table = wave_table(first + np.arange(cells_y), period_y)
        edge = np.zeros((2 * KX, cells_y))
        edge[:, [0, -1]] = wave_table(np.array([first - 1, first + cells_y]), period_y)
        y_fwd.append(split_table(table * scaling, 1, "hlh"))
        y_back.append(split_table(np.concatenate([table, edge], axis=1), 0, "hhl"))
    return [np.stack(x_fwd), np.stack(y_fwd), np.stack(y_back),
            split_table(x_back, 0, "hl"), split_table(x_beside, 0, "hl")]


def data_dot(a, table):
    head, rest = split(a)
    return jnp.dot(
        jnp.concatenate([head, rest, head], axis=1), table, preferred_element_type=jnp.float32
    )


def two_part_dot(a, table):
    head, rest = split(a)
    depth = a.shape[1]
    heads = jnp.dot(
        jnp.concatenate([head, rest], axis=0), table[:depth], preferred_element_type=jnp.float32)
    rests = jnp.dot(head, table[depth:], preferred_element_type=jnp.float32)
    return heads[: a.shape[0]] + heads[a.shape[0] :] + rests


def columns_dot(a, table):
    head, rest = split(a)
    stacked = jnp.concatenate([head, rest, head], axis=0)
    return lax.dot_general(
        stacked, table, (((0,), (0,)), ((), ())), preferred_element_type=jnp.float32)


def emit_modes(chosen, parent, is_owner, x_fwd, y_fwd, modes, turned, work):
    devices, rows = modes.shape[0], modes.shape[1] // 2
    slabs = parent.shape[0]
    groups = slabs // GROUP
    head, rest = split(jnp.concatenate(chosen, axis=0))
    half = lax.dot_general(
        y_fwd, jnp.concatenate([head, head, rest], axis=1), (((1,), (1,)), ((), ())),
        preferred_element_type=jnp.float32)
    half = jnp.concatenate([half[:, t * LANES : (t + 1) * LANES] for t in range(groups)], axis=0)
    count = groups * 2 * KX
    work[0:count] = -data_dot(half, x_fwd)
    if count < devices * rows:
        work[count:] = jnp.zeros((devices * rows - count, 2 * LANES), jnp.float32)

    @pl.when(is_owner)
    def _():
        for i in range(KX):
            turned[:, i, :] = parent[:, i * LANES : (i + 1) * LANES]
        for t in range(groups):
            block = turned[t * GROUP : (t + 1) * GROUP].reshape(LANES, LANES).T
            span = slice(t * 2 * KX, (t + 1) * 2 * KX)
            for p in range(2):
                work[span, p * LANES : (p + 1) * LANES] += block[p * 2 * KX : (p + 1) * 2 * KX]

    for d in range(devices):
        for p in range(2):
            modes[d, p * rows : (p + 1) * rows, :] = work[
                d * rows : (d + 1) * rows, p * LANES : (p + 1) * LANES]


def fetch_all(sems, pairs):
    copies = [pltpu.make_async_copy(a, b, sems.at[i]) for i, (a, b) in enumerate(pairs)]
    for copy in copies:
        copy.start()
    return copies


def slab_of(levels, c, level_count, level_total):
    return (c // level_count) * level_total + levels[c % level_count]


def first_kernel(n_gy, level_total, levels_all, owners_all, fields_all, parent_all, x_fwd_all,
                 y_fwd_all, modes, levels, owners, fields, sems, parent, x_fwd, y_fwd, turned,
                 work):
    gx, gy = lax.axis_index("gx"), lax.axis_index("gy")
    copies = fetch_all(sems, [
        (levels_all, levels), (owners_all, owners), (fields_all, fields),
        (x_fwd_all.at[gx], x_fwd), (y_fwd_all.at[gy], y_fwd), (parent_all.at[0, 0], parent)])
    for copy in copies:
        copy.wait()
    level_count = parent.shape[0] // 3
    emit_modes(
        [fields[slab_of(levels, c, level_count, level_total)] for c in range(parent.shape[0])],
        parent, owners[0] == gx * n_gy + gy, x_fwd[...], y_fwd[...], modes, turned, work,
    )


def is_even(axis):
    return lax.rem(lax.axis_index(axis), 2) == 0


def edge_kernel(n_gy, period, fields, plume, *rest):
    level_total, cells_x, cells_y = plume.shape
    if len(rest) > 3:
        cuts, levels, first, second, cols, weights, order = rest
        weights[...] = share_weights(n_gy, period, cuts, weights.shape)
        count = levels.shape[0]
        for n in range(count):
            order[n] = levels[n]
        spot = jnp.int32(count)
        for l in range(level_total):
            found = levels[0] == l
            for n in range(1, count):
                found = found | (levels[n] == l)
            order[spot] = jnp.int32(l)
            spot = spot + jnp.where(found, 0, 1)
        chosen = [order[n] for n in range(level_total)]
        for n in range(level_total, order.shape[0]):
            order[n] = jnp.int32(0)
        for n in range(level_total):
            order[level_total + chosen[n]] = jnp.int32(n)
    else:
        first, second, cols = rest
        chosen = list(range(level_total))
    even = is_even("gx")
    lane = lax.broadcasted_iota(jnp.int32, cols.shape, 1)
    acc = jnp.zeros(cols.shape, jnp.float32)
    for c in range(4 * level_total):
        l = chosen[c % level_total]
        a = plume[l] if c >= 3 * level_total else fields[c // level_total * level_total + l]
        west, east = a[:1], a[cells_x - 1 :]
        first[c : c + 1, :] = jnp.where(even, east, west)
        second[c : c + 1, :] = jnp.where(even, west, east)
        acc = jnp.where(lane // 2 == c, pltpu.roll(a, 2 * c + 1, 1), acc)
    cols[...] = acc


def share_weights(n_gy, period, cuts, shape):
    rows = shape[0] // 2
    me = lax.axis_index("gx") * n_gy + lax.axis_index("gy")
    place = lax.broadcasted_iota(jnp.int32, shape, 0)
    lane = lax.broadcasted_iota(jnp.int32, shape, 1)
    p = (place >= rows).astype(jnp.int32)
    row = me * rows + place - p * rows
    k = 2 * (lane % KX) + p
    j = row % (2 * KX)
    slab = GROUP * (row // (2 * KX)) + lane // KX
    limit = jnp.zeros(shape, jnp.int32)
    for c in range(cuts.shape[0]):
        limit = jnp.where(slab == c, cuts[c], limit)
    keep = ((k % KX) < limit) & ((j % KX) < limit)
    factor = jnp.where(k == 0, 1.0, 2.0) * jnp.where(j == 0, 1.0, 2.0) * (1.0 / math.sqrt(period))
    return jnp.where(keep, factor, 0.0)


def beside_rows(rows):
    return -(-rows // 3)


def share_kernel(n_gx, n_gy, weights, parts, x_back, x_beside, out):
    devices = parts.shape[0]
    rows = parts.shape[1] // 2
    total = parts[0]
    for d in range(1, devices):
        total = total + parts[d]
    mismatch = total * weights[...]
    both = jnp.concatenate([mismatch[:rows], mismatch[rows:]], axis=1)
    spare = -rows % 16
    if spare:
        both = jnp.concatenate([both, jnp.zeros((spare, 2 * LANES), jnp.float32)], axis=0)
    slab_lane = lax.broadcasted_iota(jnp.int32, both.shape, 1) % LANES // KX
    chosen = [jnp.where(slab_lane == n, both, 0.0) for n in range(GROUP)]
    inner = two_part_dot(jnp.concatenate(chosen, axis=0), x_back)
    edge_all = two_part_dot(both, x_beside)
    height = rows + spare
    packed = beside_rows(rows)
    width = 2 * GROUP
    cells_x = LANES // GROUP
    slot = lax.broadcasted_iota(jnp.int32, (height, LANES), 1) // cells_x
    spot = lax.broadcasted_iota(jnp.int32, (packed, LANES), 1) // width
    for g in range(n_gx):
        first = g * cells_x // LANES * LANES
        tile = jnp.zeros((height, LANES), jnp.float32)
        for n in range(GROUP):
            piece = inner[n * height : (n + 1) * height, first : first + LANES]
            tile = jnp.where(slot == n, pltpu.roll(piece, (n - g) * cells_x % LANES, 1), tile)
        first = g * width // LANES * LANES
        beside = jnp.zeros((packed, LANES), jnp.float32)
        for m in range(3):
            piece = edge_all[m * packed : (m + 1) * packed, first : first + LANES]
            beside = jnp.where(
                spot == m, pltpu.roll(piece, (m - g) * width % LANES, 1), beside)
        for h in range(n_gy):
            out[g * n_gy + h, :rows, :] = tile[:rows]
            out[g * n_gy + h, rows:, :] = beside


def step_kernel(n_gy, step, last, level_count, shares, fields, plume, source, row_first, row_second,
                col_first, col_second, y_back, order_all, *rest):
    gx, gy = lax.axis_index("gx"), lax.axis_index("gy")
    extra = []
    if last:
        (fields_all, plume_all, order, slabs, spread, spread_edges, west, east, sems,
         fields_out, plume_out, out_sems) = rest
    else:
        (owners_all, parent_all, x_fwd_all, y_fwd_all, fields_out, plume_out, modes_all,
         order, slabs, spread, spread_edges, west, east, sems,
         owners, modes, out_sems, parent, x_fwd, y_fwd, turned, work) = rest
        extra = [(owners_all, owners), (x_fwd_all.at[gx], x_fwd), (y_fwd_all.at[gy], y_fwd),
                 (parent_all.at[0, step + 1], parent)]
    copies = fetch_all(sems, [(order_all, order)] + extra)
    even = is_even("gx")
    west[...] = jnp.where(even, row_second[...], row_first[...])
    east[...] = jnp.where(even, row_first[...], row_second[...])
    level_total, cells_x, cells_y = plume.shape
    field_rows = fields.shape[0]
    nudged = 3 * level_count
    devices = shares.shape[0]
    rows = spread.shape[0] // devices
    packed = beside_rows(rows)
    width = 2 * GROUP
    for d in range(devices):
        spread[d * rows : (d + 1) * rows] = shares[d, :rows, :]
        edge = shares[d, rows:, :]
        for m in range(3):
            count = min(packed, rows - m * packed)
            if count > 0:
                moved = pltpu.roll(edge, -m * width % LANES, 1) if m else edge
                start = d * rows + m * packed
                spread_edges[start : start + count] = moved[:count]
    y_table = y_back[gy]
    groups = nudged // GROUP
    spot_of = lax.broadcasted_iota(jnp.int32, (2 * KX, LANES), 1) // width
    edges = jnp.zeros((2 * KX, LANES), jnp.float32)
    for t in range(groups):
        piece = spread_edges[t * 2 * KX : (t + 1) * 2 * KX]
        edges = jnp.where(spot_of == t, pltpu.roll(piece, t * width, 1) if t else piece, edges)
    update_rows = columns_dot(edges, y_table)
    updates = []
    for t in range(groups):
        update = columns_dot(spread[t * 2 * KX : (t + 1) * 2 * KX], y_table)
        updates += [update[n * cells_x : (n + 1) * cells_x] for n in range(GROUP)]
    copies[0].wait()
    level_at = [order[n] for n in range(level_total)]
    source_at = [source[l] for l in level_at]
    if step == 0:
        field_at = [fields[f * level_total + l] for f in range(3) for l in level_at]
        ash_at = [plume[l] for l in level_at]
        above_at = [plume[jnp.minimum(l + 1, level_total - 1)] for l in level_at]
    else:
        field_at = [fields[c] for c in range(field_rows)]
        ash_at = [plume[n] for n in range(level_total)]
        above_at = [plume[order[level_total + l + 1]] for l in level_at]
    falling = [jnp.where(l + 1 < level_total, 0.3, 0.0).astype(jnp.float32) for l in level_at]
    inner = slice(PAD, PAD + cells_x)
    beside = {}
    for c, a in enumerate(field_at + ash_at):
        n = c % level_total
        before, after = west[c : c + 1, :], east[c : c + 1, :]
        if c < field_rows and n < level_count:
            k = c // level_total * level_count + n
            a = a + updates[k][:, :cells_y]
            before = before + update_rows[2 * k : 2 * k + 1, :cells_y]
            after = after + update_rows[2 * k + 1 : 2 * k + 2, :cells_y]
            beside[c] = updates[k][:, cells_y:]
        slabs[c, inner] = a
        slabs[c, PAD - 1 : PAD] = before
        slabs[c, PAD + cells_x : PAD + cells_x + 1] = after

    lane = lax.broadcasted_iota(jnp.int32, (cells_x, cells_y), 1)
    first, final = lane == 0, lane == cells_y - 1
    even = is_even("gy")
    north = jnp.where(even, col_first[...], col_second[...])
    south = jnp.where(even, col_second[...], col_first[...])
    columns = jnp.where(
        lane % 2 == 0, pltpu.roll(north, cells_y - 1, 1), pltpu.roll(south, 1, 1))

    def advance(c, parts):
        centre, to_west, to_east, to_south, to_north = parts
        a = slabs[c, inner]
        column = pltpu.roll(columns, cells_y - 1 - 2 * c, 1)
        if c in beside:
            column = column + beside[c]
        return (
            centre * a
            + to_west * slabs[c, PAD - 1 : PAD - 1 + cells_x]
            + to_east * slabs[c, PAD + 1 : PAD + 1 + cells_x]
            + to_south * jnp.where(first, column, pltpu.roll(a, 1, 1))
            + to_north * jnp.where(final, column, pltpu.roll(a, cells_y - 1, 1))
        )

    def weights_at(n):
        u, v = slabs[n, inner], slabs[level_total + n, inner]
        neighbours = (
            0.1 + 0.1 * jnp.maximum(u, 0.0), 0.1 - 0.1 * jnp.minimum(u, 0.0),
            0.1 + 0.1 * jnp.maximum(v, 0.0), 0.1 - 0.1 * jnp.minimum(v, 0.0),
        )
        centre = 1.0 - (neighbours[0] + neighbours[1] + neighbours[2] + neighbours[3])
        return centre, neighbours

    def advance_fields(n, parts):
        results = []
        for f in range(3):
            c = f * level_total + n
            results.append(advance(c, (parts[0],) + parts[1]))
            fields_out[c] = results[f]
        return results

    def advance_ash(n, parts):
        settled = advance(field_rows + n, (parts[0] - 0.3,) + parts[1])
        plume_out[n] = settled + falling[n] * above_at[n] + source_at[n]

    if last:
        sent = []
        for n in range(level_total):
            parts = weights_at(n)
            advance_fields(n, parts)
            advance_ash(n, parts)
            pairs = [(fields_out.at[f * level_total + n],
                      fields_all.at[f * level_total + level_at[n]]) for f in range(3)]
            pairs.append((plume_out.at[n], plume_all.at[level_at[n]]))
            sent += fetch_all(out_sems.at[pl.ds(4 * n, 4)], pairs)
        for copy in sent:
            copy.wait()
        return
    results = [advance_fields(n, weights_at(n)) for n in range(level_count)]
    for copy in copies[1:]:
        copy.wait()
    emit_modes(
        [results[n][f] for f in range(3) for n in range(level_count)],
        parent, owners[step + 1] == gx * n_gy + gy, x_fwd[...], y_fwd[...], modes, turned, work,
    )
    sent = fetch_all(out_sems, [(modes, modes_all)])
    for n in range(level_total):
        parts = weights_at(n)
        if n >= level_count:
            advance_fields(n, parts)
        advance_ash(n, parts)
    sent[0].wait()


def exchange(axis, first, second):
    count = lax.axis_size(axis)
    received = []
    for start, data in ((0, first), (1, second)):
        pairs = [(i, i + 1) for i in range(start, count - 1, 2)]
        received.append(lax.ppermute(data, axis, pairs + [(b, a) for a, b in pairs]))
    return received


def local(tables, fields, levels, cuts, parent_modes, owners, plume, source):
    n_gx, n_gy = lax.axis_size("gx"), lax.axis_size("gy")
    devices = n_gx * n_gy
    level_total, cells_x, cells_y = plume.shape
    period = n_gx * cells_x * n_gy * cells_y
    nudged = 3 * levels.shape[0]
    field_rows = 3 * level_total
    total = field_rows + level_total
    rows = -(-(nudged // GROUP * 2 * KX) // devices)
    flat = fields.reshape(field_rows, cells_x, cells_y)
    cuts = cuts.reshape(-1)
    f32 = functools.partial(jax.ShapeDtypeStruct, dtype=jnp.float32)
    x_fwd, y_fwd, y_back, x_back, x_beside = (jnp.asarray(t) for t in tables)

    def vmem(*shape):
        return pltpu.VMEM(shape, jnp.float32)

    def table_space(table):
        return pltpu.VMEM(table.shape[1:], table.dtype)

    def limit(mib):
        return pltpu.CompilerParams(vmem_limit_bytes=mib * 1024 * 1024)

    mode_shape = f32((devices, 2 * rows, LANES))
    step_scratch = [vmem(total, cells_x + 2 * PAD, cells_y), vmem(devices * rows, LANES), vmem(devices * rows, LANES),
                    vmem(total, cells_y), vmem(total, cells_y), pltpu.SemaphoreType.DMA((5,))]
    levels_space = pltpu.SMEM(levels.shape, jnp.int32)
    owners_space = pltpu.SMEM(owners.shape, jnp.int32)
    order_shape = (3 * level_total,)
    order_space = pltpu.SMEM(order_shape, jnp.int32)
    raw_levels = levels
    levels, owners = in_hbm(levels), in_hbm(owners)
    mode_scratch = [vmem(nudged, 4 * KX * KX), table_space(x_fwd),
                    table_space(y_fwd), vmem(nudged, KX, LANES),
                    vmem(devices * rows, 2 * LANES)]
    inner_scratch = [owners_space, vmem(*mode_shape.shape), pltpu.SemaphoreType.DMA((1,))]
    inner_scratch += mode_scratch
    last_scratch = [vmem(field_rows, cells_x, cells_y), vmem(level_total, cells_x, cells_y),
                    pltpu.SemaphoreType.DMA((4 * level_total,))]

    modes = pl.pallas_call(
        functools.partial(first_kernel, n_gy, level_total),
        out_shape=mode_shape,
        in_specs=[HBM] * 6,
        out_specs=VMEM,
        scratch_shapes=[levels_space, owners_space, vmem(field_rows, cells_x, cells_y),
                        pltpu.SemaphoreType.DMA((6,))] + mode_scratch,
        compiler_params=limit(8),
        name="first_modes",
    )(levels, owners, *map(in_hbm, (flat, parent_modes, x_fwd, y_fwd)))
    for step in range(STEPS):
        last = step == STEPS - 1
        edge_shapes = [f32((total, cells_y)), f32((total, cells_y)), f32((cells_x, 2 * total))]
        edge_operands = [flat, plume]
        if step == 0:
            edge_shapes += [f32((2 * rows, LANES)),
                            jax.ShapeDtypeStruct(order_shape, jnp.int32)]
            edge_operands += [cuts, raw_levels]
        edges = pl.pallas_call(
            functools.partial(edge_kernel, n_gy, period),
            out_shape=edge_shapes,
            in_specs=[VMEM, VMEM, SMEM, SMEM][: len(edge_operands)],
            out_specs=[VMEM, VMEM, VMEM, VMEM, SMEM][: len(edge_shapes)],
            compiler_params=limit(8),
            name="edges",
        )(*edge_operands)
        if step == 0:
            weights, order = edges[3], in_hbm(edges[4])
        to_first, to_second, cols = edges[:3]
        row_first, row_second = exchange("gx", to_first, to_second)
        parts = lax.all_to_all(modes, AXES, 0, 0, tiled=True)
        parts, row_first, row_second = lax.optimization_barrier((parts, row_first, row_second))
        share = pl.pallas_call(
            functools.partial(share_kernel, n_gx, n_gy),
            out_shape=f32((devices, rows + beside_rows(rows), LANES)),
            in_specs=[VMEM] * 4,
            out_specs=VMEM,
            compiler_params=limit(8),
            name="share_sum",
        )(weights, parts, x_back, x_beside)
        share, cols = lax.optimization_barrier((share, cols))
        col_first, col_second = exchange("gy", cols, cols)
        shares = lax.all_to_all(share, AXES, 0, 0, tiled=True)
        out_shape = [f32(flat.shape), f32(plume.shape)]
        out_specs = [HBM if last else VMEM] * 2
        operands = [shares, flat, plume, source, row_first, row_second, col_first, col_second,
                    y_back, order]
        if not last:
            out_shape.append(pltpu.HBM(mode_shape.shape, jnp.float32))
            out_specs.append(HBM)
            operands += [owners, in_hbm(parent_modes), in_hbm(x_fwd), in_hbm(y_fwd)]
        results = pl.pallas_call(
            functools.partial(step_kernel, n_gy, step, last, levels.shape[0]),
            out_shape=out_shape,
            in_specs=[VMEM] * 9 + [HBM] * (len(operands) - 9),
            out_specs=out_specs,
            scratch_shapes=[order_space] + step_scratch + (last_scratch if last else inner_scratch),
            compiler_params=limit(20),
            name="final_step" if last else "inner_step",
        )(*operands)
        if last:
            flat, plume = results
        else:
            flat, plume, modes = results
    return flat.reshape(fields.shape), plume


def solution(mesh):
    in_specs = (
        P(None, None, "gx", "gy"),
        P(),
        P(),
        P(("gx", "gy"), None, None, None),
        P(),
        P(None, "gx", "gy"),
        P(None, "gx", "gy"),
    )
    out_specs = (P(None, None, "gx", "gy"), P(None, "gx", "gy"))
    n_gx, n_gy = mesh.shape["gx"], mesh.shape["gy"]

    def whole(fields, levels, cuts, parent_modes, owners, plume, source):
        tables = build_tables(n_gx, n_gy, plume.shape[1] // n_gx, plume.shape[2] // n_gy)
        return jax.shard_map(
            functools.partial(local, tables), mesh=mesh, in_specs=in_specs, out_specs=out_specs,
            check_vma=False,
        )(fields, levels, cuts, parent_modes, owners, plume, source)

    return whole
```

```python
import functools
import math

import jax
import jax.numpy as jnp
import ml_dtypes
import numpy as np
from jax import lax
from jax.experimental import pallas as pl
from jax.experimental.pallas import tpu as pltpu
from jax.sharding import PartitionSpec as P

KX = 32
STEPS = 2
GROUP = 4
LANES = GROUP * KX
PAD = 8
VMEM = pl.BlockSpec(memory_space=pltpu.VMEM)
SMEM = pl.BlockSpec(memory_space=pltpu.SMEM)
HBM = pl.BlockSpec(memory_space=pltpu.HBM)
AXES = ("gx", "gy")


def in_hbm(array):
    return pltpu.with_memory_space_constraint(array, pltpu.HBM)


def wave_table(positions, period):
    wavenum = np.arange(KX)[:, None]
    phase = (wavenum * positions[None, :] % period) * (2.0 * math.pi / period)
    inside = (positions >= 0) & (positions < period)
    return np.concatenate([np.cos(phase), np.sin(phase)], axis=0) * inside[None, :]


def split(a):
    head = a.astype(jnp.bfloat16)
    return head, (a - head.astype(jnp.float32)).astype(jnp.bfloat16)


def split_table(table, axis, order):
    head = table.astype(ml_dtypes.bfloat16)
    rest = (table - head.astype(np.float64)).astype(ml_dtypes.bfloat16)
    return np.concatenate([head if part == "h" else rest for part in order], axis=axis)


def per_slab(table):
    return np.kron(np.eye(GROUP), table)


def build_tables(n_gx, n_gy, cells_x, cells_y):
    period_x, period_y = n_gx * cells_x, n_gy * cells_y
    scaling = 1.0 / math.sqrt(period_x * period_y)
    parity = [np.arange(p, 2 * KX, 2) for p in range(2)]
    x_fwd, y_fwd, y_back, inner, outer = [], [], [], [], []
    for g in range(n_gx):
        first = g * cells_x
        table = wave_table(first + np.arange(cells_x), period_x)
        x_fwd.append(split_table(
            np.concatenate([per_slab(table[rows].T) for rows in parity], axis=1), 0, "hhl"))
        beside = wave_table(np.array([first - 1, first + cells_x]), period_x)
        inner.append(np.concatenate([np.tile(table[rows], (GROUP, 1)) for rows in parity], axis=0))
        outer.append(np.concatenate([per_slab(beside[rows]) for rows in parity], axis=0))
    spare = -(2 * GROUP * n_gx) % LANES
    x_back = np.concatenate(inner, axis=1)
    x_beside = np.concatenate(outer + [np.zeros((2 * LANES, spare))], axis=1)
    for g in range(n_gy):
        first = g * cells_y
        table = wave_table(first + np.arange(cells_y), period_y)
        edge = np.zeros((2 * KX, cells_y))
        edge[:, [0, -1]] = wave_table(np.array([first - 1, first + cells_y]), period_y)
        y_fwd.append(split_table(table * scaling, 1, "hlh"))
        y_back.append(split_table(np.concatenate([table, edge], axis=1), 0, "hhl"))
    return [np.stack(x_fwd), np.stack(y_fwd), np.stack(y_back),
            split_table(x_back, 0, "hl"), split_table(x_beside, 0, "hl")]


def data_dot(a, table):
    head, rest = split(a)
    return jnp.dot(
        jnp.concatenate([head, rest, head], axis=1), table, preferred_element_type=jnp.float32
    )


def two_part_dot(a, table):
    head, rest = split(a)
    depth = a.shape[1]
    heads = jnp.dot(
        jnp.concatenate([head, rest], axis=0), table[:depth], preferred_element_type=jnp.float32)
    rests = jnp.dot(head, table[depth:], preferred_element_type=jnp.float32)
    return heads[: a.shape[0]] + heads[a.shape[0] :] + rests


def columns_dot(a, table):
    head, rest = split(a)
    stacked = jnp.concatenate([head, rest, head], axis=0)
    return lax.dot_general(
        stacked, table, (((0,), (0,)), ((), ())), preferred_element_type=jnp.float32)


def emit_modes(chosen, parent, is_owner, x_fwd, y_fwd, modes, turned, work):
    devices, rows = modes.shape[0], modes.shape[1] // 2
    slabs = parent.shape[0]
    groups = slabs // GROUP
    head, rest = split(jnp.concatenate(chosen, axis=0))
    half = lax.dot_general(
        y_fwd, jnp.concatenate([head, head, rest], axis=1), (((1,), (1,)), ((), ())),
        preferred_element_type=jnp.float32)
    half = jnp.concatenate([half[:, t * LANES : (t + 1) * LANES] for t in range(groups)], axis=0)
    count = groups * 2 * KX
    work[0:count] = -data_dot(half, x_fwd)
    if count < devices * rows:
        work[count:] = jnp.zeros((devices * rows - count, 2 * LANES), jnp.float32)

    @pl.when(is_owner)
    def _():
        for i in range(KX):
            turned[:, i, :] = parent[:, i * LANES : (i + 1) * LANES]
        for t in range(groups):
            block = turned[t * GROUP : (t + 1) * GROUP].reshape(LANES, LANES).T
            span = slice(t * 2 * KX, (t + 1) * 2 * KX)
            for p in range(2):
                work[span, p * LANES : (p + 1) * LANES] += block[p * 2 * KX : (p + 1) * 2 * KX]

    for d in range(devices):
        for p in range(2):
            modes[d, p * rows : (p + 1) * rows, :] = work[
                d * rows : (d + 1) * rows, p * LANES : (p + 1) * LANES]


def fetch_all(sems, pairs):
    copies = [pltpu.make_async_copy(a, b, sems.at[i]) for i, (a, b) in enumerate(pairs)]
    for copy in copies:
        copy.start()
    return copies


def slab_of(levels, c, level_count, level_total):
    return (c // level_count) * level_total + levels[c % level_count]


def first_kernel(n_gy, level_total, levels_all, owners_all, fields_all, parent_all, x_fwd_all,
                 y_fwd_all, modes, levels, owners, fields, sems, parent, x_fwd, y_fwd, turned,
                 work):
    gx, gy = lax.axis_index("gx"), lax.axis_index("gy")
    copies = fetch_all(sems, [
        (levels_all, levels), (owners_all, owners), (fields_all, fields),
        (x_fwd_all.at[gx], x_fwd), (y_fwd_all.at[gy], y_fwd), (parent_all.at[0, 0], parent)])
    for copy in copies:
        copy.wait()
    level_count = parent.shape[0] // 3
    emit_modes(
        [fields[slab_of(levels, c, level_count, level_total)] for c in range(parent.shape[0])],
        parent, owners[0] == gx * n_gy + gy, x_fwd[...], y_fwd[...], modes, turned, work,
    )


def is_even(axis):
    return lax.rem(lax.axis_index(axis), 2) == 0


def edge_kernel(n_gy, period, cuts, levels, fields, plume, first, second, cols, weights, order):
    level_total = plume.shape[0]
    weights[...] = share_weights(n_gy, period, cuts, weights.shape)
    count = levels.shape[0]
    for n in range(count):
        order[n] = levels[n]
    spot = jnp.int32(count)
    for l in range(level_total):
        found = levels[0] == l
        for n in range(1, count):
            found = found | (levels[n] == l)
        order[spot] = jnp.int32(l)
        spot = spot + jnp.where(found, 0, 1)
    chosen = [order[n] for n in range(level_total)]
    for n in range(level_total, order.shape[0]):
        order[n] = jnp.int32(0)
    for n in range(level_total):
        order[level_total + chosen[n]] = jnp.int32(n)
    slabs = [fields[f * level_total + l] for f in range(3) for l in chosen]
    emit_edges(slabs + [plume[l] for l in chosen], first, second, cols)


def emit_edges(slabs, first, second, cols):
    even = is_even("gx")
    lane = lax.broadcasted_iota(jnp.int32, cols.shape, 1)
    acc = jnp.zeros(cols.shape, jnp.float32)
    for c, a in enumerate(slabs):
        west, east = a[:1], a[a.shape[0] - 1 :]
        first[c : c + 1, :] = jnp.where(even, east, west)
        second[c : c + 1, :] = jnp.where(even, west, east)
        acc = jnp.where(lane // 2 == c, pltpu.roll(a, 2 * c + 1, 1), acc)
    cols[...] = acc


def share_weights(n_gy, period, cuts, shape):
    rows = shape[0] // 2
    me = lax.axis_index("gx") * n_gy + lax.axis_index("gy")
    place = lax.broadcasted_iota(jnp.int32, shape, 0)
    lane = lax.broadcasted_iota(jnp.int32, shape, 1)
    p = (place >= rows).astype(jnp.int32)
    row = me * rows + place - p * rows
    k = 2 * (lane % KX) + p
    j = row % (2 * KX)
    slab = GROUP * (row // (2 * KX)) + lane // KX
    limit = jnp.zeros(shape, jnp.int32)
    for c in range(cuts.shape[0]):
        limit = jnp.where(slab == c, cuts[c], limit)
    keep = ((k % KX) < limit) & ((j % KX) < limit)
    factor = jnp.where(k == 0, 1.0, 2.0) * jnp.where(j == 0, 1.0, 2.0) * (1.0 / math.sqrt(period))
    return jnp.where(keep, factor, 0.0)


def beside_rows(rows):
    return -(-rows // 3)


def share_kernel(n_gx, n_gy, weights, parts, x_back, x_beside, out):
    devices = parts.shape[0]
    rows = parts.shape[1] // 2
    total = parts[0]
    for d in range(1, devices):
        total = total + parts[d]
    mismatch = total * weights[...]
    both = jnp.concatenate([mismatch[:rows], mismatch[rows:]], axis=1)
    spare = -rows % 16
    if spare:
        both = jnp.concatenate([both, jnp.zeros((spare, 2 * LANES), jnp.float32)], axis=0)
    slab_lane = lax.broadcasted_iota(jnp.int32, both.shape, 1) % LANES // KX
    chosen = [jnp.where(slab_lane == n, both, 0.0) for n in range(GROUP)]
    inner = two_part_dot(jnp.concatenate(chosen, axis=0), x_back)
    edge_all = two_part_dot(both, x_beside)
    height = rows + spare
    packed = beside_rows(rows)
    width = 2 * GROUP
    cells_x = LANES // GROUP
    slot = lax.broadcasted_iota(jnp.int32, (height, LANES), 1) // cells_x
    spot = lax.broadcasted_iota(jnp.int32, (packed, LANES), 1) // width
    for g in range(n_gx):
        first = g * cells_x // LANES * LANES
        tile = jnp.zeros((height, LANES), jnp.float32)
        for n in range(GROUP):
            piece = inner[n * height : (n + 1) * height, first : first + LANES]
            tile = jnp.where(slot == n, pltpu.roll(piece, (n - g) * cells_x % LANES, 1), tile)
        first = g * width // LANES * LANES
        beside = jnp.zeros((packed, LANES), jnp.float32)
        for m in range(3):
            piece = edge_all[m * packed : (m + 1) * packed, first : first + LANES]
            beside = jnp.where(
                spot == m, pltpu.roll(piece, (m - g) * width % LANES, 1), beside)
        for h in range(n_gy):
            out[g * n_gy + h, :rows, :] = tile[:rows]
            out[g * n_gy + h, rows:, :] = beside


class Halo:
    def __init__(self, row_first, row_second, col_first, col_second, west, east):
        even = is_even("gx")
        west[...] = jnp.where(even, row_second[...], row_first[...])
        east[...] = jnp.where(even, row_first[...], row_second[...])
        self.west, self.east = west, east
        even = is_even("gy")
        north = jnp.where(even, col_first[...], col_second[...])
        south = jnp.where(even, col_second[...], col_first[...])
        shape = north.shape
        lane = lax.broadcasted_iota(jnp.int32, shape, 1)
        self.last = shape[1] - 1
        self.at_first, self.at_last = lane == 0, lane == self.last
        self.columns = jnp.where(
            lane % 2 == 0, pltpu.roll(north, self.last, 1), pltpu.roll(south, 1, 1))

    def rows(self, c):
        return self.west[c : c + 1, :], self.east[c : c + 1, :]

    def column(self, c):
        return pltpu.roll(self.columns, self.last - 2 * c, 1)

    def move(self, slab, column, parts):
        centre, to_west, to_east, to_south, to_north = parts
        cells_x = column.shape[0]
        a = slab[PAD : PAD + cells_x]
        return (
            centre * a
            + to_west * slab[PAD - 1 : PAD - 1 + cells_x]
            + to_east * slab[PAD + 1 : PAD + 1 + cells_x]
            + to_south * jnp.where(self.at_first, column, pltpu.roll(a, 1, 1))
            + to_north * jnp.where(self.at_last, column, pltpu.roll(a, self.last, 1))
        )


def place(slab, a, rows):
    cells_x = a.shape[0]
    slab[PAD : PAD + cells_x] = a
    slab[PAD - 1 : PAD] = rows[0]
    slab[PAD + cells_x : PAD + cells_x + 1] = rows[1]


def wind_weights(u, v):
    neighbours = (
        0.1 + 0.1 * jnp.maximum(u, 0.0), 0.1 - 0.1 * jnp.minimum(u, 0.0),
        0.1 + 0.1 * jnp.maximum(v, 0.0), 0.1 - 0.1 * jnp.minimum(v, 0.0),
    )
    centre = 1.0 - (neighbours[0] + neighbours[1] + neighbours[2] + neighbours[3])
    return (centre,) + neighbours


def settling(parts):
    return (parts[0] - 0.3,) + parts[1:]


def above(l, level_total):
    return jnp.where(l + 1 < level_total, 0.3, 0.0).astype(jnp.float32)


def nudge_updates(shares, spread, spread_edges, y_table, nudged, cells_x):
    devices = shares.shape[0]
    rows = spread.shape[0] // devices
    packed = beside_rows(rows)
    width = 2 * GROUP
    for d in range(devices):
        spread[d * rows : (d + 1) * rows] = shares[d, :rows, :]
        edge = shares[d, rows:, :]
        for m in range(3):
            count = min(packed, rows - m * packed)
            if count > 0:
                moved = pltpu.roll(edge, -m * width % LANES, 1) if m else edge
                start = d * rows + m * packed
                spread_edges[start : start + count] = moved[:count]
    groups = nudged // GROUP
    spot_of = lax.broadcasted_iota(jnp.int32, (2 * KX, LANES), 1) // width
    edges = jnp.zeros((2 * KX, LANES), jnp.float32)
    for t in range(groups):
        piece = spread_edges[t * 2 * KX : (t + 1) * 2 * KX]
        edges = jnp.where(spot_of == t, pltpu.roll(piece, t * width, 1) if t else piece, edges)
    update_rows = columns_dot(edges, y_table)
    updates = []
    for t in range(groups):
        update = columns_dot(spread[t * 2 * KX : (t + 1) * 2 * KX], y_table)
        updates += [update[n * cells_x : (n + 1) * cells_x] for n in range(GROUP)]
    return updates, update_rows


def nudged_kernel(n_gy, step, last, level_count, level_total, shares, fields, row_first, row_second,
                  col_first, col_second, y_back, order_all, *rest):
    gx, gy = lax.axis_index("gx"), lax.axis_index("gy")
    cells_x, cells_y = fields.shape[1:]
    nudged = 3 * level_count
    if last:
        (plume, source, _, _, fields_all, plume_all, order, slabs, spread, spread_edges, west, east,
         sems, fields_out, plume_out, out_sems) = rest
        extra = []
    else:
        (owners_all, parent_all, x_fwd_all, y_fwd_all, fields_out, winds_out, modes,
         order, slabs, spread, spread_edges, west, east, sems,
         owners, parent, x_fwd, y_fwd, turned, work) = rest
        extra = [(owners_all, owners), (x_fwd_all.at[gx], x_fwd), (y_fwd_all.at[gy], y_fwd),
                 (parent_all.at[0, step + 1], parent)]
    copies = fetch_all(sems, [(order_all, order)] + extra)
    halo = Halo(row_first, row_second, col_first, col_second, west, east)
    updates, update_rows = nudge_updates(
        shares, spread, spread_edges, y_back[gy], nudged, cells_x)
    copies[0].wait()
    level_at = [order[n] for n in range(level_count)]
    beside = []
    for k in range(nudged):
        f, n = k // level_count, k % level_count
        a = fields[f * level_total + level_at[n]] if step == 0 else fields[k]
        before, after = halo.rows(f * level_total + n)
        place(slabs.at[k], a + updates[k][:, :cells_y],
              (before + update_rows[2 * k : 2 * k + 1, :cells_y],
               after + update_rows[2 * k + 1 : 2 * k + 2, :cells_y]))
        beside.append(updates[k][:, cells_y:])
    inner = slice(PAD, PAD + cells_x)
    results = [None] * nudged
    sent = []
    for n in range(level_count):
        u, v = slabs[n, inner], slabs[level_count + n, inner]
        parts = wind_weights(u, v)
        for f in range(3):
            k = f * level_count + n
            column = halo.column(f * level_total + n) + beside[k]
            results[k] = halo.move(slabs[k], column, parts)
            fields_out[k] = results[k]
        if not last:
            winds_out[n] = u
            winds_out[level_count + n] = v
            continue
        l = level_at[n]
        c = 3 * level_total + n
        place(slabs.at[nudged + n], plume[n], halo.rows(c))
        settled = halo.move(slabs[nudged + n], halo.column(c), settling(parts))
        plume_out[n] = settled + above(l, level_total) * plume[order[level_total + l + 1]] + source[l]
        pairs = [(fields_out.at[f * level_count + n], fields_all.at[f * level_total + l])
                 for f in range(3)] + [(plume_out.at[n], plume_all.at[l])]
        sent += fetch_all(out_sems.at[pl.ds(4 * n, 4)], pairs)
    if last:
        for copy in sent:
            copy.wait()
        return
    for copy in copies[1:]:
        copy.wait()
    emit_modes(results, parent, owners[step + 1] == gx * n_gy + gy, x_fwd[...], y_fwd[...], modes,
               turned, work)


def others_kernel(step, last, level_count, fields, plume, source, row_first, row_second, col_first,
                  col_second, order_all, *rest):
    level_total, cells_x, cells_y = plume.shape
    if last:
        fields_all, plume_all, order, slab, west, east, sems, fields_out, plume_out, out_sems = rest
    else:
        (done, winds, fields_out, plume_out, first, second, cols, order, slab, west, east,
         sems) = rest
    copies = fetch_all(sems, [(order_all, order)])
    halo = Halo(row_first, row_second, col_first, col_second, west, east)
    copies[0].wait()
    level_at = [order[n] for n in range(level_total)]
    kept = level_total - level_count
    sent = []
    results = {}
    for n in range(level_count if last else 0, level_total):
        l = level_at[n]
        m = n - level_count
        if m < 0:
            parts = wind_weights(winds[n], winds[level_count + n])
        else:
            given = [fields[f * level_total + l] if step == 0 else fields[f * kept + m]
                     for f in range(3)]
            parts = wind_weights(given[0], given[1])
            for f in range(3):
                c = f * level_total + n
                place(slab.at[4 * n + f], given[f], halo.rows(c))
                results[c] = halo.move(slab[4 * n + f], halo.column(c), parts)
                fields_out[f * kept + m] = results[c]
        c = 3 * level_total + n
        place(slab.at[4 * n + 3], plume[l] if step == 0 else plume[n], halo.rows(c))
        higher = (jnp.minimum(l + 1, level_total - 1) if step == 0 else order[level_total + l + 1])
        results[c] = (halo.move(slab[4 * n + 3], halo.column(c), settling(parts))
                      + above(l, level_total) * plume[higher] + source[l])
        plume_out[m if last else n] = results[c]
        if last:
            pairs = [(fields_out.at[f * kept + m], fields_all.at[f * level_total + l])
                     for f in range(3)] + [(plume_out.at[m], plume_all.at[l])]
            sent += fetch_all(out_sems.at[pl.ds(4 * m, 4)], pairs)
    for copy in sent:
        copy.wait()
    if not last:
        for f in range(3):
            for n in range(level_count):
                results[f * level_total + n] = done[f * level_count + n]
        emit_edges([results[c] for c in range(4 * level_total)], first, second, cols)


def exchange(axis, first, second):
    count = lax.axis_size(axis)
    received = []
    for start, data in ((0, first), (1, second)):
        pairs = [(i, i + 1) for i in range(start, count - 1, 2)]
        received.append(lax.ppermute(data, axis, pairs + [(b, a) for a, b in pairs]))
    return received


def local(tables, fields, levels, cuts, parent_modes, owners, plume, source):
    n_gx, n_gy = lax.axis_size("gx"), lax.axis_size("gy")
    devices = n_gx * n_gy
    level_total, cells_x, cells_y = plume.shape
    period = n_gx * cells_x * n_gy * cells_y
    nudged = 3 * levels.shape[0]
    field_rows = 3 * level_total
    total = field_rows + level_total
    rows = -(-(nudged // GROUP * 2 * KX) // devices)
    flat = fields.reshape(field_rows, cells_x, cells_y)
    cuts = cuts.reshape(-1)
    f32 = functools.partial(jax.ShapeDtypeStruct, dtype=jnp.float32)
    x_fwd, y_fwd, y_back, x_back, x_beside = (jnp.asarray(t) for t in tables)

    def vmem(*shape):
        return pltpu.VMEM(shape, jnp.float32)

    def table_space(table):
        return pltpu.VMEM(table.shape[1:], table.dtype)

    def limit(mib):
        return pltpu.CompilerParams(vmem_limit_bytes=mib * 1024 * 1024)

    count = levels.shape[0]
    kept = level_total - count
    mode_shape = f32((devices, 2 * rows, LANES))
    order_shape = (3 * level_total,)
    edge_shapes = [f32((total, cells_y)), f32((total, cells_y)), f32((cells_x, 2 * total))]
    levels_space = pltpu.SMEM(levels.shape, jnp.int32)
    owners_space = pltpu.SMEM(owners.shape, jnp.int32)
    order_space = pltpu.SMEM(order_shape, jnp.int32)
    rows_space = vmem(total, cells_y)
    mode_scratch = [vmem(nudged, 4 * KX * KX), table_space(x_fwd),
                    table_space(y_fwd), vmem(nudged, KX, LANES),
                    vmem(devices * rows, 2 * LANES)]
    nudged_scratch = [order_space, vmem(nudged + count, cells_x + 2 * PAD, cells_y),
                      vmem(devices * rows, LANES), vmem(devices * rows, LANES),
                      rows_space, rows_space, pltpu.SemaphoreType.DMA((5,))]
    others_scratch = [order_space, vmem(total, cells_x + 2 * PAD, cells_y), rows_space, rows_space,
                      pltpu.SemaphoreType.DMA((1,))]

    def out_scratch(slabs):
        return [vmem(3 * slabs, cells_x, cells_y), vmem(slabs, cells_x, cells_y),
                pltpu.SemaphoreType.DMA((4 * slabs,))]

    modes = pl.pallas_call(
        functools.partial(first_kernel, n_gy, level_total),
        out_shape=mode_shape,
        in_specs=[HBM] * 6,
        out_specs=VMEM,
        scratch_shapes=[levels_space, owners_space, vmem(field_rows, cells_x, cells_y),
                        pltpu.SemaphoreType.DMA((6,))] + mode_scratch,
        compiler_params=limit(8),
        name="first_modes",
    )(*map(in_hbm, (levels, owners, flat, parent_modes, x_fwd, y_fwd)))
    *edges, weights, order = pl.pallas_call(
        functools.partial(edge_kernel, n_gy, period),
        out_shape=edge_shapes
        + [f32((2 * rows, LANES)), jax.ShapeDtypeStruct(order_shape, jnp.int32)],
        in_specs=[SMEM, SMEM, VMEM, VMEM],
        out_specs=[VMEM] * 4 + [SMEM],
        compiler_params=limit(8),
        name="edges",
    )(cuts, levels, flat, plume)
    order = in_hbm(order)
    others = flat
    for step in range(STEPS):
        last = step == STEPS - 1
        to_first, to_second, cols = edges
        col_first, col_second = exchange("gy", cols, cols)
        parts = lax.all_to_all(modes, AXES, 0, 0, tiled=True)
        parts, col_first, col_second = lax.optimization_barrier((parts, col_first, col_second))
        share = pl.pallas_call(
            functools.partial(share_kernel, n_gx, n_gy),
            out_shape=f32((devices, rows + beside_rows(rows), LANES)),
            in_specs=[VMEM] * 4,
            out_specs=VMEM,
            compiler_params=limit(8),
            name="share_sum",
        )(weights, parts, x_back, x_beside)
        share, to_first, to_second = lax.optimization_barrier((share, to_first, to_second))
        row_first, row_second = exchange("gx", to_first, to_second)
        halo = [row_first, row_second, col_first, col_second]
        shares = lax.all_to_all(share, AXES, 0, 0, tiled=True)
        if last:
            final = pl.pallas_call(
                functools.partial(others_kernel, step, True, count),
                out_shape=[f32((field_rows, cells_x, cells_y)), f32(plume.shape)],
                in_specs=[VMEM] * 7 + [HBM],
                out_specs=[HBM] * 2,
                scratch_shapes=others_scratch + out_scratch(kept),
                compiler_params=limit(8),
                name="last_others",
            )(others, plume, source, *halo, order)
            flat, plume = pl.pallas_call(
                functools.partial(nudged_kernel, n_gy, step, True, count, level_total),
                out_shape=[f32((field_rows, cells_x, cells_y)), f32(plume.shape)],
                in_specs=[VMEM] * 7 + [HBM] + [VMEM] * 2 + [HBM] * 2,
                out_specs=[HBM] * 2,
                scratch_shapes=nudged_scratch + out_scratch(count),
                input_output_aliases={10: 0, 11: 1},
                compiler_params=limit(12),
                name="last_nudged",
            )(shares, flat, *halo, y_back, order, plume, source, *final)
        else:
            done, winds, modes = pl.pallas_call(
                functools.partial(nudged_kernel, n_gy, step, False, count, level_total),
                out_shape=[f32((nudged, cells_x, cells_y)), f32((2 * count, cells_x, cells_y)),
                           mode_shape],
                in_specs=[VMEM] * 7 + [HBM] * 5,
                out_specs=[VMEM] * 3,
                scratch_shapes=nudged_scratch + [owners_space] + mode_scratch,
                compiler_params=limit(12),
                name="inner_nudged",
            )(shares, flat, *halo, y_back, order,
              *map(in_hbm, (owners, parent_modes, x_fwd, y_fwd)))
            others, plume, *edges = pl.pallas_call(
                functools.partial(others_kernel, step, False, count),
                out_shape=[f32((3 * kept, cells_x, cells_y)), f32(plume.shape)] + edge_shapes,
                in_specs=[VMEM] * 7 + [HBM] + [VMEM] * 2,
                out_specs=[VMEM] * 5,
                scratch_shapes=others_scratch,
                compiler_params=limit(8),
                name="inner_others",
            )(others, plume, source, *halo, order, done, winds)
            flat = done
    return flat.reshape(fields.shape), plume


def solution(mesh):
    in_specs = (
        P(None, None, "gx", "gy"),
        P(),
        P(),
        P(("gx", "gy"), None, None, None),
        P(),
        P(None, "gx", "gy"),
        P(None, "gx", "gy"),
    )
    out_specs = (P(None, None, "gx", "gy"), P(None, "gx", "gy"))
    n_gx, n_gy = mesh.shape["gx"], mesh.shape["gy"]

    def whole(fields, levels, cuts, parent_modes, owners, plume, source):
        tables = build_tables(n_gx, n_gy, plume.shape[1] // n_gx, plume.shape[2] // n_gy)
        return jax.shard_map(
            functools.partial(local, tables), mesh=mesh, in_specs=in_specs, out_specs=out_specs,
            check_vma=False,
        )(fields, levels, cuts, parent_modes, owners, plume, source)

    return whole
```

```python
import functools
import math

import jax
import jax.numpy as jnp
import ml_dtypes
import numpy as np
from jax import lax
from jax.experimental import pallas as pl
from jax.experimental.pallas import tpu as pltpu
from jax.sharding import PartitionSpec as P

KX = 32
STEPS = 2
GROUP = 4
LANES = GROUP * KX
PAD = 8
VMEM = pl.BlockSpec(memory_space=pltpu.VMEM)
SMEM = pl.BlockSpec(memory_space=pltpu.SMEM)
HBM = pl.BlockSpec(memory_space=pltpu.HBM)
AXES = ("gx", "gy")


def in_hbm(array):
    return pltpu.with_memory_space_constraint(array, pltpu.HBM)


def wave_table(positions, period):
    wavenum = np.arange(KX)[:, None]
    phase = (wavenum * positions[None, :] % period) * (2.0 * math.pi / period)
    inside = (positions >= 0) & (positions < period)
    return np.concatenate([np.cos(phase), np.sin(phase)], axis=0) * inside[None, :]


def split(a):
    head = a.astype(jnp.bfloat16)
    return head, (a - head.astype(jnp.float32)).astype(jnp.bfloat16)


def split_table(table, axis, order):
    head = table.astype(ml_dtypes.bfloat16)
    rest = (table - head.astype(np.float64)).astype(ml_dtypes.bfloat16)
    return np.concatenate([head if part == "h" else rest for part in order], axis=axis)


def per_slab(table):
    return np.kron(np.eye(GROUP), table)


def build_tables(n_gx, n_gy, cells_x, cells_y):
    period_x, period_y = n_gx * cells_x, n_gy * cells_y
    scaling = 1.0 / math.sqrt(period_x * period_y)
    parity = [np.arange(p, 2 * KX, 2) for p in range(2)]
    x_fwd, y_fwd, y_back, inner, outer = [], [], [], [], []
    for g in range(n_gx):
        first = g * cells_x
        table = wave_table(first + np.arange(cells_x), period_x)
        x_fwd.append(split_table(
            np.concatenate([per_slab(table[rows].T) for rows in parity], axis=1), 0, "hhl"))
        beside = wave_table(np.array([first - 1, first + cells_x]), period_x)
        inner.append(np.concatenate([np.tile(table[rows], (GROUP, 1)) for rows in parity], axis=0))
        outer.append(np.concatenate([per_slab(beside[rows]) for rows in parity], axis=0))
    spare = -(2 * GROUP * n_gx) % LANES
    x_back = np.concatenate(inner, axis=1)
    x_beside = np.concatenate(outer + [np.zeros((2 * LANES, spare))], axis=1)
    for g in range(n_gy):
        first = g * cells_y
        table = wave_table(first + np.arange(cells_y), period_y)
        edge = np.zeros((2 * KX, cells_y))
        edge[:, [0, -1]] = wave_table(np.array([first - 1, first + cells_y]), period_y)
        y_fwd.append(split_table(table * scaling, 1, "hlh"))
        y_back.append(split_table(np.concatenate([table, edge], axis=1), 0, "hhl"))
    return [np.stack(x_fwd), np.stack(y_fwd), np.stack(y_back),
            split_table(x_back, 0, "hl"), split_table(x_beside, 0, "hl")]


def data_dot(a, table):
    head, rest = split(a)
    return jnp.dot(
        jnp.concatenate([head, rest, head], axis=1), table, preferred_element_type=jnp.float32
    )


def two_part_dot(a, table):
    head, rest = split(a)
    depth = a.shape[1]
    heads = jnp.dot(
        jnp.concatenate([head, rest], axis=0), table[:depth], preferred_element_type=jnp.float32)
    rests = jnp.dot(head, table[depth:], preferred_element_type=jnp.float32)
    return heads[: a.shape[0]] + heads[a.shape[0] :] + rests


def columns_dot(a, table):
    head, rest = split(a)
    stacked = jnp.concatenate([head, rest, head], axis=0)
    return lax.dot_general(
        stacked, table, (((0,), (0,)), ((), ())), preferred_element_type=jnp.float32)


def emit_modes(chosen, parent, is_owner, x_fwd, y_fwd, modes, turned, work):
    devices, rows = modes.shape[0], modes.shape[1] // 2
    slabs = parent.shape[0]
    groups = slabs // GROUP
    head, rest = split(jnp.concatenate(chosen, axis=0))
    half = lax.dot_general(
        y_fwd, jnp.concatenate([head, head, rest], axis=1), (((1,), (1,)), ((), ())),
        preferred_element_type=jnp.float32)
    half = jnp.concatenate([half[:, t * LANES : (t + 1) * LANES] for t in range(groups)], axis=0)
    count = groups * 2 * KX
    work[0:count] = -data_dot(half, x_fwd)
    if count < devices * rows:
        work[count:] = jnp.zeros((devices * rows - count, 2 * LANES), jnp.float32)

    @pl.when(is_owner)
    def _():
        for i in range(KX):
            turned[:, i, :] = parent[:, i * LANES : (i + 1) * LANES]
        for t in range(groups):
            block = turned[t * GROUP : (t + 1) * GROUP].reshape(LANES, LANES).T
            span = slice(t * 2 * KX, (t + 1) * 2 * KX)
            for p in range(2):
                work[span, p * LANES : (p + 1) * LANES] += block[p * 2 * KX : (p + 1) * 2 * KX]

    for d in range(devices):
        for p in range(2):
            modes[d, p * rows : (p + 1) * rows, :] = work[
                d * rows : (d + 1) * rows, p * LANES : (p + 1) * LANES]


def fetch_all(sems, pairs):
    copies = [pltpu.make_async_copy(a, b, sems.at[i]) for i, (a, b) in enumerate(pairs)]
    for copy in copies:
        copy.start()
    return copies


def slab_of(levels, c, level_count, level_total):
    return (c // level_count) * level_total + levels[c % level_count]


def first_kernel(n_gy, level_total, levels_all, owners_all, fields_all, parent_all, x_fwd_all,
                 y_fwd_all, modes, levels, owners, fields, sems, parent, x_fwd, y_fwd, turned,
                 work):
    gx, gy = lax.axis_index("gx"), lax.axis_index("gy")
    copies = fetch_all(sems, [
        (levels_all, levels), (owners_all, owners), (fields_all, fields),
        (x_fwd_all.at[gx], x_fwd), (y_fwd_all.at[gy], y_fwd), (parent_all.at[0, 0], parent)])
    for copy in copies:
        copy.wait()
    level_count = parent.shape[0] // 3
    emit_modes(
        [fields[slab_of(levels, c, level_count, level_total)] for c in range(parent.shape[0])],
        parent, owners[0] == gx * n_gy + gy, x_fwd[...], y_fwd[...], modes, turned, work,
    )


def is_even(axis):
    return lax.rem(lax.axis_index(axis), 2) == 0


def edge_kernel(n_gy, period, cuts, levels, fields, plume, y_back_all, first, second, cols, weights,
                nudged, others, y_back, order, sems):
    copies = fetch_all(sems, [(y_back_all.at[lax.axis_index("gy")], y_back)])
    level_total = plume.shape[0]
    weights[...] = share_weights(n_gy, period, cuts, weights.shape)
    count = levels.shape[0]
    for n in range(count):
        order[n] = levels[n]
    spot = jnp.int32(count)
    for l in range(level_total):
        found = levels[0] == l
        for n in range(1, count):
            found = found | (levels[n] == l)
        order[spot] = jnp.int32(l)
        spot = spot + jnp.where(found, 0, 1)
    chosen = [order[n] for n in range(level_total)]
    for n in range(level_total, order.shape[0]):
        order[n] = jnp.int32(0)
    for n in range(level_total):
        order[level_total + chosen[n]] = jnp.int32(n)
    slabs = [fields[f * level_total + l] for f in range(3) for l in chosen]
    emit_edges(slabs + [plume[l] for l in chosen], first, second, cols)
    kept = level_total - count
    for c, a in enumerate(slabs):
        f, n = c // level_total, c % level_total
        if n < count:
            nudged[f * count + n] = a
        else:
            others[f * kept + n - count] = a
    for copy in copies:
        copy.wait()


def emit_edges(slabs, first, second, cols):
    even = is_even("gx")
    lane = lax.broadcasted_iota(jnp.int32, cols.shape, 1)
    acc = jnp.zeros(cols.shape, jnp.float32)
    for c, a in enumerate(slabs):
        west, east = a[:1], a[a.shape[0] - 1 :]
        first[c : c + 1, :] = jnp.where(even, east, west)
        second[c : c + 1, :] = jnp.where(even, west, east)
        acc = jnp.where(lane // 2 == c, pltpu.roll(a, 2 * c + 1, 1), acc)
    cols[...] = acc


def share_weights(n_gy, period, cuts, shape):
    rows = shape[0] // 2
    me = lax.axis_index("gx") * n_gy + lax.axis_index("gy")
    place = lax.broadcasted_iota(jnp.int32, shape, 0)
    lane = lax.broadcasted_iota(jnp.int32, shape, 1)
    p = (place >= rows).astype(jnp.int32)
    row = me * rows + place - p * rows
    k = 2 * (lane % KX) + p
    j = row % (2 * KX)
    slab = GROUP * (row // (2 * KX)) + lane // KX
    limit = jnp.zeros(shape, jnp.int32)
    for c in range(cuts.shape[0]):
        limit = jnp.where(slab == c, cuts[c], limit)
    keep = ((k % KX) < limit) & ((j % KX) < limit)
    factor = jnp.where(k == 0, 1.0, 2.0) * jnp.where(j == 0, 1.0, 2.0) * (1.0 / math.sqrt(period))
    return jnp.where(keep, factor, 0.0)


def beside_rows(rows):
    return -(-rows // 3)


def share_kernel(n_gx, n_gy, weights, parts, x_back, x_beside, out):
    devices = parts.shape[0]
    rows = parts.shape[1] // 2
    total = parts[0]
    for d in range(1, devices):
        total = total + parts[d]
    mismatch = total * weights[...]
    both = jnp.concatenate([mismatch[:rows], mismatch[rows:]], axis=1)
    spare = -rows % 16
    if spare:
        both = jnp.concatenate([both, jnp.zeros((spare, 2 * LANES), jnp.float32)], axis=0)
    slab_lane = lax.broadcasted_iota(jnp.int32, both.shape, 1) % LANES // KX
    chosen = [jnp.where(slab_lane == n, both, 0.0) for n in range(GROUP)]
    inner = two_part_dot(jnp.concatenate(chosen, axis=0), x_back)
    edge_all = two_part_dot(both, x_beside)
    height = rows + spare
    packed = beside_rows(rows)
    width = 2 * GROUP
    cells_x = LANES // GROUP
    slot = lax.broadcasted_iota(jnp.int32, (height, LANES), 1) // cells_x
    spot = lax.broadcasted_iota(jnp.int32, (packed, LANES), 1) // width
    for g in range(n_gx):
        first = g * cells_x // LANES * LANES
        tile = jnp.zeros((height, LANES), jnp.float32)
        for n in range(GROUP):
            piece = inner[n * height : (n + 1) * height, first : first + LANES]
            tile = jnp.where(slot == n, pltpu.roll(piece, (n - g) * cells_x % LANES, 1), tile)
        first = g * width // LANES * LANES
        beside = jnp.zeros((packed, LANES), jnp.float32)
        for m in range(3):
            piece = edge_all[m * packed : (m + 1) * packed, first : first + LANES]
            beside = jnp.where(
                spot == m, pltpu.roll(piece, (m - g) * width % LANES, 1), beside)
        for h in range(n_gy):
            out[g * n_gy + h, :rows, :] = tile[:rows]
            out[g * n_gy + h, rows:, :] = beside


class Halo:
    def __init__(self, row_first, row_second, col_first, col_second, west, east):
        even = is_even("gx")
        west[...] = jnp.where(even, row_second[...], row_first[...])
        east[...] = jnp.where(even, row_first[...], row_second[...])
        self.west, self.east = west, east
        even = is_even("gy")
        north = jnp.where(even, col_first[...], col_second[...])
        south = jnp.where(even, col_second[...], col_first[...])
        shape = north.shape
        lane = lax.broadcasted_iota(jnp.int32, shape, 1)
        self.last = shape[1] - 1
        self.at_first, self.at_last = lane == 0, lane == self.last
        self.columns = jnp.where(
            lane % 2 == 0, pltpu.roll(north, self.last, 1), pltpu.roll(south, 1, 1))

    def rows(self, c):
        return self.west[c : c + 1, :], self.east[c : c + 1, :]

    def column(self, c):
        return pltpu.roll(self.columns, self.last - 2 * c, 1)

    def move(self, slab, column, parts):
        centre, to_west, to_east, to_south, to_north = parts
        cells_x = column.shape[0]
        a = slab[PAD : PAD + cells_x]
        return (
            centre * a
            + to_west * slab[PAD - 1 : PAD - 1 + cells_x]
            + to_east * slab[PAD + 1 : PAD + 1 + cells_x]
            + to_south * jnp.where(self.at_first, column, pltpu.roll(a, 1, 1))
            + to_north * jnp.where(self.at_last, column, pltpu.roll(a, self.last, 1))
        )


def place(slab, a, rows):
    cells_x = a.shape[0]
    slab[PAD : PAD + cells_x] = a
    slab[PAD - 1 : PAD] = rows[0]
    slab[PAD + cells_x : PAD + cells_x + 1] = rows[1]


def wind_weights(u, v):
    neighbours = (
        0.1 + 0.1 * jnp.maximum(u, 0.0), 0.1 - 0.1 * jnp.minimum(u, 0.0),
        0.1 + 0.1 * jnp.maximum(v, 0.0), 0.1 - 0.1 * jnp.minimum(v, 0.0),
    )
    centre = 1.0 - (neighbours[0] + neighbours[1] + neighbours[2] + neighbours[3])
    return (centre,) + neighbours


def settling(parts):
    return (parts[0] - 0.3,) + parts[1:]


def above(l, level_total):
    return jnp.where(l + 1 < level_total, 0.3, 0.0).astype(jnp.float32)


def nudge_updates(shares, spread, spread_edges, y_table, nudged, cells_x):
    devices = shares.shape[0]
    rows = spread.shape[0] // devices
    packed = beside_rows(rows)
    width = 2 * GROUP
    for d in range(devices):
        spread[d * rows : (d + 1) * rows] = shares[d, :rows, :]
        edge = shares[d, rows:, :]
        for m in range(3):
            count = min(packed, rows - m * packed)
            if count > 0:
                moved = pltpu.roll(edge, -m * width % LANES, 1) if m else edge
                start = d * rows + m * packed
                spread_edges[start : start + count] = moved[:count]
    groups = nudged // GROUP
    spot_of = lax.broadcasted_iota(jnp.int32, (2 * KX, LANES), 1) // width
    edges = jnp.zeros((2 * KX, LANES), jnp.float32)
    for t in range(groups):
        piece = spread_edges[t * 2 * KX : (t + 1) * 2 * KX]
        edges = jnp.where(spot_of == t, pltpu.roll(piece, t * width, 1) if t else piece, edges)
    update_rows = columns_dot(edges, y_table)
    updates = []
    for t in range(groups):
        update = columns_dot(spread[t * 2 * KX : (t + 1) * 2 * KX], y_table)
        updates += [update[n * cells_x : (n + 1) * cells_x] for n in range(GROUP)]
    return updates, update_rows


def nudged_kernel(n_gy, step, last, level_count, level_total, shares, fields, row_first, row_second,
                  col_first, col_second, y_back, order_all, *rest):
    gx, gy = lax.axis_index("gx"), lax.axis_index("gy")
    cells_x, cells_y = fields.shape[1:]
    nudged = 3 * level_count
    if last:
        (plume, source, _, _, fields_all, plume_all, order, slabs, spread, spread_edges, west, east,
         sems, fields_out, plume_out, out_sems) = rest
        extra = []
    else:
        (owners_all, parent_all, x_fwd_all, y_fwd_all, fields_out, winds_out, modes,
         order, slabs, spread, spread_edges, west, east, sems,
         owners, parent, x_fwd, y_fwd, turned, work) = rest
        extra = [(owners_all, owners), (x_fwd_all.at[gx], x_fwd), (y_fwd_all.at[gy], y_fwd),
                 (parent_all.at[0, step + 1], parent)]
    copies = fetch_all(sems, [(order_all, order)] + extra)
    halo = Halo(row_first, row_second, col_first, col_second, west, east)
    updates, update_rows = nudge_updates(
        shares, spread, spread_edges, y_back[...], nudged, cells_x)
    copies[0].wait()
    level_at = [order[n] for n in range(level_count)]
    beside = []
    for k in range(nudged):
        f, n = k // level_count, k % level_count
        a = fields[k]
        before, after = halo.rows(f * level_total + n)
        place(slabs.at[k], a + updates[k][:, :cells_y],
              (before + update_rows[2 * k : 2 * k + 1, :cells_y],
               after + update_rows[2 * k + 1 : 2 * k + 2, :cells_y]))
        beside.append(updates[k][:, cells_y:])
    inner = slice(PAD, PAD + cells_x)
    results = [None] * nudged
    sent = []
    for n in range(level_count):
        u, v = slabs[n, inner], slabs[level_count + n, inner]
        parts = wind_weights(u, v)
        for f in range(3):
            k = f * level_count + n
            column = halo.column(f * level_total + n) + beside[k]
            results[k] = halo.move(slabs[k], column, parts)
            fields_out[k] = results[k]
        if not last:
            winds_out[n] = u
            winds_out[level_count + n] = v
            continue
        l = level_at[n]
        c = 3 * level_total + n
        place(slabs.at[nudged + n], plume[n], halo.rows(c))
        settled = halo.move(slabs[nudged + n], halo.column(c), settling(parts))
        plume_out[n] = settled + above(l, level_total) * plume[order[level_total + l + 1]] + source[l]
        pairs = [(fields_out.at[f * level_count + n], fields_all.at[f * level_total + l])
                 for f in range(3)] + [(plume_out.at[n], plume_all.at[l])]
        sent += fetch_all(out_sems.at[pl.ds(4 * n, 4)], pairs)
    if last:
        for copy in sent:
            copy.wait()
        return
    for copy in copies[1:]:
        copy.wait()
    emit_modes(results, parent, owners[step + 1] == gx * n_gy + gy, x_fwd[...], y_fwd[...], modes,
               turned, work)


def others_kernel(step, last, level_count, fields, plume, source, row_first, row_second, col_first,
                  col_second, order_all, *rest):
    level_total, cells_x, cells_y = plume.shape
    if last:
        fields_all, plume_all, order, slab, west, east, sems, fields_out, plume_out, out_sems = rest
    else:
        (done, winds, fields_out, plume_out, first, second, cols, order, slab, west, east,
         sems, plume_here, source_here) = rest
    copies = fetch_all(sems, [(order_all, order)])
    if not last:
        copies += fetch_all(
            sems.at[pl.ds(1, 2)], [(plume, plume_here), (source, source_here)])
        plume, source = plume_here, source_here
    halo = Halo(row_first, row_second, col_first, col_second, west, east)
    for copy in copies:
        copy.wait()
    level_at = [order[n] for n in range(level_total)]
    kept = level_total - level_count
    sent = []
    results = {}
    for n in range(level_count if last else 0, level_total):
        l = level_at[n]
        m = n - level_count
        if m < 0:
            parts = wind_weights(winds[n], winds[level_count + n])
        else:
            given = [fields[f * kept + m] for f in range(3)]
            parts = wind_weights(given[0], given[1])
            for f in range(3):
                c = f * level_total + n
                place(slab.at[4 * n + f], given[f], halo.rows(c))
                results[c] = halo.move(slab[4 * n + f], halo.column(c), parts)
                fields_out[f * kept + m] = results[c]
        c = 3 * level_total + n
        place(slab.at[4 * n + 3], plume[l] if step == 0 else plume[n], halo.rows(c))
        higher = (jnp.minimum(l + 1, level_total - 1) if step == 0 else order[level_total + l + 1])
        results[c] = (halo.move(slab[4 * n + 3], halo.column(c), settling(parts))
                      + above(l, level_total) * plume[higher] + source[l])
        plume_out[m if last else n] = results[c]
        if last:
            pairs = [(fields_out.at[f * kept + m], fields_all.at[f * level_total + l])
                     for f in range(3)] + [(plume_out.at[m], plume_all.at[l])]
            sent += fetch_all(out_sems.at[pl.ds(4 * m, 4)], pairs)
    for copy in sent:
        copy.wait()
    if not last:
        for f in range(3):
            for n in range(level_count):
                results[f * level_total + n] = done[f * level_count + n]
        emit_edges([results[c] for c in range(4 * level_total)], first, second, cols)


def exchange(axis, first, second):
    count = lax.axis_size(axis)
    received = []
    for start, data in ((0, first), (1, second)):
        pairs = [(i, i + 1) for i in range(start, count - 1, 2)]
        received.append(lax.ppermute(data, axis, pairs + [(b, a) for a, b in pairs]))
    return received


def local(tables, fields, levels, cuts, parent_modes, owners, plume, source):
    n_gx, n_gy = lax.axis_size("gx"), lax.axis_size("gy")
    devices = n_gx * n_gy
    level_total, cells_x, cells_y = plume.shape
    period = n_gx * cells_x * n_gy * cells_y
    nudged = 3 * levels.shape[0]
    field_rows = 3 * level_total
    total = field_rows + level_total
    rows = -(-(nudged // GROUP * 2 * KX) // devices)
    flat = fields.reshape(field_rows, cells_x, cells_y)
    cuts = cuts.reshape(-1)
    f32 = functools.partial(jax.ShapeDtypeStruct, dtype=jnp.float32)
    x_fwd, y_fwd, y_back, x_back, x_beside = (jnp.asarray(t) for t in tables)

    def vmem(*shape):
        return pltpu.VMEM(shape, jnp.float32)

    def table_space(table):
        return pltpu.VMEM(table.shape[1:], table.dtype)

    def limit(mib):
        return pltpu.CompilerParams(vmem_limit_bytes=mib * 1024 * 1024)

    count = levels.shape[0]
    kept = level_total - count
    mode_shape = f32((devices, 2 * rows, LANES))
    order_shape = (3 * level_total,)
    edge_shapes = [f32((total, cells_y)), f32((total, cells_y)), f32((cells_x, 2 * total))]
    levels_space = pltpu.SMEM(levels.shape, jnp.int32)
    owners_space = pltpu.SMEM(owners.shape, jnp.int32)
    order_space = pltpu.SMEM(order_shape, jnp.int32)
    rows_space = vmem(total, cells_y)
    mode_scratch = [vmem(nudged, 4 * KX * KX), table_space(x_fwd),
                    table_space(y_fwd), vmem(nudged, KX, LANES),
                    vmem(devices * rows, 2 * LANES)]
    nudged_scratch = [order_space, vmem(nudged + count, cells_x + 2 * PAD, cells_y),
                      vmem(devices * rows, LANES), vmem(devices * rows, LANES),
                      rows_space, rows_space, pltpu.SemaphoreType.DMA((5,))]
    others_scratch = [order_space, vmem(total, cells_x + 2 * PAD, cells_y), rows_space, rows_space,
                      pltpu.SemaphoreType.DMA((3,))]
    ash_space = vmem(level_total, cells_x, cells_y)

    def out_scratch(slabs):
        return [vmem(3 * slabs, cells_x, cells_y), vmem(slabs, cells_x, cells_y),
                pltpu.SemaphoreType.DMA((4 * slabs,))]

    modes = pl.pallas_call(
        functools.partial(first_kernel, n_gy, level_total),
        out_shape=mode_shape,
        in_specs=[HBM] * 6,
        out_specs=VMEM,
        scratch_shapes=[levels_space, owners_space, vmem(field_rows, cells_x, cells_y),
                        pltpu.SemaphoreType.DMA((6,))] + mode_scratch,
        compiler_params=limit(8),
        name="first_modes",
    )(*map(in_hbm, (levels, owners, flat, parent_modes, x_fwd, y_fwd)))
    field_shapes = [f32((3 * count, cells_x, cells_y)), f32((3 * kept, cells_x, cells_y))]
    *edges, weights, flat_nudged, others, y_back, order = pl.pallas_call(
        functools.partial(edge_kernel, n_gy, period),
        out_shape=edge_shapes
        + [f32((2 * rows, LANES))] + field_shapes
        + [jax.ShapeDtypeStruct(y_back.shape[1:], y_back.dtype),
           jax.ShapeDtypeStruct(order_shape, jnp.int32)],
        in_specs=[SMEM, SMEM, VMEM, VMEM, HBM],
        out_specs=[VMEM] * 7 + [SMEM],
        scratch_shapes=[pltpu.SemaphoreType.DMA((1,))],
        compiler_params=limit(8),
        name="edges",
    )(cuts, levels, flat, plume, in_hbm(y_back))
    order = in_hbm(order)
    flat = flat_nudged
    for step in range(STEPS):
        last = step == STEPS - 1
        to_first, to_second, cols = edges
        col_first, col_second = exchange("gy", cols, cols)
        parts = lax.all_to_all(modes, AXES, 0, 0, tiled=True)
        parts, col_first, col_second = lax.optimization_barrier((parts, col_first, col_second))
        share = pl.pallas_call(
            functools.partial(share_kernel, n_gx, n_gy),
            out_shape=f32((devices, rows + beside_rows(rows), LANES)),
            in_specs=[VMEM] * 4,
            out_specs=VMEM,
            compiler_params=limit(8),
            name="share_sum",
        )(weights, parts, x_back, x_beside)
        share, to_first, to_second = lax.optimization_barrier((share, to_first, to_second))
        row_first, row_second = exchange("gx", to_first, to_second)
        halo = [row_first, row_second, col_first, col_second]
        shares = lax.all_to_all(share, AXES, 0, 0, tiled=True)
        if last:
            final = pl.pallas_call(
                functools.partial(others_kernel, step, True, count),
                out_shape=[f32((field_rows, cells_x, cells_y)), f32(plume.shape)],
                in_specs=[VMEM] * 7 + [HBM],
                out_specs=[HBM] * 2,
                scratch_shapes=others_scratch + out_scratch(kept),
                compiler_params=limit(8),
                name="last_others",
            )(others, plume, source, *halo, order)
            flat, plume = pl.pallas_call(
                functools.partial(nudged_kernel, n_gy, step, True, count, level_total),
                out_shape=[f32((field_rows, cells_x, cells_y)), f32(plume.shape)],
                in_specs=[VMEM] * 7 + [HBM] + [VMEM] * 2 + [HBM] * 2,
                out_specs=[HBM] * 2,
                scratch_shapes=nudged_scratch + out_scratch(count),
                input_output_aliases={10: 0, 11: 1},
                compiler_params=limit(12),
                name="last_nudged",
            )(shares, flat, *halo, y_back, order, plume, source, *final)
        else:
            done, winds, modes = pl.pallas_call(
                functools.partial(nudged_kernel, n_gy, step, False, count, level_total),
                out_shape=[f32((nudged, cells_x, cells_y)), f32((2 * count, cells_x, cells_y)),
                           mode_shape],
                in_specs=[VMEM] * 7 + [HBM] * 5,
                out_specs=[VMEM] * 3,
                scratch_shapes=nudged_scratch + [owners_space] + mode_scratch,
                compiler_params=limit(12),
                name="inner_nudged",
            )(shares, flat, *halo, y_back, order,
              *map(in_hbm, (owners, parent_modes, x_fwd, y_fwd)))
            others, plume, *edges = pl.pallas_call(
                functools.partial(others_kernel, step, False, count),
                out_shape=[f32((3 * kept, cells_x, cells_y)), f32(plume.shape)] + edge_shapes,
                in_specs=[VMEM] + [HBM] * 2 + [VMEM] * 4 + [HBM] + [VMEM] * 2,
                out_specs=[VMEM] * 5,
                scratch_shapes=others_scratch + [ash_space, ash_space],
                compiler_params=limit(8),
                name="inner_others",
            )(others, in_hbm(plume), in_hbm(source), *halo, order, done, winds)
            flat = done
    return flat.reshape(fields.shape), plume


def solution(mesh):
    in_specs = (
        P(None, None, "gx", "gy"),
        P(),
        P(),
        P(("gx", "gy"), None, None, None),
        P(),
        P(None, "gx", "gy"),
        P(None, "gx", "gy"),
    )
    out_specs = (P(None, None, "gx", "gy"), P(None, "gx", "gy"))
    n_gx, n_gy = mesh.shape["gx"], mesh.shape["gy"]

    def whole(fields, levels, cuts, parent_modes, owners, plume, source):
        tables = build_tables(n_gx, n_gy, plume.shape[1] // n_gx, plume.shape[2] // n_gy)
        return jax.shard_map(
            functools.partial(local, tables), mesh=mesh, in_specs=in_specs, out_specs=out_specs,
            check_vma=False,
        )(fields, levels, cuts, parent_modes, owners, plume, source)

    return whole
```

```python
import functools
import math

import jax
import jax.numpy as jnp
import ml_dtypes
import numpy as np
from jax import lax
from jax.experimental import pallas as pl
from jax.experimental.pallas import tpu as pltpu
from jax.sharding import PartitionSpec as P

KX = 32
STEPS = 2
GROUP = 4
LANES = GROUP * KX
PAD = 8
VMEM = pl.BlockSpec(memory_space=pltpu.VMEM)
SMEM = pl.BlockSpec(memory_space=pltpu.SMEM)
HBM = pl.BlockSpec(memory_space=pltpu.HBM)
AXES = ("gx", "gy")


def in_hbm(array):
    return pltpu.with_memory_space_constraint(array, pltpu.HBM)


def wave_table(positions, period):
    wavenum = np.arange(KX)[:, None]
    phase = (wavenum * positions[None, :] % period) * (2.0 * math.pi / period)
    inside = (positions >= 0) & (positions < period)
    return np.concatenate([np.cos(phase), np.sin(phase)], axis=0) * inside[None, :]


def split(a):
    head = a.astype(jnp.bfloat16)
    return head, (a - head.astype(jnp.float32)).astype(jnp.bfloat16)


def split_table(table, axis, order):
    head = table.astype(ml_dtypes.bfloat16)
    rest = (table - head.astype(np.float64)).astype(ml_dtypes.bfloat16)
    return np.concatenate([head if part == "h" else rest for part in order], axis=axis)


def per_slab(table):
    return np.kron(np.eye(GROUP), table)


def build_tables(n_gx, n_gy, cells_x, cells_y):
    period_x, period_y = n_gx * cells_x, n_gy * cells_y
    scaling = 1.0 / math.sqrt(period_x * period_y)
    parity = [np.arange(p, 2 * KX, 2) for p in range(2)]
    x_fwd, y_fwd, y_back, inner, outer = [], [], [], [], []
    for g in range(n_gx):
        first = g * cells_x
        table = wave_table(first + np.arange(cells_x), period_x)
        x_fwd.append(split_table(
            np.concatenate([per_slab(table[rows].T) for rows in parity], axis=1), 0, "hhl"))
        beside = wave_table(np.array([first - 1, first + cells_x]), period_x)
        inner.append(np.concatenate([np.tile(table[rows], (GROUP, 1)) for rows in parity], axis=0))
        outer.append(np.concatenate([per_slab(beside[rows]) for rows in parity], axis=0))
    spare = -(2 * GROUP * n_gx) % LANES
    x_back = np.concatenate(inner, axis=1)
    x_beside = np.concatenate(outer + [np.zeros((2 * LANES, spare))], axis=1)
    for g in range(n_gy):
        first = g * cells_y
        table = wave_table(first + np.arange(cells_y), period_y)
        edge = np.zeros((2 * KX, cells_y))
        edge[:, [0, -1]] = wave_table(np.array([first - 1, first + cells_y]), period_y)
        y_fwd.append(split_table(table * scaling, 1, "hlh"))
        y_back.append(split_table(np.concatenate([table, edge], axis=1), 0, "hhl"))
    return [np.stack(x_fwd), np.stack(y_fwd), np.stack(y_back),
            split_table(x_back, 0, "hl"), split_table(x_beside, 0, "hl")]


def data_dot(a, table):
    head, rest = split(a)
    return jnp.dot(
        jnp.concatenate([head, rest, head], axis=1), table, preferred_element_type=jnp.float32
    )


def two_part_dot(a, table):
    head, rest = split(a)
    depth = a.shape[1]
    heads = jnp.dot(
        jnp.concatenate([head, rest], axis=0), table[:depth], preferred_element_type=jnp.float32)
    rests = jnp.dot(head, table[depth:], preferred_element_type=jnp.float32)
    return heads[: a.shape[0]] + heads[a.shape[0] :] + rests


def columns_dot(a, table):
    head, rest = split(a)
    stacked = jnp.concatenate([head, rest, head], axis=0)
    return lax.dot_general(
        stacked, table, (((0,), (0,)), ((), ())), preferred_element_type=jnp.float32)


def halvings(n_gx, n_gy):
    return [(axis, 1 << b) for axis, count in (("gx", n_gx), ("gy", n_gy))
            for b in range(count.bit_length() - 1)]


def share_places(n_gx, n_gy):
    places = []
    for device in range(n_gx * n_gy):
        index = {"gx": device // n_gy, "gy": device % n_gy}
        spot = 0
        for axis, bit in halvings(n_gx, n_gy):
            spot = 2 * spot + (index[axis] & bit > 0)
        places.append(spot)
    return places


def bit_of(axis, bit):
    return lax.rem(lax.axis_index(axis) // bit, 2)


def emit_modes(chosen, parent, is_owner, places, split_by, x_fwd, y_fwd, keep, send, modes, turned,
               work):
    devices, rows = modes.shape[0], modes.shape[1] // 2
    slabs = parent.shape[0]
    groups = slabs // GROUP
    head, rest = split(jnp.concatenate(chosen, axis=0))
    half = lax.dot_general(
        y_fwd, jnp.concatenate([head, head, rest], axis=1), (((1,), (1,)), ((), ())),
        preferred_element_type=jnp.float32)
    half = jnp.concatenate([half[:, t * LANES : (t + 1) * LANES] for t in range(groups)], axis=0)
    count = groups * 2 * KX
    work[0:count] = -data_dot(half, x_fwd)
    if count < devices * rows:
        work[count:] = jnp.zeros((devices * rows - count, 2 * LANES), jnp.float32)

    @pl.when(is_owner)
    def _():
        for i in range(KX):
            turned[:, i, :] = parent[:, i * LANES : (i + 1) * LANES]
        for t in range(groups):
            block = turned[t * GROUP : (t + 1) * GROUP].reshape(LANES, LANES).T
            span = slice(t * 2 * KX, (t + 1) * 2 * KX)
            for p in range(2):
                work[span, p * LANES : (p + 1) * LANES] += block[p * 2 * KX : (p + 1) * 2 * KX]

    for d in range(devices):
        for p in range(2):
            modes[places[d], p * rows : (p + 1) * rows, :] = work[
                d * rows : (d + 1) * rows, p * LANES : (p + 1) * LANES]
    count = devices // 2
    mine = bit_of(*split_by)
    keep[...] = modes[pl.ds(mine * count, count)]
    send[...] = modes[pl.ds((1 - mine) * count, count)]


def fold_kernel(split_by, kept, received, keep, send):
    count = keep.shape[0]
    mine = bit_of(*split_by)
    for out, start in ((keep, mine * count), (send, (1 - mine) * count)):
        for i in range(count):
            out[i] = kept[start + i] + received[start + i]


def fetch_all(sems, pairs):
    copies = [pltpu.make_async_copy(a, b, sems.at[i]) for i, (a, b) in enumerate(pairs)]
    for copy in copies:
        copy.start()
    return copies


def slab_of(levels, c, level_count, level_total):
    return (c // level_count) * level_total + levels[c % level_count]


def first_kernel(n_gy, level_total, places, split_by, levels_all, owners_all, fields_all, parent_all,
                 x_fwd_all, y_fwd_all, keep, send, levels, owners, fields, sems, parent, x_fwd, y_fwd,
                 modes, turned, work):
    gx, gy = lax.axis_index("gx"), lax.axis_index("gy")
    copies = fetch_all(sems, [
        (levels_all, levels), (owners_all, owners), (fields_all, fields),
        (x_fwd_all.at[gx], x_fwd), (y_fwd_all.at[gy], y_fwd), (parent_all.at[0, 0], parent)])
    for copy in copies:
        copy.wait()
    level_count = parent.shape[0] // 3
    emit_modes(
        [fields[slab_of(levels, c, level_count, level_total)] for c in range(parent.shape[0])],
        parent, owners[0] == gx * n_gy + gy, places, split_by, x_fwd[...], y_fwd[...], keep, send,
        modes, turned, work,
    )


def is_even(axis):
    return lax.rem(lax.axis_index(axis), 2) == 0


def edge_kernel(n_gy, period, cuts, levels, fields, plume, y_back_all, first, second, cols, weights,
                nudged, others, y_back, order, sems):
    copies = fetch_all(sems, [(y_back_all.at[lax.axis_index("gy")], y_back)])
    level_total = plume.shape[0]
    weights[...] = share_weights(n_gy, period, cuts, weights.shape)
    count = levels.shape[0]
    for n in range(count):
        order[n] = levels[n]
    spot = jnp.int32(count)
    for l in range(level_total):
        found = levels[0] == l
        for n in range(1, count):
            found = found | (levels[n] == l)
        order[spot] = jnp.int32(l)
        spot = spot + jnp.where(found, 0, 1)
    chosen = [order[n] for n in range(level_total)]
    for n in range(level_total, order.shape[0]):
        order[n] = jnp.int32(0)
    for n in range(level_total):
        order[level_total + chosen[n]] = jnp.int32(n)
    slabs = [fields[f * level_total + l] for f in range(3) for l in chosen]
    emit_edges(slabs + [plume[l] for l in chosen], first, second, cols)
    kept = level_total - count
    for c, a in enumerate(slabs):
        f, n = c // level_total, c % level_total
        if n < count:
            nudged[f * count + n] = a
        else:
            others[f * kept + n - count] = a
    for copy in copies:
        copy.wait()


def emit_edges(slabs, first, second, cols):
    even = is_even("gx")
    lane = lax.broadcasted_iota(jnp.int32, cols.shape, 1)
    acc = jnp.zeros(cols.shape, jnp.float32)
    for c, a in enumerate(slabs):
        west, east = a[:1], a[a.shape[0] - 1 :]
        first[c : c + 1, :] = jnp.where(even, east, west)
        second[c : c + 1, :] = jnp.where(even, west, east)
        acc = jnp.where(lane // 2 == c, pltpu.roll(a, 2 * c + 1, 1), acc)
    cols[...] = acc


def share_weights(n_gy, period, cuts, shape):
    rows = shape[0] // 2
    me = lax.axis_index("gx") * n_gy + lax.axis_index("gy")
    place = lax.broadcasted_iota(jnp.int32, shape, 0)
    lane = lax.broadcasted_iota(jnp.int32, shape, 1)
    p = (place >= rows).astype(jnp.int32)
    row = me * rows + place - p * rows
    k = 2 * (lane % KX) + p
    j = row % (2 * KX)
    slab = GROUP * (row // (2 * KX)) + lane // KX
    limit = jnp.zeros(shape, jnp.int32)
    for c in range(cuts.shape[0]):
        limit = jnp.where(slab == c, cuts[c], limit)
    keep = ((k % KX) < limit) & ((j % KX) < limit)
    factor = jnp.where(k == 0, 1.0, 2.0) * jnp.where(j == 0, 1.0, 2.0) * (1.0 / math.sqrt(period))
    return jnp.where(keep, factor, 0.0)


def beside_rows(rows):
    return -(-rows // 3)


def share_kernel(n_gx, n_gy, weights, kept, received, x_back, x_beside, out):
    rows = kept.shape[1] // 2
    mismatch = (kept[0] + received[0]) * weights[...]
    both = jnp.concatenate([mismatch[:rows], mismatch[rows:]], axis=1)
    spare = -rows % 16
    if spare:
        both = jnp.concatenate([both, jnp.zeros((spare, 2 * LANES), jnp.float32)], axis=0)
    slab_lane = lax.broadcasted_iota(jnp.int32, both.shape, 1) % LANES // KX
    chosen = [jnp.where(slab_lane == n, both, 0.0) for n in range(GROUP)]
    inner = two_part_dot(jnp.concatenate(chosen, axis=0), x_back)
    edge_all = two_part_dot(both, x_beside)
    height = rows + spare
    packed = beside_rows(rows)
    width = 2 * GROUP
    cells_x = LANES // GROUP
    slot = lax.broadcasted_iota(jnp.int32, (height, LANES), 1) // cells_x
    spot = lax.broadcasted_iota(jnp.int32, (packed, LANES), 1) // width
    for g in range(n_gx):
        first = g * cells_x // LANES * LANES
        tile = jnp.zeros((height, LANES), jnp.float32)
        for n in range(GROUP):
            piece = inner[n * height : (n + 1) * height, first : first + LANES]
            tile = jnp.where(slot == n, pltpu.roll(piece, (n - g) * cells_x % LANES, 1), tile)
        first = g * width // LANES * LANES
        beside = jnp.zeros((packed, LANES), jnp.float32)
        for m in range(3):
            piece = edge_all[m * packed : (m + 1) * packed, first : first + LANES]
            beside = jnp.where(
                spot == m, pltpu.roll(piece, (m - g) * width % LANES, 1), beside)
        for h in range(n_gy):
            out[g * n_gy + h, :rows, :] = tile[:rows]
            out[g * n_gy + h, rows:, :] = beside


class Halo:
    def __init__(self, row_first, row_second, col_first, col_second, west, east):
        even = is_even("gx")
        west[...] = jnp.where(even, row_second[...], row_first[...])
        east[...] = jnp.where(even, row_first[...], row_second[...])
        self.west, self.east = west, east
        even = is_even("gy")
        north = jnp.where(even, col_first[...], col_second[...])
        south = jnp.where(even, col_second[...], col_first[...])
        shape = north.shape
        lane = lax.broadcasted_iota(jnp.int32, shape, 1)
        self.last = shape[1] - 1
        self.at_first, self.at_last = lane == 0, lane == self.last
        self.columns = jnp.where(
            lane % 2 == 0, pltpu.roll(north, self.last, 1), pltpu.roll(south, 1, 1))

    def rows(self, c):
        return self.west[c : c + 1, :], self.east[c : c + 1, :]

    def column(self, c):
        return pltpu.roll(self.columns, self.last - 2 * c, 1)

    def move(self, slab, column, parts):
        centre, to_west, to_east, to_south, to_north = parts
        cells_x = column.shape[0]
        a = slab[PAD : PAD + cells_x]
        return (
            centre * a
            + to_west * slab[PAD - 1 : PAD - 1 + cells_x]
            + to_east * slab[PAD + 1 : PAD + 1 + cells_x]
            + to_south * jnp.where(self.at_first, column, pltpu.roll(a, 1, 1))
            + to_north * jnp.where(self.at_last, column, pltpu.roll(a, self.last, 1))
        )


def place(slab, a, rows):
    cells_x = a.shape[0]
    slab[PAD : PAD + cells_x] = a
    slab[PAD - 1 : PAD] = rows[0]
    slab[PAD + cells_x : PAD + cells_x + 1] = rows[1]


def wind_weights(u, v):
    neighbours = (
        0.1 + 0.1 * jnp.maximum(u, 0.0), 0.1 - 0.1 * jnp.minimum(u, 0.0),
        0.1 + 0.1 * jnp.maximum(v, 0.0), 0.1 - 0.1 * jnp.minimum(v, 0.0),
    )
    centre = 1.0 - (neighbours[0] + neighbours[1] + neighbours[2] + neighbours[3])
    return (centre,) + neighbours


def settling(parts):
    return (parts[0] - 0.3,) + parts[1:]


def above(l, level_total):
    return jnp.where(l + 1 < level_total, 0.3, 0.0).astype(jnp.float32)


def nudge_updates(shares, spread, spread_edges, y_table, nudged, cells_x):
    devices = shares.shape[0]
    rows = spread.shape[0] // devices
    packed = beside_rows(rows)
    width = 2 * GROUP
    for d in range(devices):
        spread[d * rows : (d + 1) * rows] = shares[d, :rows, :]
        edge = shares[d, rows:, :]
        for m in range(3):
            count = min(packed, rows - m * packed)
            if count > 0:
                moved = pltpu.roll(edge, -m * width % LANES, 1) if m else edge
                start = d * rows + m * packed
                spread_edges[start : start + count] = moved[:count]
    groups = nudged // GROUP
    spot_of = lax.broadcasted_iota(jnp.int32, (2 * KX, LANES), 1) // width
    edges = jnp.zeros((2 * KX, LANES), jnp.float32)
    for t in range(groups):
        piece = spread_edges[t * 2 * KX : (t + 1) * 2 * KX]
        edges = jnp.where(spot_of == t, pltpu.roll(piece, t * width, 1) if t else piece, edges)
    update_rows = columns_dot(edges, y_table)
    updates = []
    for t in range(groups):
        update = columns_dot(spread[t * 2 * KX : (t + 1) * 2 * KX], y_table)
        updates += [update[n * cells_x : (n + 1) * cells_x] for n in range(GROUP)]
    return updates, update_rows


def nudged_kernel(n_gy, step, last, level_count, level_total, places, split_by, shares, fields, row_first, row_second,
                  col_first, col_second, y_back, order_all, *rest):
    gx, gy = lax.axis_index("gx"), lax.axis_index("gy")
    cells_x, cells_y = fields.shape[1:]
    nudged = 3 * level_count
    if last:
        (plume, source, _, _, fields_all, plume_all, order, slabs, spread, spread_edges, west, east,
         sems, fields_out, plume_out, out_sems) = rest
        extra = []
    else:
        (owners_all, parent_all, x_fwd_all, y_fwd_all, fields_out, winds_out, keep, send,
         order, slabs, spread, spread_edges, west, east, sems,
         owners, parent, x_fwd, y_fwd, modes, turned, work) = rest
        extra = [(owners_all, owners), (x_fwd_all.at[gx], x_fwd), (y_fwd_all.at[gy], y_fwd),
                 (parent_all.at[0, step + 1], parent)]
    copies = fetch_all(sems, [(order_all, order)] + extra)
    halo = Halo(row_first, row_second, col_first, col_second, west, east)
    updates, update_rows = nudge_updates(
        shares, spread, spread_edges, y_back[...], nudged, cells_x)
    copies[0].wait()
    level_at = [order[n] for n in range(level_count)]
    beside = []
    for k in range(nudged):
        f, n = k // level_count, k % level_count
        a = fields[k]
        before, after = halo.rows(f * level_total + n)
        place(slabs.at[k], a + updates[k][:, :cells_y],
              (before + update_rows[2 * k : 2 * k + 1, :cells_y],
               after + update_rows[2 * k + 1 : 2 * k + 2, :cells_y]))
        beside.append(updates[k][:, cells_y:])
    inner = slice(PAD, PAD + cells_x)
    results = [None] * nudged
    sent = []
    for n in range(level_count):
        u, v = slabs[n, inner], slabs[level_count + n, inner]
        parts = wind_weights(u, v)
        for f in range(3):
            k = f * level_count + n
            column = halo.column(f * level_total + n) + beside[k]
            results[k] = halo.move(slabs[k], column, parts)
            fields_out[k] = results[k]
        if not last:
            winds_out[n] = u
            winds_out[level_count + n] = v
            continue
        l = level_at[n]
        c = 3 * level_total + n
        place(slabs.at[nudged + n], plume[n], halo.rows(c))
        settled = halo.move(slabs[nudged + n], halo.column(c), settling(parts))
        plume_out[n] = settled + above(l, level_total) * plume[order[level_total + l + 1]] + source[l]
        pairs = [(fields_out.at[f * level_count + n], fields_all.at[f * level_total + l])
                 for f in range(3)] + [(plume_out.at[n], plume_all.at[l])]
        sent += fetch_all(out_sems.at[pl.ds(4 * n, 4)], pairs)
    if last:
        for copy in sent:
            copy.wait()
        return
    for copy in copies[1:]:
        copy.wait()
    emit_modes(results, parent, owners[step + 1] == gx * n_gy + gy, places, split_by, x_fwd[...],
               y_fwd[...], keep, send, modes, turned, work)


def others_kernel(step, last, level_count, fields, plume, source, row_first, row_second, col_first,
                  col_second, order_all, *rest):
    level_total, cells_x, cells_y = plume.shape
    if last:
        fields_all, plume_all, order, slab, west, east, sems, fields_out, plume_out, out_sems = rest
    else:
        (done, winds, fields_out, plume_out, first, second, cols, order, slab, west, east,
         sems, plume_here, source_here) = rest
    copies = fetch_all(sems, [(order_all, order)])
    if not last:
        copies += fetch_all(
            sems.at[pl.ds(1, 2)], [(plume, plume_here), (source, source_here)])
        plume, source = plume_here, source_here
    halo = Halo(row_first, row_second, col_first, col_second, west, east)
    for copy in copies:
        copy.wait()
    level_at = [order[n] for n in range(level_total)]
    kept = level_total - level_count
    sent = []
    results = {}
    for n in range(level_count if last else 0, level_total):
        l = level_at[n]
        m = n - level_count
        if m < 0:
            parts = wind_weights(winds[n], winds[level_count + n])
        else:
            given = [fields[f * kept + m] for f in range(3)]
            parts = wind_weights(given[0], given[1])
            for f in range(3):
                c = f * level_total + n
                place(slab.at[4 * n + f], given[f], halo.rows(c))
                results[c] = halo.move(slab[4 * n + f], halo.column(c), parts)
                fields_out[f * kept + m] = results[c]
        c = 3 * level_total + n
        place(slab.at[4 * n + 3], plume[l] if step == 0 else plume[n], halo.rows(c))
        higher = (jnp.minimum(l + 1, level_total - 1) if step == 0 else order[level_total + l + 1])
        results[c] = (halo.move(slab[4 * n + 3], halo.column(c), settling(parts))
                      + above(l, level_total) * plume[higher] + source[l])
        plume_out[m if last else n] = results[c]
        if last:
            pairs = [(fields_out.at[f * kept + m], fields_all.at[f * level_total + l])
                     for f in range(3)] + [(plume_out.at[m], plume_all.at[l])]
            sent += fetch_all(out_sems.at[pl.ds(4 * m, 4)], pairs)
    for copy in sent:
        copy.wait()
    if not last:
        for f in range(3):
            for n in range(level_count):
                results[f * level_total + n] = done[f * level_count + n]
        emit_edges([results[c] for c in range(4 * level_total)], first, second, cols)


def exchange(axis, first, second):
    count = lax.axis_size(axis)
    received = []
    for start, data in ((0, first), (1, second)):
        pairs = [(i, i + 1) for i in range(start, count - 1, 2)]
        received.append(lax.ppermute(data, axis, pairs + [(b, a) for a, b in pairs]))
    return received


def local(tables, fields, levels, cuts, parent_modes, owners, plume, source):
    n_gx, n_gy = lax.axis_size("gx"), lax.axis_size("gy")
    devices = n_gx * n_gy
    level_total, cells_x, cells_y = plume.shape
    period = n_gx * cells_x * n_gy * cells_y
    nudged = 3 * levels.shape[0]
    field_rows = 3 * level_total
    total = field_rows + level_total
    rows = -(-(nudged // GROUP * 2 * KX) // devices)
    flat = fields.reshape(field_rows, cells_x, cells_y)
    cuts = cuts.reshape(-1)
    f32 = functools.partial(jax.ShapeDtypeStruct, dtype=jnp.float32)
    x_fwd, y_fwd, y_back, x_back, x_beside = (jnp.asarray(t) for t in tables)

    def vmem(*shape):
        return pltpu.VMEM(shape, jnp.float32)

    def table_space(table):
        return pltpu.VMEM(table.shape[1:], table.dtype)

    def limit(mib):
        return pltpu.CompilerParams(vmem_limit_bytes=mib * 1024 * 1024)

    count = levels.shape[0]
    kept = level_total - count
    half_shapes = [f32((devices // 2, 2 * rows, LANES))] * 2
    steps = halvings(n_gx, n_gy)
    places = share_places(n_gx, n_gy)
    order_shape = (3 * level_total,)
    edge_shapes = [f32((total, cells_y)), f32((total, cells_y)), f32((cells_x, 2 * total))]
    levels_space = pltpu.SMEM(levels.shape, jnp.int32)
    owners_space = pltpu.SMEM(owners.shape, jnp.int32)
    order_space = pltpu.SMEM(order_shape, jnp.int32)
    rows_space = vmem(total, cells_y)
    mode_scratch = [vmem(nudged, 4 * KX * KX), table_space(x_fwd),
                    table_space(y_fwd), vmem(devices, 2 * rows, LANES), vmem(nudged, KX, LANES),
                    vmem(devices * rows, 2 * LANES)]
    nudged_scratch = [order_space, vmem(nudged + count, cells_x + 2 * PAD, cells_y),
                      vmem(devices * rows, LANES), vmem(devices * rows, LANES),
                      rows_space, rows_space, pltpu.SemaphoreType.DMA((5,))]
    others_scratch = [order_space, vmem(total, cells_x + 2 * PAD, cells_y), rows_space, rows_space,
                      pltpu.SemaphoreType.DMA((3,))]
    ash_space = vmem(level_total, cells_x, cells_y)

    def out_scratch(slabs):
        return [vmem(3 * slabs, cells_x, cells_y), vmem(slabs, cells_x, cells_y),
                pltpu.SemaphoreType.DMA((4 * slabs,))]

    keep, send = pl.pallas_call(
        functools.partial(first_kernel, n_gy, level_total, places, steps[0]),
        out_shape=half_shapes,
        in_specs=[HBM] * 6,
        out_specs=[VMEM] * 2,
        scratch_shapes=[levels_space, owners_space, vmem(field_rows, cells_x, cells_y),
                        pltpu.SemaphoreType.DMA((6,))] + mode_scratch,
        compiler_params=limit(8),
        name="first_modes",
    )(*map(in_hbm, (levels, owners, flat, parent_modes, x_fwd, y_fwd)))
    field_shapes = [f32((3 * count, cells_x, cells_y)), f32((3 * kept, cells_x, cells_y))]
    *edges, weights, flat_nudged, others, y_back, order = pl.pallas_call(
        functools.partial(edge_kernel, n_gy, period),
        out_shape=edge_shapes
        + [f32((2 * rows, LANES))] + field_shapes
        + [jax.ShapeDtypeStruct(y_back.shape[1:], y_back.dtype),
           jax.ShapeDtypeStruct(order_shape, jnp.int32)],
        in_specs=[SMEM, SMEM, VMEM, VMEM, HBM],
        out_specs=[VMEM] * 7 + [SMEM],
        scratch_shapes=[pltpu.SemaphoreType.DMA((1,))],
        compiler_params=limit(8),
        name="edges",
    )(cuts, levels, flat, plume, in_hbm(y_back))
    order = in_hbm(order)
    flat = flat_nudged
    for step in range(STEPS):
        last = step == STEPS - 1
        to_first, to_second, cols = edges
        for n, (axis, bit) in enumerate(steps):
            received = lax.ppermute(
                send, axis, [(i, i ^ bit) for i in range(lax.axis_size(axis))])
            if n + 1 < len(steps):
                half = f32((keep.shape[0] // 2,) + keep.shape[1:])
                keep, send = pl.pallas_call(
                    functools.partial(fold_kernel, steps[n + 1]),
                    out_shape=[half] * 2,
                    in_specs=[VMEM] * 2,
                    out_specs=[VMEM] * 2,
                    compiler_params=limit(4),
                    name="fold",
                )(keep, received)
            if n == 0:
                send, cols = lax.optimization_barrier((send, cols))
                col_first, col_second = exchange("gy", cols, cols)
        received, col_first, col_second = lax.optimization_barrier(
            (received, col_first, col_second))
        share = pl.pallas_call(
            functools.partial(share_kernel, n_gx, n_gy),
            out_shape=f32((devices, rows + beside_rows(rows), LANES)),
            in_specs=[VMEM] * 5,
            out_specs=VMEM,
            compiler_params=limit(8),
            name="share_sum",
        )(weights, keep, received, x_back, x_beside)
        share, to_first, to_second = lax.optimization_barrier((share, to_first, to_second))
        row_first, row_second = exchange("gx", to_first, to_second)
        halo = [row_first, row_second, col_first, col_second]
        shares = lax.all_to_all(share, AXES, 0, 0, tiled=True)
        if last:
            final = pl.pallas_call(
                functools.partial(others_kernel, step, True, count),
                out_shape=[f32((field_rows, cells_x, cells_y)), f32(plume.shape)],
                in_specs=[VMEM] * 7 + [HBM],
                out_specs=[HBM] * 2,
                scratch_shapes=others_scratch + out_scratch(kept),
                compiler_params=limit(8),
                name="last_others",
            )(others, plume, source, *halo, order)
            flat, plume = pl.pallas_call(
                functools.partial(nudged_kernel, n_gy, step, True, count, level_total, None, None),
                out_shape=[f32((field_rows, cells_x, cells_y)), f32(plume.shape)],
                in_specs=[VMEM] * 7 + [HBM] + [VMEM] * 2 + [HBM] * 2,
                out_specs=[HBM] * 2,
                scratch_shapes=nudged_scratch + out_scratch(count),
                input_output_aliases={10: 0, 11: 1},
                compiler_params=limit(12),
                name="last_nudged",
            )(shares, flat, *halo, y_back, order, plume, source, *final)
        else:
            done, winds, keep, send = pl.pallas_call(
                functools.partial(nudged_kernel, n_gy, step, False, count, level_total, places,
                                  steps[0]),
                out_shape=[f32((nudged, cells_x, cells_y)), f32((2 * count, cells_x, cells_y))]
                + half_shapes,
                in_specs=[VMEM] * 7 + [HBM] * 5,
                out_specs=[VMEM] * 4,
                scratch_shapes=nudged_scratch + [owners_space] + mode_scratch,
                compiler_params=limit(12),
                name="inner_nudged",
            )(shares, flat, *halo, y_back, order,
              *map(in_hbm, (owners, parent_modes, x_fwd, y_fwd)))
            others, plume, *edges = pl.pallas_call(
                functools.partial(others_kernel, step, False, count),
                out_shape=[f32((3 * kept, cells_x, cells_y)), f32(plume.shape)] + edge_shapes,
                in_specs=[VMEM] + [HBM] * 2 + [VMEM] * 4 + [HBM] + [VMEM] * 2,
                out_specs=[VMEM] * 5,
                scratch_shapes=others_scratch + [ash_space, ash_space],
                compiler_params=limit(8),
                name="inner_others",
            )(others, in_hbm(plume), in_hbm(source), *halo, order, done, winds)
            flat = done
    return flat.reshape(fields.shape), plume


def solution(mesh):
    in_specs = (
        P(None, None, "gx", "gy"),
        P(),
        P(),
        P(("gx", "gy"), None, None, None),
        P(),
        P(None, "gx", "gy"),
        P(None, "gx", "gy"),
    )
    out_specs = (P(None, None, "gx", "gy"), P(None, "gx", "gy"))
    n_gx, n_gy = mesh.shape["gx"], mesh.shape["gy"]

    def whole(fields, levels, cuts, parent_modes, owners, plume, source):
        tables = build_tables(n_gx, n_gy, plume.shape[1] // n_gx, plume.shape[2] // n_gy)
        return jax.shard_map(
            functools.partial(local, tables), mesh=mesh, in_specs=in_specs, out_specs=out_specs,
            check_vma=False,
        )(fields, levels, cuts, parent_modes, owners, plume, source)

    return whole
```

```python
import functools
import math

import jax
import jax.numpy as jnp
import ml_dtypes
import numpy as np
from jax import lax
from jax.experimental import pallas as pl
from jax.experimental.pallas import tpu as pltpu
from jax.sharding import PartitionSpec as P

KX = 32
STEPS = 2
GROUP = 4
LANES = GROUP * KX
PAD = 8
VMEM = pl.BlockSpec(memory_space=pltpu.VMEM)
SMEM = pl.BlockSpec(memory_space=pltpu.SMEM)
HBM = pl.BlockSpec(memory_space=pltpu.HBM)
AXES = ("gx", "gy")


def in_hbm(array):
    return pltpu.with_memory_space_constraint(array, pltpu.HBM)


def wave_table(positions, period):
    wavenum = np.arange(KX)[:, None]
    phase = (wavenum * positions[None, :] % period) * (2.0 * math.pi / period)
    inside = (positions >= 0) & (positions < period)
    return np.concatenate([np.cos(phase), np.sin(phase)], axis=0) * inside[None, :]


def split(a):
    head = a.astype(jnp.bfloat16)
    return head, (a - head.astype(jnp.float32)).astype(jnp.bfloat16)


def split_table(table, axis, order):
    head = table.astype(ml_dtypes.bfloat16)
    rest = (table - head.astype(np.float64)).astype(ml_dtypes.bfloat16)
    return np.concatenate([head if part == "h" else rest for part in order], axis=axis)


def per_slab(table):
    return np.kron(np.eye(GROUP), table)


def build_tables(n_gx, n_gy, cells_x, cells_y):
    period_x, period_y = n_gx * cells_x, n_gy * cells_y
    scaling = 1.0 / math.sqrt(period_x * period_y)
    parity = [np.arange(p, 2 * KX, 2) for p in range(2)]
    x_fwd, y_fwd, y_back, inner, outer = [], [], [], [], []
    for g in range(n_gx):
        first = g * cells_x
        table = wave_table(first + np.arange(cells_x), period_x)
        x_fwd.append(split_table(
            np.concatenate([per_slab(table[rows].T) for rows in parity], axis=1), 0, "hhl"))
        beside = wave_table(np.array([first - 1, first + cells_x]), period_x)
        inner.append(np.concatenate([np.tile(table[rows], (GROUP, 1)) for rows in parity], axis=0))
        outer.append(np.concatenate([per_slab(beside[rows]) for rows in parity], axis=0))
    spare = -(2 * GROUP * n_gx) % LANES
    x_back = np.concatenate(inner, axis=1)
    x_beside = np.concatenate(outer + [np.zeros((2 * LANES, spare))], axis=1)
    for g in range(n_gy):
        first = g * cells_y
        table = wave_table(first + np.arange(cells_y), period_y)
        edge = np.zeros((2 * KX, cells_y))
        edge[:, [0, -1]] = wave_table(np.array([first - 1, first + cells_y]), period_y)
        y_fwd.append(split_table(table * scaling, 1, "hlh"))
        y_back.append(split_table(np.concatenate([table, edge], axis=1), 0, "hhl"))
    return [np.stack(x_fwd), np.stack(y_fwd), np.stack(y_back),
            split_table(x_back, 0, "hl"), split_table(x_beside, 0, "hl")]


def data_dot(a, table):
    head, rest = split(a)
    return jnp.dot(
        jnp.concatenate([head, rest, head], axis=1), table, preferred_element_type=jnp.float32
    )


def two_part_dot(a, table):
    head, rest = split(a)
    depth = a.shape[1]
    heads = jnp.dot(
        jnp.concatenate([head, rest], axis=0), table[:depth], preferred_element_type=jnp.float32)
    rests = jnp.dot(head, table[depth:], preferred_element_type=jnp.float32)
    return heads[: a.shape[0]] + heads[a.shape[0] :] + rests


def columns_dot(a, table):
    head, rest = split(a)
    stacked = jnp.concatenate([head, rest, head], axis=0)
    return lax.dot_general(
        stacked, table, (((0,), (0,)), ((), ())), preferred_element_type=jnp.float32)


def core():
    return lax.rem(lax.axis_index("gx"), 2)


def share_places(n_gx, n_gy):
    return [(d // n_gy % 2 * (n_gx // 2) + d // n_gy // 2) * n_gy + d % n_gy
            for d in range(n_gx * n_gy)]


def emit_modes(chosen, parent, is_owner, places, x_fwd, y_fwd, keep, send, modes, turned, work):
    devices, rows = modes.shape[0], modes.shape[1] // 2
    slabs = parent.shape[0]
    groups = slabs // GROUP
    head, rest = split(jnp.concatenate(chosen, axis=0))
    half = lax.dot_general(
        y_fwd, jnp.concatenate([head, head, rest], axis=1), (((1,), (1,)), ((), ())),
        preferred_element_type=jnp.float32)
    half = jnp.concatenate([half[:, t * LANES : (t + 1) * LANES] for t in range(groups)], axis=0)
    count = groups * 2 * KX
    work[0:count] = -data_dot(half, x_fwd)
    if count < devices * rows:
        work[count:] = jnp.zeros((devices * rows - count, 2 * LANES), jnp.float32)

    @pl.when(is_owner)
    def _():
        for i in range(KX):
            turned[:, i, :] = parent[:, i * LANES : (i + 1) * LANES]
        for t in range(groups):
            block = turned[t * GROUP : (t + 1) * GROUP].reshape(LANES, LANES).T
            span = slice(t * 2 * KX, (t + 1) * 2 * KX)
            for p in range(2):
                work[span, p * LANES : (p + 1) * LANES] += block[p * 2 * KX : (p + 1) * 2 * KX]

    for d in range(devices):
        for p in range(2):
            modes[places[d], p * rows : (p + 1) * rows, :] = work[
                d * rows : (d + 1) * rows, p * LANES : (p + 1) * LANES]
    count = devices // 2
    mine = core()
    keep[...] = modes[pl.ds(mine * count, count)]
    send[...] = modes[pl.ds((1 - mine) * count, count)]


def add_kernel(kept, received, out):
    out[...] = kept[...] + received[...]


def fetch_all(sems, pairs):
    copies = [pltpu.make_async_copy(a, b, sems.at[i]) for i, (a, b) in enumerate(pairs)]
    for copy in copies:
        copy.start()
    return copies


def slab_of(levels, c, level_count, level_total):
    return (c // level_count) * level_total + levels[c % level_count]


def first_kernel(n_gy, level_total, places, levels_all, owners_all, fields_all, parent_all,
                 x_fwd_all, y_fwd_all, keep, send, levels, owners, fields, sems, parent, x_fwd, y_fwd,
                 modes, turned, work):
    gx, gy = lax.axis_index("gx"), lax.axis_index("gy")
    copies = fetch_all(sems, [
        (levels_all, levels), (owners_all, owners), (fields_all, fields),
        (x_fwd_all.at[gx], x_fwd), (y_fwd_all.at[gy], y_fwd), (parent_all.at[0, 0], parent)])
    for copy in copies:
        copy.wait()
    level_count = parent.shape[0] // 3
    emit_modes(
        [fields[slab_of(levels, c, level_count, level_total)] for c in range(parent.shape[0])],
        parent, owners[0] == gx * n_gy + gy, places, x_fwd[...], y_fwd[...], keep, send,
        modes, turned, work,
    )


def is_even(axis):
    return lax.rem(lax.axis_index(axis), 2) == 0


def edge_kernel(n_gy, period, cuts, levels, fields, plume, y_back_all, first, second, cols, weights,
                nudged, others, y_back, order, sems):
    copies = fetch_all(sems, [(y_back_all.at[lax.axis_index("gy")], y_back)])
    level_total = plume.shape[0]
    weights[...] = share_weights(n_gy, period, cuts, weights.shape)
    count = levels.shape[0]
    for n in range(count):
        order[n] = levels[n]
    spot = jnp.int32(count)
    for l in range(level_total):
        found = levels[0] == l
        for n in range(1, count):
            found = found | (levels[n] == l)
        order[spot] = jnp.int32(l)
        spot = spot + jnp.where(found, 0, 1)
    chosen = [order[n] for n in range(level_total)]
    for n in range(level_total, order.shape[0]):
        order[n] = jnp.int32(0)
    for n in range(level_total):
        order[level_total + chosen[n]] = jnp.int32(n)
    slabs = [fields[f * level_total + l] for f in range(3) for l in chosen]
    emit_edges(slabs + [plume[l] for l in chosen], first, second, cols)
    kept = level_total - count
    for c, a in enumerate(slabs):
        f, n = c // level_total, c % level_total
        if n < count:
            nudged[f * count + n] = a
        else:
            others[f * kept + n - count] = a
    for copy in copies:
        copy.wait()


def emit_edges(slabs, first, second, cols):
    even = is_even("gx")
    lane = lax.broadcasted_iota(jnp.int32, cols.shape, 1)
    acc = jnp.zeros(cols.shape, jnp.float32)
    for c, a in enumerate(slabs):
        west, east = a[:1], a[a.shape[0] - 1 :]
        first[c : c + 1, :] = jnp.where(even, east, west)
        second[c : c + 1, :] = jnp.where(even, west, east)
        acc = jnp.where(lane // 2 == c, pltpu.roll(a, 2 * c + 1, 1), acc)
    cols[...] = acc


def share_weights(n_gy, period, cuts, shape):
    rows = shape[0] // 2
    me = lax.axis_index("gx") * n_gy + lax.axis_index("gy")
    place = lax.broadcasted_iota(jnp.int32, shape, 0)
    lane = lax.broadcasted_iota(jnp.int32, shape, 1)
    p = (place >= rows).astype(jnp.int32)
    row = me * rows + place - p * rows
    k = 2 * (lane % KX) + p
    j = row % (2 * KX)
    slab = GROUP * (row // (2 * KX)) + lane // KX
    limit = jnp.zeros(shape, jnp.int32)
    for c in range(cuts.shape[0]):
        limit = jnp.where(slab == c, cuts[c], limit)
    keep = ((k % KX) < limit) & ((j % KX) < limit)
    factor = jnp.where(k == 0, 1.0, 2.0) * jnp.where(j == 0, 1.0, 2.0) * (1.0 / math.sqrt(period))
    return jnp.where(keep, factor, 0.0)


def beside_rows(rows):
    return -(-rows // 3)


def share_kernel(n_gx, n_gy, weights, parts, x_back, x_beside, out):
    rows = parts.shape[1] // 2
    total = parts[0]
    for d in range(1, parts.shape[0]):
        total = total + parts[d]
    mismatch = total * weights[...]
    both = jnp.concatenate([mismatch[:rows], mismatch[rows:]], axis=1)
    spare = -rows % 16
    if spare:
        both = jnp.concatenate([both, jnp.zeros((spare, 2 * LANES), jnp.float32)], axis=0)
    slab_lane = lax.broadcasted_iota(jnp.int32, both.shape, 1) % LANES // KX
    chosen = [jnp.where(slab_lane == n, both, 0.0) for n in range(GROUP)]
    inner = two_part_dot(jnp.concatenate(chosen, axis=0), x_back)
    edge_all = two_part_dot(both, x_beside)
    height = rows + spare
    packed = beside_rows(rows)
    width = 2 * GROUP
    cells_x = LANES // GROUP
    slot = lax.broadcasted_iota(jnp.int32, (height, LANES), 1) // cells_x
    spot = lax.broadcasted_iota(jnp.int32, (packed, LANES), 1) // width
    for g in range(n_gx):
        first = g * cells_x // LANES * LANES
        tile = jnp.zeros((height, LANES), jnp.float32)
        for n in range(GROUP):
            piece = inner[n * height : (n + 1) * height, first : first + LANES]
            tile = jnp.where(slot == n, pltpu.roll(piece, (n - g) * cells_x % LANES, 1), tile)
        first = g * width // LANES * LANES
        beside = jnp.zeros((packed, LANES), jnp.float32)
        for m in range(3):
            piece = edge_all[m * packed : (m + 1) * packed, first : first + LANES]
            beside = jnp.where(
                spot == m, pltpu.roll(piece, (m - g) * width % LANES, 1), beside)
        for h in range(n_gy):
            out[g * n_gy + h, :rows, :] = tile[:rows]
            out[g * n_gy + h, rows:, :] = beside


class Halo:
    def __init__(self, row_first, row_second, col_first, col_second, west, east):
        even = is_even("gx")
        west[...] = jnp.where(even, row_second[...], row_first[...])
        east[...] = jnp.where(even, row_first[...], row_second[...])
        self.west, self.east = west, east
        even = is_even("gy")
        north = jnp.where(even, col_first[...], col_second[...])
        south = jnp.where(even, col_second[...], col_first[...])
        shape = north.shape
        lane = lax.broadcasted_iota(jnp.int32, shape, 1)
        self.last = shape[1] - 1
        self.at_first, self.at_last = lane == 0, lane == self.last
        self.columns = jnp.where(
            lane % 2 == 0, pltpu.roll(north, self.last, 1), pltpu.roll(south, 1, 1))

    def rows(self, c):
        return self.west[c : c + 1, :], self.east[c : c + 1, :]

    def column(self, c):
        return pltpu.roll(self.columns, self.last - 2 * c, 1)

    def move(self, slab, column, parts):
        centre, to_west, to_east, to_south, to_north = parts
        cells_x = column.shape[0]
        a = slab[PAD : PAD + cells_x]
        return (
            centre * a
            + to_west * slab[PAD - 1 : PAD - 1 + cells_x]
            + to_east * slab[PAD + 1 : PAD + 1 + cells_x]
            + to_south * jnp.where(self.at_first, column, pltpu.roll(a, 1, 1))
            + to_north * jnp.where(self.at_last, column, pltpu.roll(a, self.last, 1))
        )


def place(slab, a, rows):
    cells_x = a.shape[0]
    slab[PAD : PAD + cells_x] = a
    slab[PAD - 1 : PAD] = rows[0]
    slab[PAD + cells_x : PAD + cells_x + 1] = rows[1]


def wind_weights(u, v):
    neighbours = (
        0.1 + 0.1 * jnp.maximum(u, 0.0), 0.1 - 0.1 * jnp.minimum(u, 0.0),
        0.1 + 0.1 * jnp.maximum(v, 0.0), 0.1 - 0.1 * jnp.minimum(v, 0.0),
    )
    centre = 1.0 - (neighbours[0] + neighbours[1] + neighbours[2] + neighbours[3])
    return (centre,) + neighbours


def settling(parts):
    return (parts[0] - 0.3,) + parts[1:]


def above(l, level_total):
    return jnp.where(l + 1 < level_total, 0.3, 0.0).astype(jnp.float32)


def nudge_updates(shares, spread, spread_edges, y_table, nudged, cells_x):
    devices = shares.shape[0]
    rows = spread.shape[0] // devices
    packed = beside_rows(rows)
    width = 2 * GROUP
    for d in range(devices):
        spread[d * rows : (d + 1) * rows] = shares[d, :rows, :]
        edge = shares[d, rows:, :]
        for m in range(3):
            count = min(packed, rows - m * packed)
            if count > 0:
                moved = pltpu.roll(edge, -m * width % LANES, 1) if m else edge
                start = d * rows + m * packed
                spread_edges[start : start + count] = moved[:count]
    groups = nudged // GROUP
    spot_of = lax.broadcasted_iota(jnp.int32, (2 * KX, LANES), 1) // width
    edges = jnp.zeros((2 * KX, LANES), jnp.float32)
    for t in range(groups):
        piece = spread_edges[t * 2 * KX : (t + 1) * 2 * KX]
        edges = jnp.where(spot_of == t, pltpu.roll(piece, t * width, 1) if t else piece, edges)
    update_rows = columns_dot(edges, y_table)
    updates = []
    for t in range(groups):
        update = columns_dot(spread[t * 2 * KX : (t + 1) * 2 * KX], y_table)
        updates += [update[n * cells_x : (n + 1) * cells_x] for n in range(GROUP)]
    return updates, update_rows


def nudged_kernel(n_gy, step, last, level_count, level_total, places, shares, fields, row_first, row_second,
                  col_first, col_second, y_back, order_all, *rest):
    gx, gy = lax.axis_index("gx"), lax.axis_index("gy")
    cells_x, cells_y = fields.shape[1:]
    nudged = 3 * level_count
    if last:
        (plume, source, _, _, fields_all, plume_all, order, slabs, spread, spread_edges, west, east,
         sems, fields_out, plume_out, out_sems) = rest
        extra = []
    else:
        (owners_all, parent_all, x_fwd_all, y_fwd_all, fields_out, winds_out, keep, send,
         order, slabs, spread, spread_edges, west, east, sems,
         owners, parent, x_fwd, y_fwd, modes, turned, work) = rest
        extra = [(owners_all, owners), (x_fwd_all.at[gx], x_fwd), (y_fwd_all.at[gy], y_fwd),
                 (parent_all.at[0, step + 1], parent)]
    copies = fetch_all(sems, [(order_all, order)] + extra)
    halo = Halo(row_first, row_second, col_first, col_second, west, east)
    updates, update_rows = nudge_updates(
        shares, spread, spread_edges, y_back[...], nudged, cells_x)
    copies[0].wait()
    level_at = [order[n] for n in range(level_count)]
    beside = []
    for k in range(nudged):
        f, n = k // level_count, k % level_count
        a = fields[k]
        before, after = halo.rows(f * level_total + n)
        place(slabs.at[k], a + updates[k][:, :cells_y],
              (before + update_rows[2 * k : 2 * k + 1, :cells_y],
               after + update_rows[2 * k + 1 : 2 * k + 2, :cells_y]))
        beside.append(updates[k][:, cells_y:])
    inner = slice(PAD, PAD + cells_x)
    results = [None] * nudged
    sent = []
    for n in range(level_count):
        u, v = slabs[n, inner], slabs[level_count + n, inner]
        parts = wind_weights(u, v)
        for f in range(3):
            k = f * level_count + n
            column = halo.column(f * level_total + n) + beside[k]
            results[k] = halo.move(slabs[k], column, parts)
            fields_out[k] = results[k]
        if not last:
            winds_out[n] = u
            winds_out[level_count + n] = v
            continue
        l = level_at[n]
        c = 3 * level_total + n
        place(slabs.at[nudged + n], plume[n], halo.rows(c))
        settled = halo.move(slabs[nudged + n], halo.column(c), settling(parts))
        plume_out[n] = settled + above(l, level_total) * plume[order[level_total + l + 1]] + source[l]
        pairs = [(fields_out.at[f * level_count + n], fields_all.at[f * level_total + l])
                 for f in range(3)] + [(plume_out.at[n], plume_all.at[l])]
        sent += fetch_all(out_sems.at[pl.ds(4 * n, 4)], pairs)
    if last:
        for copy in sent:
            copy.wait()
        return
    for copy in copies[1:]:
        copy.wait()
    emit_modes(results, parent, owners[step + 1] == gx * n_gy + gy, places, x_fwd[...], y_fwd[...],
               keep, send, modes, turned, work)


def others_kernel(step, last, level_count, fields, plume, source, row_first, row_second, col_first,
                  col_second, order_all, *rest):
    level_total, cells_x, cells_y = plume.shape
    if last:
        fields_all, plume_all, order, slab, west, east, sems, fields_out, plume_out, out_sems = rest
    else:
        (done, winds, fields_out, plume_out, first, second, cols, order, slab, west, east,
         sems, plume_here, source_here) = rest
    copies = fetch_all(sems, [(order_all, order)])
    if not last:
        copies += fetch_all(
            sems.at[pl.ds(1, 2)], [(plume, plume_here), (source, source_here)])
        plume, source = plume_here, source_here
    halo = Halo(row_first, row_second, col_first, col_second, west, east)
    for copy in copies:
        copy.wait()
    level_at = [order[n] for n in range(level_total)]
    kept = level_total - level_count
    sent = []
    results = {}
    for n in range(level_count if last else 0, level_total):
        l = level_at[n]
        m = n - level_count
        if m < 0:
            parts = wind_weights(winds[n], winds[level_count + n])
        else:
            given = [fields[f * kept + m] for f in range(3)]
            parts = wind_weights(given[0], given[1])
            for f in range(3):
                c = f * level_total + n
                place(slab.at[4 * n + f], given[f], halo.rows(c))
                results[c] = halo.move(slab[4 * n + f], halo.column(c), parts)
                fields_out[f * kept + m] = results[c]
        c = 3 * level_total + n
        place(slab.at[4 * n + 3], plume[l] if step == 0 else plume[n], halo.rows(c))
        higher = (jnp.minimum(l + 1, level_total - 1) if step == 0 else order[level_total + l + 1])
        results[c] = (halo.move(slab[4 * n + 3], halo.column(c), settling(parts))
                      + above(l, level_total) * plume[higher] + source[l])
        plume_out[m if last else n] = results[c]
        if last:
            pairs = [(fields_out.at[f * kept + m], fields_all.at[f * level_total + l])
                     for f in range(3)] + [(plume_out.at[m], plume_all.at[l])]
            sent += fetch_all(out_sems.at[pl.ds(4 * m, 4)], pairs)
    for copy in sent:
        copy.wait()
    if not last:
        for f in range(3):
            for n in range(level_count):
                results[f * level_total + n] = done[f * level_count + n]
        emit_edges([results[c] for c in range(4 * level_total)], first, second, cols)


def exchange(axis, first, second):
    count = lax.axis_size(axis)
    received = []
    for start, data in ((0, first), (1, second)):
        pairs = [(i, i + 1) for i in range(start, count - 1, 2)]
        received.append(lax.ppermute(data, axis, pairs + [(b, a) for a, b in pairs]))
    return received


def local(tables, fields, levels, cuts, parent_modes, owners, plume, source):
    n_gx, n_gy = lax.axis_size("gx"), lax.axis_size("gy")
    devices = n_gx * n_gy
    level_total, cells_x, cells_y = plume.shape
    period = n_gx * cells_x * n_gy * cells_y
    nudged = 3 * levels.shape[0]
    field_rows = 3 * level_total
    total = field_rows + level_total
    rows = -(-(nudged // GROUP * 2 * KX) // devices)
    flat = fields.reshape(field_rows, cells_x, cells_y)
    cuts = cuts.reshape(-1)
    f32 = functools.partial(jax.ShapeDtypeStruct, dtype=jnp.float32)
    x_fwd, y_fwd, y_back, x_back, x_beside = (jnp.asarray(t) for t in tables)

    def vmem(*shape):
        return pltpu.VMEM(shape, jnp.float32)

    def table_space(table):
        return pltpu.VMEM(table.shape[1:], table.dtype)

    def limit(mib):
        return pltpu.CompilerParams(vmem_limit_bytes=mib * 1024 * 1024)

    count = levels.shape[0]
    kept = level_total - count
    half_shapes = [f32((devices // 2, 2 * rows, LANES))] * 2
    places = share_places(n_gx, n_gy)
    same_core = [[gx * n_gy + gy for gx in range(c, n_gx, 2) for gy in range(n_gy)] for c in range(2)]
    order_shape = (3 * level_total,)
    edge_shapes = [f32((total, cells_y)), f32((total, cells_y)), f32((cells_x, 2 * total))]
    levels_space = pltpu.SMEM(levels.shape, jnp.int32)
    owners_space = pltpu.SMEM(owners.shape, jnp.int32)
    order_space = pltpu.SMEM(order_shape, jnp.int32)
    rows_space = vmem(total, cells_y)
    mode_scratch = [vmem(nudged, 4 * KX * KX), table_space(x_fwd),
                    table_space(y_fwd), vmem(devices, 2 * rows, LANES), vmem(nudged, KX, LANES),
                    vmem(devices * rows, 2 * LANES)]
    nudged_scratch = [order_space, vmem(nudged + count, cells_x + 2 * PAD, cells_y),
                      vmem(devices * rows, LANES), vmem(devices * rows, LANES),
                      rows_space, rows_space, pltpu.SemaphoreType.DMA((5,))]
    others_scratch = [order_space, vmem(total, cells_x + 2 * PAD, cells_y), rows_space, rows_space,
                      pltpu.SemaphoreType.DMA((3,))]
    ash_space = vmem(level_total, cells_x, cells_y)

    def out_scratch(slabs):
        return [vmem(3 * slabs, cells_x, cells_y), vmem(slabs, cells_x, cells_y),
                pltpu.SemaphoreType.DMA((4 * slabs,))]

    keep, send = pl.pallas_call(
        functools.partial(first_kernel, n_gy, level_total, places),
        out_shape=half_shapes,
        in_specs=[HBM] * 6,
        out_specs=[VMEM] * 2,
        scratch_shapes=[levels_space, owners_space, vmem(field_rows, cells_x, cells_y),
                        pltpu.SemaphoreType.DMA((6,))] + mode_scratch,
        compiler_params=limit(8),
        name="first_modes",
    )(*map(in_hbm, (levels, owners, flat, parent_modes, x_fwd, y_fwd)))
    field_shapes = [f32((3 * count, cells_x, cells_y)), f32((3 * kept, cells_x, cells_y))]
    for step in range(STEPS):
        last = step == STEPS - 1
        received = lax.ppermute(send, "gx", [(i, i ^ 1) for i in range(n_gx)])
        modes = pl.pallas_call(
            add_kernel,
            out_shape=half_shapes[0],
            in_specs=[VMEM] * 2,
            out_specs=VMEM,
            compiler_params=limit(4),
            name="add_cores",
        )(keep, received)
        if step == 0:
            modes, flat = lax.optimization_barrier((modes, flat))
            *edges, weights, flat_nudged, others, y_back, order = pl.pallas_call(
                functools.partial(edge_kernel, n_gy, period),
                out_shape=edge_shapes
                + [f32((2 * rows, LANES))] + field_shapes
                + [jax.ShapeDtypeStruct(y_back.shape[1:], y_back.dtype),
                   jax.ShapeDtypeStruct(order_shape, jnp.int32)],
                in_specs=[SMEM, SMEM, VMEM, VMEM, HBM],
                out_specs=[VMEM] * 7 + [SMEM],
                scratch_shapes=[pltpu.SemaphoreType.DMA((1,))],
                compiler_params=limit(8),
                name="edges",
            )(cuts, levels, flat, plume, in_hbm(y_back))
            order = in_hbm(order)
            flat = flat_nudged
        else:
            modes, others = lax.optimization_barrier((modes, others))
            others, plume, *edges = pl.pallas_call(
                functools.partial(others_kernel, 0, False, count),
                out_shape=[f32((3 * kept, cells_x, cells_y)), f32(plume.shape)] + edge_shapes,
                in_specs=[VMEM] + [HBM] * 2 + [VMEM] * 4 + [HBM] + [VMEM] * 2,
                out_specs=[VMEM] * 5,
                scratch_shapes=others_scratch + [ash_space, ash_space],
                compiler_params=limit(8),
                name="inner_others",
            )(others, in_hbm(plume), in_hbm(source), *halo, order, flat, winds)
        to_first, to_second, cols = edges
        col_first, col_second = exchange("gy", cols, cols)
        parts = lax.all_to_all(modes, AXES, 0, 0, axis_index_groups=same_core, tiled=True)
        parts, col_first, col_second = lax.optimization_barrier((parts, col_first, col_second))
        share = pl.pallas_call(
            functools.partial(share_kernel, n_gx, n_gy),
            out_shape=f32((devices, rows + beside_rows(rows), LANES)),
            in_specs=[VMEM] * 4,
            out_specs=VMEM,
            compiler_params=limit(8),
            name="share_sum",
        )(weights, parts, x_back, x_beside)
        share, to_first, to_second = lax.optimization_barrier((share, to_first, to_second))
        row_first, row_second = exchange("gx", to_first, to_second)
        halo = [row_first, row_second, col_first, col_second]
        shares = lax.all_to_all(share, AXES, 0, 0, tiled=True)
        if last:
            final = pl.pallas_call(
                functools.partial(others_kernel, step, True, count),
                out_shape=[f32((field_rows, cells_x, cells_y)), f32(plume.shape)],
                in_specs=[VMEM] * 7 + [HBM],
                out_specs=[HBM] * 2,
                scratch_shapes=others_scratch + out_scratch(kept),
                compiler_params=limit(8),
                name="last_others",
            )(others, plume, source, *halo, order)
            flat, plume = pl.pallas_call(
                functools.partial(nudged_kernel, n_gy, step, True, count, level_total, None),
                out_shape=[f32((field_rows, cells_x, cells_y)), f32(plume.shape)],
                in_specs=[VMEM] * 7 + [HBM] + [VMEM] * 2 + [HBM] * 2,
                out_specs=[HBM] * 2,
                scratch_shapes=nudged_scratch + out_scratch(count),
                input_output_aliases={10: 0, 11: 1},
                compiler_params=limit(12),
                name="last_nudged",
            )(shares, flat, *halo, y_back, order, plume, source, *final)
        else:
            flat, winds, keep, send = pl.pallas_call(
                functools.partial(nudged_kernel, n_gy, step, False, count, level_total, places),
                out_shape=[f32((nudged, cells_x, cells_y)), f32((2 * count, cells_x, cells_y))]
                + half_shapes,
                in_specs=[VMEM] * 7 + [HBM] * 5,
                out_specs=[VMEM] * 4,
                scratch_shapes=nudged_scratch + [owners_space] + mode_scratch,
                compiler_params=limit(12),
                name="inner_nudged",
            )(shares, flat, *halo, y_back, order,
              *map(in_hbm, (owners, parent_modes, x_fwd, y_fwd)))
    return flat.reshape(fields.shape), plume


def solution(mesh):
    in_specs = (
        P(None, None, "gx", "gy"),
        P(),
        P(),
        P(("gx", "gy"), None, None, None),
        P(),
        P(None, "gx", "gy"),
        P(None, "gx", "gy"),
    )
    out_specs = (P(None, None, "gx", "gy"), P(None, "gx", "gy"))
    n_gx, n_gy = mesh.shape["gx"], mesh.shape["gy"]

    def whole(fields, levels, cuts, parent_modes, owners, plume, source):
        tables = build_tables(n_gx, n_gy, plume.shape[1] // n_gx, plume.shape[2] // n_gy)
        return jax.shard_map(
            functools.partial(local, tables), mesh=mesh, in_specs=in_specs, out_specs=out_specs,
            check_vma=False,
        )(fields, levels, cuts, parent_modes, owners, plume, source)

    return whole
```

```python
import functools
import math

import jax
import jax.numpy as jnp
import ml_dtypes
import numpy as np
from jax import lax
from jax.experimental import pallas as pl
from jax.experimental.pallas import tpu as pltpu
from jax.sharding import PartitionSpec as P

KX = 32
STEPS = 2
GROUP = 4
LANES = GROUP * KX
PAD = 8
VMEM = pl.BlockSpec(memory_space=pltpu.VMEM)
SMEM = pl.BlockSpec(memory_space=pltpu.SMEM)
HBM = pl.BlockSpec(memory_space=pltpu.HBM)
AXES = ("gx", "gy")


def in_hbm(array):
    return pltpu.with_memory_space_constraint(array, pltpu.HBM)


def wave_table(positions, period):
    wavenum = np.arange(KX)[:, None]
    phase = (wavenum * positions[None, :] % period) * (2.0 * math.pi / period)
    inside = (positions >= 0) & (positions < period)
    return np.concatenate([np.cos(phase), np.sin(phase)], axis=0) * inside[None, :]


def split(a):
    head = a.astype(jnp.bfloat16)
    return head, (a - head.astype(jnp.float32)).astype(jnp.bfloat16)


def split_table(table, axis, order):
    head = table.astype(ml_dtypes.bfloat16)
    rest = (table - head.astype(np.float64)).astype(ml_dtypes.bfloat16)
    return np.concatenate([head if part == "h" else rest for part in order], axis=axis)


def per_slab(table):
    return np.kron(np.eye(GROUP), table)


def build_tables(n_gx, n_gy, cells_x, cells_y):
    period_x, period_y = n_gx * cells_x, n_gy * cells_y
    scaling = 1.0 / math.sqrt(period_x * period_y)
    parity = [np.arange(p, 2 * KX, 2) for p in range(2)]
    x_fwd, y_fwd, y_back, inner, outer = [], [], [], [], []
    for g in range(n_gx):
        first = g * cells_x
        table = wave_table(first + np.arange(cells_x), period_x)
        x_fwd.append(split_table(
            np.concatenate([per_slab(table[rows].T) for rows in parity], axis=1), 0, "hhl"))
        beside = wave_table(np.array([first - 1, first + cells_x]), period_x)
        inner.append(np.concatenate([np.tile(table[rows], (GROUP, 1)) for rows in parity], axis=0))
        outer.append(np.concatenate([per_slab(beside[rows]) for rows in parity], axis=0))
    spare = -(2 * GROUP * n_gx) % LANES
    x_back = np.concatenate(inner, axis=1)
    x_beside = np.concatenate(outer + [np.zeros((2 * LANES, spare))], axis=1)
    for g in range(n_gy):
        first = g * cells_y
        table = wave_table(first + np.arange(cells_y), period_y)
        edge = np.zeros((2 * KX, cells_y))
        edge[:, [0, -1]] = wave_table(np.array([first - 1, first + cells_y]), period_y)
        y_fwd.append(split_table(table * scaling, 1, "hlh"))
        y_back.append(split_table(np.concatenate([table, edge], axis=1), 0, "hhl"))
    return [np.stack(x_fwd), np.stack(y_fwd), np.stack(y_back),
            split_table(x_back, 0, "hl"), split_table(x_beside, 0, "hl")]


def data_dot(a, table):
    head, rest = split(a)
    return jnp.dot(
        jnp.concatenate([head, rest, head], axis=1), table, preferred_element_type=jnp.float32
    )


def two_part_dot(a, table):
    head, rest = split(a)
    depth = a.shape[1]
    heads = jnp.dot(
        jnp.concatenate([head, rest], axis=0), table[:depth], preferred_element_type=jnp.float32)
    rests = jnp.dot(head, table[depth:], preferred_element_type=jnp.float32)
    return heads[: a.shape[0]] + heads[a.shape[0] :] + rests


def columns_dot(a, table):
    head, rest = split(a)
    stacked = jnp.concatenate([head, rest, head], axis=0)
    return lax.dot_general(
        stacked, table, (((0,), (0,)), ((), ())), preferred_element_type=jnp.float32)


def core():
    return lax.rem(lax.axis_index("gx"), 2)


def share_places(n_gx, n_gy):
    return [(d // n_gy % 2 * (n_gx // 2) + d // n_gy // 2) * n_gy + d % n_gy
            for d in range(n_gx * n_gy)]


def emit_modes(chosen, parent, is_owner, places, x_fwd, y_fwd, keep, send, modes, turned, work):
    devices, rows = modes.shape[0], modes.shape[1] // 2
    slabs = parent.shape[0]
    groups = slabs // GROUP
    head, rest = split(jnp.concatenate(chosen, axis=0))
    half = lax.dot_general(
        y_fwd, jnp.concatenate([head, head, rest], axis=1), (((1,), (1,)), ((), ())),
        preferred_element_type=jnp.float32)
    half = jnp.concatenate([half[:, t * LANES : (t + 1) * LANES] for t in range(groups)], axis=0)
    count = groups * 2 * KX
    work[0:count] = -data_dot(half, x_fwd)
    if count < devices * rows:
        work[count:] = jnp.zeros((devices * rows - count, 2 * LANES), jnp.float32)

    @pl.when(is_owner)
    def _():
        for i in range(KX):
            turned[:, i, :] = parent[:, i * LANES : (i + 1) * LANES]
        for t in range(groups):
            block = turned[t * GROUP : (t + 1) * GROUP].reshape(LANES, LANES).T
            span = slice(t * 2 * KX, (t + 1) * 2 * KX)
            for p in range(2):
                work[span, p * LANES : (p + 1) * LANES] += block[p * 2 * KX : (p + 1) * 2 * KX]

    for d in range(devices):
        for p in range(2):
            modes[places[d], p * rows : (p + 1) * rows, :] = work[
                d * rows : (d + 1) * rows, p * LANES : (p + 1) * LANES]
    count = devices // 2
    mine = core()
    keep[...] = modes[pl.ds(mine * count, count)]
    send[...] = modes[pl.ds((1 - mine) * count, count)]


def add_kernel(kept, received, out):
    out[...] = kept[...] + received[...]


def fetch_all(sems, pairs):
    copies = [pltpu.make_async_copy(a, b, sems.at[i]) for i, (a, b) in enumerate(pairs)]
    for copy in copies:
        copy.start()
    return copies


def slab_of(levels, c, level_count, level_total):
    return (c // level_count) * level_total + levels[c % level_count]


def first_kernel(n_gy, level_total, places, levels_all, owners_all, fields_all, parent_all,
                 x_fwd_all, y_fwd_all, keep, send, levels, owners, fields, sems, parent, x_fwd, y_fwd,
                 modes, turned, work):
    gx, gy = lax.axis_index("gx"), lax.axis_index("gy")
    copies = fetch_all(sems, [
        (levels_all, levels), (owners_all, owners), (fields_all, fields),
        (x_fwd_all.at[gx], x_fwd), (y_fwd_all.at[gy], y_fwd), (parent_all.at[0, 0], parent)])
    for copy in copies:
        copy.wait()
    level_count = parent.shape[0] // 3
    emit_modes(
        [fields[slab_of(levels, c, level_count, level_total)] for c in range(parent.shape[0])],
        parent, owners[0] == gx * n_gy + gy, places, x_fwd[...], y_fwd[...], keep, send,
        modes, turned, work,
    )


def is_even(axis):
    return lax.rem(lax.axis_index(axis), 2) == 0


def edge_kernel(fields, plume, first, second, cols):
    slabs = [fields[c] for c in range(fields.shape[0])]
    emit_edges(slabs + [plume[l] for l in range(plume.shape[0])], first, second, cols)


def prepare_kernel(n_gy, period, level_total, cuts, levels, fields, y_back_all, weights, nudged, others,
                   y_back, order, sems):
    copies = fetch_all(sems, [(y_back_all.at[lax.axis_index("gy")], y_back)])
    weights[...] = share_weights(n_gy, period, cuts, weights.shape)
    count = levels.shape[0]
    for n in range(count):
        order[n] = levels[n]
    spot = jnp.int32(count)
    for l in range(level_total):
        found = levels[0] == l
        for n in range(1, count):
            found = found | (levels[n] == l)
        order[spot] = jnp.int32(l)
        spot = spot + jnp.where(found, 0, 1)
    chosen = [order[n] for n in range(level_total)]
    for n in range(level_total, order.shape[0]):
        order[n] = jnp.int32(0)
    for n in range(level_total):
        order[level_total + chosen[n]] = jnp.int32(n)
    slabs = [fields[f * level_total + l] for f in range(3) for l in chosen]
    kept = level_total - count
    for c, a in enumerate(slabs):
        f, n = c // level_total, c % level_total
        if n < count:
            nudged[f * count + n] = a
        else:
            others[f * kept + n - count] = a
    for copy in copies:
        copy.wait()


def emit_edges(slabs, first, second, cols):
    even = is_even("gx")
    lane = lax.broadcasted_iota(jnp.int32, cols.shape, 1)
    acc = jnp.zeros(cols.shape, jnp.float32)
    for c, a in enumerate(slabs):
        west, east = a[:1], a[a.shape[0] - 1 :]
        first[c : c + 1, :] = jnp.where(even, east, west)
        second[c : c + 1, :] = jnp.where(even, west, east)
        acc = jnp.where(lane // 2 == c, pltpu.roll(a, 2 * c + 1, 1), acc)
    cols[...] = acc


def share_weights(n_gy, period, cuts, shape):
    rows = shape[0] // 2
    me = lax.axis_index("gx") * n_gy + lax.axis_index("gy")
    place = lax.broadcasted_iota(jnp.int32, shape, 0)
    lane = lax.broadcasted_iota(jnp.int32, shape, 1)
    p = (place >= rows).astype(jnp.int32)
    row = me * rows + place - p * rows
    k = 2 * (lane % KX) + p
    j = row % (2 * KX)
    slab = GROUP * (row // (2 * KX)) + lane // KX
    limit = jnp.zeros(shape, jnp.int32)
    for c in range(cuts.shape[0]):
        limit = jnp.where(slab == c, cuts[c], limit)
    keep = ((k % KX) < limit) & ((j % KX) < limit)
    factor = jnp.where(k == 0, 1.0, 2.0) * jnp.where(j == 0, 1.0, 2.0) * (1.0 / math.sqrt(period))
    return jnp.where(keep, factor, 0.0)


def beside_rows(rows):
    return -(-rows // 3)


def share_kernel(n_gx, n_gy, weights, parts, x_back, x_beside, out):
    rows = parts.shape[1] // 2
    total = parts[0]
    for d in range(1, parts.shape[0]):
        total = total + parts[d]
    mismatch = total * weights[...]
    both = jnp.concatenate([mismatch[:rows], mismatch[rows:]], axis=1)
    spare = -rows % 16
    if spare:
        both = jnp.concatenate([both, jnp.zeros((spare, 2 * LANES), jnp.float32)], axis=0)
    slab_lane = lax.broadcasted_iota(jnp.int32, both.shape, 1) % LANES // KX
    chosen = [jnp.where(slab_lane == n, both, 0.0) for n in range(GROUP)]
    inner = two_part_dot(jnp.concatenate(chosen, axis=0), x_back)
    edge_all = two_part_dot(both, x_beside)
    height = rows + spare
    packed = beside_rows(rows)
    width = 2 * GROUP
    cells_x = LANES // GROUP
    slot = lax.broadcasted_iota(jnp.int32, (height, LANES), 1) // cells_x
    spot = lax.broadcasted_iota(jnp.int32, (packed, LANES), 1) // width
    for g in range(n_gx):
        first = g * cells_x // LANES * LANES
        tile = jnp.zeros((height, LANES), jnp.float32)
        for n in range(GROUP):
            piece = inner[n * height : (n + 1) * height, first : first + LANES]
            tile = jnp.where(slot == n, pltpu.roll(piece, (n - g) * cells_x % LANES, 1), tile)
        first = g * width // LANES * LANES
        beside = jnp.zeros((packed, LANES), jnp.float32)
        for m in range(3):
            piece = edge_all[m * packed : (m + 1) * packed, first : first + LANES]
            beside = jnp.where(
                spot == m, pltpu.roll(piece, (m - g) * width % LANES, 1), beside)
        for h in range(n_gy):
            out[g * n_gy + h, :rows, :] = tile[:rows]
            out[g * n_gy + h, rows:, :] = beside


class Halo:
    def __init__(self, row_first, row_second, col_first, col_second, west, east):
        even = is_even("gx")
        west[...] = jnp.where(even, row_second[...], row_first[...])
        east[...] = jnp.where(even, row_first[...], row_second[...])
        self.west, self.east = west, east
        even = is_even("gy")
        north = jnp.where(even, col_first[...], col_second[...])
        south = jnp.where(even, col_second[...], col_first[...])
        shape = north.shape
        lane = lax.broadcasted_iota(jnp.int32, shape, 1)
        self.last = shape[1] - 1
        self.at_first, self.at_last = lane == 0, lane == self.last
        self.columns = jnp.where(
            lane % 2 == 0, pltpu.roll(north, self.last, 1), pltpu.roll(south, 1, 1))

    def rows(self, c):
        return self.west[pl.ds(c, 1), :], self.east[pl.ds(c, 1), :]

    def column(self, c):
        return pltpu.roll(self.columns, self.last - 2 * c, 1)

    def move(self, slab, column, parts):
        centre, to_west, to_east, to_south, to_north = parts
        cells_x = column.shape[0]
        a = slab[PAD : PAD + cells_x]
        return (
            centre * a
            + to_west * slab[PAD - 1 : PAD - 1 + cells_x]
            + to_east * slab[PAD + 1 : PAD + 1 + cells_x]
            + to_south * jnp.where(self.at_first, column, pltpu.roll(a, 1, 1))
            + to_north * jnp.where(self.at_last, column, pltpu.roll(a, self.last, 1))
        )


def place(slab, a, rows):
    cells_x = a.shape[0]
    slab[PAD : PAD + cells_x] = a
    slab[PAD - 1 : PAD] = rows[0]
    slab[PAD + cells_x : PAD + cells_x + 1] = rows[1]


def wind_weights(u, v):
    neighbours = (
        0.1 + 0.1 * jnp.maximum(u, 0.0), 0.1 - 0.1 * jnp.minimum(u, 0.0),
        0.1 + 0.1 * jnp.maximum(v, 0.0), 0.1 - 0.1 * jnp.minimum(v, 0.0),
    )
    centre = 1.0 - (neighbours[0] + neighbours[1] + neighbours[2] + neighbours[3])
    return (centre,) + neighbours


def settling(parts):
    return (parts[0] - 0.3,) + parts[1:]


def above(l, level_total):
    return jnp.where(l + 1 < level_total, 0.3, 0.0).astype(jnp.float32)


def nudge_updates(shares, spread, spread_edges, y_table, nudged, cells_x):
    devices = shares.shape[0]
    rows = spread.shape[0] // devices
    packed = beside_rows(rows)
    width = 2 * GROUP
    for d in range(devices):
        spread[d * rows : (d + 1) * rows] = shares[d, :rows, :]
        edge = shares[d, rows:, :]
        for m in range(3):
            count = min(packed, rows - m * packed)
            if count > 0:
                moved = pltpu.roll(edge, -m * width % LANES, 1) if m else edge
                start = d * rows + m * packed
                spread_edges[start : start + count] = moved[:count]
    groups = nudged // GROUP
    spot_of = lax.broadcasted_iota(jnp.int32, (2 * KX, LANES), 1) // width
    edges = jnp.zeros((2 * KX, LANES), jnp.float32)
    for t in range(groups):
        piece = spread_edges[t * 2 * KX : (t + 1) * 2 * KX]
        edges = jnp.where(spot_of == t, pltpu.roll(piece, t * width, 1) if t else piece, edges)
    update_rows = columns_dot(edges, y_table)
    updates = []
    for t in range(groups):
        update = columns_dot(spread[t * 2 * KX : (t + 1) * 2 * KX], y_table)
        updates += [update[n * cells_x : (n + 1) * cells_x] for n in range(GROUP)]
    return updates, update_rows


def nudged_kernel(n_gy, step, last, level_count, level_total, places, shares, fields, row_first, row_second,
                  col_first, col_second, y_back, order_all, *rest):
    gx, gy = lax.axis_index("gx"), lax.axis_index("gy")
    cells_x, cells_y = fields.shape[1:]
    nudged = 3 * level_count
    if last:
        (plume, source, _, _, fields_all, plume_all, order, slabs, spread, spread_edges, west, east,
         sems, fields_out, plume_out, out_sems) = rest
        extra = []
    else:
        (owners_all, parent_all, x_fwd_all, y_fwd_all, fields_out, winds_out, keep, send,
         order, slabs, spread, spread_edges, west, east, sems,
         owners, parent, x_fwd, y_fwd, modes, turned, work) = rest
        extra = [(owners_all, owners), (x_fwd_all.at[gx], x_fwd), (y_fwd_all.at[gy], y_fwd),
                 (parent_all.at[0, step + 1], parent)]
    copies = fetch_all(sems, [(order_all, order)] + extra)
    halo = Halo(row_first, row_second, col_first, col_second, west, east)
    updates, update_rows = nudge_updates(
        shares, spread, spread_edges, y_back[...], nudged, cells_x)
    copies[0].wait()
    level_at = [order[n] for n in range(level_count)]
    halo_at = level_at if step == 0 else list(range(level_count))
    beside = []
    for k in range(nudged):
        f, n = k // level_count, k % level_count
        a = fields[k]
        before, after = halo.rows(f * level_total + halo_at[n])
        place(slabs.at[k], a + updates[k][:, :cells_y],
              (before + update_rows[2 * k : 2 * k + 1, :cells_y],
               after + update_rows[2 * k + 1 : 2 * k + 2, :cells_y]))
        beside.append(updates[k][:, cells_y:])
    inner = slice(PAD, PAD + cells_x)
    results = [None] * nudged
    sent = []
    for n in range(level_count):
        u, v = slabs[n, inner], slabs[level_count + n, inner]
        parts = wind_weights(u, v)
        for f in range(3):
            k = f * level_count + n
            column = halo.column(f * level_total + halo_at[n]) + beside[k]
            results[k] = halo.move(slabs[k], column, parts)
            fields_out[k] = results[k]
        if not last:
            winds_out[n] = u
            winds_out[level_count + n] = v
            continue
        l = level_at[n]
        c = 3 * level_total + n
        place(slabs.at[nudged + n], plume[n], halo.rows(c))
        settled = halo.move(slabs[nudged + n], halo.column(c), settling(parts))
        plume_out[n] = settled + above(l, level_total) * plume[order[level_total + l + 1]] + source[l]
        pairs = [(fields_out.at[f * level_count + n], fields_all.at[f * level_total + l])
                 for f in range(3)] + [(plume_out.at[n], plume_all.at[l])]
        sent += fetch_all(out_sems.at[pl.ds(4 * n, 4)], pairs)
    if last:
        for copy in sent:
            copy.wait()
        return
    for copy in copies[1:]:
        copy.wait()
    emit_modes(results, parent, owners[step + 1] == gx * n_gy + gy, places, x_fwd[...], y_fwd[...],
               keep, send, modes, turned, work)


def others_kernel(step, last, level_count, fields, plume, source, row_first, row_second, col_first,
                  col_second, order_all, *rest):
    level_total, cells_x, cells_y = plume.shape
    if last:
        fields_all, plume_all, order, slab, west, east, sems, fields_out, plume_out, out_sems = rest
    else:
        (done, winds, fields_out, plume_out, first, second, cols, order, slab, west, east,
         sems) = rest
    copies = fetch_all(sems, [(order_all, order)])
    halo = Halo(row_first, row_second, col_first, col_second, west, east)
    for copy in copies:
        copy.wait()
    level_at = [order[n] for n in range(level_total)]
    kept = level_total - level_count
    sent = []
    results = {}
    for n in range(level_count if last else 0, level_total):
        l = level_at[n]
        m = n - level_count
        if m < 0:
            parts = wind_weights(winds[n], winds[level_count + n])
        else:
            given = [fields[f * kept + m] for f in range(3)]
            parts = wind_weights(given[0], given[1])
            for f in range(3):
                c = f * level_total + n
                beyond = f * level_total + l if step == 0 else c
                place(slab.at[4 * n + f], given[f], halo.rows(beyond))
                results[c] = halo.move(slab[4 * n + f], halo.column(beyond), parts)
                fields_out[f * kept + m] = results[c]
        c = 3 * level_total + n
        beyond = 3 * level_total + l if step == 0 else c
        place(slab.at[4 * n + 3], plume[l] if step == 0 else plume[n], halo.rows(beyond))
        higher = (jnp.minimum(l + 1, level_total - 1) if step == 0 else order[level_total + l + 1])
        results[c] = (halo.move(slab[4 * n + 3], halo.column(beyond), settling(parts))
                      + above(l, level_total) * plume[higher] + source[l])
        plume_out[m if last else n] = results[c]
        if last:
            pairs = [(fields_out.at[f * kept + m], fields_all.at[f * level_total + l])
                     for f in range(3)] + [(plume_out.at[m], plume_all.at[l])]
            sent += fetch_all(out_sems.at[pl.ds(4 * m, 4)], pairs)
    for copy in sent:
        copy.wait()
    if not last:
        for f in range(3):
            for n in range(level_count):
                results[f * level_total + n] = done[f * level_count + n]
        emit_edges([results[c] for c in range(4 * level_total)], first, second, cols)


def exchange(axis, first, second):
    count = lax.axis_size(axis)
    received = []
    for start, data in ((0, first), (1, second)):
        pairs = [(i, i + 1) for i in range(start, count - 1, 2)]
        received.append(lax.ppermute(data, axis, pairs + [(b, a) for a, b in pairs]))
    return received


def local(tables, fields, levels, cuts, parent_modes, owners, plume, source):
    n_gx, n_gy = lax.axis_size("gx"), lax.axis_size("gy")
    devices = n_gx * n_gy
    level_total, cells_x, cells_y = plume.shape
    period = n_gx * cells_x * n_gy * cells_y
    nudged = 3 * levels.shape[0]
    field_rows = 3 * level_total
    total = field_rows + level_total
    rows = -(-(nudged // GROUP * 2 * KX) // devices)
    flat = fields.reshape(field_rows, cells_x, cells_y)
    cuts = cuts.reshape(-1)
    f32 = functools.partial(jax.ShapeDtypeStruct, dtype=jnp.float32)
    x_fwd, y_fwd, y_back, x_back, x_beside = (jnp.asarray(t) for t in tables)

    def vmem(*shape):
        return pltpu.VMEM(shape, jnp.float32)

    def table_space(table):
        return pltpu.VMEM(table.shape[1:], table.dtype)

    def limit(mib):
        return pltpu.CompilerParams(vmem_limit_bytes=mib * 1024 * 1024)

    count = levels.shape[0]
    kept = level_total - count
    half_shapes = [f32((devices // 2, 2 * rows, LANES))] * 2
    places = share_places(n_gx, n_gy)
    same_core = [[gx * n_gy + gy for gx in range(c, n_gx, 2) for gy in range(n_gy)] for c in range(2)]
    order_shape = (3 * level_total,)
    edge_shapes = [f32((total, cells_y)), f32((total, cells_y)), f32((cells_x, 2 * total))]
    levels_space = pltpu.SMEM(levels.shape, jnp.int32)
    owners_space = pltpu.SMEM(owners.shape, jnp.int32)
    order_space = pltpu.SMEM(order_shape, jnp.int32)
    rows_space = vmem(total, cells_y)
    mode_scratch = [vmem(nudged, 4 * KX * KX), table_space(x_fwd),
                    table_space(y_fwd), vmem(devices, 2 * rows, LANES), vmem(nudged, KX, LANES),
                    vmem(devices * rows, 2 * LANES)]
    nudged_scratch = [order_space, vmem(nudged + count, cells_x + 2 * PAD, cells_y),
                      vmem(devices * rows, LANES), vmem(devices * rows, LANES),
                      rows_space, rows_space, pltpu.SemaphoreType.DMA((5,))]
    others_scratch = [order_space, vmem(total, cells_x + 2 * PAD, cells_y), rows_space, rows_space,
                      pltpu.SemaphoreType.DMA((1,))]

    def out_scratch(slabs):
        return [vmem(3 * slabs, cells_x, cells_y), vmem(slabs, cells_x, cells_y),
                pltpu.SemaphoreType.DMA((4 * slabs,))]

    keep, send = pl.pallas_call(
        functools.partial(first_kernel, n_gy, level_total, places),
        out_shape=half_shapes,
        in_specs=[HBM] * 6,
        out_specs=[VMEM] * 2,
        scratch_shapes=[levels_space, owners_space, vmem(field_rows, cells_x, cells_y),
                        pltpu.SemaphoreType.DMA((6,))] + mode_scratch,
        compiler_params=limit(8),
        name="first_modes",
    )(*map(in_hbm, (levels, owners, flat, parent_modes, x_fwd, y_fwd)))
    for step in range(STEPS):
        last = step == STEPS - 1
        received = lax.ppermute(send, "gx", [(i, i ^ 1) for i in range(n_gx)])
        modes = pl.pallas_call(
            add_kernel,
            out_shape=half_shapes[0],
            in_specs=[VMEM] * 2,
            out_specs=VMEM,
            compiler_params=limit(4),
            name="add_cores",
        )(keep, received)
        if step == 0:
            modes, flat = lax.optimization_barrier((modes, flat))
            edges = pl.pallas_call(
                edge_kernel,
                out_shape=edge_shapes,
                in_specs=[VMEM] * 2,
                out_specs=[VMEM] * 3,
                compiler_params=limit(8),
                name="edges",
            )(flat, plume)
            weights, flat_nudged, others, y_back, order = pl.pallas_call(
                functools.partial(prepare_kernel, n_gy, period, level_total),
                out_shape=[f32((2 * rows, LANES)), f32((3 * count, cells_x, cells_y)),
                           f32((3 * kept, cells_x, cells_y)),
                           jax.ShapeDtypeStruct(y_back.shape[1:], y_back.dtype),
                           jax.ShapeDtypeStruct(order_shape, jnp.int32)],
                in_specs=[SMEM, SMEM, VMEM, HBM],
                out_specs=[VMEM] * 4 + [SMEM],
                scratch_shapes=[pltpu.SemaphoreType.DMA((1,))],
                compiler_params=limit(8),
                name="prepare",
            )(cuts, levels, flat, in_hbm(y_back))
            order = in_hbm(order)
            flat = flat_nudged
        else:
            modes, others = lax.optimization_barrier((modes, others))
            others, plume, *edges = pl.pallas_call(
                functools.partial(others_kernel, 0, False, count),
                out_shape=[f32((3 * kept, cells_x, cells_y)), f32(plume.shape)] + edge_shapes,
                in_specs=[VMEM] * 7 + [HBM] + [VMEM] * 2,
                out_specs=[VMEM] * 5,
                scratch_shapes=others_scratch,
                compiler_params=limit(8),
                name="inner_others",
            )(others, plume, source, *halo, order, flat, winds)
        to_first, to_second, cols = edges
        col_first, col_second = exchange("gy", cols, cols)
        parts = lax.all_to_all(modes, AXES, 0, 0, axis_index_groups=same_core, tiled=True)
        parts, col_first, col_second = lax.optimization_barrier((parts, col_first, col_second))
        share = pl.pallas_call(
            functools.partial(share_kernel, n_gx, n_gy),
            out_shape=f32((devices, rows + beside_rows(rows), LANES)),
            in_specs=[VMEM] * 4,
            out_specs=VMEM,
            compiler_params=limit(8),
            name="share_sum",
        )(weights, parts, x_back, x_beside)
        share, to_first, to_second = lax.optimization_barrier((share, to_first, to_second))
        row_first, row_second = exchange("gx", to_first, to_second)
        halo = [row_first, row_second, col_first, col_second]
        shares = lax.all_to_all(share, AXES, 0, 0, tiled=True)
        if last:
            final = pl.pallas_call(
                functools.partial(others_kernel, step, True, count),
                out_shape=[f32((field_rows, cells_x, cells_y)), f32(plume.shape)],
                in_specs=[VMEM] * 7 + [HBM],
                out_specs=[HBM] * 2,
                scratch_shapes=others_scratch + out_scratch(kept),
                compiler_params=limit(8),
                name="last_others",
            )(others, plume, source, *halo, order)
            flat, plume = pl.pallas_call(
                functools.partial(nudged_kernel, n_gy, step, True, count, level_total, None),
                out_shape=[f32((field_rows, cells_x, cells_y)), f32(plume.shape)],
                in_specs=[VMEM] * 7 + [HBM] + [VMEM] * 2 + [HBM] * 2,
                out_specs=[HBM] * 2,
                scratch_shapes=nudged_scratch + out_scratch(count),
                input_output_aliases={10: 0, 11: 1},
                compiler_params=limit(12),
                name="last_nudged",
            )(shares, flat, *halo, y_back, order, plume, source, *final)
        else:
            flat, winds, keep, send = pl.pallas_call(
                functools.partial(nudged_kernel, n_gy, step, False, count, level_total, places),
                out_shape=[f32((nudged, cells_x, cells_y)), f32((2 * count, cells_x, cells_y))]
                + half_shapes,
                in_specs=[VMEM] * 7 + [HBM] * 5,
                out_specs=[VMEM] * 4,
                scratch_shapes=nudged_scratch + [owners_space] + mode_scratch,
                compiler_params=limit(12),
                name="inner_nudged",
            )(shares, flat, *halo, y_back, order,
              *map(in_hbm, (owners, parent_modes, x_fwd, y_fwd)))
    return flat.reshape(fields.shape), plume


def solution(mesh):
    in_specs = (
        P(None, None, "gx", "gy"),
        P(),
        P(),
        P(("gx", "gy"), None, None, None),
        P(),
        P(None, "gx", "gy"),
        P(None, "gx", "gy"),
    )
    out_specs = (P(None, None, "gx", "gy"), P(None, "gx", "gy"))
    n_gx, n_gy = mesh.shape["gx"], mesh.shape["gy"]

    def whole(fields, levels, cuts, parent_modes, owners, plume, source):
        tables = build_tables(n_gx, n_gy, plume.shape[1] // n_gx, plume.shape[2] // n_gy)
        return jax.shard_map(
            functools.partial(local, tables), mesh=mesh, in_specs=in_specs, out_specs=out_specs,
            check_vma=False,
        )(fields, levels, cuts, parent_modes, owners, plume, source)

    return whole
```

```python
import functools
import math

import jax
import jax.numpy as jnp
import ml_dtypes
import numpy as np
from jax import lax
from jax.experimental import pallas as pl
from jax.experimental.pallas import tpu as pltpu
from jax.sharding import PartitionSpec as P

KX = 32
STEPS = 2
GROUP = 4
LANES = GROUP * KX
PAD = 8
VMEM = pl.BlockSpec(memory_space=pltpu.VMEM)
SMEM = pl.BlockSpec(memory_space=pltpu.SMEM)
HBM = pl.BlockSpec(memory_space=pltpu.HBM)
AXES = ("gx", "gy")


def in_hbm(array):
    return pltpu.with_memory_space_constraint(array, pltpu.HBM)


def wave_table(positions, period):
    wavenum = np.arange(KX)[:, None]
    phase = (wavenum * positions[None, :] % period) * (2.0 * math.pi / period)
    inside = (positions >= 0) & (positions < period)
    return np.concatenate([np.cos(phase), np.sin(phase)], axis=0) * inside[None, :]


def split(a):
    head = a.astype(jnp.bfloat16)
    return head, (a - head.astype(jnp.float32)).astype(jnp.bfloat16)


def split_table(table, axis, order):
    head = table.astype(ml_dtypes.bfloat16)
    rest = (table - head.astype(np.float64)).astype(ml_dtypes.bfloat16)
    return np.concatenate([head if part == "h" else rest for part in order], axis=axis)


def per_slab(table):
    return np.kron(np.eye(GROUP), table)


def build_tables(n_gx, n_gy, cells_x, cells_y):
    period_x, period_y = n_gx * cells_x, n_gy * cells_y
    scaling = 1.0 / math.sqrt(period_x * period_y)
    parity = [np.arange(p, 2 * KX, 2) for p in range(2)]
    x_fwd, y_fwd, y_back, inner, outer = [], [], [], [], []
    for g in range(n_gx):
        first = g * cells_x
        table = wave_table(first + np.arange(cells_x), period_x)
        x_fwd.append(split_table(
            np.concatenate([per_slab(table[rows].T) for rows in parity], axis=1), 0, "hhl"))
        beside = wave_table(np.array([first - 1, first + cells_x]), period_x)
        inner.append(np.concatenate([np.tile(table[rows], (GROUP, 1)) for rows in parity], axis=0))
        outer.append(np.concatenate([per_slab(beside[rows]) for rows in parity], axis=0))
    spare = -(2 * GROUP * n_gx) % LANES
    x_back = np.concatenate(inner, axis=1)
    x_beside = np.concatenate(outer + [np.zeros((2 * LANES, spare))], axis=1)
    for g in range(n_gy):
        first = g * cells_y
        table = wave_table(first + np.arange(cells_y), period_y)
        edge = np.zeros((2 * KX, cells_y))
        edge[:, [0, -1]] = wave_table(np.array([first - 1, first + cells_y]), period_y)
        y_fwd.append(split_table(table * scaling, 1, "hlh"))
        y_back.append(split_table(np.concatenate([table, edge], axis=1), 0, "hhl"))
    return [np.stack(x_fwd), np.stack(y_fwd), np.stack(y_back),
            split_table(x_back, 0, "hl"), split_table(x_beside, 0, "hl")]


def data_dot(a, table):
    head, rest = split(a)
    return jnp.dot(
        jnp.concatenate([head, rest, head], axis=1), table, preferred_element_type=jnp.float32
    )


def two_part_dot(a, table):
    head, rest = split(a)
    depth = a.shape[1]
    heads = jnp.dot(
        jnp.concatenate([head, rest], axis=0), table[:depth], preferred_element_type=jnp.float32)
    rests = jnp.dot(head, table[depth:], preferred_element_type=jnp.float32)
    return heads[: a.shape[0]] + heads[a.shape[0] :] + rests


def columns_dot(a, table):
    head, rest = split(a)
    stacked = jnp.concatenate([head, rest, head], axis=0)
    return lax.dot_general(
        stacked, table, (((0,), (0,)), ((), ())), preferred_element_type=jnp.float32)


def core():
    return lax.rem(lax.axis_index("gx"), 2)


def share_places(n_gx, n_gy):
    return [(d // n_gy % 2 * (n_gx // 2) + d // n_gy // 2) * n_gy + d % n_gy
            for d in range(n_gx * n_gy)]


def emit_modes(chosen, parent, is_owner, places, x_fwd, y_fwd, keep, send, turned, work):
    devices, rows = len(places), keep.shape[1] // 2
    slabs = parent.shape[0]
    groups = slabs // GROUP
    head, rest = split(jnp.concatenate(chosen, axis=0))
    half = lax.dot_general(
        y_fwd, jnp.concatenate([head, head, rest], axis=1), (((1,), (1,)), ((), ())),
        preferred_element_type=jnp.float32)
    half = jnp.concatenate([half[:, t * LANES : (t + 1) * LANES] for t in range(groups)], axis=0)
    count = groups * 2 * KX
    work[0:count] = -data_dot(half, x_fwd)
    if count < devices * rows:
        work[count:] = jnp.zeros((devices * rows - count, 2 * LANES), jnp.float32)

    @pl.when(is_owner)
    def _():
        for i in range(KX):
            turned[:, i, :] = parent[:, i * LANES : (i + 1) * LANES]
        for t in range(groups):
            block = turned[t * GROUP : (t + 1) * GROUP].reshape(LANES, LANES).T
            span = slice(t * 2 * KX, (t + 1) * 2 * KX)
            for p in range(2):
                work[span, p * LANES : (p + 1) * LANES] += block[p * 2 * KX : (p + 1) * 2 * KX]

    count = devices // 2
    for mine in range(2):
        @pl.when(core() == mine)
        def _(mine=mine):
            for d in range(devices):
                half = keep if places[d] // count == mine else send
                for p in range(2):
                    half[places[d] % count, p * rows : (p + 1) * rows, :] = work[
                        d * rows : (d + 1) * rows, p * LANES : (p + 1) * LANES]


def add_kernel(kept, received, out):
    out[...] = kept[...] + received[...]


def fetch_all(sems, pairs):
    copies = [pltpu.make_async_copy(a, b, sems.at[i]) for i, (a, b) in enumerate(pairs)]
    for copy in copies:
        copy.start()
    return copies


def slab_of(levels, c, level_count, level_total):
    return (c // level_count) * level_total + levels[c % level_count]


def first_kernel(n_gy, level_total, places, levels_all, owners_all, fields_all, parent_all,
                 x_fwd_all, y_fwd_all, keep, send, levels, owners, fields, sems, parent, x_fwd, y_fwd,
                 turned, work):
    gx, gy = lax.axis_index("gx"), lax.axis_index("gy")
    copies = fetch_all(sems, [
        (levels_all, levels), (owners_all, owners), (fields_all, fields),
        (x_fwd_all.at[gx], x_fwd), (y_fwd_all.at[gy], y_fwd), (parent_all.at[0, 0], parent)])
    for copy in copies:
        copy.wait()
    level_count = parent.shape[0] // 3
    emit_modes(
        [fields[slab_of(levels, c, level_count, level_total)] for c in range(parent.shape[0])],
        parent, owners[0] == gx * n_gy + gy, places, x_fwd[...], y_fwd[...], keep, send,
        turned, work,
    )


def is_even(axis):
    return lax.rem(lax.axis_index(axis), 2) == 0


def edge_kernel(n_gy, period, cuts, fields, plume, first, second, cols, weights):
    weights[...] = share_weights(n_gy, period, cuts, weights.shape)
    slabs = [fields[c] for c in range(fields.shape[0])]
    emit_edges(slabs + [plume[l] for l in range(plume.shape[0])], first, second, cols)


def prepare_kernel(level_total, levels, fields, y_back_all, nudged, others, y_back, order, sems):
    copies = fetch_all(sems, [(y_back_all.at[lax.axis_index("gy")], y_back)])
    count = levels.shape[0]
    for n in range(count):
        order[n] = levels[n]
    spot = jnp.int32(count)
    for l in range(level_total):
        found = levels[0] == l
        for n in range(1, count):
            found = found | (levels[n] == l)
        order[spot] = jnp.int32(l)
        spot = spot + jnp.where(found, 0, 1)
    chosen = [order[n] for n in range(level_total)]
    for n in range(level_total, order.shape[0]):
        order[n] = jnp.int32(0)
    for n in range(level_total):
        order[level_total + chosen[n]] = jnp.int32(n)
    slabs = [fields[f * level_total + l] for f in range(3) for l in chosen]
    kept = level_total - count
    for c, a in enumerate(slabs):
        f, n = c // level_total, c % level_total
        if n < count:
            nudged[f * count + n] = a
        else:
            others[f * kept + n - count] = a
    for copy in copies:
        copy.wait()


def emit_edges(slabs, first, second, cols):
    even = is_even("gx")
    lane = lax.broadcasted_iota(jnp.int32, cols.shape, 1)
    acc = jnp.zeros(cols.shape, jnp.float32)
    for c, a in enumerate(slabs):
        west, east = a[:1], a[a.shape[0] - 1 :]
        first[c : c + 1, :] = jnp.where(even, east, west)
        second[c : c + 1, :] = jnp.where(even, west, east)
        acc = jnp.where(lane // 2 == c, pltpu.roll(a, 2 * c + 1, 1), acc)
    cols[...] = acc


def share_weights(n_gy, period, cuts, shape):
    rows = shape[0] // 2
    me = lax.axis_index("gx") * n_gy + lax.axis_index("gy")
    place = lax.broadcasted_iota(jnp.int32, shape, 0)
    lane = lax.broadcasted_iota(jnp.int32, shape, 1)
    p = (place >= rows).astype(jnp.int32)
    row = me * rows + place - p * rows
    k = 2 * (lane % KX) + p
    j = row % (2 * KX)
    slab = GROUP * (row // (2 * KX)) + lane // KX
    limit = jnp.zeros(shape, jnp.int32)
    for c in range(cuts.shape[0]):
        limit = jnp.where(slab == c, cuts[c], limit)
    keep = ((k % KX) < limit) & ((j % KX) < limit)
    factor = jnp.where(k == 0, 1.0, 2.0) * jnp.where(j == 0, 1.0, 2.0) * (1.0 / math.sqrt(period))
    return jnp.where(keep, factor, 0.0)


def beside_rows(rows):
    return -(-rows // 3)


def share_kernel(n_gx, n_gy, weights, parts, x_back, x_beside, out):
    rows = parts.shape[1] // 2
    total = parts[0]
    for d in range(1, parts.shape[0]):
        total = total + parts[d]
    mismatch = total * weights[...]
    both = jnp.concatenate([mismatch[:rows], mismatch[rows:]], axis=1)
    spare = -rows % 16
    if spare:
        both = jnp.concatenate([both, jnp.zeros((spare, 2 * LANES), jnp.float32)], axis=0)
    slab_lane = lax.broadcasted_iota(jnp.int32, both.shape, 1) % LANES // KX
    chosen = [jnp.where(slab_lane == n, both, 0.0) for n in range(GROUP)]
    inner = two_part_dot(jnp.concatenate(chosen, axis=0), x_back)
    edge_all = two_part_dot(both, x_beside)
    height = rows + spare
    packed = beside_rows(rows)
    width = 2 * GROUP
    cells_x = LANES // GROUP
    slot = lax.broadcasted_iota(jnp.int32, (height, LANES), 1) // cells_x
    spot = lax.broadcasted_iota(jnp.int32, (packed, LANES), 1) // width
    for g in range(n_gx):
        first = g * cells_x // LANES * LANES
        tile = jnp.zeros((height, LANES), jnp.float32)
        for n in range(GROUP):
            piece = inner[n * height : (n + 1) * height, first : first + LANES]
            tile = jnp.where(slot == n, pltpu.roll(piece, (n - g) * cells_x % LANES, 1), tile)
        first = g * width // LANES * LANES
        beside = jnp.zeros((packed, LANES), jnp.float32)
        for m in range(3):
            piece = edge_all[m * packed : (m + 1) * packed, first : first + LANES]
            beside = jnp.where(
                spot == m, pltpu.roll(piece, (m - g) * width % LANES, 1), beside)
        for h in range(n_gy):
            out[g * n_gy + h, :rows, :] = tile[:rows]
            out[g * n_gy + h, rows:, :] = beside


class Halo:
    def __init__(self, row_first, row_second, col_first, col_second, west, east):
        even = is_even("gx")
        west[...] = jnp.where(even, row_second[...], row_first[...])
        east[...] = jnp.where(even, row_first[...], row_second[...])
        self.west, self.east = west, east
        even = is_even("gy")
        north = jnp.where(even, col_first[...], col_second[...])
        south = jnp.where(even, col_second[...], col_first[...])
        shape = north.shape
        lane = lax.broadcasted_iota(jnp.int32, shape, 1)
        self.last = shape[1] - 1
        self.at_first, self.at_last = lane == 0, lane == self.last
        self.columns = jnp.where(
            lane % 2 == 0, pltpu.roll(north, self.last, 1), pltpu.roll(south, 1, 1))

    def rows(self, c):
        return self.west[pl.ds(c, 1), :], self.east[pl.ds(c, 1), :]

    def column(self, c):
        return pltpu.roll(self.columns, self.last - 2 * c, 1)

    def move(self, slab, column, parts):
        centre, to_west, to_east, to_south, to_north = parts
        cells_x = column.shape[0]
        a = slab[PAD : PAD + cells_x]
        return (
            centre * a
            + to_west * slab[PAD - 1 : PAD - 1 + cells_x]
            + to_east * slab[PAD + 1 : PAD + 1 + cells_x]
            + to_south * jnp.where(self.at_first, column, pltpu.roll(a, 1, 1))
            + to_north * jnp.where(self.at_last, column, pltpu.roll(a, self.last, 1))
        )


def place(slab, a, rows):
    cells_x = a.shape[0]
    slab[PAD : PAD + cells_x] = a
    slab[PAD - 1 : PAD] = rows[0]
    slab[PAD + cells_x : PAD + cells_x + 1] = rows[1]


def wind_weights(u, v):
    neighbours = (
        0.1 + 0.1 * jnp.maximum(u, 0.0), 0.1 - 0.1 * jnp.minimum(u, 0.0),
        0.1 + 0.1 * jnp.maximum(v, 0.0), 0.1 - 0.1 * jnp.minimum(v, 0.0),
    )
    centre = 1.0 - (neighbours[0] + neighbours[1] + neighbours[2] + neighbours[3])
    return (centre,) + neighbours


def settling(parts):
    return (parts[0] - 0.3,) + parts[1:]


def above(l, level_total):
    return jnp.where(l + 1 < level_total, 0.3, 0.0).astype(jnp.float32)


def nudge_updates(shares, spread, spread_edges, y_table, nudged, cells_x):
    devices = shares.shape[0]
    rows = spread.shape[0] // devices
    packed = beside_rows(rows)
    width = 2 * GROUP
    for d in range(devices):
        spread[d * rows : (d + 1) * rows] = shares[d, :rows, :]
        edge = shares[d, rows:, :]
        for m in range(3):
            count = min(packed, rows - m * packed)
            if count > 0:
                moved = pltpu.roll(edge, -m * width % LANES, 1) if m else edge
                start = d * rows + m * packed
                spread_edges[start : start + count] = moved[:count]
    groups = nudged // GROUP
    spot_of = lax.broadcasted_iota(jnp.int32, (2 * KX, LANES), 1) // width
    edges = jnp.zeros((2 * KX, LANES), jnp.float32)
    for t in range(groups):
        piece = spread_edges[t * 2 * KX : (t + 1) * 2 * KX]
        edges = jnp.where(spot_of == t, pltpu.roll(piece, t * width, 1) if t else piece, edges)
    update_rows = columns_dot(edges, y_table)
    updates = []
    for t in range(groups):
        update = columns_dot(spread[t * 2 * KX : (t + 1) * 2 * KX], y_table)
        updates += [update[n * cells_x : (n + 1) * cells_x] for n in range(GROUP)]
    return updates, update_rows


def nudged_kernel(n_gy, step, last, level_count, level_total, places, shares, fields, row_first, row_second,
                  col_first, col_second, y_back, order_all, *rest):
    gx, gy = lax.axis_index("gx"), lax.axis_index("gy")
    cells_x, cells_y = fields.shape[1:]
    nudged = 3 * level_count
    if last:
        (plume, source, _, _, fields_all, plume_all, order, slabs, spread, spread_edges, west, east,
         sems, fields_out, plume_out, out_sems) = rest
        extra = []
    else:
        (owners_all, parent_all, x_fwd_all, y_fwd_all, fields_out, winds_out, keep, send,
         order, slabs, spread, spread_edges, west, east, sems,
         owners, parent, x_fwd, y_fwd, turned, work) = rest
        extra = [(owners_all, owners), (x_fwd_all.at[gx], x_fwd), (y_fwd_all.at[gy], y_fwd),
                 (parent_all.at[0, step + 1], parent)]
    copies = fetch_all(sems, [(order_all, order)] + extra)
    halo = Halo(row_first, row_second, col_first, col_second, west, east)
    updates, update_rows = nudge_updates(
        shares, spread, spread_edges, y_back[...], nudged, cells_x)
    copies[0].wait()
    level_at = [order[n] for n in range(level_count)]
    halo_at = level_at if step == 0 else list(range(level_count))
    beside = []
    for k in range(nudged):
        f, n = k // level_count, k % level_count
        a = fields[k]
        before, after = halo.rows(f * level_total + halo_at[n])
        place(slabs.at[k], a + updates[k][:, :cells_y],
              (before + update_rows[2 * k : 2 * k + 1, :cells_y],
               after + update_rows[2 * k + 1 : 2 * k + 2, :cells_y]))
        beside.append(updates[k][:, cells_y:])
    inner = slice(PAD, PAD + cells_x)
    results = [None] * nudged
    sent = []
    for n in range(level_count):
        u, v = slabs[n, inner], slabs[level_count + n, inner]
        parts = wind_weights(u, v)
        for f in range(3):
            k = f * level_count + n
            column = halo.column(f * level_total + halo_at[n]) + beside[k]
            results[k] = halo.move(slabs[k], column, parts)
            fields_out[k] = results[k]
        if not last:
            winds_out[n] = u
            winds_out[level_count + n] = v
            continue
        l = level_at[n]
        c = 3 * level_total + n
        place(slabs.at[nudged + n], plume[n], halo.rows(c))
        settled = halo.move(slabs[nudged + n], halo.column(c), settling(parts))
        plume_out[n] = settled + above(l, level_total) * plume[order[level_total + l + 1]] + source[l]
        pairs = [(fields_out.at[f * level_count + n], fields_all.at[f * level_total + l])
                 for f in range(3)] + [(plume_out.at[n], plume_all.at[l])]
        sent += fetch_all(out_sems.at[pl.ds(4 * n, 4)], pairs)
    if last:
        for copy in sent:
            copy.wait()
        return
    for copy in copies[1:]:
        copy.wait()
    emit_modes(results, parent, owners[step + 1] == gx * n_gy + gy, places, x_fwd[...], y_fwd[...],
               keep, send, turned, work)


def others_kernel(step, last, level_count, fields, plume, source, row_first, row_second, col_first,
                  col_second, order, *rest):
    level_total, cells_x, cells_y = plume.shape
    if last:
        fields_all, plume_all, slab, west, east, fields_out, plume_out, out_sems = rest
    else:
        done, winds, fields_out, plume_out, first, second, cols, slab, west, east = rest
    halo = Halo(row_first, row_second, col_first, col_second, west, east)
    level_at = [order[n] for n in range(level_total)]
    kept = level_total - level_count
    sent = []
    results = {}
    for n in range(level_count if last else 0, level_total):
        l = level_at[n]
        m = n - level_count
        if m < 0:
            parts = wind_weights(winds[n], winds[level_count + n])
        else:
            given = [fields[f * kept + m] for f in range(3)]
            parts = wind_weights(given[0], given[1])
            for f in range(3):
                c = f * level_total + n
                beyond = f * level_total + l if step == 0 else c
                place(slab.at[4 * n + f], given[f], halo.rows(beyond))
                results[c] = halo.move(slab[4 * n + f], halo.column(beyond), parts)
                fields_out[f * kept + m] = results[c]
        c = 3 * level_total + n
        beyond = 3 * level_total + l if step == 0 else c
        place(slab.at[4 * n + 3], plume[l] if step == 0 else plume[n], halo.rows(beyond))
        higher = (jnp.minimum(l + 1, level_total - 1) if step == 0 else order[level_total + l + 1])
        results[c] = (halo.move(slab[4 * n + 3], halo.column(beyond), settling(parts))
                      + above(l, level_total) * plume[higher] + source[l])
        plume_out[m if last else n] = results[c]
        if last:
            pairs = [(fields_out.at[f * kept + m], fields_all.at[f * level_total + l])
                     for f in range(3)] + [(plume_out.at[m], plume_all.at[l])]
            sent += fetch_all(out_sems.at[pl.ds(4 * m, 4)], pairs)
    for copy in sent:
        copy.wait()
    if not last:
        for f in range(3):
            for n in range(level_count):
                results[f * level_total + n] = done[f * level_count + n]
        emit_edges([results[c] for c in range(4 * level_total)], first, second, cols)


def exchange(axis, first, second):
    count = lax.axis_size(axis)
    received = []
    for start, data in ((0, first), (1, second)):
        pairs = [(i, i + 1) for i in range(start, count - 1, 2)]
        received.append(lax.ppermute(data, axis, pairs + [(b, a) for a, b in pairs]))
    return received


def local(tables, fields, levels, cuts, parent_modes, owners, plume, source):
    n_gx, n_gy = lax.axis_size("gx"), lax.axis_size("gy")
    devices = n_gx * n_gy
    level_total, cells_x, cells_y = plume.shape
    period = n_gx * cells_x * n_gy * cells_y
    nudged = 3 * levels.shape[0]
    field_rows = 3 * level_total
    total = field_rows + level_total
    rows = -(-(nudged // GROUP * 2 * KX) // devices)
    flat = fields.reshape(field_rows, cells_x, cells_y)
    cuts = cuts.reshape(-1)
    f32 = functools.partial(jax.ShapeDtypeStruct, dtype=jnp.float32)
    x_fwd, y_fwd, y_back, x_back, x_beside = (jnp.asarray(t) for t in tables)

    def vmem(*shape):
        return pltpu.VMEM(shape, jnp.float32)

    def table_space(table):
        return pltpu.VMEM(table.shape[1:], table.dtype)

    def limit(mib):
        return pltpu.CompilerParams(vmem_limit_bytes=mib * 1024 * 1024)

    count = levels.shape[0]
    kept = level_total - count
    half_shapes = [f32((devices // 2, 2 * rows, LANES))] * 2
    places = share_places(n_gx, n_gy)
    same_core = [[gx * n_gy + gy for gx in range(c, n_gx, 2) for gy in range(n_gy)] for c in range(2)]
    order_shape = (3 * level_total,)
    edge_shapes = [f32((total, cells_y)), f32((total, cells_y)), f32((cells_x, 2 * total))]
    levels_space = pltpu.SMEM(levels.shape, jnp.int32)
    owners_space = pltpu.SMEM(owners.shape, jnp.int32)
    order_space = pltpu.SMEM(order_shape, jnp.int32)
    rows_space = vmem(total, cells_y)
    mode_scratch = [vmem(nudged, 4 * KX * KX), table_space(x_fwd),
                    table_space(y_fwd), vmem(nudged, KX, LANES),
                    vmem(devices * rows, 2 * LANES)]
    nudged_scratch = [order_space, vmem(nudged + count, cells_x + 2 * PAD, cells_y),
                      vmem(devices * rows, LANES), vmem(devices * rows, LANES),
                      rows_space, rows_space, pltpu.SemaphoreType.DMA((5,))]
    others_scratch = [vmem(total, cells_x + 2 * PAD, cells_y), rows_space, rows_space]

    def out_scratch(slabs):
        return [vmem(3 * slabs, cells_x, cells_y), vmem(slabs, cells_x, cells_y),
                pltpu.SemaphoreType.DMA((4 * slabs,))]

    keep, send = pl.pallas_call(
        functools.partial(first_kernel, n_gy, level_total, places),
        out_shape=half_shapes,
        in_specs=[HBM] * 6,
        out_specs=[VMEM] * 2,
        scratch_shapes=[levels_space, owners_space, vmem(field_rows, cells_x, cells_y),
                        pltpu.SemaphoreType.DMA((6,))] + mode_scratch,
        compiler_params=limit(8),
        name="first_modes",
    )(*map(in_hbm, (levels, owners, flat, parent_modes, x_fwd, y_fwd)))
    for step in range(STEPS):
        last = step == STEPS - 1
        received = lax.ppermute(send, "gx", [(i, i ^ 1) for i in range(n_gx)])
        modes = pl.pallas_call(
            add_kernel,
            out_shape=half_shapes[0],
            in_specs=[VMEM] * 2,
            out_specs=VMEM,
            compiler_params=limit(4),
            name="add_cores",
        )(keep, received)
        if step == 0:
            modes, flat = lax.optimization_barrier((modes, flat))
            *edges, weights = pl.pallas_call(
                functools.partial(edge_kernel, n_gy, period),
                out_shape=edge_shapes + [f32((2 * rows, LANES))],
                in_specs=[SMEM, VMEM, VMEM],
                out_specs=[VMEM] * 4,
                compiler_params=limit(8),
                name="edges",
            )(cuts, flat, plume)
        else:
            modes, others = lax.optimization_barrier((modes, others))
            others, plume, *edges = pl.pallas_call(
                functools.partial(others_kernel, 0, False, count),
                out_shape=[f32((3 * kept, cells_x, cells_y)), f32(plume.shape)] + edge_shapes,
                in_specs=[VMEM] * 7 + [SMEM] + [VMEM] * 2,
                out_specs=[VMEM] * 5,
                scratch_shapes=others_scratch,
                compiler_params=limit(8),
                name="inner_others",
            )(others, plume, source, *halo, order, flat, winds)
        to_first, to_second, cols = edges
        col_first, col_second = exchange("gy", cols, cols)
        parts = lax.all_to_all(modes, AXES, 0, 0, axis_index_groups=same_core, tiled=True)
        parts, col_first, col_second = lax.optimization_barrier((parts, col_first, col_second))
        share = pl.pallas_call(
            functools.partial(share_kernel, n_gx, n_gy),
            out_shape=f32((devices, rows + beside_rows(rows), LANES)),
            in_specs=[VMEM] * 4,
            out_specs=VMEM,
            compiler_params=limit(8),
            name="share_sum",
        )(weights, parts, x_back, x_beside)
        share, to_first, to_second = lax.optimization_barrier((share, to_first, to_second))
        row_first, row_second = exchange("gx", to_first, to_second)
        halo = [row_first, row_second, col_first, col_second]
        if step == 0:
            share, levels = lax.optimization_barrier((share, levels))
            flat, others, y_back, order = pl.pallas_call(
                functools.partial(prepare_kernel, level_total),
                out_shape=[f32((3 * count, cells_x, cells_y)), f32((3 * kept, cells_x, cells_y)),
                           jax.ShapeDtypeStruct(y_back.shape[1:], y_back.dtype),
                           jax.ShapeDtypeStruct(order_shape, jnp.int32)],
                in_specs=[SMEM, VMEM, HBM],
                out_specs=[VMEM] * 3 + [SMEM],
                scratch_shapes=[pltpu.SemaphoreType.DMA((1,))],
                compiler_params=limit(8),
                name="prepare",
            )(levels, flat, in_hbm(y_back))
        shares = lax.all_to_all(share, AXES, 0, 0, tiled=True)
        if last:
            final = pl.pallas_call(
                functools.partial(others_kernel, step, True, count),
                out_shape=[f32((field_rows, cells_x, cells_y)), f32(plume.shape)],
                in_specs=[VMEM] * 7 + [SMEM],
                out_specs=[HBM] * 2,
                scratch_shapes=others_scratch + out_scratch(kept),
                compiler_params=limit(8),
                name="last_others",
            )(others, plume, source, *halo, order)
            flat, plume = pl.pallas_call(
                functools.partial(nudged_kernel, n_gy, step, True, count, level_total, None),
                out_shape=[f32((field_rows, cells_x, cells_y)), f32(plume.shape)],
                in_specs=[VMEM] * 7 + [HBM] + [VMEM] * 2 + [HBM] * 2,
                out_specs=[HBM] * 2,
                scratch_shapes=nudged_scratch + out_scratch(count),
                input_output_aliases={10: 0, 11: 1},
                compiler_params=limit(12),
                name="last_nudged",
            )(shares, flat, *halo, y_back, in_hbm(order), plume, source, *final)
        else:
            flat, winds, keep, send = pl.pallas_call(
                functools.partial(nudged_kernel, n_gy, step, False, count, level_total, places),
                out_shape=[f32((nudged, cells_x, cells_y)), f32((2 * count, cells_x, cells_y))]
                + half_shapes,
                in_specs=[VMEM] * 7 + [HBM] * 5,
                out_specs=[VMEM] * 4,
                scratch_shapes=nudged_scratch + [owners_space] + mode_scratch,
                compiler_params=limit(12),
                name="inner_nudged",
            )(shares, flat, *halo, y_back, in_hbm(order),
              *map(in_hbm, (owners, parent_modes, x_fwd, y_fwd)))
    return flat.reshape(fields.shape), plume


def solution(mesh):
    in_specs = (
        P(None, None, "gx", "gy"),
        P(),
        P(),
        P(("gx", "gy"), None, None, None),
        P(),
        P(None, "gx", "gy"),
        P(None, "gx", "gy"),
    )
    out_specs = (P(None, None, "gx", "gy"), P(None, "gx", "gy"))
    n_gx, n_gy = mesh.shape["gx"], mesh.shape["gy"]

    def whole(fields, levels, cuts, parent_modes, owners, plume, source):
        tables = build_tables(n_gx, n_gy, plume.shape[1] // n_gx, plume.shape[2] // n_gy)
        return jax.shard_map(
            functools.partial(local, tables), mesh=mesh, in_specs=in_specs, out_specs=out_specs,
            check_vma=False,
        )(fields, levels, cuts, parent_modes, owners, plume, source)

    return whole
```

```python
import functools
import math

import jax
import jax.numpy as jnp
import ml_dtypes
import numpy as np
from jax import lax
from jax.experimental import pallas as pl
from jax.experimental.pallas import tpu as pltpu
from jax.sharding import PartitionSpec as P

KX = 32
STEPS = 2
GROUP = 4
LANES = GROUP * KX
PAD = 8
VMEM = pl.BlockSpec(memory_space=pltpu.VMEM)
SMEM = pl.BlockSpec(memory_space=pltpu.SMEM)
HBM = pl.BlockSpec(memory_space=pltpu.HBM)
AXES = ("gx", "gy")


def in_hbm(array):
    return pltpu.with_memory_space_constraint(array, pltpu.HBM)


def wave_table(positions, period):
    wavenum = np.arange(KX)[:, None]
    phase = (wavenum * positions[None, :] % period) * (2.0 * math.pi / period)
    inside = (positions >= 0) & (positions < period)
    return np.concatenate([np.cos(phase), np.sin(phase)], axis=0) * inside[None, :]


def split(a):
    head = a.astype(jnp.bfloat16)
    return head, (a - head.astype(jnp.float32)).astype(jnp.bfloat16)


def split_table(table, axis, order):
    head = table.astype(ml_dtypes.bfloat16)
    rest = (table - head.astype(np.float64)).astype(ml_dtypes.bfloat16)
    return np.concatenate([head if part == "h" else rest for part in order], axis=axis)


def per_slab(table):
    return np.kron(np.eye(GROUP), table)


def build_tables(n_gx, n_gy, cells_x, cells_y):
    period_x, period_y = n_gx * cells_x, n_gy * cells_y
    scaling = 1.0 / math.sqrt(period_x * period_y)
    parity = [np.arange(p, 2 * KX, 2) for p in range(2)]
    x_fwd, y_fwd, y_back, inner, outer = [], [], [], [], []
    for g in range(n_gx):
        first = g * cells_x
        table = wave_table(first + np.arange(cells_x), period_x)
        x_fwd.append(split_table(
            np.concatenate([per_slab(table[rows].T) for rows in parity], axis=1), 0, "hhl"))
        beside = wave_table(np.array([first - 1, first + cells_x]), period_x)
        inner.append(np.concatenate([np.tile(table[rows], (GROUP, 1)) for rows in parity], axis=0))
        outer.append(np.concatenate([per_slab(beside[rows]) for rows in parity], axis=0))
    spare = -(2 * GROUP * n_gx) % LANES
    x_back = np.concatenate(inner, axis=1)
    x_beside = np.concatenate(outer + [np.zeros((2 * LANES, spare))], axis=1)
    for g in range(n_gy):
        first = g * cells_y
        table = wave_table(first + np.arange(cells_y), period_y)
        edge = np.zeros((2 * KX, cells_y))
        edge[:, [0, -1]] = wave_table(np.array([first - 1, first + cells_y]), period_y)
        y_fwd.append(split_table(table * scaling, 1, "hlh"))
        y_back.append(split_table(np.concatenate([table, edge], axis=1), 0, "hhl"))
    return [np.stack(x_fwd), np.stack(y_fwd), np.stack(y_back),
            split_table(x_back, 0, "hl"), split_table(x_beside, 0, "hl")]


def data_dot(a, table):
    head, rest = split(a)
    return jnp.dot(
        jnp.concatenate([head, rest, head], axis=1), table, preferred_element_type=jnp.float32
    )


def two_part_dot(a, table):
    head, rest = split(a)
    depth = a.shape[1]
    heads = jnp.dot(
        jnp.concatenate([head, rest], axis=0), table[:depth], preferred_element_type=jnp.float32)
    rests = jnp.dot(head, table[depth:], preferred_element_type=jnp.float32)
    return heads[: a.shape[0]] + heads[a.shape[0] :] + rests


def columns_dot(a, table):
    head, rest = split(a)
    stacked = jnp.concatenate([head, rest, head], axis=0)
    return lax.dot_general(
        stacked, table, (((0,), (0,)), ((), ())), preferred_element_type=jnp.float32)


def core():
    return lax.rem(lax.axis_index("gx"), 2)


def ranking(n_gx, n_gy):
    return sorted(range(n_gx * n_gy), key=lambda d: (abs(2 * (d % n_gy) - (n_gy - 1)), d))


def core_groups(n_gx, n_gy):
    return [[d for d in ranking(n_gx, n_gy) if d // n_gy % 2 == c] for c in range(2)]


def share_places(n_gx, n_gy):
    places = {}
    for c, group in enumerate(core_groups(n_gx, n_gy)):
        places.update({d: c * len(group) + i for i, d in enumerate(group)})
    return [places[d] for d in range(n_gx * n_gy)]


def emit_modes(chosen, parent, is_owner, places, x_fwd, y_fwd, keep, send, turned, work):
    devices, rows = len(places), keep.shape[1] // 2
    slabs = parent.shape[0]
    groups = slabs // GROUP
    head, rest = split(jnp.concatenate(chosen, axis=0))
    half = lax.dot_general(
        y_fwd, jnp.concatenate([head, head, rest], axis=1), (((1,), (1,)), ((), ())),
        preferred_element_type=jnp.float32)
    half = jnp.concatenate([half[:, t * LANES : (t + 1) * LANES] for t in range(groups)], axis=0)
    count = groups * 2 * KX
    work[0:count] = -data_dot(half, x_fwd)
    if count < devices * rows:
        work[count:] = jnp.zeros((devices * rows - count, 2 * LANES), jnp.float32)

    @pl.when(is_owner)
    def _():
        for i in range(KX):
            turned[:, i, :] = parent[:, i * LANES : (i + 1) * LANES]
        for t in range(groups):
            block = turned[t * GROUP : (t + 1) * GROUP].reshape(LANES, LANES).T
            span = slice(t * 2 * KX, (t + 1) * 2 * KX)
            for p in range(2):
                work[span, p * LANES : (p + 1) * LANES] += block[p * 2 * KX : (p + 1) * 2 * KX]

    count = devices // 2
    for mine in range(2):
        @pl.when(core() == mine)
        def _(mine=mine):
            for d in range(devices):
                half = keep if places[d] // count == mine else send
                for p in range(2):
                    half[places[d] % count, p * rows : (p + 1) * rows, :] = work[
                        d * rows : (d + 1) * rows, p * LANES : (p + 1) * LANES]


def add_kernel(kept, received, out):
    out[...] = kept[...] + received[...]


def fetch_all(sems, pairs):
    copies = [pltpu.make_async_copy(a, b, sems.at[i]) for i, (a, b) in enumerate(pairs)]
    for copy in copies:
        copy.start()
    return copies


def slab_of(levels, c, level_count, level_total):
    return (c // level_count) * level_total + levels[c % level_count]


def first_kernel(n_gy, level_total, places, levels_all, owners_all, fields_all, parent_all,
                 x_fwd_all, y_fwd_all, keep, send, levels, owners, fields, sems, parent, x_fwd, y_fwd,
                 turned, work):
    gx, gy = lax.axis_index("gx"), lax.axis_index("gy")
    copies = fetch_all(sems, [
        (levels_all, levels), (owners_all, owners), (fields_all, fields),
        (x_fwd_all.at[gx], x_fwd), (y_fwd_all.at[gy], y_fwd), (parent_all.at[0, 0], parent)])
    for copy in copies:
        copy.wait()
    level_count = parent.shape[0] // 3
    emit_modes(
        [fields[slab_of(levels, c, level_count, level_total)] for c in range(parent.shape[0])],
        parent, owners[0] == gx * n_gy + gy, places, x_fwd[...], y_fwd[...], keep, send,
        turned, work,
    )


def is_even(axis):
    return lax.rem(lax.axis_index(axis), 2) == 0


def edge_kernel(n_gy, period, cuts, fields, plume, first, second, cols, weights):
    weights[...] = share_weights(n_gy, period, cuts, weights.shape)
    slabs = [fields[c] for c in range(fields.shape[0])]
    emit_edges(slabs + [plume[l] for l in range(plume.shape[0])], first, second, cols)


def prepare_kernel(level_total, levels, fields, y_back_all, nudged, others, y_back, order, sems):
    copies = fetch_all(sems, [(y_back_all.at[lax.axis_index("gy")], y_back)])
    count = levels.shape[0]
    for n in range(count):
        order[n] = levels[n]
    spot = jnp.int32(count)
    for l in range(level_total):
        found = levels[0] == l
        for n in range(1, count):
            found = found | (levels[n] == l)
        order[spot] = jnp.int32(l)
        spot = spot + jnp.where(found, 0, 1)
    chosen = [order[n] for n in range(level_total)]
    for n in range(level_total, order.shape[0]):
        order[n] = jnp.int32(0)
    for n in range(level_total):
        order[level_total + chosen[n]] = jnp.int32(n)
    slabs = [fields[f * level_total + l] for f in range(3) for l in chosen]
    kept = level_total - count
    for c, a in enumerate(slabs):
        f, n = c // level_total, c % level_total
        if n < count:
            nudged[f * count + n] = a
        else:
            others[f * kept + n - count] = a
    for copy in copies:
        copy.wait()


def emit_edges(slabs, first, second, cols):
    even = is_even("gx")
    lane = lax.broadcasted_iota(jnp.int32, cols.shape, 1)
    acc = jnp.zeros(cols.shape, jnp.float32)
    for c, a in enumerate(slabs):
        west, east = a[:1], a[a.shape[0] - 1 :]
        first[c : c + 1, :] = jnp.where(even, east, west)
        second[c : c + 1, :] = jnp.where(even, west, east)
        acc = jnp.where(lane // 2 == c, pltpu.roll(a, 2 * c + 1, 1), acc)
    cols[...] = acc


def share_weights(n_gy, period, cuts, shape):
    rows = shape[0] // 2
    me = lax.axis_index("gx") * n_gy + lax.axis_index("gy")
    place = lax.broadcasted_iota(jnp.int32, shape, 0)
    lane = lax.broadcasted_iota(jnp.int32, shape, 1)
    p = (place >= rows).astype(jnp.int32)
    row = me * rows + place - p * rows
    k = 2 * (lane % KX) + p
    j = row % (2 * KX)
    slab = GROUP * (row // (2 * KX)) + lane // KX
    limit = jnp.zeros(shape, jnp.int32)
    for c in range(cuts.shape[0]):
        limit = jnp.where(slab == c, cuts[c], limit)
    keep = ((k % KX) < limit) & ((j % KX) < limit)
    factor = jnp.where(k == 0, 1.0, 2.0) * jnp.where(j == 0, 1.0, 2.0) * (1.0 / math.sqrt(period))
    return jnp.where(keep, factor, 0.0)


def beside_rows(rows):
    return -(-rows // 3)


def share_kernel(n_gx, n_gy, weights, parts, x_back, x_beside, out):
    rows = parts.shape[1] // 2
    total = parts[0]
    for d in range(1, parts.shape[0]):
        total = total + parts[d]
    mismatch = total * weights[...]
    both = jnp.concatenate([mismatch[:rows], mismatch[rows:]], axis=1)
    spare = -rows % 16
    if spare:
        both = jnp.concatenate([both, jnp.zeros((spare, 2 * LANES), jnp.float32)], axis=0)
    slab_lane = lax.broadcasted_iota(jnp.int32, both.shape, 1) % LANES // KX
    chosen = [jnp.where(slab_lane == n, both, 0.0) for n in range(GROUP)]
    inner = two_part_dot(jnp.concatenate(chosen, axis=0), x_back)
    edge_all = two_part_dot(both, x_beside)
    height = rows + spare
    packed = beside_rows(rows)
    width = 2 * GROUP
    cells_x = LANES // GROUP
    slot = lax.broadcasted_iota(jnp.int32, (height, LANES), 1) // cells_x
    spot = lax.broadcasted_iota(jnp.int32, (packed, LANES), 1) // width
    spot_at = {d: i for i, d in enumerate(ranking(n_gx, n_gy))}
    for g in range(n_gx):
        first = g * cells_x // LANES * LANES
        tile = jnp.zeros((height, LANES), jnp.float32)
        for n in range(GROUP):
            piece = inner[n * height : (n + 1) * height, first : first + LANES]
            tile = jnp.where(slot == n, pltpu.roll(piece, (n - g) * cells_x % LANES, 1), tile)
        first = g * width // LANES * LANES
        beside = jnp.zeros((packed, LANES), jnp.float32)
        for m in range(3):
            piece = edge_all[m * packed : (m + 1) * packed, first : first + LANES]
            beside = jnp.where(
                spot == m, pltpu.roll(piece, (m - g) * width % LANES, 1), beside)
        for h in range(n_gy):
            out[spot_at[g * n_gy + h], :rows, :] = tile[:rows]
            out[spot_at[g * n_gy + h], rows:, :] = beside


class Halo:
    def __init__(self, row_first, row_second, col_first, col_second, west, east):
        even = is_even("gx")
        west[...] = jnp.where(even, row_second[...], row_first[...])
        east[...] = jnp.where(even, row_first[...], row_second[...])
        self.west, self.east = west, east
        even = is_even("gy")
        north = jnp.where(even, col_first[...], col_second[...])
        south = jnp.where(even, col_second[...], col_first[...])
        shape = north.shape
        lane = lax.broadcasted_iota(jnp.int32, shape, 1)
        self.last = shape[1] - 1
        self.at_first, self.at_last = lane == 0, lane == self.last
        self.columns = jnp.where(
            lane % 2 == 0, pltpu.roll(north, self.last, 1), pltpu.roll(south, 1, 1))

    def rows(self, c):
        return self.west[pl.ds(c, 1), :], self.east[pl.ds(c, 1), :]

    def column(self, c):
        return pltpu.roll(self.columns, self.last - 2 * c, 1)

    def move(self, slab, column, parts):
        centre, to_west, to_east, to_south, to_north = parts
        cells_x = column.shape[0]
        a = slab[PAD : PAD + cells_x]
        return (
            centre * a
            + to_west * slab[PAD - 1 : PAD - 1 + cells_x]
            + to_east * slab[PAD + 1 : PAD + 1 + cells_x]
            + to_south * jnp.where(self.at_first, column, pltpu.roll(a, 1, 1))
            + to_north * jnp.where(self.at_last, column, pltpu.roll(a, self.last, 1))
        )


def place(slab, a, rows):
    cells_x = a.shape[0]
    slab[PAD : PAD + cells_x] = a
    slab[PAD - 1 : PAD] = rows[0]
    slab[PAD + cells_x : PAD + cells_x + 1] = rows[1]


def wind_weights(u, v):
    neighbours = (
        0.1 + 0.1 * jnp.maximum(u, 0.0), 0.1 - 0.1 * jnp.minimum(u, 0.0),
        0.1 + 0.1 * jnp.maximum(v, 0.0), 0.1 - 0.1 * jnp.minimum(v, 0.0),
    )
    centre = 1.0 - (neighbours[0] + neighbours[1] + neighbours[2] + neighbours[3])
    return (centre,) + neighbours


def settling(parts):
    return (parts[0] - 0.3,) + parts[1:]


def above(l, level_total):
    return jnp.where(l + 1 < level_total, 0.3, 0.0).astype(jnp.float32)


def nudge_updates(ranks, shares, spread, spread_edges, y_table, nudged, cells_x):
    devices = shares.shape[0]
    rows = spread.shape[0] // devices
    packed = beside_rows(rows)
    width = 2 * GROUP
    for i, d in enumerate(ranks):
        spread[d * rows : (d + 1) * rows] = shares[i, :rows, :]
        edge = shares[i, rows:, :]
        for m in range(3):
            count = min(packed, rows - m * packed)
            if count > 0:
                moved = pltpu.roll(edge, -m * width % LANES, 1) if m else edge
                start = d * rows + m * packed
                spread_edges[start : start + count] = moved[:count]
    groups = nudged // GROUP
    spot_of = lax.broadcasted_iota(jnp.int32, (2 * KX, LANES), 1) // width
    edges = jnp.zeros((2 * KX, LANES), jnp.float32)
    for t in range(groups):
        piece = spread_edges[t * 2 * KX : (t + 1) * 2 * KX]
        edges = jnp.where(spot_of == t, pltpu.roll(piece, t * width, 1) if t else piece, edges)
    update_rows = columns_dot(edges, y_table)
    updates = []
    for t in range(groups):
        update = columns_dot(spread[t * 2 * KX : (t + 1) * 2 * KX], y_table)
        updates += [update[n * cells_x : (n + 1) * cells_x] for n in range(GROUP)]
    return updates, update_rows


def nudged_kernel(n_gy, step, last, level_count, level_total, ranks, places, shares, fields, row_first, row_second,
                  col_first, col_second, y_back, order_all, *rest):
    gx, gy = lax.axis_index("gx"), lax.axis_index("gy")
    cells_x, cells_y = fields.shape[1:]
    nudged = 3 * level_count
    if last:
        (plume, source, _, _, fields_all, plume_all, order, slabs, spread, spread_edges, west, east,
         sems, fields_out, plume_out, out_sems) = rest
        extra = []
    else:
        (owners_all, parent_all, x_fwd_all, y_fwd_all, fields_out, winds_out, keep, send,
         order, slabs, spread, spread_edges, west, east, sems,
         owners, parent, x_fwd, y_fwd, turned, work) = rest
        extra = [(owners_all, owners), (x_fwd_all.at[gx], x_fwd), (y_fwd_all.at[gy], y_fwd),
                 (parent_all.at[0, step + 1], parent)]
    copies = fetch_all(sems, [(order_all, order)] + extra)
    halo = Halo(row_first, row_second, col_first, col_second, west, east)
    updates, update_rows = nudge_updates(
        ranks, shares, spread, spread_edges, y_back[...], nudged, cells_x)
    copies[0].wait()
    level_at = [order[n] for n in range(level_count)]
    halo_at = level_at if step == 0 else list(range(level_count))
    beside = []
    for k in range(nudged):
        f, n = k // level_count, k % level_count
        a = fields[k]
        before, after = halo.rows(f * level_total + halo_at[n])
        place(slabs.at[k], a + updates[k][:, :cells_y],
              (before + update_rows[2 * k : 2 * k + 1, :cells_y],
               after + update_rows[2 * k + 1 : 2 * k + 2, :cells_y]))
        beside.append(updates[k][:, cells_y:])
    inner = slice(PAD, PAD + cells_x)
    results = [None] * nudged
    sent = []
    for n in range(level_count):
        u, v = slabs[n, inner], slabs[level_count + n, inner]
        parts = wind_weights(u, v)
        for f in range(3):
            k = f * level_count + n
            column = halo.column(f * level_total + halo_at[n]) + beside[k]
            results[k] = halo.move(slabs[k], column, parts)
            fields_out[k] = results[k]
        if not last:
            winds_out[n] = u
            winds_out[level_count + n] = v
            continue
        l = level_at[n]
        c = 3 * level_total + n
        place(slabs.at[nudged + n], plume[n], halo.rows(c))
        settled = halo.move(slabs[nudged + n], halo.column(c), settling(parts))
        plume_out[n] = settled + above(l, level_total) * plume[order[level_total + l + 1]] + source[l]
        pairs = [(fields_out.at[f * level_count + n], fields_all.at[f * level_total + l])
                 for f in range(3)] + [(plume_out.at[n], plume_all.at[l])]
        sent += fetch_all(out_sems.at[pl.ds(4 * n, 4)], pairs)
    if last:
        for copy in sent:
            copy.wait()
        return
    for copy in copies[1:]:
        copy.wait()
    emit_modes(results, parent, owners[step + 1] == gx * n_gy + gy, places, x_fwd[...], y_fwd[...],
               keep, send, turned, work)


def others_kernel(step, last, level_count, fields, plume, source, row_first, row_second, col_first,
                  col_second, order, *rest):
    level_total, cells_x, cells_y = plume.shape
    if last:
        fields_all, plume_all, slab, west, east, fields_out, plume_out, out_sems = rest
    else:
        done, winds, fields_out, plume_out, first, second, cols, slab, west, east = rest
    halo = Halo(row_first, row_second, col_first, col_second, west, east)
    level_at = [order[n] for n in range(level_total)]
    kept = level_total - level_count
    sent = []
    results = {}
    for n in range(level_count if last else 0, level_total):
        l = level_at[n]
        m = n - level_count
        if m < 0:
            parts = wind_weights(winds[n], winds[level_count + n])
        else:
            given = [fields[f * kept + m] for f in range(3)]
            parts = wind_weights(given[0], given[1])
            for f in range(3):
                c = f * level_total + n
                beyond = f * level_total + l if step == 0 else c
                place(slab.at[4 * n + f], given[f], halo.rows(beyond))
                results[c] = halo.move(slab[4 * n + f], halo.column(beyond), parts)
                fields_out[f * kept + m] = results[c]
        c = 3 * level_total + n
        beyond = 3 * level_total + l if step == 0 else c
        place(slab.at[4 * n + 3], plume[l] if step == 0 else plume[n], halo.rows(beyond))
        higher = (jnp.minimum(l + 1, level_total - 1) if step == 0 else order[level_total + l + 1])
        results[c] = (halo.move(slab[4 * n + 3], halo.column(beyond), settling(parts))
                      + above(l, level_total) * plume[higher] + source[l])
        plume_out[m if last else n] = results[c]
        if last:
            pairs = [(fields_out.at[f * kept + m], fields_all.at[f * level_total + l])
                     for f in range(3)] + [(plume_out.at[m], plume_all.at[l])]
            sent += fetch_all(out_sems.at[pl.ds(4 * m, 4)], pairs)
    for copy in sent:
        copy.wait()
    if not last:
        for f in range(3):
            for n in range(level_count):
                results[f * level_total + n] = done[f * level_count + n]
        emit_edges([results[c] for c in range(4 * level_total)], first, second, cols)


def exchange(axis, first, second):
    count = lax.axis_size(axis)
    received = []
    for start, data in ((0, first), (1, second)):
        pairs = [(i, i + 1) for i in range(start, count - 1, 2)]
        received.append(lax.ppermute(data, axis, pairs + [(b, a) for a, b in pairs]))
    return received


def local(tables, fields, levels, cuts, parent_modes, owners, plume, source):
    n_gx, n_gy = lax.axis_size("gx"), lax.axis_size("gy")
    devices = n_gx * n_gy
    level_total, cells_x, cells_y = plume.shape
    period = n_gx * cells_x * n_gy * cells_y
    nudged = 3 * levels.shape[0]
    field_rows = 3 * level_total
    total = field_rows + level_total
    rows = -(-(nudged // GROUP * 2 * KX) // devices)
    flat = fields.reshape(field_rows, cells_x, cells_y)
    cuts = cuts.reshape(-1)
    f32 = functools.partial(jax.ShapeDtypeStruct, dtype=jnp.float32)
    x_fwd, y_fwd, y_back, x_back, x_beside = (jnp.asarray(t) for t in tables)

    def vmem(*shape):
        return pltpu.VMEM(shape, jnp.float32)

    def table_space(table):
        return pltpu.VMEM(table.shape[1:], table.dtype)

    def limit(mib):
        return pltpu.CompilerParams(vmem_limit_bytes=mib * 1024 * 1024)

    count = levels.shape[0]
    kept = level_total - count
    half_shapes = [f32((devices // 2, 2 * rows, LANES))] * 2
    places = share_places(n_gx, n_gy)
    ranks = ranking(n_gx, n_gy)
    order_shape = (3 * level_total,)
    edge_shapes = [f32((total, cells_y)), f32((total, cells_y)), f32((cells_x, 2 * total))]
    levels_space = pltpu.SMEM(levels.shape, jnp.int32)
    owners_space = pltpu.SMEM(owners.shape, jnp.int32)
    order_space = pltpu.SMEM(order_shape, jnp.int32)
    rows_space = vmem(total, cells_y)
    mode_scratch = [vmem(nudged, 4 * KX * KX), table_space(x_fwd),
                    table_space(y_fwd), vmem(nudged, KX, LANES),
                    vmem(devices * rows, 2 * LANES)]
    nudged_scratch = [order_space, vmem(nudged + count, cells_x + 2 * PAD, cells_y),
                      vmem(devices * rows, LANES), vmem(devices * rows, LANES),
                      rows_space, rows_space, pltpu.SemaphoreType.DMA((5,))]
    others_scratch = [vmem(total, cells_x + 2 * PAD, cells_y), rows_space, rows_space]

    def out_scratch(slabs):
        return [vmem(3 * slabs, cells_x, cells_y), vmem(slabs, cells_x, cells_y),
                pltpu.SemaphoreType.DMA((4 * slabs,))]

    keep, send = pl.pallas_call(
        functools.partial(first_kernel, n_gy, level_total, places),
        out_shape=half_shapes,
        in_specs=[HBM] * 6,
        out_specs=[VMEM] * 2,
        scratch_shapes=[levels_space, owners_space, vmem(field_rows, cells_x, cells_y),
                        pltpu.SemaphoreType.DMA((6,))] + mode_scratch,
        compiler_params=limit(8),
        name="first_modes",
    )(*map(in_hbm, (levels, owners, flat, parent_modes, x_fwd, y_fwd)))
    for step in range(STEPS):
        last = step == STEPS - 1
        received = lax.ppermute(send, "gx", [(i, i ^ 1) for i in range(n_gx)])
        modes = pl.pallas_call(
            add_kernel,
            out_shape=half_shapes[0],
            in_specs=[VMEM] * 2,
            out_specs=VMEM,
            compiler_params=limit(4),
            name="add_cores",
        )(keep, received)
        if step == 0:
            modes, flat = lax.optimization_barrier((modes, flat))
            *edges, weights = pl.pallas_call(
                functools.partial(edge_kernel, n_gy, period),
                out_shape=edge_shapes + [f32((2 * rows, LANES))],
                in_specs=[SMEM, VMEM, VMEM],
                out_specs=[VMEM] * 4,
                compiler_params=limit(8),
                name="edges",
            )(cuts, flat, plume)
        else:
            modes, others = lax.optimization_barrier((modes, others))
            others, plume, *edges = pl.pallas_call(
                functools.partial(others_kernel, 0, False, count),
                out_shape=[f32((3 * kept, cells_x, cells_y)), f32(plume.shape)] + edge_shapes,
                in_specs=[VMEM] * 7 + [SMEM] + [VMEM] * 2,
                out_specs=[VMEM] * 5,
                scratch_shapes=others_scratch,
                compiler_params=limit(8),
                name="inner_others",
            )(others, plume, source, *halo, order, flat, winds)
        to_first, to_second, cols = edges
        col_first, col_second = exchange("gy", cols, cols)
        parts = lax.all_to_all(modes, AXES, 0, 0, axis_index_groups=core_groups(n_gx, n_gy),
                               tiled=True)
        parts, col_first, col_second = lax.optimization_barrier((parts, col_first, col_second))
        share = pl.pallas_call(
            functools.partial(share_kernel, n_gx, n_gy),
            out_shape=f32((devices, rows + beside_rows(rows), LANES)),
            in_specs=[VMEM] * 4,
            out_specs=VMEM,
            compiler_params=limit(8),
            name="share_sum",
        )(weights, parts, x_back, x_beside)
        share, to_first, to_second = lax.optimization_barrier((share, to_first, to_second))
        row_first, row_second = exchange("gx", to_first, to_second)
        halo = [row_first, row_second, col_first, col_second]
        if step == 0:
            share, levels = lax.optimization_barrier((share, levels))
            flat, others, y_back, order = pl.pallas_call(
                functools.partial(prepare_kernel, level_total),
                out_shape=[f32((3 * count, cells_x, cells_y)), f32((3 * kept, cells_x, cells_y)),
                           jax.ShapeDtypeStruct(y_back.shape[1:], y_back.dtype),
                           jax.ShapeDtypeStruct(order_shape, jnp.int32)],
                in_specs=[SMEM, VMEM, HBM],
                out_specs=[VMEM] * 3 + [SMEM],
                scratch_shapes=[pltpu.SemaphoreType.DMA((1,))],
                compiler_params=limit(8),
                name="prepare",
            )(levels, flat, in_hbm(y_back))
        shares = lax.all_to_all(share, AXES, 0, 0, axis_index_groups=[ranks], tiled=True)
        if last:
            final = pl.pallas_call(
                functools.partial(others_kernel, step, True, count),
                out_shape=[f32((field_rows, cells_x, cells_y)), f32(plume.shape)],
                in_specs=[VMEM] * 7 + [SMEM],
                out_specs=[HBM] * 2,
                scratch_shapes=others_scratch + out_scratch(kept),
                compiler_params=limit(8),
                name="last_others",
            )(others, plume, source, *halo, order)
            flat, plume = pl.pallas_call(
                functools.partial(nudged_kernel, n_gy, step, True, count, level_total, ranks, None),
                out_shape=[f32((field_rows, cells_x, cells_y)), f32(plume.shape)],
                in_specs=[VMEM] * 7 + [HBM] + [VMEM] * 2 + [HBM] * 2,
                out_specs=[HBM] * 2,
                scratch_shapes=nudged_scratch + out_scratch(count),
                input_output_aliases={10: 0, 11: 1},
                compiler_params=limit(12),
                name="last_nudged",
            )(shares, flat, *halo, y_back, in_hbm(order), plume, source, *final)
        else:
            flat, winds, keep, send = pl.pallas_call(
                functools.partial(nudged_kernel, n_gy, step, False, count, level_total, ranks, places),
                out_shape=[f32((nudged, cells_x, cells_y)), f32((2 * count, cells_x, cells_y))]
                + half_shapes,
                in_specs=[VMEM] * 7 + [HBM] * 5,
                out_specs=[VMEM] * 4,
                scratch_shapes=nudged_scratch + [owners_space] + mode_scratch,
                compiler_params=limit(12),
                name="inner_nudged",
            )(shares, flat, *halo, y_back, in_hbm(order),
              *map(in_hbm, (owners, parent_modes, x_fwd, y_fwd)))
    return flat.reshape(fields.shape), plume


def solution(mesh):
    in_specs = (
        P(None, None, "gx", "gy"),
        P(),
        P(),
        P(("gx", "gy"), None, None, None),
        P(),
        P(None, "gx", "gy"),
        P(None, "gx", "gy"),
    )
    out_specs = (P(None, None, "gx", "gy"), P(None, "gx", "gy"))
    n_gx, n_gy = mesh.shape["gx"], mesh.shape["gy"]

    def whole(fields, levels, cuts, parent_modes, owners, plume, source):
        tables = build_tables(n_gx, n_gy, plume.shape[1] // n_gx, plume.shape[2] // n_gy)
        return jax.shard_map(
            functools.partial(local, tables), mesh=mesh, in_specs=in_specs, out_specs=out_specs,
            check_vma=False,
        )(fields, levels, cuts, parent_modes, owners, plume, source)

    return whole
```

```python
import functools
import math

import jax
import jax.numpy as jnp
import ml_dtypes
import numpy as np
from jax import lax
from jax.experimental import pallas as pl
from jax.experimental.pallas import tpu as pltpu
from jax.sharding import PartitionSpec as P

KX = 32
STEPS = 2
GROUP = 4
LANES = GROUP * KX
PAD = 8
VMEM = pl.BlockSpec(memory_space=pltpu.VMEM)
SMEM = pl.BlockSpec(memory_space=pltpu.SMEM)
HBM = pl.BlockSpec(memory_space=pltpu.HBM)
AXES = ("gx", "gy")


def in_hbm(array):
    return pltpu.with_memory_space_constraint(array, pltpu.HBM)


def wave_table(positions, period):
    wavenum = np.arange(KX)[:, None]
    phase = (wavenum * positions[None, :] % period) * (2.0 * math.pi / period)
    inside = (positions >= 0) & (positions < period)
    return np.concatenate([np.cos(phase), np.sin(phase)], axis=0) * inside[None, :]


def split(a):
    head = a.astype(jnp.bfloat16)
    return head, (a - head.astype(jnp.float32)).astype(jnp.bfloat16)


def split_table(table, axis, order):
    head = table.astype(ml_dtypes.bfloat16)
    rest = (table - head.astype(np.float64)).astype(ml_dtypes.bfloat16)
    return np.concatenate([head if part == "h" else rest for part in order], axis=axis)


def per_slab(table):
    return np.kron(np.eye(GROUP), table)


def build_tables(n_gx, n_gy, cells_x, cells_y):
    period_x, period_y = n_gx * cells_x, n_gy * cells_y
    scaling = 1.0 / math.sqrt(period_x * period_y)
    parity = [np.arange(p, 2 * KX, 2) for p in range(2)]
    x_fwd, y_fwd, y_back, inner, outer = [], [], [], [], []
    for g in range(n_gx):
        first = g * cells_x
        table = wave_table(first + np.arange(cells_x), period_x)
        x_fwd.append(split_table(
            np.concatenate([per_slab(table[rows].T) for rows in parity], axis=1), 0, "hhl"))
        beside = wave_table(np.array([first - 1, first + cells_x]), period_x)
        inner.append(np.concatenate([np.tile(table[rows], (GROUP, 1)) for rows in parity], axis=0))
        outer.append(np.concatenate([per_slab(beside[rows]) for rows in parity], axis=0))
    spare = -(2 * GROUP * n_gx) % LANES
    x_back = np.concatenate(inner, axis=1)
    x_beside = np.concatenate(outer + [np.zeros((2 * LANES, spare))], axis=1)
    for g in range(n_gy):
        first = g * cells_y
        table = wave_table(first + np.arange(cells_y), period_y)
        edge = np.zeros((2 * KX, cells_y))
        edge[:, [0, -1]] = wave_table(np.array([first - 1, first + cells_y]), period_y)
        y_fwd.append(split_table(table * scaling, 1, "hlh"))
        y_back.append(split_table(np.concatenate([table, edge], axis=1), 0, "hhl"))
    return [np.stack(x_fwd), np.stack(y_fwd), np.stack(y_back),
            split_table(x_back, 0, "hl"), split_table(x_beside, 0, "hl")]


def data_dot(a, table):
    head, rest = split(a)
    return jnp.dot(
        jnp.concatenate([head, rest, head], axis=1), table, preferred_element_type=jnp.float32
    )


def two_part_dot(a, table):
    head, rest = split(a)
    depth = a.shape[1]
    heads = jnp.dot(
        jnp.concatenate([head, rest], axis=0), table[:depth], preferred_element_type=jnp.float32)
    rests = jnp.dot(head, table[depth:], preferred_element_type=jnp.float32)
    return heads[: a.shape[0]] + heads[a.shape[0] :] + rests


def columns_dot(a, table):
    head, rest = split(a)
    stacked = jnp.concatenate([head, rest, head], axis=0)
    return lax.dot_general(
        stacked, table, (((0,), (0,)), ((), ())), preferred_element_type=jnp.float32)


def core():
    return lax.rem(lax.axis_index("gx"), 2)


def ranking(n_gx, n_gy, sign):
    return sorted(range(n_gx * n_gy), key=lambda d: (sign * abs(2 * (d % n_gy) - (n_gy - 1)), d))


def core_groups(n_gx, n_gy):
    return [[d for d in ranking(n_gx, n_gy, 1) if d // n_gy % 2 == c] for c in range(2)]


def share_places(n_gx, n_gy):
    places = {}
    for c, group in enumerate(core_groups(n_gx, n_gy)):
        places.update({d: c * len(group) + i for i, d in enumerate(group)})
    return [places[d] for d in range(n_gx * n_gy)]


def emit_modes(chosen, parent, is_owner, places, x_fwd, y_fwd, keep, send, turned, work):
    devices, rows = len(places), keep.shape[1] // 2
    slabs = parent.shape[0]
    groups = slabs // GROUP
    head, rest = split(jnp.concatenate(chosen, axis=0))
    half = lax.dot_general(
        y_fwd, jnp.concatenate([head, head, rest], axis=1), (((1,), (1,)), ((), ())),
        preferred_element_type=jnp.float32)
    half = jnp.concatenate([half[:, t * LANES : (t + 1) * LANES] for t in range(groups)], axis=0)
    count = groups * 2 * KX
    work[0:count] = -data_dot(half, x_fwd)
    if count < devices * rows:
        work[count:] = jnp.zeros((devices * rows - count, 2 * LANES), jnp.float32)

    @pl.when(is_owner)
    def _():
        for i in range(KX):
            turned[:, i, :] = parent[:, i * LANES : (i + 1) * LANES]
        for t in range(groups):
            block = turned[t * GROUP : (t + 1) * GROUP].reshape(LANES, LANES).T
            span = slice(t * 2 * KX, (t + 1) * 2 * KX)
            for p in range(2):
                work[span, p * LANES : (p + 1) * LANES] += block[p * 2 * KX : (p + 1) * 2 * KX]

    count = devices // 2
    for mine in range(2):
        @pl.when(core() == mine)
        def _(mine=mine):
            for d in range(devices):
                half = keep if places[d] // count == mine else send
                for p in range(2):
                    half[places[d] % count, p * rows : (p + 1) * rows, :] = work[
                        d * rows : (d + 1) * rows, p * LANES : (p + 1) * LANES]


def add_kernel(kept, received, out):
    out[...] = kept[...] + received[...]


def fetch_all(sems, pairs):
    copies = [pltpu.make_async_copy(a, b, sems.at[i]) for i, (a, b) in enumerate(pairs)]
    for copy in copies:
        copy.start()
    return copies


def slab_of(levels, c, level_count, level_total):
    return (c // level_count) * level_total + levels[c % level_count]


def first_kernel(n_gy, level_total, places, levels_all, owners_all, fields_all, parent_all,
                 x_fwd_all, y_fwd_all, keep, send, levels, owners, fields, sems, parent, x_fwd, y_fwd,
                 turned, work):
    gx, gy = lax.axis_index("gx"), lax.axis_index("gy")
    copies = fetch_all(sems, [
        (levels_all, levels), (owners_all, owners), (fields_all, fields),
        (x_fwd_all.at[gx], x_fwd), (y_fwd_all.at[gy], y_fwd), (parent_all.at[0, 0], parent)])
    for copy in copies:
        copy.wait()
    level_count = parent.shape[0] // 3
    emit_modes(
        [fields[slab_of(levels, c, level_count, level_total)] for c in range(parent.shape[0])],
        parent, owners[0] == gx * n_gy + gy, places, x_fwd[...], y_fwd[...], keep, send,
        turned, work,
    )


def is_even(axis):
    return lax.rem(lax.axis_index(axis), 2) == 0


def edge_kernel(n_gy, period, cuts, fields, plume, first, second, cols, weights):
    weights[...] = share_weights(n_gy, period, cuts, weights.shape)
    slabs = [fields[c] for c in range(fields.shape[0])]
    emit_edges(slabs + [plume[l] for l in range(plume.shape[0])], first, second, cols)


def prepare_kernel(level_total, levels, fields, y_back_all, nudged, others, y_back, order, sems):
    copies = fetch_all(sems, [(y_back_all.at[lax.axis_index("gy")], y_back)])
    count = levels.shape[0]
    for n in range(count):
        order[n] = levels[n]
    spot = jnp.int32(count)
    for l in range(level_total):
        found = levels[0] == l
        for n in range(1, count):
            found = found | (levels[n] == l)
        order[spot] = jnp.int32(l)
        spot = spot + jnp.where(found, 0, 1)
    chosen = [order[n] for n in range(level_total)]
    for n in range(level_total, order.shape[0]):
        order[n] = jnp.int32(0)
    for n in range(level_total):
        order[level_total + chosen[n]] = jnp.int32(n)
    slabs = [fields[f * level_total + l] for f in range(3) for l in chosen]
    kept = level_total - count
    for c, a in enumerate(slabs):
        f, n = c // level_total, c % level_total
        if n < count:
            nudged[f * count + n] = a
        else:
            others[f * kept + n - count] = a
    for copy in copies:
        copy.wait()


def emit_edges(slabs, first, second, cols):
    even = is_even("gx")
    lane = lax.broadcasted_iota(jnp.int32, cols.shape, 1)
    acc = jnp.zeros(cols.shape, jnp.float32)
    for c, a in enumerate(slabs):
        west, east = a[:1], a[a.shape[0] - 1 :]
        first[c : c + 1, :] = jnp.where(even, east, west)
        second[c : c + 1, :] = jnp.where(even, west, east)
        acc = jnp.where(lane // 2 == c, pltpu.roll(a, 2 * c + 1, 1), acc)
    cols[...] = acc


def share_weights(n_gy, period, cuts, shape):
    rows = shape[0] // 2
    me = lax.axis_index("gx") * n_gy + lax.axis_index("gy")
    place = lax.broadcasted_iota(jnp.int32, shape, 0)
    lane = lax.broadcasted_iota(jnp.int32, shape, 1)
    p = (place >= rows).astype(jnp.int32)
    row = me * rows + place - p * rows
    k = 2 * (lane % KX) + p
    j = row % (2 * KX)
    slab = GROUP * (row // (2 * KX)) + lane // KX
    limit = jnp.zeros(shape, jnp.int32)
    for c in range(cuts.shape[0]):
        limit = jnp.where(slab == c, cuts[c], limit)
    keep = ((k % KX) < limit) & ((j % KX) < limit)
    factor = jnp.where(k == 0, 1.0, 2.0) * jnp.where(j == 0, 1.0, 2.0) * (1.0 / math.sqrt(period))
    return jnp.where(keep, factor, 0.0)


def beside_rows(rows):
    return -(-rows // 3)


def share_kernel(n_gx, n_gy, weights, parts, x_back, x_beside, out):
    rows = parts.shape[1] // 2
    total = parts[0]
    for d in range(1, parts.shape[0]):
        total = total + parts[d]
    mismatch = total * weights[...]
    both = jnp.concatenate([mismatch[:rows], mismatch[rows:]], axis=1)
    spare = -rows % 16
    if spare:
        both = jnp.concatenate([both, jnp.zeros((spare, 2 * LANES), jnp.float32)], axis=0)
    slab_lane = lax.broadcasted_iota(jnp.int32, both.shape, 1) % LANES // KX
    chosen = [jnp.where(slab_lane == n, both, 0.0) for n in range(GROUP)]
    inner = two_part_dot(jnp.concatenate(chosen, axis=0), x_back)
    edge_all = two_part_dot(both, x_beside)
    height = rows + spare
    packed = beside_rows(rows)
    width = 2 * GROUP
    cells_x = LANES // GROUP
    slot = lax.broadcasted_iota(jnp.int32, (height, LANES), 1) // cells_x
    spot = lax.broadcasted_iota(jnp.int32, (packed, LANES), 1) // width
    spot_at = {d: i for i, d in enumerate(ranking(n_gx, n_gy, -1))}
    for g in range(n_gx):
        first = g * cells_x // LANES * LANES
        tile = jnp.zeros((height, LANES), jnp.float32)
        for n in range(GROUP):
            piece = inner[n * height : (n + 1) * height, first : first + LANES]
            tile = jnp.where(slot == n, pltpu.roll(piece, (n - g) * cells_x % LANES, 1), tile)
        first = g * width // LANES * LANES
        beside = jnp.zeros((packed, LANES), jnp.float32)
        for m in range(3):
            piece = edge_all[m * packed : (m + 1) * packed, first : first + LANES]
            beside = jnp.where(
                spot == m, pltpu.roll(piece, (m - g) * width % LANES, 1), beside)
        for h in range(n_gy):
            out[spot_at[g * n_gy + h], :rows, :] = tile[:rows]
            out[spot_at[g * n_gy + h], rows:, :] = beside


class Halo:
    def __init__(self, row_first, row_second, col_first, col_second, west, east):
        even = is_even("gx")
        west[...] = jnp.where(even, row_second[...], row_first[...])
        east[...] = jnp.where(even, row_first[...], row_second[...])
        self.west, self.east = west, east
        even = is_even("gy")
        north = jnp.where(even, col_first[...], col_second[...])
        south = jnp.where(even, col_second[...], col_first[...])
        shape = north.shape
        lane = lax.broadcasted_iota(jnp.int32, shape, 1)
        self.last = shape[1] - 1
        self.at_first, self.at_last = lane == 0, lane == self.last
        self.columns = jnp.where(
            lane % 2 == 0, pltpu.roll(north, self.last, 1), pltpu.roll(south, 1, 1))

    def rows(self, c):
        return self.west[pl.ds(c, 1), :], self.east[pl.ds(c, 1), :]

    def column(self, c):
        return pltpu.roll(self.columns, self.last - 2 * c, 1)

    def move(self, slab, column, parts):
        centre, to_west, to_east, to_south, to_north = parts
        cells_x = column.shape[0]
        a = slab[PAD : PAD + cells_x]
        return (
            centre * a
            + to_west * slab[PAD - 1 : PAD - 1 + cells_x]
            + to_east * slab[PAD + 1 : PAD + 1 + cells_x]
            + to_south * jnp.where(self.at_first, column, pltpu.roll(a, 1, 1))
            + to_north * jnp.where(self.at_last, column, pltpu.roll(a, self.last, 1))
        )


def place(slab, a, rows):
    cells_x = a.shape[0]
    slab[PAD : PAD + cells_x] = a
    slab[PAD - 1 : PAD] = rows[0]
    slab[PAD + cells_x : PAD + cells_x + 1] = rows[1]


def wind_weights(u, v):
    neighbours = (
        0.1 + 0.1 * jnp.maximum(u, 0.0), 0.1 - 0.1 * jnp.minimum(u, 0.0),
        0.1 + 0.1 * jnp.maximum(v, 0.0), 0.1 - 0.1 * jnp.minimum(v, 0.0),
    )
    centre = 1.0 - (neighbours[0] + neighbours[1] + neighbours[2] + neighbours[3])
    return (centre,) + neighbours


def settling(parts):
    return (parts[0] - 0.3,) + parts[1:]


def above(l, level_total):
    return jnp.where(l + 1 < level_total, 0.3, 0.0).astype(jnp.float32)


def nudge_updates(ranks, shares, spread, spread_edges, y_table, nudged, cells_x):
    devices = shares.shape[0]
    rows = spread.shape[0] // devices
    packed = beside_rows(rows)
    width = 2 * GROUP
    for i, d in enumerate(ranks):
        spread[d * rows : (d + 1) * rows] = shares[i, :rows, :]
        edge = shares[i, rows:, :]
        for m in range(3):
            count = min(packed, rows - m * packed)
            if count > 0:
                moved = pltpu.roll(edge, -m * width % LANES, 1) if m else edge
                start = d * rows + m * packed
                spread_edges[start : start + count] = moved[:count]
    groups = nudged // GROUP
    spot_of = lax.broadcasted_iota(jnp.int32, (2 * KX, LANES), 1) // width
    edges = jnp.zeros((2 * KX, LANES), jnp.float32)
    for t in range(groups):
        piece = spread_edges[t * 2 * KX : (t + 1) * 2 * KX]
        edges = jnp.where(spot_of == t, pltpu.roll(piece, t * width, 1) if t else piece, edges)
    update_rows = columns_dot(edges, y_table)
    updates = []
    for t in range(groups):
        update = columns_dot(spread[t * 2 * KX : (t + 1) * 2 * KX], y_table)
        updates += [update[n * cells_x : (n + 1) * cells_x] for n in range(GROUP)]
    return updates, update_rows


def nudged_kernel(n_gy, step, last, level_count, level_total, ranks, places, shares, fields, row_first, row_second,
                  col_first, col_second, y_back, order_all, *rest):
    gx, gy = lax.axis_index("gx"), lax.axis_index("gy")
    cells_x, cells_y = fields.shape[1:]
    nudged = 3 * level_count
    if last:
        (plume, source, _, _, fields_all, plume_all, order, slabs, spread, spread_edges, west, east,
         sems, fields_out, plume_out, out_sems) = rest
        extra = []
    else:
        (owners_all, parent_all, x_fwd_all, y_fwd_all, fields_out, winds_out, keep, send,
         order, slabs, spread, spread_edges, west, east, sems,
         owners, parent, x_fwd, y_fwd, turned, work) = rest
        extra = [(owners_all, owners), (x_fwd_all.at[gx], x_fwd), (y_fwd_all.at[gy], y_fwd),
                 (parent_all.at[0, step + 1], parent)]
    copies = fetch_all(sems, [(order_all, order)] + extra)
    halo = Halo(row_first, row_second, col_first, col_second, west, east)
    updates, update_rows = nudge_updates(
        ranks, shares, spread, spread_edges, y_back[...], nudged, cells_x)
    copies[0].wait()
    level_at = [order[n] for n in range(level_count)]
    halo_at = level_at if step == 0 else list(range(level_count))
    beside = []
    for k in range(nudged):
        f, n = k // level_count, k % level_count
        a = fields[k]
        before, after = halo.rows(f * level_total + halo_at[n])
        place(slabs.at[k], a + updates[k][:, :cells_y],
              (before + update_rows[2 * k : 2 * k + 1, :cells_y],
               after + update_rows[2 * k + 1 : 2 * k + 2, :cells_y]))
        beside.append(updates[k][:, cells_y:])
    inner = slice(PAD, PAD + cells_x)
    results = [None] * nudged
    sent = []
    for n in range(level_count):
        u, v = slabs[n, inner], slabs[level_count + n, inner]
        parts = wind_weights(u, v)
        for f in range(3):
            k = f * level_count + n
            column = halo.column(f * level_total + halo_at[n]) + beside[k]
            results[k] = halo.move(slabs[k], column, parts)
            fields_out[k] = results[k]
        if not last:
            winds_out[n] = u
            winds_out[level_count + n] = v
            continue
        l = level_at[n]
        c = 3 * level_total + n
        place(slabs.at[nudged + n], plume[n], halo.rows(c))
        settled = halo.move(slabs[nudged + n], halo.column(c), settling(parts))
        plume_out[n] = settled + above(l, level_total) * plume[order[level_total + l + 1]] + source[l]
        pairs = [(fields_out.at[f * level_count + n], fields_all.at[f * level_total + l])
                 for f in range(3)] + [(plume_out.at[n], plume_all.at[l])]
        sent += fetch_all(out_sems.at[pl.ds(4 * n, 4)], pairs)
    if last:
        for copy in sent:
            copy.wait()
        return
    for copy in copies[1:]:
        copy.wait()
    emit_modes(results, parent, owners[step + 1] == gx * n_gy + gy, places, x_fwd[...], y_fwd[...],
               keep, send, turned, work)


def others_kernel(step, last, level_count, fields, plume, source, row_first, row_second, col_first,
                  col_second, order, *rest):
    level_total, cells_x, cells_y = plume.shape
    if last:
        fields_all, plume_all, slab, west, east, fields_out, plume_out, out_sems = rest
    else:
        done, winds, fields_out, plume_out, first, second, cols, slab, west, east = rest
    halo = Halo(row_first, row_second, col_first, col_second, west, east)
    level_at = [order[n] for n in range(level_total)]
    kept = level_total - level_count
    sent = []
    results = {}
    for n in range(level_count if last else 0, level_total):
        l = level_at[n]
        m = n - level_count
        if m < 0:
            parts = wind_weights(winds[n], winds[level_count + n])
        else:
            given = [fields[f * kept + m] for f in range(3)]
            parts = wind_weights(given[0], given[1])
            for f in range(3):
                c = f * level_total + n
                beyond = f * level_total + l if step == 0 else c
                place(slab.at[4 * n + f], given[f], halo.rows(beyond))
                results[c] = halo.move(slab[4 * n + f], halo.column(beyond), parts)
                fields_out[f * kept + m] = results[c]
        c = 3 * level_total + n
        beyond = 3 * level_total + l if step == 0 else c
        place(slab.at[4 * n + 3], plume[l] if step == 0 else plume[n], halo.rows(beyond))
        higher = (jnp.minimum(l + 1, level_total - 1) if step == 0 else order[level_total + l + 1])
        results[c] = (halo.move(slab[4 * n + 3], halo.column(beyond), settling(parts))
                      + above(l, level_total) * plume[higher] + source[l])
        plume_out[m if last else n] = results[c]
        if last:
            pairs = [(fields_out.at[f * kept + m], fields_all.at[f * level_total + l])
                     for f in range(3)] + [(plume_out.at[m], plume_all.at[l])]
            sent += fetch_all(out_sems.at[pl.ds(4 * m, 4)], pairs)
    for copy in sent:
        copy.wait()
    if not last:
        for f in range(3):
            for n in range(level_count):
                results[f * level_total + n] = done[f * level_count + n]
        emit_edges([results[c] for c in range(4 * level_total)], first, second, cols)


def exchange(axis, first, second):
    count = lax.axis_size(axis)
    received = []
    for start, data in ((0, first), (1, second)):
        pairs = [(i, i + 1) for i in range(start, count - 1, 2)]
        received.append(lax.ppermute(data, axis, pairs + [(b, a) for a, b in pairs]))
    return received


def local(tables, fields, levels, cuts, parent_modes, owners, plume, source):
    n_gx, n_gy = lax.axis_size("gx"), lax.axis_size("gy")
    devices = n_gx * n_gy
    level_total, cells_x, cells_y = plume.shape
    period = n_gx * cells_x * n_gy * cells_y
    nudged = 3 * levels.shape[0]
    field_rows = 3 * level_total
    total = field_rows + level_total
    rows = -(-(nudged // GROUP * 2 * KX) // devices)
    flat = fields.reshape(field_rows, cells_x, cells_y)
    cuts = cuts.reshape(-1)
    f32 = functools.partial(jax.ShapeDtypeStruct, dtype=jnp.float32)
    x_fwd, y_fwd, y_back, x_back, x_beside = (jnp.asarray(t) for t in tables)

    def vmem(*shape):
        return pltpu.VMEM(shape, jnp.float32)

    def table_space(table):
        return pltpu.VMEM(table.shape[1:], table.dtype)

    def limit(mib):
        return pltpu.CompilerParams(vmem_limit_bytes=mib * 1024 * 1024)

    count = levels.shape[0]
    kept = level_total - count
    half_shapes = [f32((devices // 2, 2 * rows, LANES))] * 2
    places = share_places(n_gx, n_gy)
    ranks = ranking(n_gx, n_gy, -1)
    order_shape = (3 * level_total,)
    edge_shapes = [f32((total, cells_y)), f32((total, cells_y)), f32((cells_x, 2 * total))]
    levels_space = pltpu.SMEM(levels.shape, jnp.int32)
    owners_space = pltpu.SMEM(owners.shape, jnp.int32)
    order_space = pltpu.SMEM(order_shape, jnp.int32)
    rows_space = vmem(total, cells_y)
    mode_scratch = [vmem(nudged, 4 * KX * KX), table_space(x_fwd),
                    table_space(y_fwd), vmem(nudged, KX, LANES),
                    vmem(devices * rows, 2 * LANES)]
    nudged_scratch = [order_space, vmem(nudged + count, cells_x + 2 * PAD, cells_y),
                      vmem(devices * rows, LANES), vmem(devices * rows, LANES),
                      rows_space, rows_space, pltpu.SemaphoreType.DMA((5,))]
    others_scratch = [vmem(total, cells_x + 2 * PAD, cells_y), rows_space, rows_space]

    def out_scratch(slabs):
        return [vmem(3 * slabs, cells_x, cells_y), vmem(slabs, cells_x, cells_y),
                pltpu.SemaphoreType.DMA((4 * slabs,))]

    keep, send = pl.pallas_call(
        functools.partial(first_kernel, n_gy, level_total, places),
        out_shape=half_shapes,
        in_specs=[HBM] * 6,
        out_specs=[VMEM] * 2,
        scratch_shapes=[levels_space, owners_space, vmem(field_rows, cells_x, cells_y),
                        pltpu.SemaphoreType.DMA((6,))] + mode_scratch,
        compiler_params=limit(8),
        name="first_modes",
    )(*map(in_hbm, (levels, owners, flat, parent_modes, x_fwd, y_fwd)))
    for step in range(STEPS):
        last = step == STEPS - 1
        received = lax.ppermute(send, "gx", [(i, i ^ 1) for i in range(n_gx)])
        modes = pl.pallas_call(
            add_kernel,
            out_shape=half_shapes[0],
            in_specs=[VMEM] * 2,
            out_specs=VMEM,
            compiler_params=limit(4),
            name="add_cores",
        )(keep, received)
        if step == 0:
            modes, flat = lax.optimization_barrier((modes, flat))
            *edges, weights = pl.pallas_call(
                functools.partial(edge_kernel, n_gy, period),
                out_shape=edge_shapes + [f32((2 * rows, LANES))],
                in_specs=[SMEM, VMEM, VMEM],
                out_specs=[VMEM] * 4,
                compiler_params=limit(8),
                name="edges",
            )(cuts, flat, plume)
        else:
            modes, others = lax.optimization_barrier((modes, others))
            others, plume, *edges = pl.pallas_call(
                functools.partial(others_kernel, 0, False, count),
                out_shape=[f32((3 * kept, cells_x, cells_y)), f32(plume.shape)] + edge_shapes,
                in_specs=[VMEM] * 7 + [SMEM] + [VMEM] * 2,
                out_specs=[VMEM] * 5,
                scratch_shapes=others_scratch,
                compiler_params=limit(8),
                name="inner_others",
            )(others, plume, source, *halo, order, flat, winds)
        to_first, to_second, cols = edges
        col_first, col_second = exchange("gy", cols, cols)
        parts = lax.all_to_all(modes, AXES, 0, 0, axis_index_groups=core_groups(n_gx, n_gy),
                               tiled=True)
        parts, col_first, col_second = lax.optimization_barrier((parts, col_first, col_second))
        share = pl.pallas_call(
            functools.partial(share_kernel, n_gx, n_gy),
            out_shape=f32((devices, rows + beside_rows(rows), LANES)),
            in_specs=[VMEM] * 4,
            out_specs=VMEM,
            compiler_params=limit(8),
            name="share_sum",
        )(weights, parts, x_back, x_beside)
        share, to_first, to_second = lax.optimization_barrier((share, to_first, to_second))
        row_first, row_second = exchange("gx", to_first, to_second)
        halo = [row_first, row_second, col_first, col_second]
        if step == 0:
            share, levels = lax.optimization_barrier((share, levels))
            flat, others, y_back, order = pl.pallas_call(
                functools.partial(prepare_kernel, level_total),
                out_shape=[f32((3 * count, cells_x, cells_y)), f32((3 * kept, cells_x, cells_y)),
                           jax.ShapeDtypeStruct(y_back.shape[1:], y_back.dtype),
                           jax.ShapeDtypeStruct(order_shape, jnp.int32)],
                in_specs=[SMEM, VMEM, HBM],
                out_specs=[VMEM] * 3 + [SMEM],
                scratch_shapes=[pltpu.SemaphoreType.DMA((1,))],
                compiler_params=limit(8),
                name="prepare",
            )(levels, flat, in_hbm(y_back))
        shares = lax.all_to_all(share, AXES, 0, 0, axis_index_groups=[ranks], tiled=True)
        if last:
            final = pl.pallas_call(
                functools.partial(others_kernel, step, True, count),
                out_shape=[f32((field_rows, cells_x, cells_y)), f32(plume.shape)],
                in_specs=[VMEM] * 7 + [SMEM],
                out_specs=[HBM] * 2,
                scratch_shapes=others_scratch + out_scratch(kept),
                compiler_params=limit(8),
                name="last_others",
            )(others, plume, source, *halo, order)
            flat, plume = pl.pallas_call(
                functools.partial(nudged_kernel, n_gy, step, True, count, level_total, ranks, None),
                out_shape=[f32((field_rows, cells_x, cells_y)), f32(plume.shape)],
                in_specs=[VMEM] * 7 + [HBM] + [VMEM] * 2 + [HBM] * 2,
                out_specs=[HBM] * 2,
                scratch_shapes=nudged_scratch + out_scratch(count),
                input_output_aliases={10: 0, 11: 1},
                compiler_params=limit(12),
                name="last_nudged",
            )(shares, flat, *halo, y_back, in_hbm(order), plume, source, *final)
        else:
            flat, winds, keep, send = pl.pallas_call(
                functools.partial(nudged_kernel, n_gy, step, False, count, level_total, ranks, places),
                out_shape=[f32((nudged, cells_x, cells_y)), f32((2 * count, cells_x, cells_y))]
                + half_shapes,
                in_specs=[VMEM] * 7 + [HBM] * 5,
                out_specs=[VMEM] * 4,
                scratch_shapes=nudged_scratch + [owners_space] + mode_scratch,
                compiler_params=limit(12),
                name="inner_nudged",
            )(shares, flat, *halo, y_back, in_hbm(order),
              *map(in_hbm, (owners, parent_modes, x_fwd, y_fwd)))
    return flat.reshape(fields.shape), plume


def solution(mesh):
    in_specs = (
        P(None, None, "gx", "gy"),
        P(),
        P(),
        P(("gx", "gy"), None, None, None),
        P(),
        P(None, "gx", "gy"),
        P(None, "gx", "gy"),
    )
    out_specs = (P(None, None, "gx", "gy"), P(None, "gx", "gy"))
    n_gx, n_gy = mesh.shape["gx"], mesh.shape["gy"]

    def whole(fields, levels, cuts, parent_modes, owners, plume, source):
        tables = build_tables(n_gx, n_gy, plume.shape[1] // n_gx, plume.shape[2] // n_gy)
        return jax.shard_map(
            functools.partial(local, tables), mesh=mesh, in_specs=in_specs, out_specs=out_specs,
            check_vma=False,
        )(fields, levels, cuts, parent_modes, owners, plume, source)

    return whole
```

```python
import functools
import math

import jax
import jax.numpy as jnp
import ml_dtypes
import numpy as np
from jax import lax
from jax.experimental import pallas as pl
from jax.experimental.pallas import tpu as pltpu
from jax.sharding import PartitionSpec as P

KX = 32
STEPS = 2
GROUP = 4
LANES = GROUP * KX
PAD = 8
VMEM = pl.BlockSpec(memory_space=pltpu.VMEM)
SMEM = pl.BlockSpec(memory_space=pltpu.SMEM)
HBM = pl.BlockSpec(memory_space=pltpu.HBM)
AXES = ("gx", "gy")


def in_hbm(array):
    return pltpu.with_memory_space_constraint(array, pltpu.HBM)


def wave_table(positions, period):
    wavenum = np.arange(KX)[:, None]
    phase = (wavenum * positions[None, :] % period) * (2.0 * math.pi / period)
    inside = (positions >= 0) & (positions < period)
    return np.concatenate([np.cos(phase), np.sin(phase)], axis=0) * inside[None, :]


def split(a):
    head = a.astype(jnp.bfloat16)
    return head, (a - head.astype(jnp.float32)).astype(jnp.bfloat16)


def split_table(table, axis, order):
    head = table.astype(ml_dtypes.bfloat16)
    rest = (table - head.astype(np.float64)).astype(ml_dtypes.bfloat16)
    return np.concatenate([head if part == "h" else rest for part in order], axis=axis)


def per_slab(table):
    return np.kron(np.eye(GROUP), table)


def build_tables(n_gx, n_gy, cells_x, cells_y):
    period_x, period_y = n_gx * cells_x, n_gy * cells_y
    scaling = 1.0 / math.sqrt(period_x * period_y)
    parity = [np.arange(p, 2 * KX, 2) for p in range(2)]
    x_fwd, y_fwd, y_back, inner, outer = [], [], [], [], []
    for g in range(n_gx):
        first = g * cells_x
        table = wave_table(first + np.arange(cells_x), period_x)
        x_fwd.append(split_table(
            np.concatenate([per_slab(table[rows].T) for rows in parity], axis=1), 0, "hhl"))
        beside = wave_table(np.array([first - 1, first + cells_x]), period_x)
        inner.append(np.concatenate([np.tile(table[rows], (GROUP, 1)) for rows in parity], axis=0))
        outer.append(np.concatenate([per_slab(beside[rows]) for rows in parity], axis=0))
    spare = -(2 * GROUP * n_gx) % LANES
    x_back = np.concatenate(inner, axis=1)
    x_beside = np.concatenate(outer + [np.zeros((2 * LANES, spare))], axis=1)
    for g in range(n_gy):
        first = g * cells_y
        table = wave_table(first + np.arange(cells_y), period_y)
        edge = np.zeros((2 * KX, cells_y))
        edge[:, [0, -1]] = wave_table(np.array([first - 1, first + cells_y]), period_y)
        y_fwd.append(split_table(table * scaling, 1, "hlh"))
        y_back.append(split_table(np.concatenate([table, edge], axis=1), 0, "hhl"))
    return [np.stack(x_fwd), np.stack(y_fwd), np.stack(y_back),
            split_table(x_back, 0, "hl"), split_table(x_beside, 0, "hl")]


def data_dot(a, table):
    head, rest = split(a)
    return jnp.dot(
        jnp.concatenate([head, rest, head], axis=1), table, preferred_element_type=jnp.float32
    )


def two_part_dot(a, table):
    head, rest = split(a)
    depth = a.shape[1]
    heads = jnp.dot(
        jnp.concatenate([head, rest], axis=0), table[:depth], preferred_element_type=jnp.float32)
    rests = jnp.dot(head, table[depth:], preferred_element_type=jnp.float32)
    return heads[: a.shape[0]] + heads[a.shape[0] :] + rests


def columns_dot(a, table):
    head, rest = split(a)
    stacked = jnp.concatenate([head, rest, head], axis=0)
    return lax.dot_general(
        stacked, table, (((0,), (0,)), ((), ())), preferred_element_type=jnp.float32)


def core():
    return lax.rem(lax.axis_index("gx"), 2)


def ranking(n_gx, n_gy):
    return sorted(range(n_gx * n_gy), key=lambda d: (abs(2 * (d % n_gy) - (n_gy - 1)), d))


def core_groups(n_gx, n_gy):
    return [[d for d in ranking(n_gx, n_gy) if d // n_gy % 2 == c] for c in range(2)]


def share_places(n_gx, n_gy):
    places = {}
    for c, group in enumerate(core_groups(n_gx, n_gy)):
        places.update({d: c * len(group) + i for i, d in enumerate(group)})
    return [places[d] for d in range(n_gx * n_gy)]


def emit_modes(chosen, parent, parent_copy, is_owner, places, x_fwd, y_fwd, keep, send, turned, work):
    devices, rows = len(places), keep.shape[1] // 2
    slabs = parent.shape[0]
    groups = slabs // GROUP
    head, rest = split(jnp.concatenate(chosen, axis=0))
    half = lax.dot_general(
        y_fwd, jnp.concatenate([head, head, rest], axis=1), (((1,), (1,)), ((), ())),
        preferred_element_type=jnp.float32)
    half = jnp.concatenate([half[:, t * LANES : (t + 1) * LANES] for t in range(groups)], axis=0)
    count = groups * 2 * KX
    work[0:count] = -data_dot(half, x_fwd)
    if count < devices * rows:
        work[count:] = jnp.zeros((devices * rows - count, 2 * LANES), jnp.float32)

    parent_copy.wait()

    @pl.when(is_owner)
    def _():
        for i in range(KX):
            turned[:, i, :] = parent[:, i * LANES : (i + 1) * LANES]
        for t in range(groups):
            block = turned[t * GROUP : (t + 1) * GROUP].reshape(LANES, LANES).T
            span = slice(t * 2 * KX, (t + 1) * 2 * KX)
            for p in range(2):
                work[span, p * LANES : (p + 1) * LANES] += block[p * 2 * KX : (p + 1) * 2 * KX]

    count = devices // 2
    for mine in range(2):
        @pl.when(core() == mine)
        def _(mine=mine):
            for d in range(devices):
                half = keep if places[d] // count == mine else send
                for p in range(2):
                    half[places[d] % count, p * rows : (p + 1) * rows, :] = work[
                        d * rows : (d + 1) * rows, p * LANES : (p + 1) * LANES]


def add_kernel(kept, received, out):
    out[...] = kept[...] + received[...]


def fetch_all(sems, pairs):
    copies = [pltpu.make_async_copy(a, b, sems.at[i]) for i, (a, b) in enumerate(pairs)]
    for copy in copies:
        copy.start()
    return copies


def slab_of(levels, c, level_count, level_total):
    return (c // level_count) * level_total + levels[c % level_count]


def first_kernel(n_gy, level_total, places, levels_all, owners_all, fields_all, parent_all,
                 x_fwd_all, y_fwd_all, keep, send, levels, owners, fields, sems, parent, x_fwd, y_fwd,
                 turned, work):
    gx, gy = lax.axis_index("gx"), lax.axis_index("gy")
    copies = fetch_all(sems, [
        (levels_all, levels), (owners_all, owners), (fields_all, fields),
        (x_fwd_all.at[gx], x_fwd), (y_fwd_all.at[gy], y_fwd), (parent_all.at[0, 0], parent)])
    for copy in copies[:-1]:
        copy.wait()
    level_count = parent.shape[0] // 3
    emit_modes(
        [fields[slab_of(levels, c, level_count, level_total)] for c in range(parent.shape[0])],
        parent, copies[-1], owners[0] == gx * n_gy + gy, places, x_fwd[...], y_fwd[...], keep, send,
        turned, work,
    )


def is_even(axis):
    return lax.rem(lax.axis_index(axis), 2) == 0


def edge_kernel(n_gy, period, cuts, fields, plume, first, second, cols, weights):
    weights[...] = share_weights(n_gy, period, cuts, weights.shape)
    slabs = [fields[c] for c in range(fields.shape[0])]
    emit_edges(slabs + [plume[l] for l in range(plume.shape[0])], first, second, cols)


def prepare_kernel(level_total, levels, fields, y_back_all, nudged, others, y_back, order, sems):
    copies = fetch_all(sems, [(y_back_all.at[lax.axis_index("gy")], y_back)])
    count = levels.shape[0]
    for n in range(count):
        order[n] = levels[n]
    spot = jnp.int32(count)
    for l in range(level_total):
        found = levels[0] == l
        for n in range(1, count):
            found = found | (levels[n] == l)
        order[spot] = jnp.int32(l)
        spot = spot + jnp.where(found, 0, 1)
    chosen = [order[n] for n in range(level_total)]
    for n in range(level_total, order.shape[0]):
        order[n] = jnp.int32(0)
    for n in range(level_total):
        order[level_total + chosen[n]] = jnp.int32(n)
    slabs = [fields[f * level_total + l] for f in range(3) for l in chosen]
    kept = level_total - count
    for c, a in enumerate(slabs):
        f, n = c // level_total, c % level_total
        if n < count:
            nudged[f * count + n] = a
        else:
            others[f * kept + n - count] = a
    for copy in copies:
        copy.wait()


def emit_edges(slabs, first, second, cols):
    even = is_even("gx")
    lane = lax.broadcasted_iota(jnp.int32, cols.shape, 1)
    acc = jnp.zeros(cols.shape, jnp.float32)
    for c, a in enumerate(slabs):
        west, east = a[:1], a[a.shape[0] - 1 :]
        first[c : c + 1, :] = jnp.where(even, east, west)
        second[c : c + 1, :] = jnp.where(even, west, east)
        acc = jnp.where(lane // 2 == c, pltpu.roll(a, 2 * c + 1, 1), acc)
    cols[...] = acc


def share_weights(n_gy, period, cuts, shape):
    rows = shape[0] // 2
    me = lax.axis_index("gx") * n_gy + lax.axis_index("gy")
    place = lax.broadcasted_iota(jnp.int32, shape, 0)
    lane = lax.broadcasted_iota(jnp.int32, shape, 1)
    p = (place >= rows).astype(jnp.int32)
    row = me * rows + place - p * rows
    k = 2 * (lane % KX) + p
    j = row % (2 * KX)
    slab = GROUP * (row // (2 * KX)) + lane // KX
    limit = jnp.zeros(shape, jnp.int32)
    for c in range(cuts.shape[0]):
        limit = jnp.where(slab == c, cuts[c], limit)
    keep = ((k % KX) < limit) & ((j % KX) < limit)
    factor = jnp.where(k == 0, 1.0, 2.0) * jnp.where(j == 0, 1.0, 2.0) * (1.0 / math.sqrt(period))
    return jnp.where(keep, factor, 0.0)


def beside_rows(rows):
    return -(-rows // 3)


def share_kernel(n_gx, n_gy, weights, parts, x_back, x_beside, out):
    rows = parts.shape[1] // 2
    total = parts[0]
    for d in range(1, parts.shape[0]):
        total = total + parts[d]
    mismatch = total * weights[...]
    both = jnp.concatenate([mismatch[:rows], mismatch[rows:]], axis=1)
    spare = -rows % 16
    if spare:
        both = jnp.concatenate([both, jnp.zeros((spare, 2 * LANES), jnp.float32)], axis=0)
    slab_lane = lax.broadcasted_iota(jnp.int32, both.shape, 1) % LANES // KX
    chosen = [jnp.where(slab_lane == n, both, 0.0) for n in range(GROUP)]
    inner = two_part_dot(jnp.concatenate(chosen, axis=0), x_back)
    edge_all = two_part_dot(both, x_beside)
    height = rows + spare
    packed = beside_rows(rows)
    width = 2 * GROUP
    cells_x = LANES // GROUP
    slot = lax.broadcasted_iota(jnp.int32, (height, LANES), 1) // cells_x
    spot = lax.broadcasted_iota(jnp.int32, (packed, LANES), 1) // width
    spot_at = {d: i for i, d in enumerate(ranking(n_gx, n_gy))}
    for g in range(n_gx):
        first = g * cells_x // LANES * LANES
        tile = jnp.zeros((height, LANES), jnp.float32)
        for n in range(GROUP):
            piece = inner[n * height : (n + 1) * height, first : first + LANES]
            tile = jnp.where(slot == n, pltpu.roll(piece, (n - g) * cells_x % LANES, 1), tile)
        first = g * width // LANES * LANES
        beside = jnp.zeros((packed, LANES), jnp.float32)
        for m in range(3):
            piece = edge_all[m * packed : (m + 1) * packed, first : first + LANES]
            beside = jnp.where(
                spot == m, pltpu.roll(piece, (m - g) * width % LANES, 1), beside)
        for h in range(n_gy):
            out[spot_at[g * n_gy + h], :rows, :] = tile[:rows]
            out[spot_at[g * n_gy + h], rows:, :] = beside


class Halo:
    def __init__(self, row_first, row_second, col_first, col_second, west, east):
        even = is_even("gx")
        west[...] = jnp.where(even, row_second[...], row_first[...])
        east[...] = jnp.where(even, row_first[...], row_second[...])
        self.west, self.east = west, east
        even = is_even("gy")
        north = jnp.where(even, col_first[...], col_second[...])
        south = jnp.where(even, col_second[...], col_first[...])
        shape = north.shape
        lane = lax.broadcasted_iota(jnp.int32, shape, 1)
        self.last = shape[1] - 1
        self.at_first, self.at_last = lane == 0, lane == self.last
        self.columns = jnp.where(
            lane % 2 == 0, pltpu.roll(north, self.last, 1), pltpu.roll(south, 1, 1))

    def rows(self, c):
        return self.west[pl.ds(c, 1), :], self.east[pl.ds(c, 1), :]

    def column(self, c):
        return pltpu.roll(self.columns, self.last - 2 * c, 1)

    def move(self, slab, column, parts):
        centre, to_west, to_east, to_south, to_north = parts
        cells_x = column.shape[0]
        a = slab[PAD : PAD + cells_x]
        return (
            centre * a
            + to_west * slab[PAD - 1 : PAD - 1 + cells_x]
            + to_east * slab[PAD + 1 : PAD + 1 + cells_x]
            + to_south * jnp.where(self.at_first, column, pltpu.roll(a, 1, 1))
            + to_north * jnp.where(self.at_last, column, pltpu.roll(a, self.last, 1))
        )


def place(slab, a, rows):
    cells_x = a.shape[0]
    slab[PAD : PAD + cells_x] = a
    slab[PAD - 1 : PAD] = rows[0]
    slab[PAD + cells_x : PAD + cells_x + 1] = rows[1]


def wind_weights(u, v):
    neighbours = (
        0.1 + 0.1 * jnp.maximum(u, 0.0), 0.1 - 0.1 * jnp.minimum(u, 0.0),
        0.1 + 0.1 * jnp.maximum(v, 0.0), 0.1 - 0.1 * jnp.minimum(v, 0.0),
    )
    centre = 1.0 - (neighbours[0] + neighbours[1] + neighbours[2] + neighbours[3])
    return (centre,) + neighbours


def settling(parts):
    return (parts[0] - 0.3,) + parts[1:]


def above(l, level_total):
    return jnp.where(l + 1 < level_total, 0.3, 0.0).astype(jnp.float32)


def nudge_updates(ranks, shares, spread, spread_edges, y_table, nudged, cells_x):
    devices = shares.shape[0]
    rows = spread.shape[0] // devices
    packed = beside_rows(rows)
    width = 2 * GROUP
    for i, d in enumerate(ranks):
        spread[d * rows : (d + 1) * rows] = shares[i, :rows, :]
        edge = shares[i, rows:, :]
        for m in range(3):
            count = min(packed, rows - m * packed)
            if count > 0:
                moved = pltpu.roll(edge, -m * width % LANES, 1) if m else edge
                start = d * rows + m * packed
                spread_edges[start : start + count] = moved[:count]
    groups = nudged // GROUP
    spot_of = lax.broadcasted_iota(jnp.int32, (2 * KX, LANES), 1) // width
    edges = jnp.zeros((2 * KX, LANES), jnp.float32)
    for t in range(groups):
        piece = spread_edges[t * 2 * KX : (t + 1) * 2 * KX]
        edges = jnp.where(spot_of == t, pltpu.roll(piece, t * width, 1) if t else piece, edges)
    update_rows = columns_dot(edges, y_table)
    updates = []
    for t in range(groups):
        update = columns_dot(spread[t * 2 * KX : (t + 1) * 2 * KX], y_table)
        updates += [update[n * cells_x : (n + 1) * cells_x] for n in range(GROUP)]
    return updates, update_rows


def nudged_kernel(n_gy, step, last, level_count, level_total, ranks, places, shares, fields, row_first, row_second,
                  col_first, col_second, y_back, order_all, *rest):
    gx, gy = lax.axis_index("gx"), lax.axis_index("gy")
    cells_x, cells_y = fields.shape[1:]
    nudged = 3 * level_count
    if last:
        (plume, source, _, _, fields_all, plume_all, order, slabs, spread, spread_edges, west, east,
         sems, fields_out, plume_out, out_sems) = rest
        extra = []
    else:
        (owners_all, parent_all, x_fwd_all, y_fwd_all, fields_out, winds_out, keep, send,
         order, slabs, spread, spread_edges, west, east, sems,
         owners, parent, x_fwd, y_fwd, turned, work) = rest
        extra = [(owners_all, owners), (x_fwd_all.at[gx], x_fwd), (y_fwd_all.at[gy], y_fwd),
                 (parent_all.at[0, step + 1], parent)]
    copies = fetch_all(sems, [(order_all, order)] + extra)
    halo = Halo(row_first, row_second, col_first, col_second, west, east)
    updates, update_rows = nudge_updates(
        ranks, shares, spread, spread_edges, y_back[...], nudged, cells_x)
    copies[0].wait()
    level_at = [order[n] for n in range(level_count)]
    halo_at = level_at if step == 0 else list(range(level_count))
    beside = []
    for k in range(nudged):
        f, n = k // level_count, k % level_count
        a = fields[k]
        before, after = halo.rows(f * level_total + halo_at[n])
        place(slabs.at[k], a + updates[k][:, :cells_y],
              (before + update_rows[2 * k : 2 * k + 1, :cells_y],
               after + update_rows[2 * k + 1 : 2 * k + 2, :cells_y]))
        beside.append(updates[k][:, cells_y:])
    inner = slice(PAD, PAD + cells_x)
    results = [None] * nudged
    sent = []
    for n in range(level_count):
        u, v = slabs[n, inner], slabs[level_count + n, inner]
        parts = wind_weights(u, v)
        for f in range(3):
            k = f * level_count + n
            column = halo.column(f * level_total + halo_at[n]) + beside[k]
            results[k] = halo.move(slabs[k], column, parts)
            fields_out[k] = results[k]
        if not last:
            winds_out[n] = u
            winds_out[level_count + n] = v
            continue
        l = level_at[n]
        c = 3 * level_total + n
        place(slabs.at[nudged + n], plume[n], halo.rows(c))
        settled = halo.move(slabs[nudged + n], halo.column(c), settling(parts))
        plume_out[n] = settled + above(l, level_total) * plume[order[level_total + l + 1]] + source[l]
        pairs = [(fields_out.at[f * level_count + n], fields_all.at[f * level_total + l])
                 for f in range(3)] + [(plume_out.at[n], plume_all.at[l])]
        sent += fetch_all(out_sems.at[pl.ds(4 * n, 4)], pairs)
    if last:
        for copy in sent:
            copy.wait()
        return
    for copy in copies[1:-1]:
        copy.wait()
    emit_modes(results, parent, copies[-1], owners[step + 1] == gx * n_gy + gy, places, x_fwd[...], y_fwd[...],
               keep, send, turned, work)


def others_kernel(step, last, level_count, fields, plume, source, row_first, row_second, col_first,
                  col_second, order, *rest):
    level_total, cells_x, cells_y = plume.shape
    if last:
        fields_all, plume_all, slab, west, east, fields_out, plume_out, out_sems = rest
    else:
        done, winds, fields_out, plume_out, first, second, cols, slab, west, east = rest
    halo = Halo(row_first, row_second, col_first, col_second, west, east)
    level_at = [order[n] for n in range(level_total)]
    kept = level_total - level_count
    sent = []
    results = {}
    for n in range(level_count if last else 0, level_total):
        l = level_at[n]
        m = n - level_count
        if m < 0:
            parts = wind_weights(winds[n], winds[level_count + n])
        else:
            given = [fields[f * kept + m] for f in range(3)]
            parts = wind_weights(given[0], given[1])
            for f in range(3):
                c = f * level_total + n
                beyond = f * level_total + l if step == 0 else c
                place(slab.at[4 * n + f], given[f], halo.rows(beyond))
                results[c] = halo.move(slab[4 * n + f], halo.column(beyond), parts)
                fields_out[f * kept + m] = results[c]
        c = 3 * level_total + n
        beyond = 3 * level_total + l if step == 0 else c
        place(slab.at[4 * n + 3], plume[l] if step == 0 else plume[n], halo.rows(beyond))
        higher = (jnp.minimum(l + 1, level_total - 1) if step == 0 else order[level_total + l + 1])
        results[c] = (halo.move(slab[4 * n + 3], halo.column(beyond), settling(parts))
                      + above(l, level_total) * plume[higher] + source[l])
        plume_out[m if last else n] = results[c]
        if last:
            pairs = [(fields_out.at[f * kept + m], fields_all.at[f * level_total + l])
                     for f in range(3)] + [(plume_out.at[m], plume_all.at[l])]
            sent += fetch_all(out_sems.at[pl.ds(4 * m, 4)], pairs)
    for copy in sent:
        copy.wait()
    if not last:
        for f in range(3):
            for n in range(level_count):
                results[f * level_total + n] = done[f * level_count + n]
        emit_edges([results[c] for c in range(4 * level_total)], first, second, cols)


def exchange(axis, first, second):
    count = lax.axis_size(axis)
    received = []
    for start, data in ((0, first), (1, second)):
        pairs = [(i, i + 1) for i in range(start, count - 1, 2)]
        received.append(lax.ppermute(data, axis, pairs + [(b, a) for a, b in pairs]))
    return received


def local(tables, fields, levels, cuts, parent_modes, owners, plume, source):
    n_gx, n_gy = lax.axis_size("gx"), lax.axis_size("gy")
    devices = n_gx * n_gy
    level_total, cells_x, cells_y = plume.shape
    period = n_gx * cells_x * n_gy * cells_y
    nudged = 3 * levels.shape[0]
    field_rows = 3 * level_total
    total = field_rows + level_total
    rows = -(-(nudged // GROUP * 2 * KX) // devices)
    flat = fields.reshape(field_rows, cells_x, cells_y)
    cuts = cuts.reshape(-1)
    f32 = functools.partial(jax.ShapeDtypeStruct, dtype=jnp.float32)
    x_fwd, y_fwd, y_back, x_back, x_beside = (jnp.asarray(t) for t in tables)

    def vmem(*shape):
        return pltpu.VMEM(shape, jnp.float32)

    def table_space(table):
        return pltpu.VMEM(table.shape[1:], table.dtype)

    def limit(mib):
        return pltpu.CompilerParams(vmem_limit_bytes=mib * 1024 * 1024)

    count = levels.shape[0]
    kept = level_total - count
    half_shapes = [f32((devices // 2, 2 * rows, LANES))] * 2
    places = share_places(n_gx, n_gy)
    ranks = ranking(n_gx, n_gy)
    order_shape = (3 * level_total,)
    edge_shapes = [f32((total, cells_y)), f32((total, cells_y)), f32((cells_x, 2 * total))]
    levels_space = pltpu.SMEM(levels.shape, jnp.int32)
    owners_space = pltpu.SMEM(owners.shape, jnp.int32)
    order_space = pltpu.SMEM(order_shape, jnp.int32)
    rows_space = vmem(total, cells_y)
    mode_scratch = [vmem(nudged, 4 * KX * KX), table_space(x_fwd),
                    table_space(y_fwd), vmem(nudged, KX, LANES),
                    vmem(devices * rows, 2 * LANES)]
    nudged_scratch = [order_space, vmem(nudged + count, cells_x + 2 * PAD, cells_y),
                      vmem(devices * rows, LANES), vmem(devices * rows, LANES),
                      rows_space, rows_space, pltpu.SemaphoreType.DMA((5,))]
    others_scratch = [vmem(total, cells_x + 2 * PAD, cells_y), rows_space, rows_space]

    def out_scratch(slabs):
        return [vmem(3 * slabs, cells_x, cells_y), vmem(slabs, cells_x, cells_y),
                pltpu.SemaphoreType.DMA((4 * slabs,))]

    keep, send = pl.pallas_call(
        functools.partial(first_kernel, n_gy, level_total, places),
        out_shape=half_shapes,
        in_specs=[HBM] * 6,
        out_specs=[VMEM] * 2,
        scratch_shapes=[levels_space, owners_space, vmem(field_rows, cells_x, cells_y),
                        pltpu.SemaphoreType.DMA((6,))] + mode_scratch,
        compiler_params=limit(8),
        name="first_modes",
    )(*map(in_hbm, (levels, owners, flat, parent_modes, x_fwd, y_fwd)))
    for step in range(STEPS):
        last = step == STEPS - 1
        received = lax.ppermute(send, "gx", [(i, i ^ 1) for i in range(n_gx)])
        modes = pl.pallas_call(
            add_kernel,
            out_shape=half_shapes[0],
            in_specs=[VMEM] * 2,
            out_specs=VMEM,
            compiler_params=limit(4),
            name="add_cores",
        )(keep, received)
        if step == 0:
            *edges, weights = pl.pallas_call(
                functools.partial(edge_kernel, n_gy, period),
                out_shape=edge_shapes + [f32((2 * rows, LANES))],
                in_specs=[SMEM, VMEM, VMEM],
                out_specs=[VMEM] * 4,
                compiler_params=limit(8),
                name="edges",
            )(cuts, flat, plume)
        else:
            others, plume, *edges = pl.pallas_call(
                functools.partial(others_kernel, 0, False, count),
                out_shape=[f32((3 * kept, cells_x, cells_y)), f32(plume.shape)] + edge_shapes,
                in_specs=[VMEM] * 7 + [SMEM] + [VMEM] * 2,
                out_specs=[VMEM] * 5,
                scratch_shapes=others_scratch,
                compiler_params=limit(8),
                name="inner_others",
            )(others, plume, source, *halo, order, flat, winds)
        to_first, to_second, cols = edges
        col_first, col_second = exchange("gy", cols, cols)
        parts = lax.all_to_all(modes, AXES, 0, 0, axis_index_groups=core_groups(n_gx, n_gy),
                               tiled=True)
        parts, col_first, col_second = lax.optimization_barrier((parts, col_first, col_second))
        share = pl.pallas_call(
            functools.partial(share_kernel, n_gx, n_gy),
            out_shape=f32((devices, rows + beside_rows(rows), LANES)),
            in_specs=[VMEM] * 4,
            out_specs=VMEM,
            compiler_params=limit(8),
            name="share_sum",
        )(weights, parts, x_back, x_beside)
        share, to_first, to_second = lax.optimization_barrier((share, to_first, to_second))
        row_first, row_second = exchange("gx", to_first, to_second)
        halo = [row_first, row_second, col_first, col_second]
        if step == 0:
            share, levels = lax.optimization_barrier((share, levels))
            flat, others, y_back, order = pl.pallas_call(
                functools.partial(prepare_kernel, level_total),
                out_shape=[f32((3 * count, cells_x, cells_y)), f32((3 * kept, cells_x, cells_y)),
                           jax.ShapeDtypeStruct(y_back.shape[1:], y_back.dtype),
                           jax.ShapeDtypeStruct(order_shape, jnp.int32)],
                in_specs=[SMEM, VMEM, HBM],
                out_specs=[VMEM] * 3 + [SMEM],
                scratch_shapes=[pltpu.SemaphoreType.DMA((1,))],
                compiler_params=limit(8),
                name="prepare",
            )(levels, flat, in_hbm(y_back))
        shares = lax.all_to_all(share, AXES, 0, 0, axis_index_groups=[ranks], tiled=True)
        if last:
            final = pl.pallas_call(
                functools.partial(others_kernel, step, True, count),
                out_shape=[f32((field_rows, cells_x, cells_y)), f32(plume.shape)],
                in_specs=[VMEM] * 7 + [SMEM],
                out_specs=[HBM] * 2,
                scratch_shapes=others_scratch + out_scratch(kept),
                compiler_params=limit(8),
                name="last_others",
            )(others, plume, source, *halo, order)
            flat, plume = pl.pallas_call(
                functools.partial(nudged_kernel, n_gy, step, True, count, level_total, ranks, None),
                out_shape=[f32((field_rows, cells_x, cells_y)), f32(plume.shape)],
                in_specs=[VMEM] * 7 + [HBM] + [VMEM] * 2 + [HBM] * 2,
                out_specs=[HBM] * 2,
                scratch_shapes=nudged_scratch + out_scratch(count),
                input_output_aliases={10: 0, 11: 1},
                compiler_params=limit(12),
                name="last_nudged",
            )(shares, flat, *halo, y_back, in_hbm(order), plume, source, *final)
        else:
            flat, winds, keep, send = pl.pallas_call(
                functools.partial(nudged_kernel, n_gy, step, False, count, level_total, ranks, places),
                out_shape=[f32((nudged, cells_x, cells_y)), f32((2 * count, cells_x, cells_y))]
                + half_shapes,
                in_specs=[VMEM] * 7 + [HBM] * 5,
                out_specs=[VMEM] * 4,
                scratch_shapes=nudged_scratch + [owners_space] + mode_scratch,
                compiler_params=limit(12),
                name="inner_nudged",
            )(shares, flat, *halo, y_back, in_hbm(order),
              *map(in_hbm, (owners, parent_modes, x_fwd, y_fwd)))
    return flat.reshape(fields.shape), plume


def solution(mesh):
    in_specs = (
        P(None, None, "gx", "gy"),
        P(),
        P(),
        P(("gx", "gy"), None, None, None),
        P(),
        P(None, "gx", "gy"),
        P(None, "gx", "gy"),
    )
    out_specs = (P(None, None, "gx", "gy"), P(None, "gx", "gy"))
    n_gx, n_gy = mesh.shape["gx"], mesh.shape["gy"]

    def whole(fields, levels, cuts, parent_modes, owners, plume, source):
        tables = build_tables(n_gx, n_gy, plume.shape[1] // n_gx, plume.shape[2] // n_gy)
        return jax.shard_map(
            functools.partial(local, tables), mesh=mesh, in_specs=in_specs, out_specs=out_specs,
            check_vma=False,
        )(fields, levels, cuts, parent_modes, owners, plume, source)

    return whole
```

```python
import functools
import math

import jax
import jax.numpy as jnp
import ml_dtypes
import numpy as np
from jax import lax
from jax.experimental import pallas as pl
from jax.experimental.pallas import tpu as pltpu
from jax.sharding import PartitionSpec as P

KX = 32
STEPS = 2
GROUP = 4
LANES = GROUP * KX
PAD = 8
VMEM = pl.BlockSpec(memory_space=pltpu.VMEM)
SMEM = pl.BlockSpec(memory_space=pltpu.SMEM)
HBM = pl.BlockSpec(memory_space=pltpu.HBM)
AXES = ("gx", "gy")


def in_hbm(array):
    return pltpu.with_memory_space_constraint(array, pltpu.HBM)


def wave_table(positions, period):
    wavenum = np.arange(KX)[:, None]
    phase = (wavenum * positions[None, :] % period) * (2.0 * math.pi / period)
    inside = (positions >= 0) & (positions < period)
    return np.concatenate([np.cos(phase), np.sin(phase)], axis=0) * inside[None, :]


def split(a):
    head = a.astype(jnp.bfloat16)
    return head, (a - head.astype(jnp.float32)).astype(jnp.bfloat16)


def split_table(table, axis, order):
    head = table.astype(ml_dtypes.bfloat16)
    rest = (table - head.astype(np.float64)).astype(ml_dtypes.bfloat16)
    return np.concatenate([head if part == "h" else rest for part in order], axis=axis)


def per_slab(table):
    return np.kron(np.eye(GROUP), table)


def build_tables(n_gx, n_gy, cells_x, cells_y):
    period_x, period_y = n_gx * cells_x, n_gy * cells_y
    scaling = 1.0 / math.sqrt(period_x * period_y)
    parity = [np.arange(p, 2 * KX, 2) for p in range(2)]
    x_fwd, y_fwd, y_back, inner, outer = [], [], [], [], []
    for g in range(n_gx):
        first = g * cells_x
        table = wave_table(first + np.arange(cells_x), period_x)
        x_fwd.append(split_table(
            np.concatenate([per_slab(table[rows].T) for rows in parity], axis=1), 0, "hhl"))
        beside = wave_table(np.array([first - 1, first + cells_x]), period_x)
        inner.append(np.concatenate([np.tile(table[rows], (GROUP, 1)) for rows in parity], axis=0))
        outer.append(np.concatenate([per_slab(beside[rows]) for rows in parity], axis=0))
    spare = -(2 * GROUP * n_gx) % LANES
    x_back = np.concatenate(inner, axis=1)
    x_beside = np.concatenate(outer + [np.zeros((2 * LANES, spare))], axis=1)
    for g in range(n_gy):
        first = g * cells_y
        table = wave_table(first + np.arange(cells_y), period_y)
        edge = np.zeros((2 * KX, cells_y))
        edge[:, [0, -1]] = wave_table(np.array([first - 1, first + cells_y]), period_y)
        y_fwd.append(split_table(table * scaling, 1, "hlh"))
        y_back.append(split_table(np.concatenate([table, edge], axis=1), 0, "hhl"))
    return [np.stack(x_fwd), np.stack(y_fwd), np.stack(y_back),
            split_table(x_back, 0, "hl"), split_table(x_beside, 0, "hl")]


def data_dot(a, table):
    head, rest = split(a)
    return jnp.dot(
        jnp.concatenate([head, rest, head], axis=1), table, preferred_element_type=jnp.float32
    )


def two_part_dot(a, table):
    head, rest = split(a)
    depth = a.shape[1]
    heads = jnp.dot(
        jnp.concatenate([head, rest], axis=0), table[:depth], preferred_element_type=jnp.float32)
    rests = jnp.dot(head, table[depth:], preferred_element_type=jnp.float32)
    return heads[: a.shape[0]] + heads[a.shape[0] :] + rests


def columns_dot(a, table):
    head, rest = split(a)
    stacked = jnp.concatenate([head, rest, head], axis=0)
    return lax.dot_general(
        stacked, table, (((0,), (0,)), ((), ())), preferred_element_type=jnp.float32)


def core():
    return lax.rem(lax.axis_index("gx"), 2)


def ranking(n_gx, n_gy):
    return sorted(range(n_gx * n_gy), key=lambda d: (abs(2 * (d % n_gy) - (n_gy - 1)), d))


def core_groups(n_gx, n_gy):
    return [[d for d in ranking(n_gx, n_gy) if d // n_gy % 2 == c] for c in range(2)]


def share_places(n_gx, n_gy):
    places = {}
    for c, group in enumerate(core_groups(n_gx, n_gy)):
        places.update({d: c * len(group) + i for i, d in enumerate(group)})
    return [places[d] for d in range(n_gx * n_gy)]


def emit_modes(chosen, parent, parent_copy, is_owner, places, x_fwd, y_fwd, keep, send, turned, work):
    devices, rows = len(places), keep.shape[1] // 2
    slabs = parent.shape[0]
    groups = slabs // GROUP
    head, rest = split(jnp.concatenate(chosen, axis=0))
    half = lax.dot_general(
        y_fwd, jnp.concatenate([head, head, rest], axis=1), (((1,), (1,)), ((), ())),
        preferred_element_type=jnp.float32)
    half = jnp.concatenate([half[:, t * LANES : (t + 1) * LANES] for t in range(groups)], axis=0)
    count = groups * 2 * KX
    work[0:count] = -data_dot(half, x_fwd)
    if count < devices * rows:
        work[count:] = jnp.zeros((devices * rows - count, 2 * LANES), jnp.float32)

    parent_copy.wait()

    @pl.when(is_owner)
    def _():
        for i in range(KX):
            turned[:, i, :] = parent[:, i * LANES : (i + 1) * LANES]
        for t in range(groups):
            block = turned[t * GROUP : (t + 1) * GROUP].reshape(LANES, LANES).T
            span = slice(t * 2 * KX, (t + 1) * 2 * KX)
            for p in range(2):
                work[span, p * LANES : (p + 1) * LANES] += block[p * 2 * KX : (p + 1) * 2 * KX]

    count = devices // 2
    for mine in range(2):
        @pl.when(core() == mine)
        def _(mine=mine):
            for d in range(devices):
                half = keep if places[d] // count == mine else send
                for p in range(2):
                    half[places[d] % count, p * rows : (p + 1) * rows, :] = work[
                        d * rows : (d + 1) * rows, p * LANES : (p + 1) * LANES]


def add_kernel(kept, received, out):
    out[...] = kept[...] + received[...]


def fetch_all(sems, pairs):
    copies = [pltpu.make_async_copy(a, b, sems.at[i]) for i, (a, b) in enumerate(pairs)]
    for copy in copies:
        copy.start()
    return copies


def slab_of(levels, c, level_count, level_total):
    return (c // level_count) * level_total + levels[c % level_count]


def first_kernel(n_gy, level_total, places, levels_all, owners_all, fields_all, parent_all,
                 x_fwd_all, y_fwd_all, keep, send, levels, owners, fields, sems, parent, x_fwd, y_fwd,
                 turned, work):
    gx, gy = lax.axis_index("gx"), lax.axis_index("gy")
    copies = fetch_all(sems, [
        (levels_all, levels), (owners_all, owners), (fields_all, fields),
        (x_fwd_all.at[gx], x_fwd), (y_fwd_all.at[gy], y_fwd), (parent_all.at[0, 0], parent)])
    for copy in copies[:-1]:
        copy.wait()
    level_count = parent.shape[0] // 3
    emit_modes(
        [fields[slab_of(levels, c, level_count, level_total)] for c in range(parent.shape[0])],
        parent, copies[-1], owners[0] == gx * n_gy + gy, places, x_fwd[...], y_fwd[...], keep, send,
        turned, work,
    )


def is_even(axis):
    return lax.rem(lax.axis_index(axis), 2) == 0


def edge_kernel(n_gy, period, cuts, fields, plume, first, second, cols, weights):
    weights[...] = share_weights(n_gy, period, cuts, weights.shape)
    slabs = [fields[c] for c in range(fields.shape[0])]
    emit_edges(slabs + [plume[l] for l in range(plume.shape[0])], first, second, cols)


def prepare_kernel(level_total, levels, fields, y_back_all, nudged, others, y_back, order, sems):
    copies = fetch_all(sems, [(y_back_all.at[lax.axis_index("gy")], y_back)])
    count = levels.shape[0]
    for n in range(count):
        order[n] = levels[n]
    spot = jnp.int32(count)
    for l in range(level_total):
        found = levels[0] == l
        for n in range(1, count):
            found = found | (levels[n] == l)
        order[spot] = jnp.int32(l)
        spot = spot + jnp.where(found, 0, 1)
    chosen = [order[n] for n in range(level_total)]
    for n in range(level_total, order.shape[0]):
        order[n] = jnp.int32(0)
    for n in range(level_total):
        order[level_total + chosen[n]] = jnp.int32(n)
    slabs = [fields[f * level_total + l] for f in range(3) for l in chosen]
    kept = level_total - count
    for c, a in enumerate(slabs):
        f, n = c // level_total, c % level_total
        if n < count:
            nudged[f * count + n] = a
        else:
            others[f * kept + n - count] = a
    for copy in copies:
        copy.wait()


def emit_edges(slabs, first, second, cols):
    even = is_even("gx")
    lane = lax.broadcasted_iota(jnp.int32, cols.shape, 1)
    acc = jnp.zeros(cols.shape, jnp.float32)
    for c, a in enumerate(slabs):
        west, east = a[:1], a[a.shape[0] - 1 :]
        first[c : c + 1, :] = jnp.where(even, east, west)
        second[c : c + 1, :] = jnp.where(even, west, east)
        acc = jnp.where(lane // 2 == c, pltpu.roll(a, 2 * c + 1, 1), acc)
    cols[...] = acc


def share_weights(n_gy, period, cuts, shape):
    rows = shape[0] // 2
    me = lax.axis_index("gx") * n_gy + lax.axis_index("gy")
    place = lax.broadcasted_iota(jnp.int32, shape, 0)
    lane = lax.broadcasted_iota(jnp.int32, shape, 1)
    p = (place >= rows).astype(jnp.int32)
    row = me * rows + place - p * rows
    k = 2 * (lane % KX) + p
    j = row % (2 * KX)
    slab = GROUP * (row // (2 * KX)) + lane // KX
    limit = jnp.zeros(shape, jnp.int32)
    for c in range(cuts.shape[0]):
        limit = jnp.where(slab == c, cuts[c], limit)
    keep = ((k % KX) < limit) & ((j % KX) < limit)
    factor = jnp.where(k == 0, 1.0, 2.0) * jnp.where(j == 0, 1.0, 2.0) * (1.0 / math.sqrt(period))
    return jnp.where(keep, factor, 0.0)


def beside_rows(rows):
    return -(-rows // 3)


def share_kernel(n_gx, n_gy, weights, parts, x_back, x_beside, out):
    rows = parts.shape[1] // 2
    total = parts[0]
    for d in range(1, parts.shape[0]):
        total = total + parts[d]
    mismatch = total * weights[...]
    both = jnp.concatenate([mismatch[:rows], mismatch[rows:]], axis=1)
    spare = -rows % 16
    if spare:
        both = jnp.concatenate([both, jnp.zeros((spare, 2 * LANES), jnp.float32)], axis=0)
    slab_lane = lax.broadcasted_iota(jnp.int32, both.shape, 1) % LANES // KX
    chosen = [jnp.where(slab_lane == n, both, 0.0) for n in range(GROUP)]
    inner = two_part_dot(jnp.concatenate(chosen, axis=0), x_back)
    edge_all = two_part_dot(both, x_beside)
    height = rows + spare
    packed = beside_rows(rows)
    width = 2 * GROUP
    cells_x = LANES // GROUP
    slot = lax.broadcasted_iota(jnp.int32, (height, LANES), 1) // cells_x
    spot = lax.broadcasted_iota(jnp.int32, (packed, LANES), 1) // width
    spot_at = {d: i for i, d in enumerate(ranking(n_gx, n_gy))}
    for g in range(n_gx):
        first = g * cells_x // LANES * LANES
        tile = jnp.zeros((height, LANES), jnp.float32)
        for n in range(GROUP):
            piece = inner[n * height : (n + 1) * height, first : first + LANES]
            tile = jnp.where(slot == n, pltpu.roll(piece, (n - g) * cells_x % LANES, 1), tile)
        first = g * width // LANES * LANES
        beside = jnp.zeros((packed, LANES), jnp.float32)
        for m in range(3):
            piece = edge_all[m * packed : (m + 1) * packed, first : first + LANES]
            beside = jnp.where(
                spot == m, pltpu.roll(piece, (m - g) * width % LANES, 1), beside)
        for h in range(n_gy):
            out[spot_at[g * n_gy + h], :rows, :] = tile[:rows]
            out[spot_at[g * n_gy + h], rows:, :] = beside


class Halo:
    def __init__(self, row_first, row_second, col_first, col_second, west, east):
        even = is_even("gx")
        west[...] = jnp.where(even, row_second[...], row_first[...])
        east[...] = jnp.where(even, row_first[...], row_second[...])
        self.west, self.east = west, east
        even = is_even("gy")
        north = jnp.where(even, col_first[...], col_second[...])
        south = jnp.where(even, col_second[...], col_first[...])
        shape = north.shape
        lane = lax.broadcasted_iota(jnp.int32, shape, 1)
        self.last = shape[1] - 1
        self.at_first, self.at_last = lane == 0, lane == self.last
        self.columns = jnp.where(
            lane % 2 == 0, pltpu.roll(north, self.last, 1), pltpu.roll(south, 1, 1))

    def rows(self, c):
        return self.west[pl.ds(c, 1), :], self.east[pl.ds(c, 1), :]

    def column(self, c):
        return pltpu.roll(self.columns, self.last - 2 * c, 1)

    def move(self, slab, column, parts):
        centre, to_west, to_east, to_south, to_north = parts
        cells_x = column.shape[0]
        a = slab[PAD : PAD + cells_x]
        return (
            centre * a
            + to_west * slab[PAD - 1 : PAD - 1 + cells_x]
            + to_east * slab[PAD + 1 : PAD + 1 + cells_x]
            + to_south * jnp.where(self.at_first, column, pltpu.roll(a, 1, 1))
            + to_north * jnp.where(self.at_last, column, pltpu.roll(a, self.last, 1))
        )


def place(slab, a, rows):
    cells_x = a.shape[0]
    slab[PAD : PAD + cells_x] = a
    slab[PAD - 1 : PAD] = rows[0]
    slab[PAD + cells_x : PAD + cells_x + 1] = rows[1]


def wind_weights(u, v):
    neighbours = (
        0.1 + 0.1 * jnp.maximum(u, 0.0), 0.1 - 0.1 * jnp.minimum(u, 0.0),
        0.1 + 0.1 * jnp.maximum(v, 0.0), 0.1 - 0.1 * jnp.minimum(v, 0.0),
    )
    centre = 1.0 - (neighbours[0] + neighbours[1] + neighbours[2] + neighbours[3])
    return (centre,) + neighbours


def settling(parts):
    return (parts[0] - 0.3,) + parts[1:]


def above(l, level_total):
    return jnp.where(l + 1 < level_total, 0.3, 0.0).astype(jnp.float32)


def nudge_updates(ranks, shares, spread, spread_edges, y_table, nudged, cells_x):
    devices = shares.shape[0]
    rows = spread.shape[0] // devices
    packed = beside_rows(rows)
    width = 2 * GROUP
    for i, d in enumerate(ranks):
        spread[d * rows : (d + 1) * rows] = shares[i, :rows, :]
        edge = shares[i, rows:, :]
        for m in range(3):
            count = min(packed, rows - m * packed)
            if count > 0:
                moved = pltpu.roll(edge, -m * width % LANES, 1) if m else edge
                start = d * rows + m * packed
                spread_edges[start : start + count] = moved[:count]
    groups = nudged // GROUP
    spot_of = lax.broadcasted_iota(jnp.int32, (2 * KX, LANES), 1) // width
    edges = jnp.zeros((2 * KX, LANES), jnp.float32)
    for t in range(groups):
        piece = spread_edges[t * 2 * KX : (t + 1) * 2 * KX]
        edges = jnp.where(spot_of == t, pltpu.roll(piece, t * width, 1) if t else piece, edges)
    update_rows = columns_dot(edges, y_table)
    updates = []
    for t in range(groups):
        update = columns_dot(spread[t * 2 * KX : (t + 1) * 2 * KX], y_table)
        updates += [update[n * cells_x : (n + 1) * cells_x] for n in range(GROUP)]
    return updates, update_rows


def nudged_kernel(n_gy, step, last, level_count, level_total, ranks, places, shares, fields, row_first, row_second,
                  col_first, col_second, y_back, order_all, *rest):
    gx, gy = lax.axis_index("gx"), lax.axis_index("gy")
    cells_x, cells_y = fields.shape[1:]
    nudged = 3 * level_count
    if last:
        (plume, source, _, _, fields_all, plume_all, order, slabs, spread, spread_edges, west, east,
         sems, fields_out, plume_out, out_sems) = rest
        extra = []
    else:
        (owners_all, parent_all, x_fwd_all, y_fwd_all, fields_out, winds_out, keep, send,
         order, slabs, spread, spread_edges, west, east, sems,
         owners, parent, x_fwd, y_fwd, turned, work) = rest
        extra = [(owners_all, owners), (x_fwd_all.at[gx], x_fwd), (y_fwd_all.at[gy], y_fwd),
                 (parent_all.at[0, step + 1], parent)]
    copies = fetch_all(sems, [(order_all, order)] + extra)
    halo = Halo(row_first, row_second, col_first, col_second, west, east)
    updates, update_rows = nudge_updates(
        ranks, shares, spread, spread_edges, y_back[...], nudged, cells_x)
    copies[0].wait()
    level_at = [order[n] for n in range(level_count)]
    halo_at = level_at if step == 0 else list(range(level_count))
    beside = []
    for k in range(nudged):
        f, n = k // level_count, k % level_count
        a = fields[k]
        before, after = halo.rows(f * level_total + halo_at[n])
        place(slabs.at[k], a + updates[k][:, :cells_y],
              (before + update_rows[2 * k : 2 * k + 1, :cells_y],
               after + update_rows[2 * k + 1 : 2 * k + 2, :cells_y]))
        beside.append(updates[k][:, cells_y:])
    inner = slice(PAD, PAD + cells_x)
    results = [None] * nudged
    sent = []
    for n in range(level_count):
        u, v = slabs[n, inner], slabs[level_count + n, inner]
        parts = wind_weights(u, v)
        for f in range(3):
            k = f * level_count + n
            column = halo.column(f * level_total + halo_at[n]) + beside[k]
            results[k] = halo.move(slabs[k], column, parts)
            fields_out[k] = results[k]
        if not last:
            winds_out[n] = u
            winds_out[level_count + n] = v
            continue
        l = level_at[n]
        c = 3 * level_total + n
        place(slabs.at[nudged + n], plume[n], halo.rows(c))
        settled = halo.move(slabs[nudged + n], halo.column(c), settling(parts))
        plume_out[n] = settled + above(l, level_total) * plume[order[level_total + l + 1]] + source[l]
        pairs = [(fields_out.at[f * level_count + n], fields_all.at[f * level_total + l])
                 for f in range(3)] + [(plume_out.at[n], plume_all.at[l])]
        sent += fetch_all(out_sems.at[pl.ds(4 * n, 4)], pairs)
    if last:
        for copy in sent:
            copy.wait()
        return
    for copy in copies[1:-1]:
        copy.wait()
    emit_modes(results, parent, copies[-1], owners[step + 1] == gx * n_gy + gy, places, x_fwd[...], y_fwd[...],
               keep, send, turned, work)


def others_kernel(step, last, level_count, fields, plume, source, row_first, row_second, col_first,
                  col_second, order, *rest):
    level_total, cells_x, cells_y = plume.shape
    if last:
        fields_all, plume_all, slab, west, east, fields_out, plume_out, out_sems = rest
    else:
        done, winds, fields_out, plume_out, first, second, cols, slab, west, east = rest
    halo = Halo(row_first, row_second, col_first, col_second, west, east)
    level_at = [order[n] for n in range(level_total)]
    kept = level_total - level_count
    sent = []
    results = {}
    for n in range(level_count if last else 0, level_total):
        l = level_at[n]
        m = n - level_count
        if m < 0:
            parts = wind_weights(winds[n], winds[level_count + n])
        else:
            given = [fields[f * kept + m] for f in range(3)]
            parts = wind_weights(given[0], given[1])
            for f in range(3):
                c = f * level_total + n
                beyond = f * level_total + l if step == 0 else c
                place(slab.at[4 * n + f], given[f], halo.rows(beyond))
                results[c] = halo.move(slab[4 * n + f], halo.column(beyond), parts)
                fields_out[f * kept + m] = results[c]
        c = 3 * level_total + n
        beyond = 3 * level_total + l if step == 0 else c
        place(slab.at[4 * n + 3], plume[l] if step == 0 else plume[n], halo.rows(beyond))
        higher = (jnp.minimum(l + 1, level_total - 1) if step == 0 else order[level_total + l + 1])
        results[c] = (halo.move(slab[4 * n + 3], halo.column(beyond), settling(parts))
                      + above(l, level_total) * plume[higher] + source[l])
        plume_out[m if last else n] = results[c]
        if last:
            pairs = [(fields_out.at[f * kept + m], fields_all.at[f * level_total + l])
                     for f in range(3)] + [(plume_out.at[m], plume_all.at[l])]
            sent += fetch_all(out_sems.at[pl.ds(4 * m, 4)], pairs)
    for copy in sent:
        copy.wait()
    if not last:
        for f in range(3):
            for n in range(level_count):
                results[f * level_total + n] = done[f * level_count + n]
        emit_edges([results[c] for c in range(4 * level_total)], first, second, cols)


def exchange(axis, first, second):
    count = lax.axis_size(axis)
    received = []
    for start, data in ((0, first), (1, second)):
        pairs = [(i, i + 1) for i in range(start, count - 1, 2)]
        received.append(lax.ppermute(data, axis, pairs + [(b, a) for a, b in pairs]))
    return received


def local(tables, fields, levels, cuts, parent_modes, owners, plume, source):
    n_gx, n_gy = lax.axis_size("gx"), lax.axis_size("gy")
    devices = n_gx * n_gy
    level_total, cells_x, cells_y = plume.shape
    period = n_gx * cells_x * n_gy * cells_y
    nudged = 3 * levels.shape[0]
    field_rows = 3 * level_total
    total = field_rows + level_total
    rows = -(-(nudged // GROUP * 2 * KX) // devices)
    flat = fields.reshape(field_rows, cells_x, cells_y)
    cuts = cuts.reshape(-1)
    f32 = functools.partial(jax.ShapeDtypeStruct, dtype=jnp.float32)
    x_fwd, y_fwd, y_back, x_back, x_beside = (jnp.asarray(t) for t in tables)

    def vmem(*shape):
        return pltpu.VMEM(shape, jnp.float32)

    def table_space(table):
        return pltpu.VMEM(table.shape[1:], table.dtype)

    def limit(mib):
        return pltpu.CompilerParams(vmem_limit_bytes=mib * 1024 * 1024)

    count = levels.shape[0]
    kept = level_total - count
    half_shapes = [f32((devices // 2, 2 * rows, LANES))] * 2
    places = share_places(n_gx, n_gy)
    ranks = ranking(n_gx, n_gy)
    order_shape = (3 * level_total,)
    edge_shapes = [f32((total, cells_y)), f32((total, cells_y)), f32((cells_x, 2 * total))]
    levels_space = pltpu.SMEM(levels.shape, jnp.int32)
    owners_space = pltpu.SMEM(owners.shape, jnp.int32)
    order_space = pltpu.SMEM(order_shape, jnp.int32)
    rows_space = vmem(total, cells_y)
    mode_scratch = [vmem(nudged, 4 * KX * KX), table_space(x_fwd),
                    table_space(y_fwd), vmem(nudged, KX, LANES),
                    vmem(devices * rows, 2 * LANES)]
    nudged_scratch = [order_space, vmem(nudged + count, cells_x + 2 * PAD, cells_y),
                      vmem(devices * rows, LANES), vmem(devices * rows, LANES),
                      rows_space, rows_space, pltpu.SemaphoreType.DMA((5,))]
    others_scratch = [vmem(total, cells_x + 2 * PAD, cells_y), rows_space, rows_space]

    def out_scratch(slabs):
        return [vmem(3 * slabs, cells_x, cells_y), vmem(slabs, cells_x, cells_y),
                pltpu.SemaphoreType.DMA((4 * slabs,))]

    keep, send = pl.pallas_call(
        functools.partial(first_kernel, n_gy, level_total, places),
        out_shape=half_shapes,
        in_specs=[HBM] * 6,
        out_specs=[VMEM] * 2,
        scratch_shapes=[levels_space, owners_space, vmem(field_rows, cells_x, cells_y),
                        pltpu.SemaphoreType.DMA((6,))] + mode_scratch,
        compiler_params=limit(8),
        name="first_modes",
    )(*map(in_hbm, (levels, owners, flat, parent_modes, x_fwd, y_fwd)))
    for step in range(STEPS):
        last = step == STEPS - 1
        received = lax.ppermute(send, "gx", [(i, i ^ 1) for i in range(n_gx)])
        if step == 0:
            *edges, weights = pl.pallas_call(
                functools.partial(edge_kernel, n_gy, period),
                out_shape=edge_shapes + [f32((2 * rows, LANES))],
                in_specs=[SMEM, VMEM, VMEM],
                out_specs=[VMEM] * 4,
                compiler_params=limit(8),
                name="edges",
            )(cuts, flat, plume)
        else:
            others, plume, *edges = pl.pallas_call(
                functools.partial(others_kernel, 0, False, count),
                out_shape=[f32((3 * kept, cells_x, cells_y)), f32(plume.shape)] + edge_shapes,
                in_specs=[VMEM] * 7 + [SMEM] + [VMEM] * 2,
                out_specs=[VMEM] * 5,
                scratch_shapes=others_scratch,
                compiler_params=limit(8),
                name="inner_others",
            )(others, plume, source, *halo, order, flat, winds)
        received, *edges = lax.optimization_barrier((received, *edges))
        to_first, to_second, cols = edges
        modes = pl.pallas_call(
            add_kernel,
            out_shape=half_shapes[0],
            in_specs=[VMEM] * 2,
            out_specs=VMEM,
            compiler_params=limit(4),
            name="add_cores",
        )(keep, received)
        col_first, col_second = exchange("gy", cols, cols)
        parts = lax.all_to_all(modes, AXES, 0, 0, axis_index_groups=core_groups(n_gx, n_gy),
                               tiled=True)
        parts, col_first, col_second = lax.optimization_barrier((parts, col_first, col_second))
        share = pl.pallas_call(
            functools.partial(share_kernel, n_gx, n_gy),
            out_shape=f32((devices, rows + beside_rows(rows), LANES)),
            in_specs=[VMEM] * 4,
            out_specs=VMEM,
            compiler_params=limit(8),
            name="share_sum",
        )(weights, parts, x_back, x_beside)
        share, to_first, to_second = lax.optimization_barrier((share, to_first, to_second))
        row_first, row_second = exchange("gx", to_first, to_second)
        halo = [row_first, row_second, col_first, col_second]
        if step == 0:
            share, levels = lax.optimization_barrier((share, levels))
            flat, others, y_back, order = pl.pallas_call(
                functools.partial(prepare_kernel, level_total),
                out_shape=[f32((3 * count, cells_x, cells_y)), f32((3 * kept, cells_x, cells_y)),
                           jax.ShapeDtypeStruct(y_back.shape[1:], y_back.dtype),
                           jax.ShapeDtypeStruct(order_shape, jnp.int32)],
                in_specs=[SMEM, VMEM, HBM],
                out_specs=[VMEM] * 3 + [SMEM],
                scratch_shapes=[pltpu.SemaphoreType.DMA((1,))],
                compiler_params=limit(8),
                name="prepare",
            )(levels, flat, in_hbm(y_back))
        shares = lax.all_to_all(share, AXES, 0, 0, axis_index_groups=[ranks], tiled=True)
        if last:
            final = pl.pallas_call(
                functools.partial(others_kernel, step, True, count),
                out_shape=[f32((field_rows, cells_x, cells_y)), f32(plume.shape)],
                in_specs=[VMEM] * 7 + [SMEM],
                out_specs=[HBM] * 2,
                scratch_shapes=others_scratch + out_scratch(kept),
                compiler_params=limit(8),
                name="last_others",
            )(others, plume, source, *halo, order)
            flat, plume = pl.pallas_call(
                functools.partial(nudged_kernel, n_gy, step, True, count, level_total, ranks, None),
                out_shape=[f32((field_rows, cells_x, cells_y)), f32(plume.shape)],
                in_specs=[VMEM] * 7 + [HBM] + [VMEM] * 2 + [HBM] * 2,
                out_specs=[HBM] * 2,
                scratch_shapes=nudged_scratch + out_scratch(count),
                input_output_aliases={10: 0, 11: 1},
                compiler_params=limit(12),
                name="last_nudged",
            )(shares, flat, *halo, y_back, in_hbm(order), plume, source, *final)
        else:
            flat, winds, keep, send = pl.pallas_call(
                functools.partial(nudged_kernel, n_gy, step, False, count, level_total, ranks, places),
                out_shape=[f32((nudged, cells_x, cells_y)), f32((2 * count, cells_x, cells_y))]
                + half_shapes,
                in_specs=[VMEM] * 7 + [HBM] * 5,
                out_specs=[VMEM] * 4,
                scratch_shapes=nudged_scratch + [owners_space] + mode_scratch,
                compiler_params=limit(12),
                name="inner_nudged",
            )(shares, flat, *halo, y_back, in_hbm(order),
              *map(in_hbm, (owners, parent_modes, x_fwd, y_fwd)))
    return flat.reshape(fields.shape), plume


def solution(mesh):
    in_specs = (
        P(None, None, "gx", "gy"),
        P(),
        P(),
        P(("gx", "gy"), None, None, None),
        P(),
        P(None, "gx", "gy"),
        P(None, "gx", "gy"),
    )
    out_specs = (P(None, None, "gx", "gy"), P(None, "gx", "gy"))
    n_gx, n_gy = mesh.shape["gx"], mesh.shape["gy"]

    def whole(fields, levels, cuts, parent_modes, owners, plume, source):
        tables = build_tables(n_gx, n_gy, plume.shape[1] // n_gx, plume.shape[2] // n_gy)
        return jax.shard_map(
            functools.partial(local, tables), mesh=mesh, in_specs=in_specs, out_specs=out_specs,
            check_vma=False,
        )(fields, levels, cuts, parent_modes, owners, plume, source)

    return whole
```

```python
import functools
import math

import jax
import jax.numpy as jnp
import ml_dtypes
import numpy as np
from jax import lax
from jax.experimental import pallas as pl
from jax.experimental.pallas import tpu as pltpu
from jax.sharding import PartitionSpec as P

KX = 32
STEPS = 2
GROUP = 4
LANES = GROUP * KX
PAD = 8
VMEM = pl.BlockSpec(memory_space=pltpu.VMEM)
SMEM = pl.BlockSpec(memory_space=pltpu.SMEM)
HBM = pl.BlockSpec(memory_space=pltpu.HBM)
AXES = ("gx", "gy")


def in_hbm(array):
    return pltpu.with_memory_space_constraint(array, pltpu.HBM)


def wave_table(positions, period):
    wavenum = np.arange(KX)[:, None]
    phase = (wavenum * positions[None, :] % period) * (2.0 * math.pi / period)
    inside = (positions >= 0) & (positions < period)
    return np.concatenate([np.cos(phase), np.sin(phase)], axis=0) * inside[None, :]


def split(a):
    head = a.astype(jnp.bfloat16)
    return head, (a - head.astype(jnp.float32)).astype(jnp.bfloat16)


def split_table(table, axis, order):
    head = table.astype(ml_dtypes.bfloat16)
    rest = (table - head.astype(np.float64)).astype(ml_dtypes.bfloat16)
    return np.concatenate([head if part == "h" else rest for part in order], axis=axis)


def per_slab(table):
    return np.kron(np.eye(GROUP), table)


def build_tables(n_gx, n_gy, cells_x, cells_y):
    period_x, period_y = n_gx * cells_x, n_gy * cells_y
    scaling = 1.0 / math.sqrt(period_x * period_y)
    parity = [np.arange(p, 2 * KX, 2) for p in range(2)]
    x_fwd, y_fwd, y_back, inner, outer = [], [], [], [], []
    for g in range(n_gx):
        first = g * cells_x
        table = wave_table(first + np.arange(cells_x), period_x)
        x_fwd.append(split_table(
            np.concatenate([per_slab(table[rows].T) for rows in parity], axis=1), 0, "hhl"))
        beside = wave_table(np.array([first - 1, first + cells_x]), period_x)
        inner.append(np.concatenate([np.tile(table[rows], (GROUP, 1)) for rows in parity], axis=0))
        outer.append(np.concatenate([per_slab(beside[rows]) for rows in parity], axis=0))
    spare = -(2 * GROUP * n_gx) % LANES
    x_back = np.concatenate(inner, axis=1)
    x_beside = np.concatenate(outer + [np.zeros((2 * LANES, spare))], axis=1)
    for g in range(n_gy):
        first = g * cells_y
        table = wave_table(first + np.arange(cells_y), period_y)
        edge = np.zeros((2 * KX, cells_y))
        edge[:, [0, -1]] = wave_table(np.array([first - 1, first + cells_y]), period_y)
        y_fwd.append(split_table(table * scaling, 1, "hlh"))
        y_back.append(split_table(np.concatenate([table, edge], axis=1), 0, "hhl"))
    return [np.stack(x_fwd), np.stack(y_fwd), np.stack(y_back),
            split_table(x_back, 0, "hl"), split_table(x_beside, 0, "hl")]


def data_dot(a, table):
    head, rest = split(a)
    return jnp.dot(
        jnp.concatenate([head, rest, head], axis=1), table, preferred_element_type=jnp.float32
    )


def two_part_dot(a, table):
    head, rest = split(a)
    depth = a.shape[1]
    heads = jnp.dot(
        jnp.concatenate([head, rest], axis=0), table[:depth], preferred_element_type=jnp.float32)
    rests = jnp.dot(head, table[depth:], preferred_element_type=jnp.float32)
    return heads[: a.shape[0]] + heads[a.shape[0] :] + rests


def columns_dot(a, table):
    head, rest = split(a)
    stacked = jnp.concatenate([head, rest, head], axis=0)
    return lax.dot_general(
        stacked, table, (((0,), (0,)), ((), ())), preferred_element_type=jnp.float32)


def core():
    return lax.rem(lax.axis_index("gx"), 2)


def ranking(n_gx, n_gy):
    return sorted(range(n_gx * n_gy), key=lambda d: (abs(2 * (d % n_gy) - (n_gy - 1)), d))


def core_groups(n_gx, n_gy):
    return [[d for d in ranking(n_gx, n_gy) if d // n_gy % 2 == c] for c in range(2)]


def share_places(n_gx, n_gy):
    places = {}
    for c, group in enumerate(core_groups(n_gx, n_gy)):
        places.update({d: c * len(group) + i for i, d in enumerate(group)})
    return [places[d] for d in range(n_gx * n_gy)]


def emit_modes(chosen, parent, parent_copy, is_owner, places, x_fwd, y_fwd, keep, send, turned, work):
    devices, rows = len(places), keep.shape[1] // 2
    slabs = parent.shape[0]
    groups = slabs // GROUP
    head, rest = split(jnp.concatenate(chosen, axis=0))
    half = lax.dot_general(
        y_fwd, jnp.concatenate([head, head, rest], axis=1), (((1,), (1,)), ((), ())),
        preferred_element_type=jnp.float32)
    half = jnp.concatenate([half[:, t * LANES : (t + 1) * LANES] for t in range(groups)], axis=0)
    count = groups * 2 * KX
    work[0:count] = -data_dot(half, x_fwd)
    if count < devices * rows:
        work[count:] = jnp.zeros((devices * rows - count, 2 * LANES), jnp.float32)

    parent_copy.wait()

    @pl.when(is_owner)
    def _():
        for i in range(KX):
            turned[:, i, :] = parent[:, i * LANES : (i + 1) * LANES]
        for t in range(groups):
            block = turned[t * GROUP : (t + 1) * GROUP].reshape(LANES, LANES).T
            span = slice(t * 2 * KX, (t + 1) * 2 * KX)
            for p in range(2):
                work[span, p * LANES : (p + 1) * LANES] += block[p * 2 * KX : (p + 1) * 2 * KX]

    count = devices // 2
    for mine in range(2):
        @pl.when(core() == mine)
        def _(mine=mine):
            for d in range(devices):
                half = keep if places[d] // count == mine else send
                for p in range(2):
                    half[places[d] % count, p * rows : (p + 1) * rows, :] = work[
                        d * rows : (d + 1) * rows, p * LANES : (p + 1) * LANES]


def add_kernel(kept, received, out):
    out[...] = kept[...] + received[...]


def fetch_all(sems, pairs):
    copies = [pltpu.make_async_copy(a, b, sems.at[i]) for i, (a, b) in enumerate(pairs)]
    for copy in copies:
        copy.start()
    return copies


def slab_of(levels, c, level_count, level_total):
    return (c // level_count) * level_total + levels[c % level_count]


def first_kernel(n_gy, level_total, places, levels_all, owners_all, fields_all, parent_all,
                 x_fwd_all, y_fwd_all, keep, send, levels, owners, fields, sems, parent, x_fwd, y_fwd,
                 turned, work):
    gx, gy = lax.axis_index("gx"), lax.axis_index("gy")
    copies = fetch_all(sems, [
        (levels_all, levels), (owners_all, owners), (fields_all, fields),
        (x_fwd_all.at[gx], x_fwd), (y_fwd_all.at[gy], y_fwd), (parent_all.at[0, 0], parent)])
    for copy in copies[:-1]:
        copy.wait()
    level_count = parent.shape[0] // 3
    emit_modes(
        [fields[slab_of(levels, c, level_count, level_total)] for c in range(parent.shape[0])],
        parent, copies[-1], owners[0] == gx * n_gy + gy, places, x_fwd[...], y_fwd[...], keep, send,
        turned, work,
    )


def is_even(axis):
    return lax.rem(lax.axis_index(axis), 2) == 0


def edge_kernel(n_gy, period, cuts, fields, plume, first, second, cols, weights):
    weights[...] = share_weights(n_gy, period, cuts, weights.shape)
    slabs = [fields[c] for c in range(fields.shape[0])]
    emit_edges(slabs + [plume[l] for l in range(plume.shape[0])], first, second, cols)


def prepare_kernel(level_total, levels, fields, y_back_all, nudged, others, y_back, order, sems):
    copies = fetch_all(sems, [(y_back_all.at[lax.axis_index("gy")], y_back)])
    count = levels.shape[0]
    for n in range(count):
        order[n] = levels[n]
    spot = jnp.int32(count)
    for l in range(level_total):
        found = levels[0] == l
        for n in range(1, count):
            found = found | (levels[n] == l)
        order[spot] = jnp.int32(l)
        spot = spot + jnp.where(found, 0, 1)
    chosen = [order[n] for n in range(level_total)]
    for n in range(level_total, order.shape[0]):
        order[n] = jnp.int32(0)
    for n in range(level_total):
        order[level_total + chosen[n]] = jnp.int32(n)
    slabs = [fields[f * level_total + l] for f in range(3) for l in chosen]
    kept = level_total - count
    for c, a in enumerate(slabs):
        f, n = c // level_total, c % level_total
        if n < count:
            nudged[f * count + n] = a
        else:
            others[f * kept + n - count] = a
    for copy in copies:
        copy.wait()


def emit_edges(slabs, first, second, cols):
    even = is_even("gx")
    lane = lax.broadcasted_iota(jnp.int32, cols.shape, 1)
    acc = jnp.zeros(cols.shape, jnp.float32)
    for c, a in enumerate(slabs):
        west, east = a[:1], a[a.shape[0] - 1 :]
        first[c : c + 1, :] = jnp.where(even, east, west)
        second[c : c + 1, :] = jnp.where(even, west, east)
        acc = jnp.where(lane // 2 == c, pltpu.roll(a, 2 * c + 1, 1), acc)
    cols[...] = acc


def share_weights(n_gy, period, cuts, shape):
    rows = shape[0] // 2
    me = lax.axis_index("gx") * n_gy + lax.axis_index("gy")
    place = lax.broadcasted_iota(jnp.int32, shape, 0)
    lane = lax.broadcasted_iota(jnp.int32, shape, 1)
    p = (place >= rows).astype(jnp.int32)
    row = me * rows + place - p * rows
    k = 2 * (lane % KX) + p
    j = row % (2 * KX)
    slab = GROUP * (row // (2 * KX)) + lane // KX
    limit = jnp.zeros(shape, jnp.int32)
    for c in range(cuts.shape[0]):
        limit = jnp.where(slab == c, cuts[c], limit)
    keep = ((k % KX) < limit) & ((j % KX) < limit)
    factor = jnp.where(k == 0, 1.0, 2.0) * jnp.where(j == 0, 1.0, 2.0) * (1.0 / math.sqrt(period))
    return jnp.where(keep, factor, 0.0)


def beside_rows(rows):
    return -(-rows // 3)


def share_kernel(n_gx, n_gy, weights, parts, x_back, x_beside, out):
    rows = parts.shape[1] // 2
    total = parts[0]
    for d in range(1, parts.shape[0]):
        total = total + parts[d]
    mismatch = total * weights[...]
    both = jnp.concatenate([mismatch[:rows], mismatch[rows:]], axis=1)
    spare = -rows % 16
    if spare:
        both = jnp.concatenate([both, jnp.zeros((spare, 2 * LANES), jnp.float32)], axis=0)
    slab_lane = lax.broadcasted_iota(jnp.int32, both.shape, 1) % LANES // KX
    chosen = [jnp.where(slab_lane == n, both, 0.0) for n in range(GROUP)]
    inner = two_part_dot(jnp.concatenate(chosen, axis=0), x_back)
    edge_all = two_part_dot(both, x_beside)
    height = rows + spare
    packed = beside_rows(rows)
    width = 2 * GROUP
    cells_x = LANES // GROUP
    slot = lax.broadcasted_iota(jnp.int32, (height, LANES), 1) // cells_x
    spot = lax.broadcasted_iota(jnp.int32, (packed, LANES), 1) // width
    for g in range(n_gx):
        first = g * cells_x // LANES * LANES
        tile = jnp.zeros((height, LANES), jnp.float32)
        for n in range(GROUP):
            piece = inner[n * height : (n + 1) * height, first : first + LANES]
            tile = jnp.where(slot == n, pltpu.roll(piece, (n - g) * cells_x % LANES, 1), tile)
        first = g * width // LANES * LANES
        beside = jnp.zeros((packed, LANES), jnp.float32)
        for m in range(3):
            piece = edge_all[m * packed : (m + 1) * packed, first : first + LANES]
            beside = jnp.where(
                spot == m, pltpu.roll(piece, (m - g) * width % LANES, 1), beside)
        for h in range(n_gy):
            out[g * n_gy + h, :rows, :] = tile[:rows]
            out[g * n_gy + h, rows:, :] = beside


class Halo:
    def __init__(self, row_first, row_second, col_first, col_second, west, east):
        even = is_even("gx")
        west[...] = jnp.where(even, row_second[...], row_first[...])
        east[...] = jnp.where(even, row_first[...], row_second[...])
        self.west, self.east = west, east
        even = is_even("gy")
        north = jnp.where(even, col_first[...], col_second[...])
        south = jnp.where(even, col_second[...], col_first[...])
        shape = north.shape
        lane = lax.broadcasted_iota(jnp.int32, shape, 1)
        self.last = shape[1] - 1
        self.at_first, self.at_last = lane == 0, lane == self.last
        self.columns = jnp.where(
            lane % 2 == 0, pltpu.roll(north, self.last, 1), pltpu.roll(south, 1, 1))

    def rows(self, c):
        return self.west[pl.ds(c, 1), :], self.east[pl.ds(c, 1), :]

    def column(self, c):
        return pltpu.roll(self.columns, self.last - 2 * c, 1)

    def move(self, slab, column, parts):
        centre, to_west, to_east, to_south, to_north = parts
        cells_x = column.shape[0]
        a = slab[PAD : PAD + cells_x]
        return (
            centre * a
            + to_west * slab[PAD - 1 : PAD - 1 + cells_x]
            + to_east * slab[PAD + 1 : PAD + 1 + cells_x]
            + to_south * jnp.where(self.at_first, column, pltpu.roll(a, 1, 1))
            + to_north * jnp.where(self.at_last, column, pltpu.roll(a, self.last, 1))
        )


def place(slab, a, rows):
    cells_x = a.shape[0]
    slab[PAD : PAD + cells_x] = a
    slab[PAD - 1 : PAD] = rows[0]
    slab[PAD + cells_x : PAD + cells_x + 1] = rows[1]


def wind_weights(u, v):
    neighbours = (
        0.1 + 0.1 * jnp.maximum(u, 0.0), 0.1 - 0.1 * jnp.minimum(u, 0.0),
        0.1 + 0.1 * jnp.maximum(v, 0.0), 0.1 - 0.1 * jnp.minimum(v, 0.0),
    )
    centre = 1.0 - (neighbours[0] + neighbours[1] + neighbours[2] + neighbours[3])
    return (centre,) + neighbours


def settling(parts):
    return (parts[0] - 0.3,) + parts[1:]


def above(l, level_total):
    return jnp.where(l + 1 < level_total, 0.3, 0.0).astype(jnp.float32)


def nudge_updates(shares, spread, spread_edges, y_table, nudged, cells_x):
    devices = shares.shape[0]
    rows = spread.shape[0] // devices
    packed = beside_rows(rows)
    width = 2 * GROUP
    for d in range(devices):
        spread[d * rows : (d + 1) * rows] = shares[d, :rows, :]
        edge = shares[d, rows:, :]
        for m in range(3):
            count = min(packed, rows - m * packed)
            if count > 0:
                moved = pltpu.roll(edge, -m * width % LANES, 1) if m else edge
                start = d * rows + m * packed
                spread_edges[start : start + count] = moved[:count]
    groups = nudged // GROUP
    spot_of = lax.broadcasted_iota(jnp.int32, (2 * KX, LANES), 1) // width
    edges = jnp.zeros((2 * KX, LANES), jnp.float32)
    for t in range(groups):
        piece = spread_edges[t * 2 * KX : (t + 1) * 2 * KX]
        edges = jnp.where(spot_of == t, pltpu.roll(piece, t * width, 1) if t else piece, edges)
    update_rows = columns_dot(edges, y_table)
    updates = []
    for t in range(groups):
        update = columns_dot(spread[t * 2 * KX : (t + 1) * 2 * KX], y_table)
        updates += [update[n * cells_x : (n + 1) * cells_x] for n in range(GROUP)]
    return updates, update_rows


def nudged_kernel(n_gy, step, last, level_count, level_total, places, shares, fields, row_first, row_second,
                  col_first, col_second, y_back, order_all, *rest):
    gx, gy = lax.axis_index("gx"), lax.axis_index("gy")
    cells_x, cells_y = fields.shape[1:]
    nudged = 3 * level_count
    if last:
        (plume, source, _, _, fields_all, plume_all, order, slabs, spread, spread_edges, west, east,
         sems, fields_out, plume_out, out_sems) = rest
        extra = []
    else:
        (owners_all, parent_all, x_fwd_all, y_fwd_all, fields_out, winds_out, keep, send,
         order, slabs, spread, spread_edges, west, east, sems,
         owners, parent, x_fwd, y_fwd, turned, work) = rest
        extra = [(owners_all, owners), (x_fwd_all.at[gx], x_fwd), (y_fwd_all.at[gy], y_fwd),
                 (parent_all.at[0, step + 1], parent)]
    copies = fetch_all(sems, [(order_all, order)] + extra)
    halo = Halo(row_first, row_second, col_first, col_second, west, east)
    updates, update_rows = nudge_updates(
        shares, spread, spread_edges, y_back[...], nudged, cells_x)
    copies[0].wait()
    level_at = [order[n] for n in range(level_count)]
    halo_at = level_at if step == 0 else list(range(level_count))
    beside = []
    for k in range(nudged):
        f, n = k // level_count, k % level_count
        a = fields[k]
        before, after = halo.rows(f * level_total + halo_at[n])
        place(slabs.at[k], a + updates[k][:, :cells_y],
              (before + update_rows[2 * k : 2 * k + 1, :cells_y],
               after + update_rows[2 * k + 1 : 2 * k + 2, :cells_y]))
        beside.append(updates[k][:, cells_y:])
    inner = slice(PAD, PAD + cells_x)
    results = [None] * nudged
    sent = []
    for n in range(level_count):
        u, v = slabs[n, inner], slabs[level_count + n, inner]
        parts = wind_weights(u, v)
        for f in range(3):
            k = f * level_count + n
            column = halo.column(f * level_total + halo_at[n]) + beside[k]
            results[k] = halo.move(slabs[k], column, parts)
            fields_out[k] = results[k]
        if not last:
            winds_out[n] = u
            winds_out[level_count + n] = v
            continue
        l = level_at[n]
        c = 3 * level_total + n
        place(slabs.at[nudged + n], plume[n], halo.rows(c))
        settled = halo.move(slabs[nudged + n], halo.column(c), settling(parts))
        plume_out[n] = settled + above(l, level_total) * plume[order[level_total + l + 1]] + source[l]
        pairs = [(fields_out.at[f * level_count + n], fields_all.at[f * level_total + l])
                 for f in range(3)] + [(plume_out.at[n], plume_all.at[l])]
        sent += fetch_all(out_sems.at[pl.ds(4 * n, 4)], pairs)
    if last:
        for copy in sent:
            copy.wait()
        return
    for copy in copies[1:-1]:
        copy.wait()
    emit_modes(results, parent, copies[-1], owners[step + 1] == gx * n_gy + gy, places, x_fwd[...], y_fwd[...],
               keep, send, turned, work)


def others_kernel(step, last, level_count, fields, plume, source, row_first, row_second, col_first,
                  col_second, order, *rest):
    level_total, cells_x, cells_y = plume.shape
    if last:
        fields_all, plume_all, slab, west, east, fields_out, plume_out, out_sems = rest
    else:
        done, winds, fields_out, plume_out, first, second, cols, slab, west, east = rest
    halo = Halo(row_first, row_second, col_first, col_second, west, east)
    level_at = [order[n] for n in range(level_total)]
    kept = level_total - level_count
    sent = []
    results = {}
    for n in range(level_count if last else 0, level_total):
        l = level_at[n]
        m = n - level_count
        if m < 0:
            parts = wind_weights(winds[n], winds[level_count + n])
        else:
            given = [fields[f * kept + m] for f in range(3)]
            parts = wind_weights(given[0], given[1])
            for f in range(3):
                c = f * level_total + n
                beyond = f * level_total + l if step == 0 else c
                place(slab.at[4 * n + f], given[f], halo.rows(beyond))
                results[c] = halo.move(slab[4 * n + f], halo.column(beyond), parts)
                fields_out[f * kept + m] = results[c]
        c = 3 * level_total + n
        beyond = 3 * level_total + l if step == 0 else c
        place(slab.at[4 * n + 3], plume[l] if step == 0 else plume[n], halo.rows(beyond))
        higher = (jnp.minimum(l + 1, level_total - 1) if step == 0 else order[level_total + l + 1])
        results[c] = (halo.move(slab[4 * n + 3], halo.column(beyond), settling(parts))
                      + above(l, level_total) * plume[higher] + source[l])
        plume_out[m if last else n] = results[c]
        if last:
            pairs = [(fields_out.at[f * kept + m], fields_all.at[f * level_total + l])
                     for f in range(3)] + [(plume_out.at[m], plume_all.at[l])]
            sent += fetch_all(out_sems.at[pl.ds(4 * m, 4)], pairs)
    for copy in sent:
        copy.wait()
    if not last:
        for f in range(3):
            for n in range(level_count):
                results[f * level_total + n] = done[f * level_count + n]
        emit_edges([results[c] for c in range(4 * level_total)], first, second, cols)


def exchange(axis, first, second):
    count = lax.axis_size(axis)
    received = []
    for start, data in ((0, first), (1, second)):
        pairs = [(i, i + 1) for i in range(start, count - 1, 2)]
        received.append(lax.ppermute(data, axis, pairs + [(b, a) for a, b in pairs]))
    return received


def local(tables, fields, levels, cuts, parent_modes, owners, plume, source):
    n_gx, n_gy = lax.axis_size("gx"), lax.axis_size("gy")
    devices = n_gx * n_gy
    level_total, cells_x, cells_y = plume.shape
    period = n_gx * cells_x * n_gy * cells_y
    nudged = 3 * levels.shape[0]
    field_rows = 3 * level_total
    total = field_rows + level_total
    rows = -(-(nudged // GROUP * 2 * KX) // devices)
    flat = fields.reshape(field_rows, cells_x, cells_y)
    cuts = cuts.reshape(-1)
    f32 = functools.partial(jax.ShapeDtypeStruct, dtype=jnp.float32)
    x_fwd, y_fwd, y_back, x_back, x_beside = (jnp.asarray(t) for t in tables)

    def vmem(*shape):
        return pltpu.VMEM(shape, jnp.float32)

    def table_space(table):
        return pltpu.VMEM(table.shape[1:], table.dtype)

    def limit(mib):
        return pltpu.CompilerParams(vmem_limit_bytes=mib * 1024 * 1024)

    count = levels.shape[0]
    kept = level_total - count
    half_shapes = [f32((devices // 2, 2 * rows, LANES))] * 2
    places = share_places(n_gx, n_gy)
    order_shape = (3 * level_total,)
    edge_shapes = [f32((total, cells_y)), f32((total, cells_y)), f32((cells_x, 2 * total))]
    levels_space = pltpu.SMEM(levels.shape, jnp.int32)
    owners_space = pltpu.SMEM(owners.shape, jnp.int32)
    order_space = pltpu.SMEM(order_shape, jnp.int32)
    rows_space = vmem(total, cells_y)
    mode_scratch = [vmem(nudged, 4 * KX * KX), table_space(x_fwd),
                    table_space(y_fwd), vmem(nudged, KX, LANES),
                    vmem(devices * rows, 2 * LANES)]
    nudged_scratch = [order_space, vmem(nudged + count, cells_x + 2 * PAD, cells_y),
                      vmem(devices * rows, LANES), vmem(devices * rows, LANES),
                      rows_space, rows_space, pltpu.SemaphoreType.DMA((5,))]
    others_scratch = [vmem(total, cells_x + 2 * PAD, cells_y), rows_space, rows_space]

    def out_scratch(slabs):
        return [vmem(3 * slabs, cells_x, cells_y), vmem(slabs, cells_x, cells_y),
                pltpu.SemaphoreType.DMA((4 * slabs,))]

    keep, send = pl.pallas_call(
        functools.partial(first_kernel, n_gy, level_total, places),
        out_shape=half_shapes,
        in_specs=[HBM] * 6,
        out_specs=[VMEM] * 2,
        scratch_shapes=[levels_space, owners_space, vmem(field_rows, cells_x, cells_y),
                        pltpu.SemaphoreType.DMA((6,))] + mode_scratch,
        compiler_params=limit(8),
        name="first_modes",
    )(*map(in_hbm, (levels, owners, flat, parent_modes, x_fwd, y_fwd)))
    for step in range(STEPS):
        last = step == STEPS - 1
        received = lax.ppermute(send, "gx", [(i, i ^ 1) for i in range(n_gx)])
        if step == 0:
            *edges, weights = pl.pallas_call(
                functools.partial(edge_kernel, n_gy, period),
                out_shape=edge_shapes + [f32((2 * rows, LANES))],
                in_specs=[SMEM, VMEM, VMEM],
                out_specs=[VMEM] * 4,
                compiler_params=limit(8),
                name="edges",
            )(cuts, flat, plume)
        else:
            others, plume, *edges = pl.pallas_call(
                functools.partial(others_kernel, 0, False, count),
                out_shape=[f32((3 * kept, cells_x, cells_y)), f32(plume.shape)] + edge_shapes,
                in_specs=[VMEM] * 7 + [SMEM] + [VMEM] * 2,
                out_specs=[VMEM] * 5,
                scratch_shapes=others_scratch,
                compiler_params=limit(8),
                name="inner_others",
            )(others, plume, source, *halo, order, flat, winds)
        received, *edges = lax.optimization_barrier((received, *edges))
        to_first, to_second, cols = edges
        modes = pl.pallas_call(
            add_kernel,
            out_shape=half_shapes[0],
            in_specs=[VMEM] * 2,
            out_specs=VMEM,
            compiler_params=limit(4),
            name="add_cores",
        )(keep, received)
        col_first, col_second = exchange("gy", cols, cols)
        parts = lax.all_to_all(modes, AXES, 0, 0, axis_index_groups=core_groups(n_gx, n_gy),
                               tiled=True)
        parts, col_first, col_second = lax.optimization_barrier((parts, col_first, col_second))
        share = pl.pallas_call(
            functools.partial(share_kernel, n_gx, n_gy),
            out_shape=f32((devices, rows + beside_rows(rows), LANES)),
            in_specs=[VMEM] * 4,
            out_specs=VMEM,
            compiler_params=limit(8),
            name="share_sum",
        )(weights, parts, x_back, x_beside)
        share, to_first, to_second = lax.optimization_barrier((share, to_first, to_second))
        row_first, row_second = exchange("gx", to_first, to_second)
        halo = [row_first, row_second, col_first, col_second]
        if step == 0:
            share, levels = lax.optimization_barrier((share, levels))
            flat, others, y_back, order = pl.pallas_call(
                functools.partial(prepare_kernel, level_total),
                out_shape=[f32((3 * count, cells_x, cells_y)), f32((3 * kept, cells_x, cells_y)),
                           jax.ShapeDtypeStruct(y_back.shape[1:], y_back.dtype),
                           jax.ShapeDtypeStruct(order_shape, jnp.int32)],
                in_specs=[SMEM, VMEM, HBM],
                out_specs=[VMEM] * 3 + [SMEM],
                scratch_shapes=[pltpu.SemaphoreType.DMA((1,))],
                compiler_params=limit(8),
                name="prepare",
            )(levels, flat, in_hbm(y_back))
        shares = lax.all_to_all(share, AXES, 0, 0, tiled=True)
        if last:
            final = pl.pallas_call(
                functools.partial(others_kernel, step, True, count),
                out_shape=[f32((field_rows, cells_x, cells_y)), f32(plume.shape)],
                in_specs=[VMEM] * 7 + [SMEM],
                out_specs=[HBM] * 2,
                scratch_shapes=others_scratch + out_scratch(kept),
                compiler_params=limit(8),
                name="last_others",
            )(others, plume, source, *halo, order)
            flat, plume = pl.pallas_call(
                functools.partial(nudged_kernel, n_gy, step, True, count, level_total, None),
                out_shape=[f32((field_rows, cells_x, cells_y)), f32(plume.shape)],
                in_specs=[VMEM] * 7 + [HBM] + [VMEM] * 2 + [HBM] * 2,
                out_specs=[HBM] * 2,
                scratch_shapes=nudged_scratch + out_scratch(count),
                input_output_aliases={10: 0, 11: 1},
                compiler_params=limit(12),
                name="last_nudged",
            )(shares, flat, *halo, y_back, in_hbm(order), plume, source, *final)
        else:
            flat, winds, keep, send = pl.pallas_call(
                functools.partial(nudged_kernel, n_gy, step, False, count, level_total, places),
                out_shape=[f32((nudged, cells_x, cells_y)), f32((2 * count, cells_x, cells_y))]
                + half_shapes,
                in_specs=[VMEM] * 7 + [HBM] * 5,
                out_specs=[VMEM] * 4,
                scratch_shapes=nudged_scratch + [owners_space] + mode_scratch,
                compiler_params=limit(12),
                name="inner_nudged",
            )(shares, flat, *halo, y_back, in_hbm(order),
              *map(in_hbm, (owners, parent_modes, x_fwd, y_fwd)))
    return flat.reshape(fields.shape), plume


def solution(mesh):
    in_specs = (
        P(None, None, "gx", "gy"),
        P(),
        P(),
        P(("gx", "gy"), None, None, None),
        P(),
        P(None, "gx", "gy"),
        P(None, "gx", "gy"),
    )
    out_specs = (P(None, None, "gx", "gy"), P(None, "gx", "gy"))
    n_gx, n_gy = mesh.shape["gx"], mesh.shape["gy"]

    def whole(fields, levels, cuts, parent_modes, owners, plume, source):
        tables = build_tables(n_gx, n_gy, plume.shape[1] // n_gx, plume.shape[2] // n_gy)
        return jax.shard_map(
            functools.partial(local, tables), mesh=mesh, in_specs=in_specs, out_specs=out_specs,
            check_vma=False,
        )(fields, levels, cuts, parent_modes, owners, plume, source)

    return whole
```

```python
import functools
import math

import jax
import jax.numpy as jnp
import ml_dtypes
import numpy as np
from jax import lax
from jax.experimental import pallas as pl
from jax.experimental.pallas import tpu as pltpu
from jax.sharding import PartitionSpec as P

KX = 32
STEPS = 2
GROUP = 4
LANES = GROUP * KX
PAD = 8
VMEM = pl.BlockSpec(memory_space=pltpu.VMEM)
SMEM = pl.BlockSpec(memory_space=pltpu.SMEM)
HBM = pl.BlockSpec(memory_space=pltpu.HBM)
AXES = ("gx", "gy")


def in_hbm(array):
    return pltpu.with_memory_space_constraint(array, pltpu.HBM)


def wave_table(positions, period):
    wavenum = np.arange(KX)[:, None]
    phase = (wavenum * positions[None, :] % period) * (2.0 * math.pi / period)
    inside = (positions >= 0) & (positions < period)
    return np.concatenate([np.cos(phase), np.sin(phase)], axis=0) * inside[None, :]


def split(a):
    head = a.astype(jnp.bfloat16)
    return head, (a - head.astype(jnp.float32)).astype(jnp.bfloat16)


def split_table(table, axis, order):
    head = table.astype(ml_dtypes.bfloat16)
    rest = (table - head.astype(np.float64)).astype(ml_dtypes.bfloat16)
    return np.concatenate([head if part == "h" else rest for part in order], axis=axis)


def per_slab(table):
    return np.kron(np.eye(GROUP), table)


def build_tables(n_gx, n_gy, cells_x, cells_y):
    period_x, period_y = n_gx * cells_x, n_gy * cells_y
    scaling = 1.0 / math.sqrt(period_x * period_y)
    parity = [np.arange(p, 2 * KX, 2) for p in range(2)]
    x_fwd, y_fwd, y_back, inner, outer = [], [], [], [], []
    for g in range(n_gx):
        first = g * cells_x
        table = wave_table(first + np.arange(cells_x), period_x)
        x_fwd.append(split_table(
            np.concatenate([per_slab(table[rows].T) for rows in parity], axis=1), 0, "hhl"))
        beside = wave_table(np.array([first - 1, first + cells_x]), period_x)
        inner.append(np.concatenate([np.tile(table[rows], (GROUP, 1)) for rows in parity], axis=0))
        outer.append(np.concatenate([per_slab(beside[rows]) for rows in parity], axis=0))
    spare = -(2 * GROUP * n_gx) % LANES
    x_back = np.concatenate(inner, axis=1)
    x_beside = np.concatenate(outer + [np.zeros((2 * LANES, spare))], axis=1)
    for g in range(n_gy):
        first = g * cells_y
        table = wave_table(first + np.arange(cells_y), period_y)
        edge = np.zeros((2 * KX, cells_y))
        edge[:, [0, -1]] = wave_table(np.array([first - 1, first + cells_y]), period_y)
        y_fwd.append(split_table(table * scaling, 1, "hlh"))
        y_back.append(split_table(np.concatenate([table, edge], axis=1), 0, "hhl"))
    return [np.stack(x_fwd), np.stack(y_fwd), np.stack(y_back),
            split_table(x_back, 0, "hl"), split_table(x_beside, 0, "hl")]


def data_dot(a, table):
    head, rest = split(a)
    return jnp.dot(
        jnp.concatenate([head, rest, head], axis=1), table, preferred_element_type=jnp.float32
    )


def two_part_dot(a, table):
    head, rest = split(a)
    depth = a.shape[1]
    heads = jnp.dot(
        jnp.concatenate([head, rest], axis=0), table[:depth], preferred_element_type=jnp.float32)
    rests = jnp.dot(head, table[depth:], preferred_element_type=jnp.float32)
    return heads[: a.shape[0]] + heads[a.shape[0] :] + rests


def columns_dot(a, table):
    head, rest = split(a)
    stacked = jnp.concatenate([head, rest, head], axis=0)
    return lax.dot_general(
        stacked, table, (((0,), (0,)), ((), ())), preferred_element_type=jnp.float32)


def core():
    return lax.rem(lax.axis_index("gx"), 2)


def ranking(n_gx, n_gy):
    return sorted(range(n_gx * n_gy), key=lambda d: (-abs(2 * (d % n_gy) - (n_gy - 1)), d))


def core_groups(n_gx, n_gy):
    return [[d for d in ranking(n_gx, n_gy) if d // n_gy % 2 == c] for c in range(2)]


def share_places(n_gx, n_gy):
    places = {}
    for c, group in enumerate(core_groups(n_gx, n_gy)):
        places.update({d: c * len(group) + i for i, d in enumerate(group)})
    return [places[d] for d in range(n_gx * n_gy)]


def emit_modes(chosen, parent, parent_copy, is_owner, places, x_fwd, y_fwd, keep, send, turned, work):
    devices, rows = len(places), keep.shape[1] // 2
    slabs = parent.shape[0]
    groups = slabs // GROUP
    head, rest = split(jnp.concatenate(chosen, axis=0))
    half = lax.dot_general(
        y_fwd, jnp.concatenate([head, head, rest], axis=1), (((1,), (1,)), ((), ())),
        preferred_element_type=jnp.float32)
    half = jnp.concatenate([half[:, t * LANES : (t + 1) * LANES] for t in range(groups)], axis=0)
    count = groups * 2 * KX
    work[0:count] = -data_dot(half, x_fwd)
    if count < devices * rows:
        work[count:] = jnp.zeros((devices * rows - count, 2 * LANES), jnp.float32)

    parent_copy.wait()

    @pl.when(is_owner)
    def _():
        for i in range(KX):
            turned[:, i, :] = parent[:, i * LANES : (i + 1) * LANES]
        for t in range(groups):
            block = turned[t * GROUP : (t + 1) * GROUP].reshape(LANES, LANES).T
            span = slice(t * 2 * KX, (t + 1) * 2 * KX)
            for p in range(2):
                work[span, p * LANES : (p + 1) * LANES] += block[p * 2 * KX : (p + 1) * 2 * KX]

    count = devices // 2
    for mine in range(2):
        @pl.when(core() == mine)
        def _(mine=mine):
            for d in range(devices):
                half = keep if places[d] // count == mine else send
                for p in range(2):
                    half[places[d] % count, p * rows : (p + 1) * rows, :] = work[
                        d * rows : (d + 1) * rows, p * LANES : (p + 1) * LANES]


def add_kernel(kept, received, out):
    out[...] = kept[...] + received[...]


def fetch_all(sems, pairs):
    copies = [pltpu.make_async_copy(a, b, sems.at[i]) for i, (a, b) in enumerate(pairs)]
    for copy in copies:
        copy.start()
    return copies


def slab_of(levels, c, level_count, level_total):
    return (c // level_count) * level_total + levels[c % level_count]


def first_kernel(n_gy, level_total, places, levels_all, owners_all, fields_all, parent_all,
                 x_fwd_all, y_fwd_all, keep, send, levels, owners, fields, sems, parent, x_fwd, y_fwd,
                 turned, work):
    gx, gy = lax.axis_index("gx"), lax.axis_index("gy")
    copies = fetch_all(sems, [
        (levels_all, levels), (owners_all, owners), (fields_all, fields),
        (x_fwd_all.at[gx], x_fwd), (y_fwd_all.at[gy], y_fwd), (parent_all.at[0, 0], parent)])
    for copy in copies[:-1]:
        copy.wait()
    level_count = parent.shape[0] // 3
    emit_modes(
        [fields[slab_of(levels, c, level_count, level_total)] for c in range(parent.shape[0])],
        parent, copies[-1], owners[0] == gx * n_gy + gy, places, x_fwd[...], y_fwd[...], keep, send,
        turned, work,
    )


def is_even(axis):
    return lax.rem(lax.axis_index(axis), 2) == 0


def edge_kernel(n_gy, period, cuts, fields, plume, first, second, cols, weights):
    weights[...] = share_weights(n_gy, period, cuts, weights.shape)
    slabs = [fields[c] for c in range(fields.shape[0])]
    emit_edges(slabs + [plume[l] for l in range(plume.shape[0])], first, second, cols)


def prepare_kernel(level_total, levels, fields, y_back_all, nudged, others, y_back, order, sems):
    copies = fetch_all(sems, [(y_back_all.at[lax.axis_index("gy")], y_back)])
    count = levels.shape[0]
    for n in range(count):
        order[n] = levels[n]
    spot = jnp.int32(count)
    for l in range(level_total):
        found = levels[0] == l
        for n in range(1, count):
            found = found | (levels[n] == l)
        order[spot] = jnp.int32(l)
        spot = spot + jnp.where(found, 0, 1)
    chosen = [order[n] for n in range(level_total)]
    for n in range(level_total, order.shape[0]):
        order[n] = jnp.int32(0)
    for n in range(level_total):
        order[level_total + chosen[n]] = jnp.int32(n)
    slabs = [fields[f * level_total + l] for f in range(3) for l in chosen]
    kept = level_total - count
    for c, a in enumerate(slabs):
        f, n = c // level_total, c % level_total
        if n < count:
            nudged[f * count + n] = a
        else:
            others[f * kept + n - count] = a
    for copy in copies:
        copy.wait()


def emit_edges(slabs, first, second, cols):
    even = is_even("gx")
    lane = lax.broadcasted_iota(jnp.int32, cols.shape, 1)
    acc = jnp.zeros(cols.shape, jnp.float32)
    for c, a in enumerate(slabs):
        west, east = a[:1], a[a.shape[0] - 1 :]
        first[c : c + 1, :] = jnp.where(even, east, west)
        second[c : c + 1, :] = jnp.where(even, west, east)
        acc = jnp.where(lane // 2 == c, pltpu.roll(a, 2 * c + 1, 1), acc)
    cols[...] = acc


def share_weights(n_gy, period, cuts, shape):
    rows = shape[0] // 2
    me = lax.axis_index("gx") * n_gy + lax.axis_index("gy")
    place = lax.broadcasted_iota(jnp.int32, shape, 0)
    lane = lax.broadcasted_iota(jnp.int32, shape, 1)
    p = (place >= rows).astype(jnp.int32)
    row = me * rows + place - p * rows
    k = 2 * (lane % KX) + p
    j = row % (2 * KX)
    slab = GROUP * (row // (2 * KX)) + lane // KX
    limit = jnp.zeros(shape, jnp.int32)
    for c in range(cuts.shape[0]):
        limit = jnp.where(slab == c, cuts[c], limit)
    keep = ((k % KX) < limit) & ((j % KX) < limit)
    factor = jnp.where(k == 0, 1.0, 2.0) * jnp.where(j == 0, 1.0, 2.0) * (1.0 / math.sqrt(period))
    return jnp.where(keep, factor, 0.0)


def beside_rows(rows):
    return -(-rows // 3)


def share_kernel(n_gx, n_gy, weights, parts, x_back, x_beside, out):
    rows = parts.shape[1] // 2
    total = parts[0]
    for d in range(1, parts.shape[0]):
        total = total + parts[d]
    mismatch = total * weights[...]
    both = jnp.concatenate([mismatch[:rows], mismatch[rows:]], axis=1)
    spare = -rows % 16
    if spare:
        both = jnp.concatenate([both, jnp.zeros((spare, 2 * LANES), jnp.float32)], axis=0)
    slab_lane = lax.broadcasted_iota(jnp.int32, both.shape, 1) % LANES // KX
    chosen = [jnp.where(slab_lane == n, both, 0.0) for n in range(GROUP)]
    inner = two_part_dot(jnp.concatenate(chosen, axis=0), x_back)
    edge_all = two_part_dot(both, x_beside)
    height = rows + spare
    packed = beside_rows(rows)
    width = 2 * GROUP
    cells_x = LANES // GROUP
    slot = lax.broadcasted_iota(jnp.int32, (height, LANES), 1) // cells_x
    spot = lax.broadcasted_iota(jnp.int32, (packed, LANES), 1) // width
    for g in range(n_gx):
        first = g * cells_x // LANES * LANES
        tile = jnp.zeros((height, LANES), jnp.float32)
        for n in range(GROUP):
            piece = inner[n * height : (n + 1) * height, first : first + LANES]
            tile = jnp.where(slot == n, pltpu.roll(piece, (n - g) * cells_x % LANES, 1), tile)
        first = g * width // LANES * LANES
        beside = jnp.zeros((packed, LANES), jnp.float32)
        for m in range(3):
            piece = edge_all[m * packed : (m + 1) * packed, first : first + LANES]
            beside = jnp.where(
                spot == m, pltpu.roll(piece, (m - g) * width % LANES, 1), beside)
        for h in range(n_gy):
            out[g * n_gy + h, :rows, :] = tile[:rows]
            out[g * n_gy + h, rows:, :] = beside


class Halo:
    def __init__(self, row_first, row_second, col_first, col_second, west, east):
        even = is_even("gx")
        west[...] = jnp.where(even, row_second[...], row_first[...])
        east[...] = jnp.where(even, row_first[...], row_second[...])
        self.west, self.east = west, east
        even = is_even("gy")
        north = jnp.where(even, col_first[...], col_second[...])
        south = jnp.where(even, col_second[...], col_first[...])
        shape = north.shape
        lane = lax.broadcasted_iota(jnp.int32, shape, 1)
        self.last = shape[1] - 1
        self.at_first, self.at_last = lane == 0, lane == self.last
        self.columns = jnp.where(
            lane % 2 == 0, pltpu.roll(north, self.last, 1), pltpu.roll(south, 1, 1))

    def rows(self, c):
        return self.west[pl.ds(c, 1), :], self.east[pl.ds(c, 1), :]

    def column(self, c):
        return pltpu.roll(self.columns, self.last - 2 * c, 1)

    def move(self, slab, column, parts):
        centre, to_west, to_east, to_south, to_north = parts
        cells_x = column.shape[0]
        a = slab[PAD : PAD + cells_x]
        return (
            centre * a
            + to_west * slab[PAD - 1 : PAD - 1 + cells_x]
            + to_east * slab[PAD + 1 : PAD + 1 + cells_x]
            + to_south * jnp.where(self.at_first, column, pltpu.roll(a, 1, 1))
            + to_north * jnp.where(self.at_last, column, pltpu.roll(a, self.last, 1))
        )


def place(slab, a, rows):
    cells_x = a.shape[0]
    slab[PAD : PAD + cells_x] = a
    slab[PAD - 1 : PAD] = rows[0]
    slab[PAD + cells_x : PAD + cells_x + 1] = rows[1]


def wind_weights(u, v):
    neighbours = (
        0.1 + 0.1 * jnp.maximum(u, 0.0), 0.1 - 0.1 * jnp.minimum(u, 0.0),
        0.1 + 0.1 * jnp.maximum(v, 0.0), 0.1 - 0.1 * jnp.minimum(v, 0.0),
    )
    centre = 1.0 - (neighbours[0] + neighbours[1] + neighbours[2] + neighbours[3])
    return (centre,) + neighbours


def settling(parts):
    return (parts[0] - 0.3,) + parts[1:]


def above(l, level_total):
    return jnp.where(l + 1 < level_total, 0.3, 0.0).astype(jnp.float32)


def nudge_updates(shares, spread, spread_edges, y_table, nudged, cells_x):
    devices = shares.shape[0]
    rows = spread.shape[0] // devices
    packed = beside_rows(rows)
    width = 2 * GROUP
    for d in range(devices):
        spread[d * rows : (d + 1) * rows] = shares[d, :rows, :]
        edge = shares[d, rows:, :]
        for m in range(3):
            count = min(packed, rows - m * packed)
            if count > 0:
                moved = pltpu.roll(edge, -m * width % LANES, 1) if m else edge
                start = d * rows + m * packed
                spread_edges[start : start + count] = moved[:count]
    groups = nudged // GROUP
    spot_of = lax.broadcasted_iota(jnp.int32, (2 * KX, LANES), 1) // width
    edges = jnp.zeros((2 * KX, LANES), jnp.float32)
    for t in range(groups):
        piece = spread_edges[t * 2 * KX : (t + 1) * 2 * KX]
        edges = jnp.where(spot_of == t, pltpu.roll(piece, t * width, 1) if t else piece, edges)
    update_rows = columns_dot(edges, y_table)
    updates = []
    for t in range(groups):
        update = columns_dot(spread[t * 2 * KX : (t + 1) * 2 * KX], y_table)
        updates += [update[n * cells_x : (n + 1) * cells_x] for n in range(GROUP)]
    return updates, update_rows


def nudged_kernel(n_gy, step, last, level_count, level_total, places, shares, fields, row_first, row_second,
                  col_first, col_second, y_back, order_all, *rest):
    gx, gy = lax.axis_index("gx"), lax.axis_index("gy")
    cells_x, cells_y = fields.shape[1:]
    nudged = 3 * level_count
    if last:
        (plume, source, _, _, fields_all, plume_all, order, slabs, spread, spread_edges, west, east,
         sems, fields_out, plume_out, out_sems) = rest
        extra = []
    else:
        (owners_all, parent_all, x_fwd_all, y_fwd_all, fields_out, winds_out, keep, send,
         order, slabs, spread, spread_edges, west, east, sems,
         owners, parent, x_fwd, y_fwd, turned, work) = rest
        extra = [(owners_all, owners), (x_fwd_all.at[gx], x_fwd), (y_fwd_all.at[gy], y_fwd),
                 (parent_all.at[0, step + 1], parent)]
    copies = fetch_all(sems, [(order_all, order)] + extra)
    halo = Halo(row_first, row_second, col_first, col_second, west, east)
    updates, update_rows = nudge_updates(
        shares, spread, spread_edges, y_back[...], nudged, cells_x)
    copies[0].wait()
    level_at = [order[n] for n in range(level_count)]
    halo_at = level_at if step == 0 else list(range(level_count))
    beside = []
    for k in range(nudged):
        f, n = k // level_count, k % level_count
        a = fields[k]
        before, after = halo.rows(f * level_total + halo_at[n])
        place(slabs.at[k], a + updates[k][:, :cells_y],
              (before + update_rows[2 * k : 2 * k + 1, :cells_y],
               after + update_rows[2 * k + 1 : 2 * k + 2, :cells_y]))
        beside.append(updates[k][:, cells_y:])
    inner = slice(PAD, PAD + cells_x)
    results = [None] * nudged
    sent = []
    for n in range(level_count):
        u, v = slabs[n, inner], slabs[level_count + n, inner]
        parts = wind_weights(u, v)
        for f in range(3):
            k = f * level_count + n
            column = halo.column(f * level_total + halo_at[n]) + beside[k]
            results[k] = halo.move(slabs[k], column, parts)
            fields_out[k] = results[k]
        if not last:
            winds_out[n] = u
            winds_out[level_count + n] = v
            continue
        l = level_at[n]
        c = 3 * level_total + n
        place(slabs.at[nudged + n], plume[n], halo.rows(c))
        settled = halo.move(slabs[nudged + n], halo.column(c), settling(parts))
        plume_out[n] = settled + above(l, level_total) * plume[order[level_total + l + 1]] + source[l]
        pairs = [(fields_out.at[f * level_count + n], fields_all.at[f * level_total + l])
                 for f in range(3)] + [(plume_out.at[n], plume_all.at[l])]
        sent += fetch_all(out_sems.at[pl.ds(4 * n, 4)], pairs)
    if last:
        for copy in sent:
            copy.wait()
        return
    for copy in copies[1:-1]:
        copy.wait()
    emit_modes(results, parent, copies[-1], owners[step + 1] == gx * n_gy + gy, places, x_fwd[...], y_fwd[...],
               keep, send, turned, work)


def others_kernel(step, last, level_count, fields, plume, source, row_first, row_second, col_first,
                  col_second, order, *rest):
    level_total, cells_x, cells_y = plume.shape
    if last:
        fields_all, plume_all, slab, west, east, fields_out, plume_out, out_sems = rest
    else:
        done, winds, fields_out, plume_out, first, second, cols, slab, west, east = rest
    halo = Halo(row_first, row_second, col_first, col_second, west, east)
    level_at = [order[n] for n in range(level_total)]
    kept = level_total - level_count
    sent = []
    results = {}
    for n in range(level_count if last else 0, level_total):
        l = level_at[n]
        m = n - level_count
        if m < 0:
            parts = wind_weights(winds[n], winds[level_count + n])
        else:
            given = [fields[f * kept + m] for f in range(3)]
            parts = wind_weights(given[0], given[1])
            for f in range(3):
                c = f * level_total + n
                beyond = f * level_total + l if step == 0 else c
                place(slab.at[4 * n + f], given[f], halo.rows(beyond))
                results[c] = halo.move(slab[4 * n + f], halo.column(beyond), parts)
                fields_out[f * kept + m] = results[c]
        c = 3 * level_total + n
        beyond = 3 * level_total + l if step == 0 else c
        place(slab.at[4 * n + 3], plume[l] if step == 0 else plume[n], halo.rows(beyond))
        higher = (jnp.minimum(l + 1, level_total - 1) if step == 0 else order[level_total + l + 1])
        results[c] = (halo.move(slab[4 * n + 3], halo.column(beyond), settling(parts))
                      + above(l, level_total) * plume[higher] + source[l])
        plume_out[m if last else n] = results[c]
        if last:
            pairs = [(fields_out.at[f * kept + m], fields_all.at[f * level_total + l])
                     for f in range(3)] + [(plume_out.at[m], plume_all.at[l])]
            sent += fetch_all(out_sems.at[pl.ds(4 * m, 4)], pairs)
    for copy in sent:
        copy.wait()
    if not last:
        for f in range(3):
            for n in range(level_count):
                results[f * level_total + n] = done[f * level_count + n]
        emit_edges([results[c] for c in range(4 * level_total)], first, second, cols)


def exchange(axis, first, second):
    count = lax.axis_size(axis)
    received = []
    for start, data in ((0, first), (1, second)):
        pairs = [(i, i + 1) for i in range(start, count - 1, 2)]
        received.append(lax.ppermute(data, axis, pairs + [(b, a) for a, b in pairs]))
    return received


def local(tables, fields, levels, cuts, parent_modes, owners, plume, source):
    n_gx, n_gy = lax.axis_size("gx"), lax.axis_size("gy")
    devices = n_gx * n_gy
    level_total, cells_x, cells_y = plume.shape
    period = n_gx * cells_x * n_gy * cells_y
    nudged = 3 * levels.shape[0]
    field_rows = 3 * level_total
    total = field_rows + level_total
    rows = -(-(nudged // GROUP * 2 * KX) // devices)
    flat = fields.reshape(field_rows, cells_x, cells_y)
    cuts = cuts.reshape(-1)
    f32 = functools.partial(jax.ShapeDtypeStruct, dtype=jnp.float32)
    x_fwd, y_fwd, y_back, x_back, x_beside = (jnp.asarray(t) for t in tables)

    def vmem(*shape):
        return pltpu.VMEM(shape, jnp.float32)

    def table_space(table):
        return pltpu.VMEM(table.shape[1:], table.dtype)

    def limit(mib):
        return pltpu.CompilerParams(vmem_limit_bytes=mib * 1024 * 1024)

    count = levels.shape[0]
    kept = level_total - count
    half_shapes = [f32((devices // 2, 2 * rows, LANES))] * 2
    places = share_places(n_gx, n_gy)
    order_shape = (3 * level_total,)
    edge_shapes = [f32((total, cells_y)), f32((total, cells_y)), f32((cells_x, 2 * total))]
    levels_space = pltpu.SMEM(levels.shape, jnp.int32)
    owners_space = pltpu.SMEM(owners.shape, jnp.int32)
    order_space = pltpu.SMEM(order_shape, jnp.int32)
    rows_space = vmem(total, cells_y)
    mode_scratch = [vmem(nudged, 4 * KX * KX), table_space(x_fwd),
                    table_space(y_fwd), vmem(nudged, KX, LANES),
                    vmem(devices * rows, 2 * LANES)]
    nudged_scratch = [order_space, vmem(nudged + count, cells_x + 2 * PAD, cells_y),
                      vmem(devices * rows, LANES), vmem(devices * rows, LANES),
                      rows_space, rows_space, pltpu.SemaphoreType.DMA((5,))]
    others_scratch = [vmem(total, cells_x + 2 * PAD, cells_y), rows_space, rows_space]

    def out_scratch(slabs):
        return [vmem(3 * slabs, cells_x, cells_y), vmem(slabs, cells_x, cells_y),
                pltpu.SemaphoreType.DMA((4 * slabs,))]

    keep, send = pl.pallas_call(
        functools.partial(first_kernel, n_gy, level_total, places),
        out_shape=half_shapes,
        in_specs=[HBM] * 6,
        out_specs=[VMEM] * 2,
        scratch_shapes=[levels_space, owners_space, vmem(field_rows, cells_x, cells_y),
                        pltpu.SemaphoreType.DMA((6,))] + mode_scratch,
        compiler_params=limit(8),
        name="first_modes",
    )(*map(in_hbm, (levels, owners, flat, parent_modes, x_fwd, y_fwd)))
    for step in range(STEPS):
        last = step == STEPS - 1
        received = lax.ppermute(send, "gx", [(i, i ^ 1) for i in range(n_gx)])
        if step == 0:
            *edges, weights = pl.pallas_call(
                functools.partial(edge_kernel, n_gy, period),
                out_shape=edge_shapes + [f32((2 * rows, LANES))],
                in_specs=[SMEM, VMEM, VMEM],
                out_specs=[VMEM] * 4,
                compiler_params=limit(8),
                name="edges",
            )(cuts, flat, plume)
        else:
            others, plume, *edges = pl.pallas_call(
                functools.partial(others_kernel, 0, False, count),
                out_shape=[f32((3 * kept, cells_x, cells_y)), f32(plume.shape)] + edge_shapes,
                in_specs=[VMEM] * 7 + [SMEM] + [VMEM] * 2,
                out_specs=[VMEM] * 5,
                scratch_shapes=others_scratch,
                compiler_params=limit(8),
                name="inner_others",
            )(others, plume, source, *halo, order, flat, winds)
        received, *edges = lax.optimization_barrier((received, *edges))
        to_first, to_second, cols = edges
        modes = pl.pallas_call(
            add_kernel,
            out_shape=half_shapes[0],
            in_specs=[VMEM] * 2,
            out_specs=VMEM,
            compiler_params=limit(4),
            name="add_cores",
        )(keep, received)
        col_first, col_second = exchange("gy", cols, cols)
        parts = lax.all_to_all(modes, AXES, 0, 0, axis_index_groups=core_groups(n_gx, n_gy),
                               tiled=True)
        parts, col_first, col_second = lax.optimization_barrier((parts, col_first, col_second))
        share = pl.pallas_call(
            functools.partial(share_kernel, n_gx, n_gy),
            out_shape=f32((devices, rows + beside_rows(rows), LANES)),
            in_specs=[VMEM] * 4,
            out_specs=VMEM,
            compiler_params=limit(8),
            name="share_sum",
        )(weights, parts, x_back, x_beside)
        share, to_first, to_second = lax.optimization_barrier((share, to_first, to_second))
        row_first, row_second = exchange("gx", to_first, to_second)
        halo = [row_first, row_second, col_first, col_second]
        if step == 0:
            share, levels = lax.optimization_barrier((share, levels))
            flat, others, y_back, order = pl.pallas_call(
                functools.partial(prepare_kernel, level_total),
                out_shape=[f32((3 * count, cells_x, cells_y)), f32((3 * kept, cells_x, cells_y)),
                           jax.ShapeDtypeStruct(y_back.shape[1:], y_back.dtype),
                           jax.ShapeDtypeStruct(order_shape, jnp.int32)],
                in_specs=[SMEM, VMEM, HBM],
                out_specs=[VMEM] * 3 + [SMEM],
                scratch_shapes=[pltpu.SemaphoreType.DMA((1,))],
                compiler_params=limit(8),
                name="prepare",
            )(levels, flat, in_hbm(y_back))
        shares = lax.all_to_all(share, AXES, 0, 0, tiled=True)
        if last:
            final = pl.pallas_call(
                functools.partial(others_kernel, step, True, count),
                out_shape=[f32((field_rows, cells_x, cells_y)), f32(plume.shape)],
                in_specs=[VMEM] * 7 + [SMEM],
                out_specs=[HBM] * 2,
                scratch_shapes=others_scratch + out_scratch(kept),
                compiler_params=limit(8),
                name="last_others",
            )(others, plume, source, *halo, order)
            flat, plume = pl.pallas_call(
                functools.partial(nudged_kernel, n_gy, step, True, count, level_total, None),
                out_shape=[f32((field_rows, cells_x, cells_y)), f32(plume.shape)],
                in_specs=[VMEM] * 7 + [HBM] + [VMEM] * 2 + [HBM] * 2,
                out_specs=[HBM] * 2,
                scratch_shapes=nudged_scratch + out_scratch(count),
                input_output_aliases={10: 0, 11: 1},
                compiler_params=limit(12),
                name="last_nudged",
            )(shares, flat, *halo, y_back, in_hbm(order), plume, source, *final)
        else:
            flat, winds, keep, send = pl.pallas_call(
                functools.partial(nudged_kernel, n_gy, step, False, count, level_total, places),
                out_shape=[f32((nudged, cells_x, cells_y)), f32((2 * count, cells_x, cells_y))]
                + half_shapes,
                in_specs=[VMEM] * 7 + [HBM] * 5,
                out_specs=[VMEM] * 4,
                scratch_shapes=nudged_scratch + [owners_space] + mode_scratch,
                compiler_params=limit(12),
                name="inner_nudged",
            )(shares, flat, *halo, y_back, in_hbm(order),
              *map(in_hbm, (owners, parent_modes, x_fwd, y_fwd)))
    return flat.reshape(fields.shape), plume


def solution(mesh):
    in_specs = (
        P(None, None, "gx", "gy"),
        P(),
        P(),
        P(("gx", "gy"), None, None, None),
        P(),
        P(None, "gx", "gy"),
        P(None, "gx", "gy"),
    )
    out_specs = (P(None, None, "gx", "gy"), P(None, "gx", "gy"))
    n_gx, n_gy = mesh.shape["gx"], mesh.shape["gy"]

    def whole(fields, levels, cuts, parent_modes, owners, plume, source):
        tables = build_tables(n_gx, n_gy, plume.shape[1] // n_gx, plume.shape[2] // n_gy)
        return jax.shard_map(
            functools.partial(local, tables), mesh=mesh, in_specs=in_specs, out_specs=out_specs,
            check_vma=False,
        )(fields, levels, cuts, parent_modes, owners, plume, source)

    return whole
```
